32 devices in a mesh: fsdp: 4 (over x, core), ctx: 8 (over z, y).
Axes of the slice: x: 2, y: 2, z: 4, core: 2. Of those that a mesh axis runs over, the one named last changes fastest.
Arguments:
- history: bfloat16 [9, 4, 2048, 2048], P(None, 'fsdp', 'ctx'), may hold values from -6 to 6
- dense_mix: float32 [4, 9, 4, 2048], P(None, None, 'fsdp', 'ctx'), may hold values from -2.5 to 2.5
- doc_starts: int32 [4, 8], P('fsdp'), may hold values from 0 to 2048, as said below
- norm_gain: float32 [4, 2048], P(None, ('fsdp', 'ctx')), may hold values from 0.25 to 1.75
- norm_bias: float32 [4, 2048], P(None, ('fsdp', 'ctx')), may hold values from -1.25 to 1.25
- query_key_value_weight: bfloat16 [2048, 3, 2048], P(('fsdp', 'ctx')), may hold values from -0.125 to 0.125
- query_key_value_bias: float32 [3, 2048], P(None, ('fsdp', 'ctx')), may hold values from -1.75 to 1.75
- out_weight: bfloat16 [2048, 2048], P(('fsdp', 'ctx')), may hold values from -0.5 to 0.5
- out_bias: float32 [2048], P(('fsdp', 'ctx')), may hold values from -1.75 to 1.75
- up_weight: bfloat16 [2048, 8192], P(('fsdp', 'ctx')), may hold values from -0.125 to 0.125
- up_bias: float32 [8192], P(('fsdp', 'ctx')), may hold values from -1.75 to 1.75
- down_weight: bfloat16 [8192, 2048], P(('fsdp', 'ctx')), may hold values from -0.0625 to 0.0625
- down_bias: float32 [2048], P(('fsdp', 'ctx')), may hold values from -1.75 to 1.75
- root_gain: float32 [2048], P(('fsdp', 'ctx')), may hold values from 0.25 to 1.75
- mix_in_weight: float32 [2048, 40], P(('fsdp', 'ctx')), may hold values from -0.125 to 0.125
- mix_out_weight: float32 [40, 40], replicated, may hold values from -1 to 1
- mix_out_bias: float32 [40], replicated, may hold values from -3 to 3
- out_cotangent: bfloat16 [4, 2048, 2048], P('fsdp', 'ctx'), may hold values from -6 to 6
- mix_cotangent: float32 [40, 4, 2048], P(None, 'fsdp', 'ctx'), may hold values from -6 to 6
Outputs:
- block_out: bfloat16 [4, 2048, 2048], P('fsdp', 'ctx')
- next_mix: float32 [40, 4, 2048], P(None, 'fsdp', 'ctx')
- grad_history: float32 [9, 4, 2048, 2048], P(None, 'fsdp', 'ctx')
- grad_mix: float32 [4, 9, 4, 2048], P(None, None, 'fsdp', 'ctx')
- grad_norm_gain: float32 [4, 2048], P(None, ('fsdp', 'ctx'))
- grad_norm_bias: float32 [4, 2048], P(None, ('fsdp', 'ctx'))
- grad_qkv_weight: float32 [2048, 3, 2048], P(('fsdp', 'ctx'))
- grad_qkv_bias: float32 [3, 2048], P(None, ('fsdp', 'ctx'))
- grad_out_weight: float32 [2048, 2048], P(('fsdp', 'ctx'))
- grad_out_bias: float32 [2048], P(('fsdp', 'ctx'))
- grad_up_weight: float32 [2048, 8192], P(('fsdp', 'ctx'))
- grad_up_bias: float32 [8192], P(('fsdp', 'ctx'))
- grad_down_weight: float32 [8192, 2048], P(('fsdp', 'ctx'))
- grad_down_bias: float32 [2048], P(('fsdp', 'ctx'))
- grad_root_gain: float32 [2048], P(('fsdp', 'ctx'))
- grad_mix_in_weight: float32 [2048, 40], P(('fsdp', 'ctx'))
- grad_mix_out_weight: float32 [40, 40], replicated
- grad_mix_out_bias: float32 [40], replicated
The draws below stay inside these ranges and needn't reach their ends.
Inputs may be any that keep to these rules, and one draw needn't show every extreme that they name: doc_starts[g, 0] = 0 and each row never falls; sequence g's documents begin at its distinct entries below 2048; entries equal to 2048 begin none. Of the one consecutive sequence (those of one index of fsdp) one, drawn from the seed, is a single document.
All inputs are finite; a program needn't handle non-finite values.
Results may differ from the reference program's by a relative error of at most 0.013.
Values may be sent and summed in bfloat16 or wider, within the bound.
A program may use at most 576 MiB of HBM per device.

```python
import math
import jax
import jax.numpy as jnp
from jax import lax

D = 2048
HEADS = 16
HEAD_DIM = 128
FF = 8192
ROT = 32
MIX_HID = 40
HIST = 9
STREAMS = 4
MIX_OUT = 40
SEQ_LEN = 2048
NDOC = 8
SEQS = 1
SEQS_ALL = 4


def draw_doc_starts(key, part):
    cut_key, pick_key = jax.random.split(jax.random.fold_in(key, 17))
    cuts = jax.random.randint(cut_key, (SEQS_ALL, NDOC - 1), 1, SEQ_LEN, dtype=jnp.int32)
    cuts = jnp.sort(cuts, axis=1)
    chosen = jax.random.randint(pick_key, (SEQS_ALL // SEQS,), 0, SEQS, dtype=jnp.int32)
    seq_ids = jnp.arange(SEQS_ALL, dtype=jnp.int32)
    single = seq_ids % SEQS == chosen[seq_ids // SEQS]
    cuts = jnp.where(single[:, None], SEQ_LEN, cuts)
    return jnp.concatenate([jnp.zeros((SEQS_ALL, 1), jnp.int32), cuts], axis=1)


def shard_levels(rng, dims, cuts, low, top_value):
    loudness = 1.0
    for axis_at, parts in cuts:
        heights = jax.random.uniform(jax.random.fold_in(jax.random.fold_in(rng, 6), axis_at), (parts,), jnp.float32, low / len(cuts), top_value / len(cuts))
        loudness = loudness * jnp.repeat(jnp.exp(heights), dims[axis_at] // parts).reshape((-1,) + (1,) * (len(dims) - 1 - axis_at))
    return loudness


def bell_draw(own_key, dims, scale, bound, cuts=(), kind=jnp.bfloat16):
    entries = jax.random.normal(own_key, dims, jnp.float32) * scale
    if len(cuts) > 0:
        entries = shard_levels(own_key, dims, cuts, -0.22, 0.18) * entries
    return jnp.clip(entries, min=-bound, max=bound).astype(kind)


def setup_inputs(seed: int = 0) -> dict:
    key_list = jax.random.split(jax.random.key(seed), 20)
    history = bell_draw(key_list[0], (HIST, SEQS_ALL, SEQ_LEN, D), 1.0, 6.0, ((1, 4), (2, 8)))
    dense_mix = bell_draw(key_list[1], (STREAMS, HIST, SEQS_ALL, SEQ_LEN), 0.4, 2.5, ((2, 4), (3, 8)), jnp.float32)
    doc_starts = draw_doc_starts(jax.random.fold_in(key_list[19], 71), 0)
    norm_gain = jnp.clip(1.0 + 0.15 * jax.random.normal(key_list[3], (4, D), jnp.float32), 0.25, 1.75)
    norm_bias = bell_draw(key_list[4], (4, D), 0.2, 1.25, ((1, 32),), jnp.float32)
    query_key_value_weight = bell_draw(key_list[5], (D, 3, D), D ** -0.5, 0.125, ((0, 32),))
    query_key_value_bias = bell_draw(key_list[6], (3, D), 0.3, 1.75, ((1, 32),), jnp.float32)
    out_weight = bell_draw(key_list[7], (D, D), (D // 16) ** -0.5, 0.5, ((0, 32),))
    out_bias = bell_draw(key_list[8], (D,), 0.3, 1.75, ((0, 32),), jnp.float32)
    up_weight = bell_draw(key_list[9], (D, FF), D ** -0.5, 0.125, ((0, 32),))
    up_bias = bell_draw(key_list[10], (FF,), 0.3, 1.75, ((0, 32),), jnp.float32)
    down_weight = bell_draw(key_list[11], (FF, D), FF ** -0.5, 0.0625, ((0, 32),))
    down_bias = bell_draw(key_list[12], (D,), 0.3, 1.75, ((0, 32),), jnp.float32)
    root_gain = jnp.clip(1.0 + 0.15 * jax.random.normal(key_list[13], (D,), jnp.float32), 0.25, 1.75)
    mix_in_weight = bell_draw(key_list[14], (D, MIX_HID), D ** -0.5, 0.125, ((0, 32),), jnp.float32)
    mix_out_weight = bell_draw(key_list[15], (MIX_HID, MIX_OUT), MIX_HID ** -0.5, 1.0, (), jnp.float32)
    mix_out_bias = bell_draw(key_list[16], (MIX_OUT,), 0.5, 3.0, (), jnp.float32)
    out_cotangent = bell_draw(key_list[17], (SEQS_ALL, SEQ_LEN, D), 1.0, 6.0, ((0, 4), (1, 8)))
    mix_cotangent = bell_draw(key_list[18], (MIX_OUT, SEQS_ALL, SEQ_LEN), 1.0, 6.0, ((1, 4), (2, 8)), jnp.float32)
    return dict(history=history, dense_mix=dense_mix, doc_starts=doc_starts, norm_gain=norm_gain, norm_bias=norm_bias, query_key_value_weight=query_key_value_weight, query_key_value_bias=query_key_value_bias, out_weight=out_weight, out_bias=out_bias, up_weight=up_weight, up_bias=up_bias, down_weight=down_weight, down_bias=down_bias, root_gain=root_gain, mix_in_weight=mix_in_weight, mix_out_weight=mix_out_weight, mix_out_bias=mix_out_bias, out_cotangent=out_cotangent, mix_cotangent=mix_cotangent)


@jax.custom_vjp
def low(v):
    return lax.optimization_barrier(v.astype(jnp.bfloat16)).astype(jnp.float32)

@jax.custom_vjp
def low_back(v):
    return v

def low_keep(v):
    return (low(v), None)

def low_pass(kept, grad):
    return (grad,)

def back_keep(v):
    return (v, None)

def back_low(kept, grad):
    return (low(grad),)
low.defvjp(low_keep, low_pass)
low_back.defvjp(back_keep, back_low)
TOP_PRECISION = lax.Precision.HIGHEST
EPS_NORM = 1e-05
EPS_ROOT = 1e-06
NEG_BIG = -1e+30

def layer_norm(values, gain_row, shift_row):
    centre = values - lax.optimization_barrier(jnp.mean(values, axis=-1, keepdims=True))
    spread = lax.optimization_barrier(jnp.mean(centre * centre, axis=-1, keepdims=True))
    return centre * lax.rsqrt(spread + EPS_NORM) * gain_row + shift_row

def precise_gelu_curve(values):
    return jax.nn.gelu(values, approximate=False)

def rotary(values, positions, turning):
    half_rot = ROT // 2
    frequency = jnp.exp(jnp.arange(half_rot, dtype=jnp.float32) * (-2.0 * math.log(10000.0) / ROT))
    angles = positions[:, None] * frequency[None, :]
    cosine = jnp.cos(angles)[:, None, :]
    sine_part = turning * jnp.sin(angles)[:, None, :]
    front_part = values[..., :half_rot]
    back_part = values[..., half_rot:ROT]
    return jnp.concatenate([front_part * cosine - back_part * sine_part, back_part * cosine + front_part * sine_part, values[..., ROT:]], axis=-1)

def mixer(out_rows, gain_row, opening_layer, closing_layer, closing_bias):
    inverse_rms = lax.rsqrt(lax.optimization_barrier(jnp.mean(out_rows * out_rows, axis=-1, keepdims=True)) + EPS_ROOT)
    square_rooted = out_rows * inverse_rms * gain_row
    hidden_units = jnp.einsum('evw,wr->evr', square_rooted, opening_layer, precision=TOP_PRECISION)
    return jnp.einsum('hjn,nr->hjr', precise_gelu_curve(hidden_units), closing_layer, precision=TOP_PRECISION) + closing_bias

def attention(queries, keys, values, starts):
    seq_len = queries.shape[1]
    key_pos = jnp.arange(seq_len, dtype=jnp.int32)
    doc_ids = lax.optimization_barrier(jnp.sum((starts[:, None, :] <= key_pos[None, :, None]).astype(jnp.int32), axis=-1))
    block_rows = min(512, seq_len)
    scaling = HEAD_DIM ** (-0.5)

    def one_block(block_id):
        begin_row = block_id * block_rows
        query_block = lax.dynamic_slice_in_dim(queries, begin_row, block_rows, 1)
        query_ids = lax.dynamic_slice_in_dim(doc_ids, begin_row, block_rows, 1)
        query_pos = begin_row + jnp.arange(block_rows, dtype=jnp.int32)
        scores = low_back(jnp.einsum('gqhe,gkhe->ghqk', query_block, keys, precision=TOP_PRECISION) * scaling)
        visible = (query_ids[:, :, None] == doc_ids[:, None, :]) & (key_pos[None, None, :] <= query_pos[None, :, None])
        scores = jnp.where(visible[:, None], scores, NEG_BIG)
        row_peak = lax.optimization_barrier(jnp.max(scores, axis=-1, keepdims=True))
        raised = jnp.exp(scores - row_peak)
        prob_rows = raised / lax.optimization_barrier(jnp.sum(raised, axis=-1, keepdims=True))
        return jnp.einsum('ghqk,gkhe->gqhe', low(prob_rows), values, precision=TOP_PRECISION)
    blocks = lax.map(jax.checkpoint(one_block), jnp.arange(seq_len // block_rows, dtype=jnp.int32))
    return jnp.transpose(blocks, (1, 0, 2, 3, 4)).reshape(queries.shape)

def forward(history_in, weights_in, starts, params):
    norm_gain, norm_bias, query_key_value_weight, query_key_value_bias, out_weight, out_bias, up_weight, up_bias, down_weight, down_bias, root_gain, mix_in_weight, mix_out_weight, mix_out_bias = params
    groups = history_in.shape[1]
    seq_len = history_in.shape[2]
    streams = jnp.einsum('shgl,hgld->sgld', weights_in, history_in, precision=TOP_PRECISION)
    normalized_input = low(layer_norm(streams[:3], norm_gain[:3, None, None, :], norm_bias[:3, None, None, :]))
    mapped_output = jnp.einsum('tbpr,rth->tbph', normalized_input, query_key_value_weight, precision=TOP_PRECISION) + query_key_value_bias[:, None, None, :]
    heads_shape = (groups, seq_len, HEADS, HEAD_DIM)
    positions = jnp.arange(seq_len, dtype=jnp.float32)
    queries = low(rotary(low_back(mapped_output[0]).reshape(heads_shape), positions, 1.0))
    keys = low(rotary(low_back(mapped_output[1]).reshape(heads_shape), positions, 1.0))
    values = low(low_back(mapped_output[2]).reshape(heads_shape))
    attended = low(low_back(attention(queries, keys, values, starts).reshape(groups, seq_len, D)))
    hidden_res = streams[3] + low_back(jnp.einsum('gld,de->gle', attended, out_weight, precision=TOP_PRECISION) + out_bias)
    normed_mlp = low(layer_norm(hidden_res, norm_gain[3], norm_bias[3]))
    upward = low_back(jnp.einsum('gld,df->glf', normed_mlp, up_weight, precision=TOP_PRECISION) + up_bias)
    activated = low(precise_gelu_curve(upward))
    result = hidden_res + low_back(jnp.einsum('glf,fd->gld', activated, down_weight, precision=TOP_PRECISION) + down_bias)
    next_rows = mixer(result, root_gain, mix_in_weight, mix_out_weight, mix_out_bias)
    return (result, jnp.transpose(next_rows, (2, 0, 1)))

def reference(history, dense_mix, doc_starts, norm_gain, norm_bias, query_key_value_weight, query_key_value_bias, out_weight, out_bias, up_weight, up_bias, down_weight, down_bias, root_gain, mix_in_weight, mix_out_weight, mix_out_bias, out_cotangent, mix_cotangent):
    params = (norm_gain, norm_bias, query_key_value_weight.astype(jnp.float32), query_key_value_bias, out_weight.astype(jnp.float32), out_bias, up_weight.astype(jnp.float32), up_bias, down_weight.astype(jnp.float32), down_bias, root_gain, mix_in_weight, mix_out_weight, mix_out_bias)
    group_size = math.gcd(SEQS_ALL, max(1, 4096 // SEQ_LEN))
    steps_count = SEQS_ALL // group_size

    def grouped(tensor, axis_id):
        old_shape = tensor.shape
        new_shape = old_shape[:axis_id] + (steps_count, group_size) + old_shape[axis_id + 1:]
        return jnp.moveaxis(tensor.reshape(new_shape), axis_id, 0)

    def ungrouped(tensor, axis_id):
        moved_axes = jnp.moveaxis(tensor, 0, axis_id)
        old_shape = moved_axes.shape
        return moved_axes.reshape(old_shape[:axis_id] + (old_shape[axis_id] * old_shape[axis_id + 1],) + old_shape[axis_id + 2:])
    scan_items = (grouped(history, 1), grouped(dense_mix, 2), grouped(doc_starts, 0), grouped(out_cotangent, 0), grouped(mix_cotangent, 1))

    def scan_step(running, items_now):
        hist_group, mix_group, start_group, cot_group, cot_mix_group = items_now

        def run_forward(hist_float, mix_float, param_float):
            return forward(hist_float, mix_float, start_group, param_float)
        outputs, pullback = jax.vjp(run_forward, hist_group.astype(jnp.float32), mix_group, params)
        grad_hist, grad_weights, grad_params = pullback((cot_group.astype(jnp.float32), cot_mix_group))
        running = jax.tree.map(lambda total_val, part_val: total_val + part_val, running, grad_params)
        return (running, (outputs[0].astype(jnp.bfloat16), outputs[1], grad_hist, grad_weights))
    initial = jax.tree.map(jnp.zeros_like, params)
    totals, stacked = lax.scan(scan_step, initial, scan_items)
    block_out = ungrouped(stacked[0], 0)
    next_mix = ungrouped(stacked[1], 1)
    grad_history = ungrouped(stacked[2], 1)
    grad_mix = ungrouped(stacked[3], 2)
    return (block_out, next_mix, grad_history, grad_mix, totals[0], totals[1], totals[2], totals[3], totals[4], totals[5], totals[6], totals[7], totals[8], totals[9], totals[10], totals[11], totals[12], totals[13])
```

```python
import math

import jax
import jax.numpy as jnp
from jax import lax
from jax.experimental import pallas as pl
from jax.experimental.pallas import tpu as pltpu
from jax.sharding import PartitionSpec as P

HEAD_DIM = 128
ROT = 32
TOP_PRECISION = lax.Precision.HIGHEST
EPS_NORM = 1e-05
EPS_ROOT = 1e-06
NEG_BIG = -1e30
BOTH = ("fsdp", "ctx")
BF16 = jnp.bfloat16
F32 = jnp.float32
MESH = pl.DeviceIdType.MESH
ANY = pl.BlockSpec(memory_space=pl.ANY)
VMEM = pl.BlockSpec(memory_space=pltpu.VMEM)
LOG2E = 1.4426950408889634


def layer_norm(values, gain_row, shift_row):
    centre = values - jnp.mean(values, axis=-1, keepdims=True)
    spread = jnp.mean(centre * centre, axis=-1, keepdims=True)
    return centre * lax.rsqrt(spread + EPS_NORM) * gain_row + shift_row


def gelu(values):
    return jax.nn.gelu(values, approximate=False)


def rotary_tables(positions, turning):
    half = ROT // 2
    frequency = jnp.exp(jnp.arange(half, dtype=F32) * (-2.0 * math.log(10000.0) / ROT))
    angles = positions[:, None] * frequency[None, :]
    return jnp.cos(angles), turning * jnp.sin(angles)


def rotary(values, cosine, sine):
    half = ROT // 2
    front, back = values[..., :half], values[..., half:ROT]
    return jnp.concatenate(
        [front * cosine - back * sine, back * cosine + front * sine, values[..., ROT:]], axis=-1
    )


def mixer(rows, gain_row, opening, closing, closing_bias):
    inverse_rms = lax.rsqrt(jnp.mean(rows * rows, axis=-1, keepdims=True) + EPS_ROOT)
    rooted = rows * inverse_rms * gain_row
    hidden = jnp.dot(rooted, opening, precision=TOP_PRECISION)
    return jnp.dot(gelu(hidden), closing, precision=TOP_PRECISION) + closing_bias


def dot(pattern, left, right):
    return jnp.einsum(pattern, left, right, preferred_element_type=F32)


def remote(src, dst, send_sem, recv_sem, target):
    return pltpu.make_async_remote_copy(
        src_ref=src,
        dst_ref=dst,
        send_sem=send_sem,
        recv_sem=recv_sem,
        device_id=target,
        device_id_type=MESH,
    )


def greet(targets):
    barrier = pltpu.get_barrier_semaphore()
    for t in targets:
        pl.semaphore_signal(barrier, inc=1, device_id=t, device_id_type=MESH)
    pl.semaphore_wait(barrier, len(targets))


def greet_all(fn, cn, me):
    barrier = pltpu.get_barrier_semaphore()

    def hello(k, _):
        t = lax.rem(me + k, fn * cn)
        pl.semaphore_signal(
            barrier, inc=1, device_id=(t // cn, lax.rem(t, cn)), device_id_type=MESH
        )
        return 0

    lax.fori_loop(1, fn * cn, hello, 0)
    pl.semaphore_wait(barrier, fn * cn - 1)


def gather_small(x):
    fn, cn = lax.axis_size("fsdp"), lax.axis_size("ctx")
    dn = fn * cn

    def kernel(x_ref, o_ref, send, recv):
        me = lax.axis_index("fsdp") * cn + lax.axis_index("ctx")
        greet_all(fn, cn, me)

        def copy(k, slot):
            t = lax.rem(me + k, dn)
            return remote(
                x_ref, o_ref.at[slot], send.at[k], recv.at[k], (t // cn, lax.rem(t, cn))
            )

        def go(k, _):
            copy(k, me).start()
            return 0

        lax.fori_loop(1, dn, go, 0)
        o_ref[me] = x_ref[...]

        def end(k, _):
            c = copy(k, lax.rem(me + dn - k, dn))
            c.wait_send()
            c.wait_recv()
            return 0

        lax.fori_loop(1, dn, end, 0)

    return pl.pallas_call(
        kernel,
        out_shape=jax.ShapeDtypeStruct((dn, *x.shape), x.dtype),
        in_specs=[VMEM],
        out_specs=VMEM,
        scratch_shapes=[pltpu.SemaphoreType.DMA((dn,)), pltpu.SemaphoreType.DMA((dn,))],
        compiler_params=pltpu.CompilerParams(collective_id=1, has_side_effects=True),
    )(x)


def scatter_small(x):
    fn, cn = lax.axis_size("fsdp"), lax.axis_size("ctx")
    dn = fn * cn

    def kernel(x_ref, o_ref, got, send, recv):
        me = lax.axis_index("fsdp") * cn + lax.axis_index("ctx")
        greet_all(fn, cn, me)

        def copy(k):
            t = lax.rem(me + k, dn)
            return remote(
                x_ref.at[t], got.at[k], send.at[k], recv.at[k], (t // cn, lax.rem(t, cn))
            )

        def go(k, _):
            copy(k).start()
            return 0

        lax.fori_loop(1, dn, go, 0)
        o_ref[...] = x_ref[me]

        def end(k, _):
            copy(k).wait_recv()
            o_ref[...] += got[k]
            return 0

        lax.fori_loop(1, dn, end, 0)

        def sent(k, _):
            copy(k).wait_send()
            return 0

        lax.fori_loop(1, dn, sent, 0)

    return pl.pallas_call(
        kernel,
        out_shape=jax.ShapeDtypeStruct(x.shape[1:], x.dtype),
        in_specs=[VMEM],
        out_specs=VMEM,
        scratch_shapes=[
            pltpu.VMEM(x.shape, x.dtype),
            pltpu.SemaphoreType.DMA((dn,)),
            pltpu.SemaphoreType.DMA((dn,)),
        ],
        compiler_params=pltpu.CompilerParams(collective_id=2, has_side_effects=True),
    )(x)


def gather_fsdp(x, cid, parts=4):
    fn = lax.axis_size("fsdp")
    chips = fn // 2
    k_count, n, d = x.shape
    step = n // parts
    pieces = [(k, pl.ds(p * step, step)) for k in range(k_count) for p in range(parts)]
    many = len(pieces)

    def kernel(x_ref, o_ref, own_sem, s_link, r_link, s_core, r_core):
        f, c = lax.axis_index("fsdp"), lax.axis_index("ctx")
        chip, core = f // 2, lax.rem(f, 2)
        twin = (chip * 2 + 1 - core, c)

        def to(j):
            return (lax.rem(chip + j, chips) * 2 + core, c)

        def slot(j, core_id):
            return lax.rem(chip + chips - j, chips) * 2 + core_id

        greet([to(j) for j in range(1, chips)] + [twin])
        links, cores = {}, {}
        for i, (k, rows) in enumerate(pieces):
            for j in range(1, chips):
                links[i, j] = remote(
                    x_ref.at[k, rows],
                    o_ref.at[k, f, rows],
                    s_link.at[j, i],
                    r_link.at[j, i],
                    to(j),
                )
                links[i, j].start()
        for i, (k, rows) in enumerate(pieces):
            cores[i, 0] = remote(
                x_ref.at[k, rows], o_ref.at[k, f, rows], s_core.at[0, i], r_core.at[0, i], twin
            )
            cores[i, 0].start()
        own = pltpu.make_async_copy(x_ref, o_ref.at[:, f], own_sem)
        own.start()
        for i, (k, rows) in enumerate(pieces):
            for j in range(1, chips):
                here = o_ref.at[k, slot(j, core), rows]
                remote(here, here, s_link.at[j, i], r_link.at[j, i], to(j)).wait_recv()
                cores[i, j] = remote(here, here, s_core.at[j, i], r_core.at[j, i], twin)
                cores[i, j].start()
        own.wait()
        for i, (k, rows) in enumerate(pieces):
            for j in range(chips):
                there = o_ref.at[k, slot(j, 1 - core), rows]
                cores[i, j].wait_send()
                remote(there, there, s_core.at[j, i], r_core.at[j, i], twin).wait_recv()
            for j in range(1, chips):
                links[i, j].wait_send()

    return pl.pallas_call(
        kernel,
        out_shape=jax.ShapeDtypeStruct((k_count, fn, n, d), x.dtype),
        in_specs=[ANY],
        out_specs=ANY,
        scratch_shapes=[
            pltpu.SemaphoreType.DMA,
            pltpu.SemaphoreType.DMA((chips, many)),
            pltpu.SemaphoreType.DMA((chips, many)),
            pltpu.SemaphoreType.DMA((chips, many)),
            pltpu.SemaphoreType.DMA((chips, many)),
        ],
        compiler_params=pltpu.CompilerParams(collective_id=cid, has_side_effects=True),
    )(x)


def scatter_fsdp(x, cid, parts=4):
    fn = lax.axis_size("fsdp")
    chips = fn // 2
    k_count, _, n, d = x.shape
    step = n // parts
    pieces = [(k, p) for k in range(k_count) for p in range(parts)]
    many = len(pieces)

    def kernel(x_ref, o_ref, own, near, mine, far, ss, s_own, s_near, r_near, s_far, r_far):
        f, c = lax.axis_index("fsdp"), lax.axis_index("ctx")
        chip, core = f // 2, lax.rem(f, 2)
        twin = (chip * 2 + 1 - core, c)

        def chip_at(j):
            return lax.rem(chip + j, chips)

        def to(j):
            return (chip_at(j) * 2 + core, c)

        order = list(range(1, chips)) + [0]
        greet([to(j) for j in range(1, chips)] + [twin])
        nears, owns, fars, outs = {}, {}, {}, []
        for i, (k, p) in enumerate(pieces):
            rows = pl.ds(p * step, step)
            for j in order:
                owns[i, j] = pltpu.make_async_copy(
                    x_ref.at[k, chip_at(j) * 2 + core, rows], own.at[j, i], s_own.at[j, i]
                )
                owns[i, j].start()
                nears[i, j] = remote(
                    x_ref.at[k, chip_at(j) * 2 + 1 - core, rows],
                    near.at[j, i],
                    s_near.at[j, i],
                    r_near.at[j, i],
                    twin,
                )
                nears[i, j].start()
        for i in range(many):
            for j in range(1, chips):
                owns[i, j].wait()
                nears[i, j].wait_recv()
                mine[j, i] = (own[j, i].astype(F32) + near[j, i].astype(F32)).astype(BF16)
                fars[i, j] = remote(
                    mine.at[j, i], far.at[j, i], s_far.at[j, i], r_far.at[j, i], to(j)
                )
                fars[i, j].start()
        for i, (k, p) in enumerate(pieces):
            owns[i, 0].wait()
            nears[i, 0].wait_recv()
            ss[i] = own[0, i].astype(F32) + near[0, i].astype(F32)
        for i, (k, p) in enumerate(pieces):
            for j in range(1, chips):
                fars[i, j].wait_recv()
                ss[i] += far[j, i].astype(F32)
            outs.append(
                pltpu.make_async_copy(
                    ss.at[i], o_ref.at[k, pl.ds(p * step, step)], s_far.at[0, i]
                )
            )
            outs[-1].start()
        for i in range(many):
            outs[i].wait()
            for j in range(chips):
                nears[i, j].wait_send()
            for j in range(1, chips):
                fars[i, j].wait_send()

    blocks = (chips, many, step, d)
    sems = pltpu.SemaphoreType.DMA((chips, many))
    return pl.pallas_call(
        kernel,
        out_shape=jax.ShapeDtypeStruct((k_count, n, d), F32),
        in_specs=[ANY],
        out_specs=ANY,
        scratch_shapes=[
            pltpu.VMEM(blocks, BF16),
            pltpu.VMEM(blocks, BF16),
            pltpu.VMEM(blocks, BF16),
            pltpu.VMEM(blocks, BF16),
            pltpu.VMEM((many, step, d), F32),
            sems,
            sems,
            sems,
            sems,
            sems,
        ],
        compiler_params=pltpu.CompilerParams(
            collective_id=cid, has_side_effects=True, vmem_limit_bytes=56 * 2**20
        ),
    )(x)


def nt(a, b):
    return lax.dot_general(a, b, (((1,), (1,)), ((), ())), preferred_element_type=F32)


def nn(a, b):
    return lax.dot_general(a, b, (((1,), (0,)), ((), ())), preferred_element_type=F32)


def attend(q, k, v, starts, block=512):
    u, t, _ = q.shape
    scale = HEAD_DIM**-0.5 * LOG2E

    def kernel(q_ref, k_ref, v_ref, s_ref, o_ref, l_ref, vt):
        i = pl.program_id(1)

        @pl.when(i == 0)
        def _():
            vt[...] = v_ref[0].T

        rows = q_ref[0]
        first = s_ref[0]
        base = lax.broadcasted_iota(jnp.int32, (block, block), 0)
        qpos = i * block + lax.broadcasted_iota(jnp.int32, (1, block), 1)

        def one(j, carry, diagonal):
            peak, total, acc = carry
            at = pl.multiple_of(j * block, block)
            s = nt(k_ref[0, pl.ds(at, block)], rows) * scale
            kpos = base + at
            keep = kpos >= first
            if diagonal:
                keep = keep & (kpos <= qpos)
            s = jnp.where(keep, s, NEG_BIG)
            new = jnp.maximum(peak, jnp.max(s, axis=0, keepdims=True))
            p = jnp.exp2(s - new)
            shrink = jnp.exp2(peak - new)
            total = total * shrink + jnp.sum(p, axis=0, keepdims=True)
            acc = acc * shrink + nn(vt[:, pl.ds(at, block)], p.astype(BF16))
            return new, total, acc

        start = (
            jnp.full((1, block), NEG_BIG, F32),
            jnp.zeros((1, block), F32),
            jnp.zeros((HEAD_DIM, block), F32),
        )
        start = one(i, start, True)
        peak, total, acc = lax.fori_loop(0, i, lambda j, c: one(j, c, False), start)
        o_ref[0] = (acc / total).T.astype(BF16)
        l_ref[0] = peak + jnp.log2(total)

    return pl.pallas_call(
        kernel,
        grid=(u, t // block),
        in_specs=[
            pl.BlockSpec((1, block, HEAD_DIM), lambda a, b: (a, b, 0)),
            pl.BlockSpec((1, t, HEAD_DIM), lambda a, b: (a, 0, 0)),
            pl.BlockSpec((1, t, HEAD_DIM), lambda a, b: (a, 0, 0)),
            pl.BlockSpec((1, 1, block), lambda a, b: (a, 0, b)),
        ],
        out_specs=[
            pl.BlockSpec((1, block, HEAD_DIM), lambda a, b: (a, b, 0)),
            pl.BlockSpec((1, 1, block), lambda a, b: (a, 0, b)),
        ],
        out_shape=[
            jax.ShapeDtypeStruct((u, t, HEAD_DIM), BF16),
            jax.ShapeDtypeStruct((u, 1, t), F32),
        ],
        scratch_shapes=[pltpu.VMEM((HEAD_DIM, t), BF16)],
        compiler_params=pltpu.CompilerParams(vmem_limit_bytes=32 * 2**20),
        cost_estimate=pl.CostEstimate(
            flops=2 * u * t * t * HEAD_DIM, bytes_accessed=8 * u * t * 256, transcendentals=u * t * t // 2
        ),
    )(q, k, v, starts)


def attend_back(q, k, v, starts, lse, o, g, block=512):
    u, t, _ = q.shape
    scale = HEAD_DIM**-0.5

    def kernel(q_ref, k_ref, v_ref, s_ref, l_ref, o_ref, g_ref, dq_ref, dk_ref, dv_ref, kt):
        i = pl.program_id(1)

        @pl.when(i == 0)
        def _():
            kt[...] = k_ref[0].T
            dk_ref[...] = jnp.zeros_like(dk_ref)
            dv_ref[...] = jnp.zeros_like(dv_ref)

        rows, grows = q_ref[0], g_ref[0]
        first, logs = s_ref[0], l_ref[0]
        prod = o_ref[0].astype(F32) * grows.astype(F32)
        centre = jnp.sum(prod.T, axis=0, keepdims=True)
        base = lax.broadcasted_iota(jnp.int32, (block, block), 0)
        qpos = i * block + lax.broadcasted_iota(jnp.int32, (1, block), 1)

        def one(j, acc, diagonal):
            at = pl.multiple_of(j * block, block)
            here = pl.ds(at, block)
            p = jnp.exp2(nt(k_ref[0, here], rows) * (scale * LOG2E) - logs)
            kpos = base + at
            keep = kpos >= first
            if diagonal:
                keep = keep & (kpos <= qpos)
            p = jnp.where(keep, p, 0.0)
            gp = nt(v_ref[0, here], grows)
            ds = (p * (gp - centre)).astype(BF16)
            dv_ref[0, here] += nn(p.astype(BF16), grows)
            dk_ref[0, here] += nn(ds, rows) * scale
            return acc + nn(kt[:, here], ds)

        acc = one(i, jnp.zeros((HEAD_DIM, block), F32), True)
        acc = lax.fori_loop(0, i, lambda j, a: one(j, a, False), acc)
        dq_ref[0] = (acc * scale).T

    def whole(a, b):
        return (a, 0, 0)

    def part(a, b):
        return (a, b, 0)

    def row(a, b):
        return (a, 0, b)

    spec, full, line = (1, block, HEAD_DIM), (1, t, HEAD_DIM), (1, 1, block)
    return pl.pallas_call(
        kernel,
        grid=(u, t // block),
        in_specs=[
            pl.BlockSpec(spec, part),
            pl.BlockSpec(full, whole),
            pl.BlockSpec(full, whole),
            pl.BlockSpec(line, row),
            pl.BlockSpec(line, row),
            pl.BlockSpec(spec, part),
            pl.BlockSpec(spec, part),
        ],
        out_specs=[
            pl.BlockSpec(spec, part),
            pl.BlockSpec(full, whole),
            pl.BlockSpec(full, whole),
        ],
        out_shape=[jax.ShapeDtypeStruct((u, t, HEAD_DIM), F32)] * 3,
        scratch_shapes=[pltpu.VMEM((HEAD_DIM, t), BF16)],
        compiler_params=pltpu.CompilerParams(vmem_limit_bytes=48 * 2**20),
        cost_estimate=pl.CostEstimate(
            flops=5 * u * t * t * HEAD_DIM, bytes_accessed=20 * u * t * 256, transcendentals=u * t * t // 2
        ),
    )(q, k, v, starts, lse, o, g)


def body(
    history,
    dense_mix,
    doc_starts,
    norm_gain,
    norm_bias,
    qkv_weight,
    qkv_bias,
    out_weight,
    out_bias,
    up_weight,
    up_bias,
    down_weight,
    down_bias,
    root_gain,
    mix_in_weight,
    mix_out_weight,
    mix_out_bias,
    out_cotangent,
    mix_cotangent,
):
    fn, cn = lax.axis_size("fsdp"), lax.axis_size("ctx")
    dn = fn * cn
    fi, ci = lax.axis_index("fsdp"), lax.axis_index("ctx")
    hist, seqs, length, width = history.shape
    nloc = seqs * length
    ntp = fn * nloc
    rows = qkv_weight.shape[0]
    ff = up_weight.shape[1]
    wcol, fcol = width // fn, ff // fn
    heads = wcol // HEAD_DIM
    units = fn * seqs * heads // cn
    total = cn * length
    mixn = mix_in_weight.shape[1]

    def to_columns(w, cols):
        w = w.reshape(rows, fn, cols).transpose(1, 0, 2)
        return lax.all_to_all(w, "fsdp", 0, 0, tiled=True)

    def rows_over_ctx(w):
        g = lax.all_gather(w, "ctx", axis=0)
        return g.transpose(1, 0, 2, 3).reshape(fn * cn * w.shape[1], w.shape[2])

    qkv_cols = lax.all_to_all(
        qkv_weight.reshape(rows, 3, fn, wcol).transpose(2, 1, 0, 3), "fsdp", 0, 0, tiled=True
    )
    qkv_g = lax.all_gather(qkv_cols, "ctx", axis=0)
    wqkv = qkv_g.transpose(2, 1, 0, 3, 4).reshape(3, width, wcol)
    wup = rows_over_ctx(to_columns(up_weight, fcol))
    wout = lax.all_gather(out_weight, "ctx", axis=0, tiled=True)
    wdown = lax.all_gather(down_weight, "ctx", axis=0, tiled=True)

    parts = [
        norm_gain,
        norm_bias,
        qkv_bias,
        out_bias,
        up_bias,
        down_bias,
        root_gain,
        mix_in_weight,
        doc_starts.astype(F32),
    ]
    flat = jnp.concatenate([a.reshape(-1) for a in parts])
    flat = jnp.pad(flat, (0, -flat.size % 1024)).reshape(-1, 128)
    flats = gather_small(flat).reshape(dn, -1)
    pieces, at = [], 0
    for a in parts:
        pieces.append(flats[:, at : at + a.size])
        at += a.size

    def joined(piece, lead):
        return piece.reshape(dn, lead, -1).transpose(1, 0, 2).reshape(lead, -1)

    gain_all = joined(pieces[0], 4)
    shift_all = joined(pieces[1], 4)
    qkv_shift = joined(pieces[2], 3)
    out_shift = pieces[3].reshape(-1)
    up_shift = pieces[4].reshape(-1)
    down_shift = pieces[5].reshape(-1)
    root_full = pieces[6].reshape(-1)
    mix_in_full = pieces[7].reshape(width, mixn)
    starts = pieces[8].reshape(fn, cn, seqs, -1)[:, 0].astype(jnp.int32)

    hist2 = history.reshape(hist, nloc, width)
    mix2 = dense_mix.reshape(dense_mix.shape[0], hist, nloc)
    streams = jnp.zeros((dense_mix.shape[0], nloc, width), F32)
    for j in range(hist):
        streams = streams + mix2[:, j][..., None] * hist2[j].astype(F32)[None]

    def front_norm(values, gains, shifts):
        return layer_norm(values, gains[:, None, :], shifts[:, None, :])

    normed, front_pull = jax.vjp(front_norm, streams[:3], gain_all[:3], shift_all[:3])
    normed_g = gather_fsdp(normed.astype(BF16), 3).reshape(3, ntp, width)

    bias_cols = lax.dynamic_slice_in_dim(qkv_shift, fi * wcol, wcol, 1)
    projected = dot("snd,sdc->snc", normed_g, wqkv) + bias_cols[:, None, :]
    pos_local = (ci * length + jnp.arange(length, dtype=jnp.int32)).astype(F32)
    cos_l, sin_l = rotary_tables(pos_local, 1.0)
    split = projected.reshape(3, fn * seqs, length, heads, HEAD_DIM)
    turned = rotary(split[:2], cos_l[None, None, :, None], sin_l[None, None, :, None])
    low = jnp.concatenate([turned, split[2:]], axis=0).astype(BF16)

    def to_units(x):
        k = x.shape[0]
        x = x.transpose(1, 3, 0, 2, 4).reshape(cn, units, k, length, HEAD_DIM)
        x = lax.all_to_all(x, "ctx", 0, 0, tiled=True)
        return x.transpose(2, 1, 0, 3, 4).reshape(k, units, total, HEAD_DIM)

    def from_units(x):
        k = x.shape[0]
        x = x.reshape(k, units, cn, length, HEAD_DIM).transpose(2, 1, 0, 3, 4)
        x = lax.all_to_all(x, "ctx", 0, 0, tiled=True)
        x = x.reshape(fn * seqs, heads, k, length, HEAD_DIM).transpose(2, 0, 3, 1, 4)
        return x.reshape(k, ntp, wcol)

    q_u, k_u, v_u = to_units(low)
    pos_all = jnp.arange(total, dtype=jnp.int32)
    unit_ids = ci * units + jnp.arange(units, dtype=jnp.int32)
    seq_ids = unit_ids // heads
    unit_starts = starts.reshape(fn * seqs, -1)[seq_ids]
    first_key = jnp.max(
        jnp.where(unit_starts[:, None, :] <= pos_all[None, :, None], unit_starts[:, None, :], 0),
        axis=-1,
    )[:, None, :]
    att_u, lse_u = attend(q_u, k_u, v_u, first_key)
    attended = from_units(att_u[None])[0]

    def scatter_tokens(x):
        k = x.shape[0]
        x = x.astype(BF16).reshape(k, fn, nloc, width)
        return scatter_fsdp(x, 5 if k == 1 else 6)

    def gather_tokens(x):
        return gather_fsdp(x[None], 4).reshape(ntp, width)

    hidden_res = streams[3] + scatter_tokens(dot("nd,de->ne", attended, wout)[None])[0] + out_shift
    normed_mlp, mid_pull = jax.vjp(layer_norm, hidden_res, gain_all[3], shift_all[3])
    mlp_g = gather_tokens(normed_mlp.astype(BF16))
    up_cols = lax.dynamic_slice_in_dim(up_shift, fi * fcol, fcol, 0)
    upward = dot("nd,df->nf", mlp_g, wup) + up_cols
    activated, gelu_pull = jax.vjp(gelu, upward)
    act_low = activated.astype(BF16)
    result = hidden_res + scatter_tokens(dot("nf,fd->nd", act_low, wdown)[None])[0] + down_shift
    block_out = result.astype(BF16).reshape(seqs, length, width)

    next_rows, mixer_pull = jax.vjp(
        mixer, result, root_full, mix_in_full, mix_out_weight, mix_out_bias
    )
    next_mix = next_rows.T.reshape(-1, seqs, length)
    grad_result, grad_root, grad_mix_in, grad_mix_out, grad_mix_bias = mixer_pull(
        mix_cotangent.reshape(-1, nloc).T
    )
    grad_result = grad_result + out_cotangent.reshape(nloc, width).astype(F32)

    grad_branch = grad_result.astype(BF16)
    branch_g = gather_tokens(grad_branch)
    grad_down_shift = jnp.sum(grad_branch.astype(F32), axis=0)

    def scatter_ctx(x):
        return lax.psum_scatter(x.astype(BF16), "ctx", scatter_dimension=0, tiled=True)

    grad_down = scatter_ctx(dot("nf,nd->fd", act_low, branch_g)).astype(F32)
    grad_active = dot("nd,fd->nf", branch_g, wdown)
    grad_upward = gelu_pull(grad_active)[0].astype(BF16)
    grad_up_shift = jnp.sum(grad_upward.astype(F32), axis=0)

    grad_up_part = dot("nd,nf->df", mlp_g, grad_upward).reshape(fn, cn, rows, fcol)
    grad_up = scatter_ctx(grad_up_part.transpose(1, 0, 2, 3).reshape(-1, fcol))
    grad_up = grad_up.reshape(fn, rows, fcol)
    grad_up = lax.all_to_all(grad_up, "fsdp", 0, 0, tiled=True)
    grad_up = grad_up.transpose(1, 0, 2).reshape(rows, ff).astype(F32)

    grad_mlp = scatter_tokens(dot("nf,df->nd", grad_upward, wup)[None])[0]
    grad_hidden, grad_gain_mid, grad_shift_mid = mid_pull(grad_mlp)
    grad_hidden = grad_hidden + grad_result
    grad_attn = grad_hidden.astype(BF16)
    grad_out_shift = jnp.sum(grad_attn.astype(F32), axis=0)
    attn_g = gather_tokens(grad_attn)
    grad_out = scatter_ctx(dot("nd,ne->de", attended, attn_g)).astype(F32)
    grad_att = dot("ne,de->nd", attn_g, wout).astype(BF16)
    (g_u,) = to_units(grad_att.reshape(1, fn * seqs, length, heads, HEAD_DIM))
    gq, gk, gv = attend_back(q_u, k_u, v_u, first_key, lse_u, att_u, g_u)
    cos_a, sin_a = rotary_tables(pos_all.astype(F32), -1.0)
    grad_units = jnp.stack([rotary(gq, cos_a, sin_a), rotary(gk, cos_a, sin_a), gv]).astype(BF16)
    grad_proj = from_units(grad_units)
    grad_qkv_shift = jnp.sum(grad_proj.astype(F32), axis=1)

    grad_qkv_part = dot("snd,snc->sdc", normed_g, grad_proj).reshape(3, fn, cn, rows, wcol)
    grad_qkv = scatter_ctx(grad_qkv_part.transpose(2, 1, 0, 3, 4).reshape(-1, wcol))
    grad_qkv = grad_qkv.reshape(fn, 3, rows, wcol)
    grad_qkv = lax.all_to_all(grad_qkv, "fsdp", 0, 0, tiled=True)
    grad_qkv = grad_qkv.transpose(2, 1, 0, 3).reshape(rows, 3, width).astype(F32)

    grad_normed = scatter_tokens(dot("snc,sdc->snd", grad_proj, wqkv))
    grad_front, grad_gain_front, grad_shift_front = front_pull(grad_normed)
    grad_streams = jnp.concatenate([grad_front, grad_hidden[None]], axis=0)
    hist_grads, mix_grads = [], []
    for j in range(hist):
        hist_grads.append(jnp.sum(mix2[:, j][..., None] * grad_streams, axis=0))
        mix_grads.append(jnp.sum(hist2[j].astype(F32)[None] * grad_streams, axis=-1))
    grad_history = jnp.stack(hist_grads, axis=0).reshape(history.shape)
    grad_mix = jnp.stack(mix_grads, axis=1).reshape(dense_mix.shape)

    def own_columns(x, full):
        zero = jnp.zeros((x.shape[0], full), F32)
        return lax.dynamic_update_slice_in_dim(zero, x, fi * x.shape[1], 1)

    def parted(x):
        k = x.shape[0]
        return x.reshape(k, dn, -1).transpose(1, 0, 2).reshape(dn, -1)

    sums = [
        parted(jnp.concatenate([grad_gain_front, grad_gain_mid[None]], axis=0)),
        parted(jnp.concatenate([grad_shift_front, grad_shift_mid[None]], axis=0)),
        parted(own_columns(grad_qkv_shift, width)),
        parted(grad_out_shift[None]),
        parted(own_columns(grad_up_shift[None], ff)),
        parted(grad_down_shift[None]),
        parted(grad_root[None]),
        grad_mix_in.reshape(dn, -1),
    ]
    same = jnp.concatenate([grad_mix_out.reshape(-1), grad_mix_bias])
    sums.append(jnp.broadcast_to(same[None], (dn, same.size)))
    flat = jnp.concatenate(sums, axis=1)
    flat = jnp.pad(flat, ((0, 0), (0, -flat.shape[1] % 1024)))
    small = scatter_small(flat.reshape(dn, -1, 128)).reshape(-1)
    out_small, at = [], 0
    for s, shape in zip(sums[:-1], [a.shape for a in parts[:-1]], strict=True):
        out_small.append(small[at : at + s.shape[1]].reshape(shape))
        at += s.shape[1]
    (g_gain, g_shift, g_qkv_b, g_out_b, g_up_b, g_down_b, g_root, g_mix_in) = out_small
    mix_sums = small[at : at + same.size]
    cut = grad_mix_out.size
    return (
        block_out,
        next_mix,
        grad_history,
        grad_mix,
        g_gain,
        g_shift,
        grad_qkv,
        g_qkv_b,
        grad_out,
        g_out_b,
        grad_up,
        g_up_b,
        grad_down,
        g_down_b,
        g_root,
        g_mix_in,
        mix_sums[:cut].reshape(grad_mix_out.shape),
        mix_sums[cut:],
    )


def solution(mesh):
    token = P(None, "fsdp", "ctx")
    both = P(BOTH)
    cols = P(None, BOTH)
    placed = (
        token,
        P(None, None, "fsdp", "ctx"),
        P("fsdp"),
        cols,
        cols,
        both,
        cols,
        both,
        both,
        both,
        both,
        both,
        both,
        both,
        both,
        P(),
        P(),
        P("fsdp", "ctx"),
        token,
    )
    outs = (
        P("fsdp", "ctx"),
        token,
        token,
        P(None, None, "fsdp", "ctx"),
        cols,
        cols,
        both,
        cols,
        both,
        both,
        both,
        both,
        both,
        both,
        both,
        both,
        P(),
        P(),
    )
    return jax.shard_map(body, mesh=mesh, in_specs=placed, out_specs=outs, check_vma=False)
```

```python
import math

import jax
import jax.numpy as jnp
import numpy as np
from jax import lax
from jax.experimental import pallas as pl
from jax.experimental.pallas import tpu as pltpu
from jax.sharding import PartitionSpec as P

HEAD_DIM = 128
ROT = 32
TOP_PRECISION = lax.Precision.HIGHEST
EPS_NORM = 1e-05
EPS_ROOT = 1e-06
NEG_BIG = -1e30
BOTH = ("fsdp", "ctx")
BF16 = jnp.bfloat16
F32 = jnp.float32
MESH = pl.DeviceIdType.MESH
ANY = pl.BlockSpec(memory_space=pl.ANY)
VMEM = pl.BlockSpec(memory_space=pltpu.VMEM)
LOG2E = 1.4426950408889634


def layer_norm(values, gain_row, shift_row):
    centre = values - jnp.mean(values, axis=-1, keepdims=True)
    spread = jnp.mean(centre * centre, axis=-1, keepdims=True)
    return centre * lax.rsqrt(spread + EPS_NORM) * gain_row + shift_row


def gelu(values):
    return jax.nn.gelu(values, approximate=False)


def rotary_tables(count):
    half = ROT // 2
    frequency = np.exp(np.arange(half, dtype=np.float32) * np.float32(-2.0 * math.log(10000.0) / ROT))
    angles = np.arange(count, dtype=np.float32)[:, None] * frequency.astype(np.float32)[None, :]
    cosine = jnp.asarray(np.cos(angles.astype(np.float64)), F32)
    sine = jnp.asarray(np.sin(angles.astype(np.float64)), F32)
    zero, rest = jnp.zeros_like(sine), HEAD_DIM - ROT
    return jnp.stack(
        [
            jnp.pad(jnp.concatenate([cosine, cosine], 1), ((0, 0), (0, rest)), constant_values=1.0),
            jnp.pad(jnp.concatenate([zero, sine], 1), ((0, 0), (0, rest))),
            jnp.pad(jnp.concatenate([-sine, zero], 1), ((0, 0), (0, rest))),
        ]
    )


def turn(x, straight, right, left):
    half = ROT // 2
    return (
        x * straight
        + pltpu.roll(x, half, axis=1) * right
        + pltpu.roll(x, HEAD_DIM - half, axis=1) * left
    )


def mixer(rows, gain_row, opening, closing, closing_bias):
    inverse_rms = lax.rsqrt(jnp.mean(rows * rows, axis=-1, keepdims=True) + EPS_ROOT)
    rooted = rows * inverse_rms * gain_row
    hidden = jnp.dot(rooted, opening, precision=TOP_PRECISION)
    return jnp.dot(gelu(hidden), closing, precision=TOP_PRECISION) + closing_bias


def dot(pattern, left, right):
    return jnp.einsum(pattern, left, right, preferred_element_type=F32)


def remote(src, dst, send_sem, recv_sem, target):
    return pltpu.make_async_remote_copy(
        src_ref=src,
        dst_ref=dst,
        send_sem=send_sem,
        recv_sem=recv_sem,
        device_id=target,
        device_id_type=MESH,
    )


def place():
    return lax.axis_index("fsdp"), lax.axis_index("ctx")


def links_and_twin():
    chips = lax.axis_size("fsdp") // 2
    f, c = place()
    chip, core = f // 2, lax.rem(f, 2)
    return [(lax.rem(chip + j, chips) * 2 + core, c) for j in range(1, chips)] + [
        (chip * 2 + 1 - core, c)
    ]


def along_ctx():
    cn = lax.axis_size("ctx")
    f, c = place()
    return [(f, lax.rem(c + j, cn)) for j in range(1, cn)]


def along_fsdp():
    fn = lax.axis_size("fsdp")
    f, c = place()
    return [(lax.rem(f + j, fn), c) for j in range(1, fn)]


def along_both():
    return along_ctx() + along_fsdp()


def comm(cid, *tasks):
    n = len(tasks)
    counts = [len(t[5]) for t in tasks]

    def kernel(*refs):
        targets, seen = [], []
        covered = [(along_fsdp, [along_both]), (the_pair, [along_ctx])]
        for t in tasks:
            if t[0] not in seen and (t[0], seen[:1]) not in covered:
                seen.append(t[0])
                targets += t[0]()
        barrier = pltpu.get_barrier_semaphore()
        for t in targets:
            pl.semaphore_signal(barrier, inc=1, device_id=t, device_id_type=MESH)
        pl.semaphore_wait(barrier, len(targets))
        scratch = list(refs[2 * n :])
        phases = []
        for i, t in enumerate(tasks):
            mine, scratch = scratch[: counts[i]], scratch[counts[i] :]
            phases.append(t[6](refs[i], refs[n + i], *mine))
        for p in range(3):
            for ph in phases:
                ph[p]()

    out = pl.pallas_call(
        kernel,
        out_shape=[t[2] for t in tasks],
        in_specs=[t[3] for t in tasks],
        out_specs=[t[4] for t in tasks],
        scratch_shapes=[x for t in tasks for x in t[5]],
        compiler_params=pltpu.CompilerParams(
            collective_id=cid, has_side_effects=True, vmem_limit_bytes=40 * 2**20
        ),
        cost_estimate=pl.CostEstimate(flops=0, bytes_accessed=15_000_000, transcendentals=0),
    )(*[t[1] for t in tasks])
    return out


def dma(*shape):
    return pltpu.SemaphoreType.DMA(shape)


def gather_small(x):
    fn, cn = lax.axis_size("fsdp"), lax.axis_size("ctx")

    def body(x_ref, o_ref, s1, r1, s2, r2):
        f, c = place()

        def first(j):
            return remote(
                x_ref, o_ref.at[f, c], s1.at[j], r1.at[j], (f, lax.rem(c + j, cn))
            )

        def second(j):
            return remote(
                o_ref.at[f], o_ref.at[f], s2.at[j], r2.at[j], (lax.rem(f + j, fn), c)
            )

        def start():
            for j in range(1, cn):
                first(j).start()
            o_ref[f, c] = x_ref[...]

        def middle():
            for j in range(1, cn):
                there = o_ref.at[f, lax.rem(c + cn - j, cn)]
                remote(there, there, s1.at[j], r1.at[j], (f, lax.rem(c + j, cn))).wait_recv()
            for j in range(1, fn):
                second(j).start()

        def end():
            for j in range(1, fn):
                there = o_ref.at[lax.rem(f + fn - j, fn)]
                remote(there, there, s2.at[j], r2.at[j], (lax.rem(f + j, fn), c)).wait_recv()
            for j in range(1, cn):
                first(j).wait_send()
            for j in range(1, fn):
                second(j).wait_send()

        return start, middle, end

    shape = jax.ShapeDtypeStruct((fn, cn, *x.shape), x.dtype)
    return (along_both, x, shape, VMEM, VMEM, [dma(cn), dma(cn), dma(fn), dma(fn)], body)


def exchange_fsdp(x):
    fn = lax.axis_size("fsdp")

    def body(x_ref, o_ref, s, r, own):
        f, c = place()

        def copy(j, slot):
            t = lax.rem(f + j, fn)
            return remote(x_ref.at[t], o_ref.at[slot], s.at[j], r.at[j], (t, c))

        mine = pltpu.make_async_copy(x_ref.at[f], o_ref.at[f], own)

        def start():
            for j in range(1, fn):
                copy(j, f).start()
            mine.start()

        def end():
            mine.wait()
            for j in range(1, fn):
                copy(j, lax.rem(f + fn - j, fn)).wait_recv()
            for j in range(1, fn):
                copy(j, f).wait_send()

        return start, lambda: None, end

    shape = jax.ShapeDtypeStruct(x.shape, x.dtype)
    return (along_fsdp, x, shape, ANY, ANY, [dma(fn), dma(fn), dma()], body)


def exchange_ctx(x, to_units):
    cn = lax.axis_size("ctx")
    lead = x.shape[1] if to_units else x.shape[0]

    def body(x_ref, o_ref, s, r, own):
        f, c = place()

        def source(t):
            return x_ref.at[t] if to_units else x_ref.at[:, t]

        def target(slot):
            return o_ref.at[:, slot] if to_units else o_ref.at[slot]

        def copy(j, slot):
            t = lax.rem(c + j, cn)
            return remote(source(t), target(slot), s.at[j], r.at[j], (f, t))

        mine = pltpu.make_async_copy(source(c), target(c), own)

        def start():
            for j in range(1, cn):
                copy(j, c).start()
            mine.start()

        def end():
            mine.wait()
            for j in range(1, cn):
                copy(j, lax.rem(c + cn - j, cn)).wait_recv()
            for j in range(1, cn):
                copy(j, c).wait_send()

        return start, lambda: None, end

    dims = (lead, cn) if to_units else (cn, lead)
    shape = jax.ShapeDtypeStruct((*dims, *x.shape[2:]), x.dtype)
    return (along_ctx, x, shape, ANY, ANY, [dma(cn), dma(cn), dma()], body)


def the_pair():
    f, c = place()
    return [(f, c // 2 * 2 + 1 - lax.rem(c, 2))]


def exchange_pair(x):
    def body(x_ref, o_ref, s, r):
        (pair,) = the_pair()
        copy = remote(x_ref, o_ref, s, r, pair)
        return copy.start, lambda: None, copy.wait

    shape = jax.ShapeDtypeStruct(x.shape, x.dtype)
    return (the_pair, x, shape, ANY, ANY, [dma(), dma()], body)


def gather_fsdp(x, parts=4):
    fn = lax.axis_size("fsdp")
    chips = fn // 2
    n, d = x.shape
    step = n // parts
    pieces = [pl.ds(p * step, step) for p in range(parts)]

    def body(x_ref, o_ref, own_sem, s_link, r_link, s_core, r_core):
        f, c = place()
        chip, core = f // 2, lax.rem(f, 2)
        twin = (chip * 2 + 1 - core, c)
        links, cores = {}, {}

        def to(j):
            return (lax.rem(chip + j, chips) * 2 + core, c)

        def slot(j, core_id):
            return lax.rem(chip + chips - j, chips) * 2 + core_id

        own = pltpu.make_async_copy(x_ref, o_ref.at[f], own_sem)

        def start():
            for i, rows in enumerate(pieces):
                here, there = x_ref.at[rows], o_ref.at[f, rows]
                for j in range(1, chips):
                    links[i, j] = remote(here, there, s_link.at[j, i], r_link.at[j, i], to(j))
                    links[i, j].start()
            for i, rows in enumerate(pieces):
                here, there = x_ref.at[rows], o_ref.at[f, rows]
                cores[i, 0] = remote(here, there, s_core.at[0, i], r_core.at[0, i], twin)
                cores[i, 0].start()
            own.start()

        def middle():
            for i, rows in enumerate(pieces):
                for j in range(1, chips):
                    here = o_ref.at[slot(j, core), rows]
                    remote(here, here, s_link.at[j, i], r_link.at[j, i], to(j)).wait_recv()
                    cores[i, j] = remote(here, here, s_core.at[j, i], r_core.at[j, i], twin)
                    cores[i, j].start()

        def end():
            own.wait()
            for i, rows in enumerate(pieces):
                for j in range(chips):
                    there = o_ref.at[slot(j, 1 - core), rows]
                    cores[i, j].wait_send()
                    remote(there, there, s_core.at[j, i], r_core.at[j, i], twin).wait_recv()
                for j in range(1, chips):
                    links[i, j].wait_send()

        return start, middle, end

    shape = jax.ShapeDtypeStruct((fn, n, d), x.dtype)
    return (links_and_twin, x, shape, ANY, ANY, [dma()] + [dma(chips, parts)] * 4, body)


def gather_ctx(x):
    cn = lax.axis_size("ctx")
    count = cn // 2

    def body(x_ref, o_ref, own_sem, s_up, r_up, s_down, r_down, s_pair, r_pair):
        f, c = place()
        hi, lo = c // 2, lax.rem(c, 2)
        pair = (f, hi * 2 + 1 - lo)
        above = (f, lax.rem(hi + 1, count) * 2 + lo)
        below = (f, lax.rem(hi + count - 1, count) * 2 + lo)
        own = pltpu.make_async_copy(x_ref, o_ref.at[c], own_sem)

        def low(d):
            return lax.rem(hi + count - d, count)

        def high(d):
            return lax.rem(hi + d, count)

        def up(d):
            source = x_ref if d == 0 else o_ref.at[low(d) * 2 + lo]
            return remote(source, o_ref.at[low(d) * 2 + lo], s_up.at[d], r_up.at[d + 1], above)

        def down(d):
            source = x_ref if d == 0 else o_ref.at[high(d) * 2 + lo]
            return remote(
                source, o_ref.at[high(d) * 2 + lo], s_down.at[d], r_down.at[d + 1], below
            )

        def across(k, slot):
            source = x_ref if k == 0 else o_ref.at[slot * 2 + lo]
            return remote(source, o_ref.at[slot * 2 + lo], s_pair.at[k], r_pair.at[k], pair)

        def start():
            pl.when(hi < count - 1)(lambda: up(0).start())
            pl.when(hi > 0)(lambda: down(0).start())
            across(0, hi).start()
            own.start()

        def middle():
            for d in range(1, count):

                @pl.when(hi >= d)
                def _():
                    here = o_ref.at[low(d) * 2 + lo]
                    remote(here, here, s_up.at[d], r_up.at[d], above).wait_recv()
                    across(d, low(d)).start()
                    if d < count - 1:
                        pl.when(hi < count - 1)(lambda: up(d).start())

                @pl.when(hi + d < count)
                def _():
                    here = o_ref.at[high(d) * 2 + lo]
                    remote(here, here, s_down.at[d], r_down.at[d], below).wait_recv()
                    across(count - d, high(d)).start()
                    if d < count - 1:
                        pl.when(hi > 0)(lambda: down(d).start())

        def end():
            own.wait()
            across(0, hi).wait_send()
            for k in range(count):
                there = o_ref.at[low(k) * 2 + 1 - lo]
                remote(there, there, s_pair.at[k], r_pair.at[k], pair).wait_recv()
                if k > 0:
                    across(k, low(k)).wait_send()
            for d in range(count - 1):
                pl.when((hi >= d) & (hi < count - 1))(lambda d=d: up(d).wait_send())
                pl.when((hi + d < count) & (hi > 0))(lambda d=d: down(d).wait_send())

        return start, middle, end

    shape = jax.ShapeDtypeStruct((cn, *x.shape), x.dtype)
    scratch = [dma()] + [dma(count + 1)] * 4 + [dma(count)] * 2
    return (along_ctx, x, shape, ANY, ANY, scratch, body)


def scatter_fsdp(x, parts=4):
    fn = lax.axis_size("fsdp")
    chips = fn // 2
    _, n, d = x.shape
    step = n // parts

    def body(x_ref, o_ref, own, near, mine, far, ss, s_own, s_near, r_near, s_far, r_far):
        f, c = place()
        chip, core = f // 2, lax.rem(f, 2)
        twin = (chip * 2 + 1 - core, c)
        nears, owns, fars, outs = {}, {}, {}, {}

        def chip_at(j):
            return lax.rem(chip + j, chips)

        def start():
            for p in range(parts):
                rows = pl.ds(p * step, step)
                for j in list(range(1, chips)) + [0]:
                    at = chip_at(j) * 2
                    owns[p, j] = pltpu.make_async_copy(
                        x_ref.at[at + core, rows], own.at[j, p], s_own.at[j, p]
                    )
                    owns[p, j].start()
                    nears[p, j] = remote(
                        x_ref.at[at + 1 - core, rows],
                        near.at[j, p],
                        s_near.at[j, p],
                        r_near.at[j, p],
                        twin,
                    )
                    nears[p, j].start()

        def middle():
            for p in range(parts):
                for j in range(1, chips):
                    owns[p, j].wait()
                    nears[p, j].wait_recv()
                    mine[j, p] = (own[j, p].astype(F32) + near[j, p].astype(F32)).astype(BF16)
                    fars[p, j] = remote(
                        mine.at[j, p],
                        far.at[j, p],
                        s_far.at[j, p],
                        r_far.at[j, p],
                        (chip_at(j) * 2 + core, c),
                    )
                    fars[p, j].start()
            for p in range(parts):
                owns[p, 0].wait()
                nears[p, 0].wait_recv()
                ss[p] = own[0, p].astype(F32) + near[0, p].astype(F32)

        def end():
            for p in range(parts):
                for j in range(1, chips):
                    fars[p, j].wait_recv()
                    ss[p] += far[j, p].astype(F32)
                outs[p] = pltpu.make_async_copy(
                    ss.at[p], o_ref.at[pl.ds(p * step, step)], s_far.at[0, p]
                )
                outs[p].start()
            for p in range(parts):
                outs[p].wait()
                for j in range(chips):
                    nears[p, j].wait_send()
                for j in range(1, chips):
                    fars[p, j].wait_send()

        return start, middle, end

    block = pltpu.VMEM((chips, parts, step, d), BF16)
    scratch = [block] * 4 + [pltpu.VMEM((parts, step, d), F32)] + [dma(chips, parts)] * 5
    return (links_and_twin, x, jax.ShapeDtypeStruct((n, d), F32), ANY, ANY, scratch, body)


def scatter_small(x):
    fn, cn = lax.axis_size("fsdp"), lax.axis_size("ctx")

    def body(x_ref, o_ref, got, sums, got2, s1, r1, s2, r2):
        f, c = place()

        def first(j):
            t = lax.rem(f + j, fn)
            return remote(x_ref.at[t], got.at[j], s1.at[j], r1.at[j], (t, c))

        def second(j):
            t = lax.rem(c + j, cn)
            return remote(sums.at[t], got2.at[j], s2.at[j], r2.at[j], (f, t))

        def start():
            for j in range(1, fn):
                first(j).start()
            sums[...] = x_ref[f]

        def middle():
            for j in range(1, fn):
                first(j).wait_recv()
                sums[...] += got[j]
            for j in range(1, cn):
                second(j).start()
            o_ref[...] = sums[c]

        def end():
            for j in range(1, cn):
                second(j).wait_recv()
                o_ref[...] += got2[j]
            for j in range(1, fn):
                first(j).wait_send()
            for j in range(1, cn):
                second(j).wait_send()

        return start, middle, end

    tail = x.shape[2:]
    scratch = [
        pltpu.VMEM(x.shape, x.dtype),
        pltpu.VMEM(x.shape[1:], x.dtype),
        pltpu.VMEM(x.shape[1:], x.dtype),
        dma(fn),
        dma(fn),
        dma(cn),
        dma(cn),
    ]
    return (along_both, x, jax.ShapeDtypeStruct(tail, x.dtype), VMEM, VMEM, scratch, body)


def nt(a, b):
    return lax.dot_general(a, b, (((1,), (1,)), ((), ())), preferred_element_type=F32)


def nn(a, b):
    return lax.dot_general(a, b, (((1,), (0,)), ((), ())), preferred_element_type=F32)


def attend(q, k, v, starts, block=512):
    u, t, _ = q.shape
    scale = HEAD_DIM**-0.5 * LOG2E

    def kernel(q_ref, k_ref, v_ref, s_ref, o_ref, l_ref, vt):
        i = pl.program_id(1)

        @pl.when(i == 0)
        def _():
            vt[...] = v_ref[0].T

        rows = q_ref[0]
        first = s_ref[0]
        base = lax.broadcasted_iota(jnp.int32, (block, block), 0)
        qpos = i * block + lax.broadcasted_iota(jnp.int32, (1, block), 1)

        def one(j, carry, diagonal):
            peak, total, acc = carry
            at = pl.multiple_of(j * block, block)
            s = nt(k_ref[0, pl.ds(at, block)], rows) * scale
            kpos = base + at
            keep = kpos >= first
            if diagonal:
                keep = keep & (kpos <= qpos)
            s = jnp.where(keep, s, NEG_BIG)
            new = jnp.maximum(peak, jnp.max(s, axis=0, keepdims=True))
            p = jnp.exp2(s - new)
            shrink = jnp.exp2(peak - new)
            total = total * shrink + jnp.sum(p, axis=0, keepdims=True)
            acc = acc * shrink + nn(vt[:, pl.ds(at, block)], p.astype(BF16))
            return new, total, acc

        start = (
            jnp.full((1, block), NEG_BIG, F32),
            jnp.zeros((1, block), F32),
            jnp.zeros((HEAD_DIM, block), F32),
        )
        start = one(i, start, True)
        peak, total, acc = lax.fori_loop(0, i, lambda j, c: one(j, c, False), start)
        o_ref[0] = (acc / total).T.astype(BF16)
        l_ref[0] = peak + jnp.log2(total)

    return pl.pallas_call(
        kernel,
        grid=(u, t // block),
        in_specs=[
            pl.BlockSpec((1, block, HEAD_DIM), lambda a, b: (a, b, 0)),
            pl.BlockSpec((1, t, HEAD_DIM), lambda a, b: (a, 0, 0)),
            pl.BlockSpec((1, t, HEAD_DIM), lambda a, b: (a, 0, 0)),
            pl.BlockSpec((1, 1, block), lambda a, b: (a, 0, b)),
        ],
        out_specs=[
            pl.BlockSpec((1, block, HEAD_DIM), lambda a, b: (a, b, 0)),
            pl.BlockSpec((1, 1, block), lambda a, b: (a, 0, b)),
        ],
        out_shape=[
            jax.ShapeDtypeStruct((u, t, HEAD_DIM), BF16),
            jax.ShapeDtypeStruct((u, 1, t), F32),
        ],
        scratch_shapes=[pltpu.VMEM((HEAD_DIM, t), BF16)],
        compiler_params=pltpu.CompilerParams(vmem_limit_bytes=32 * 2**20),
        cost_estimate=pl.CostEstimate(
            flops=2 * u * t * t * HEAD_DIM, bytes_accessed=8 * u * t * 256, transcendentals=u * t * t // 2
        ),
    )(q, k, v, starts)


def attend_back(q, k, v, starts, lse, o, g, tables, block=512):
    u, t, _ = q.shape
    scale = HEAD_DIM**-0.5

    def kernel(
        q_ref, k_ref, v_ref, s_ref, l_ref, o_ref, g_ref, t_ref, dq_ref, dk_ref, dv_ref, kt, dk, dv
    ):
        i = pl.program_id(1)

        @pl.when(i == 0)
        def _():
            kt[...] = k_ref[0].T
            dk[...] = jnp.zeros_like(dk)
            dv[...] = jnp.zeros_like(dv)

        rows, grows = q_ref[0], g_ref[0]
        first, logs = s_ref[0], l_ref[0]
        prod = o_ref[0].astype(F32) * grows.astype(F32)
        centre = jnp.sum(prod.T, axis=0, keepdims=True)
        base = lax.broadcasted_iota(jnp.int32, (block, block), 0)
        qpos = i * block + lax.broadcasted_iota(jnp.int32, (1, block), 1)

        def one(j, acc, diagonal):
            at = pl.multiple_of(j * block, block)
            here = pl.ds(at, block)
            p = jnp.exp2(nt(k_ref[0, here], rows) * (scale * LOG2E) - logs)
            kpos = base + at
            keep = kpos >= first
            if diagonal:
                keep = keep & (kpos <= qpos)
            p = jnp.where(keep, p, 0.0)
            gp = nt(v_ref[0, here], grows)
            ds = (p * (gp - centre)).astype(BF16)
            dv[here] += nn(p.astype(BF16), grows)
            dk[here] += nn(ds, rows)
            return acc + nn(kt[:, here], ds)

        acc = one(i, jnp.zeros((HEAD_DIM, block), F32), True)
        acc = lax.fori_loop(0, i, lambda j, a: one(j, a, False), acc)
        there = pl.ds(pl.multiple_of(i * block, block), block)
        straight, right, left = t_ref[0, there], t_ref[1, there], t_ref[2, there]
        dq_ref[0] = turn((acc * scale).T, straight, -right, -left).astype(BF16)

        @pl.when(i == t // block - 1)
        def _():
            for b in range(t // block):
                at = pl.ds(b * block, block)
                dk_ref[0, at] = turn(
                    dk[at] * scale, t_ref[0, at], -t_ref[1, at], -t_ref[2, at]
                ).astype(BF16)
                dv_ref[0, at] = dv[at].astype(BF16)

    def whole(a, b):
        return (a, 0, 0)

    def part(a, b):
        return (a, b, 0)

    def row(a, b):
        return (a, 0, b)

    spec, full, line = (1, block, HEAD_DIM), (1, t, HEAD_DIM), (1, 1, block)
    return pl.pallas_call(
        kernel,
        grid=(u, t // block),
        in_specs=[
            pl.BlockSpec(spec, part),
            pl.BlockSpec(full, whole),
            pl.BlockSpec(full, whole),
            pl.BlockSpec(line, row),
            pl.BlockSpec(line, row),
            pl.BlockSpec(spec, part),
            pl.BlockSpec(spec, part),
            pl.BlockSpec((3, t, HEAD_DIM), lambda a, b: (0, 0, 0)),
        ],
        out_specs=[
            pl.BlockSpec(spec, part),
            pl.BlockSpec(full, whole),
            pl.BlockSpec(full, whole),
        ],
        out_shape=[jax.ShapeDtypeStruct((u, t, HEAD_DIM), BF16)] * 3,
        scratch_shapes=[
            pltpu.VMEM((HEAD_DIM, t), BF16),
            pltpu.VMEM((t, HEAD_DIM), F32),
            pltpu.VMEM((t, HEAD_DIM), F32),
        ],
        compiler_params=pltpu.CompilerParams(vmem_limit_bytes=48 * 2**20),
        cost_estimate=pl.CostEstimate(
            flops=5 * u * t * t * HEAD_DIM, bytes_accessed=20 * u * t * 256, transcendentals=u * t * t // 2
        ),
    )(q, k, v, starts, lse, o, g, tables)


def project(x, w, bias, tables):
    count, length, width = x.shape
    cn, fn, rows, cols = w.shape
    heads = cols // HEAD_DIM

    def kernel(*refs):
        x_ref, w_ref, b_ref = refs[:3]
        o_ref, held, sem = refs[-3:]

        @pl.when(pl.program_id(0) == 0)
        def _():
            copies = [
                pltpu.make_async_copy(w_ref.at[:, f], held.at[f], sem.at[f])
                for f in range(fn)
            ]
            for c in copies:
                c.start()
            for c in copies:
                c.wait()

        y = nn(x_ref[0], held[...].reshape(width, cols)) + b_ref[...]
        for h in range(heads):
            part = y[:, h * HEAD_DIM : (h + 1) * HEAD_DIM]
            if tables is not None:
                t_ref = refs[3]
                part = turn(part, t_ref[0], t_ref[1], t_ref[2])
            o_ref[h] = part.astype(BF16)

    extra = [] if tables is None else [tables]
    return pl.pallas_call(
        kernel,
        grid=(count,),
        in_specs=[
            pl.BlockSpec((1, length, width), lambda i: (i, 0, 0)),
            ANY,
            pl.BlockSpec((1, cols), lambda i: (0, 0)),
        ]
        + [pl.BlockSpec((3, length, HEAD_DIM), lambda i: (0, 0, 0)) for _ in extra],
        out_specs=pl.BlockSpec((heads, length, HEAD_DIM), lambda i: (i, 0, 0)),
        out_shape=jax.ShapeDtypeStruct((count * heads, length, HEAD_DIM), BF16),
        scratch_shapes=[pltpu.VMEM((fn, cn, rows, cols), BF16), dma(fn)],
        compiler_params=pltpu.CompilerParams(vmem_limit_bytes=32 * 2**20),
        cost_estimate=pl.CostEstimate(
            flops=2 * count * length * width * cols,
            bytes_accessed=2 * (count * length * (width + cols) + width * cols),
            transcendentals=0,
        ),
    )(x, w, bias, *extra)


def widen(x, w, bias, tile=256, rows_at_once=512):
    n, d = x.shape
    cn, fn, rows, cols = w.shape
    tiles = cols // tile

    def kernel(x_ref, w_ref, b_ref, a_ref, g_ref, o_ref, held, sem):
        i = pl.program_id(0)

        def copy(j, f):
            at = pl.ds(pl.multiple_of(j * tile, tile), tile)
            return pltpu.make_async_copy(w_ref.at[:, f, :, at], held.at[j, f], sem.at[j, f])

        @pl.when(i == 0)
        def _():
            for j in range(tiles):
                for f in range(fn):
                    copy(j, f).start()

        for f in range(fn):
            copy(i, f).wait()
        w_tile = held[i].reshape(d, tile)
        o_ref[...] = w_tile
        for r in range(0, n, rows_at_once):
            part = pl.ds(r, rows_at_once)
            y = nn(x_ref[part], w_tile) + b_ref[...]
            t = y * math.sqrt(0.5)
            below = 0.5 + 0.5 * lax.erf(t)
            a_ref[part] = (y * below).astype(BF16)
            density = jnp.exp(-t * t) * (1.0 / math.sqrt(2.0 * math.pi))
            g_ref[part] = (below + y * density).astype(BF16)

    column = pl.BlockSpec((n, tile), lambda i: (0, i))
    return pl.pallas_call(
        kernel,
        grid=(tiles,),
        in_specs=[
            pl.BlockSpec((n, d), lambda i: (0, 0)),
            ANY,
            pl.BlockSpec((1, tile), lambda i: (0, i)),
        ],
        out_specs=[column, column, pl.BlockSpec((d, tile), lambda i: (0, i))],
        out_shape=[
            jax.ShapeDtypeStruct((n, cols), BF16),
            jax.ShapeDtypeStruct((n, cols), BF16),
            jax.ShapeDtypeStruct((d, cols), BF16),
        ],
        scratch_shapes=[pltpu.VMEM((tiles, fn, cn, rows, tile), BF16), dma(tiles, fn)],
        compiler_params=pltpu.CompilerParams(vmem_limit_bytes=48 * 2**20),
        cost_estimate=pl.CostEstimate(
            flops=2 * n * d * cols, bytes_accessed=60_000_000, transcendentals=0
        ),
    )(x, w, bias)


def front(hist, mix, gain, shift, tokens=16, wide=256):
    h, n, d = hist.shape
    rest = gain.shape[0]

    def kernel(h_ref, m_ref, g_ref, b_ref, s_ref, n_ref):
        m = m_ref[...]
        for at in range(0, d, wide):
            cut = slice(at, at + wide)
            for s in range(4):
                acc = m[:, s * h : s * h + 1] * h_ref[0, :, cut].astype(F32)
                for j in range(1, h):
                    acc += m[:, s * h + j : s * h + j + 1] * h_ref[j, :, cut].astype(F32)
                s_ref[s, :, cut] = acc
        for s in range(rest):
            x = s_ref[s]
            centre = x - jnp.mean(x, axis=-1, keepdims=True)
            spread = jnp.mean(centre * centre, axis=-1, keepdims=True)
            y = centre * lax.rsqrt(spread + EPS_NORM) * g_ref[s : s + 1] + b_ref[s : s + 1]
            n_ref[s] = y.astype(BF16)

    return pl.pallas_call(
        kernel,
        grid=(n // tokens,),
        in_specs=[
            pl.BlockSpec((h, tokens, d), lambda i: (0, i, 0)),
            pl.BlockSpec((tokens, 128), lambda i: (i, 0)),
            pl.BlockSpec((rest, d), lambda i: (0, 0)),
            pl.BlockSpec((rest, d), lambda i: (0, 0)),
        ],
        out_specs=[
            pl.BlockSpec((4, tokens, d), lambda i: (0, i, 0)),
            pl.BlockSpec((rest, tokens, d), lambda i: (0, i, 0)),
        ],
        out_shape=[
            jax.ShapeDtypeStruct((4, n, d), F32),
            jax.ShapeDtypeStruct((rest, n, d), BF16),
        ],
        compiler_params=pltpu.CompilerParams(vmem_limit_bytes=60 * 2**20),
        cost_estimate=pl.CostEstimate(
            flops=2 * 4 * h * n * d, bytes_accessed=n * d * (2 * h + 22), transcendentals=0
        ),
    )(hist, mix, gain, shift)


def last(hist, mix, streams, gain, grads, grad_hidden, tokens=16, wide=256):
    h, n, d = hist.shape
    rest = gain.shape[0]

    def kernel(h_ref, m_ref, s_ref, g_ref, d0, d1, d2, r_ref, gh_ref, gm_ref, gg_ref, gb_ref, ds):
        @pl.when(pl.program_id(0) == 0)
        def _():
            gg_ref[...] = jnp.zeros_like(gg_ref)
            gb_ref[...] = jnp.zeros_like(gb_ref)

        for s, d_ref in enumerate((d0, d1, d2)):
            x = s_ref[s]
            centre = x - jnp.mean(x, axis=-1, keepdims=True)
            inverse = lax.rsqrt(jnp.mean(centre * centre, axis=-1, keepdims=True) + EPS_NORM)
            unit = centre * inverse
            dn = d_ref[...]
            gg_ref[s : s + 1] += jnp.sum(dn * unit, axis=0, keepdims=True)
            gb_ref[s : s + 1] += jnp.sum(dn, axis=0, keepdims=True)
            du = dn * g_ref[s : s + 1]
            ds[s] = inverse * (
                du
                - jnp.mean(du, axis=-1, keepdims=True)
                - unit * jnp.mean(du * unit, axis=-1, keepdims=True)
            )
        ds[rest] = r_ref[...]
        m = m_ref[...]
        sums = [[jnp.zeros((tokens, 128), F32) for _ in range(h)] for _ in range(4)]
        for at in range(0, d, wide):
            cut = slice(at, at + wide)
            parts = [ds[s, :, cut] for s in range(4)]
            for j in range(h):
                row = h_ref[j, :, cut].astype(F32)
                acc = m[:, j : j + 1] * parts[0]
                for s in range(1, 4):
                    acc += m[:, s * h + j : s * h + j + 1] * parts[s]
                gh_ref[j, :, cut] = acc
                for s in range(4):
                    prod = row * parts[s]
                    for b in range(0, wide, 128):
                        sums[s][j] += prod[:, b : b + 128]
        lane = lax.broadcasted_iota(jnp.int32, (tokens, 128), 1)
        total = jnp.zeros((tokens, 128), F32)
        for s in range(4):
            for j in range(h):
                value = jnp.sum(sums[s][j], axis=-1, keepdims=True)
                total = jnp.where(lane == s * h + j, value, total)
        gm_ref[...] = total

    row = pl.BlockSpec((tokens, d), lambda i: (i, 0))
    lines = pl.BlockSpec((rest, d), lambda i: (0, 0))
    return pl.pallas_call(
        kernel,
        grid=(n // tokens,),
        in_specs=[
            pl.BlockSpec((h, tokens, d), lambda i: (0, i, 0)),
            pl.BlockSpec((tokens, 128), lambda i: (i, 0)),
            pl.BlockSpec((4, tokens, d), lambda i: (0, i, 0)),
            lines,
            row,
            row,
            row,
            row,
        ],
        out_specs=[
            pl.BlockSpec((h, tokens, d), lambda i: (0, i, 0)),
            pl.BlockSpec((tokens, 128), lambda i: (i, 0)),
            lines,
            lines,
        ],
        out_shape=[
            jax.ShapeDtypeStruct((h, n, d), F32),
            jax.ShapeDtypeStruct((n, 128), F32),
            jax.ShapeDtypeStruct((rest, d), F32),
            jax.ShapeDtypeStruct((rest, d), F32),
        ],
        scratch_shapes=[pltpu.VMEM((4, tokens, d), F32)],
        compiler_params=pltpu.CompilerParams(vmem_limit_bytes=60 * 2**20),
        cost_estimate=pl.CostEstimate(
            flops=4 * 4 * h * n * d, bytes_accessed=n * d * (6 * h + 32), transcendentals=0
        ),
    )(hist, mix, streams, gain, *grads, grad_hidden)


def body(
    history,
    dense_mix,
    doc_starts,
    norm_gain,
    norm_bias,
    qkv_weight,
    qkv_bias,
    out_weight,
    out_bias,
    up_weight,
    up_bias,
    down_weight,
    down_bias,
    root_gain,
    mix_in_weight,
    mix_out_weight,
    mix_out_bias,
    out_cotangent,
    mix_cotangent,
):
    fn, cn = lax.axis_size("fsdp"), lax.axis_size("ctx")
    dn = fn * cn
    fi, ci = lax.axis_index("fsdp"), lax.axis_index("ctx")
    hist, seqs, length, width = history.shape
    nloc = seqs * length
    ntp = fn * nloc
    rows = qkv_weight.shape[0]
    ff = up_weight.shape[1]
    wcol, fcol = width // fn, ff // fn
    heads = wcol // HEAD_DIM
    units = fn * seqs * heads // cn
    total = cn * length
    mixn = mix_in_weight.shape[1]

    wdown = lax.all_gather(down_weight, "ctx", axis=0, tiled=True)

    parts = [
        norm_gain,
        norm_bias,
        qkv_bias,
        out_bias,
        up_bias,
        down_bias,
        root_gain,
        mix_in_weight,
        doc_starts.astype(F32),
    ]
    flat = jnp.concatenate([a.reshape(-1) for a in parts])
    flat = jnp.pad(flat, (0, -flat.size % 1024)).reshape(-1, 128)
    flats, qkv_cols, up_cols = comm(
        1,
        gather_small(flat),
        exchange_fsdp(qkv_weight.reshape(rows, 3, fn, wcol).transpose(2, 1, 0, 3)),
        exchange_fsdp(up_weight.reshape(rows, fn, fcol).transpose(1, 0, 2)),
    )
    flats = flats.reshape(dn, -1)
    pieces, at = [], 0
    for a in parts:
        pieces.append(flats[:, at : at + a.size])
        at += a.size

    def joined(piece, lead):
        return piece.reshape(dn, lead, -1).transpose(1, 0, 2).reshape(lead, -1)

    gain_all = joined(pieces[0], 4)
    shift_all = joined(pieces[1], 4)
    qkv_shift = joined(pieces[2], 3)
    out_shift = pieces[3].reshape(-1)
    up_shift = pieces[4].reshape(-1)
    down_shift = pieces[5].reshape(-1)
    root_full = pieces[6].reshape(-1)
    mix_in_full = pieces[7].reshape(width, mixn)
    starts = pieces[8].reshape(fn, cn, seqs, -1)[:, 0].astype(jnp.int32)

    hist2 = history.reshape(hist, nloc, width)
    mix2 = dense_mix.reshape(dense_mix.shape[0], hist, nloc)
    mixes = jnp.pad(mix2.reshape(-1, nloc).T, ((0, 0), (0, 128 - mix2.shape[0] * hist)))
    streams, normed = front(hist2, mixes, gain_all[:3], shift_all[:3])

    bias_cols = lax.dynamic_slice_in_dim(qkv_shift, fi * wcol, wcol, 1)
    tables = rotary_tables(total)
    tables_l = lax.dynamic_slice_in_dim(tables, ci * length, length, 1)

    def projected(x, w, s):
        y = project(
            x.reshape(fn * seqs, length, width),
            w,
            bias_cols[s : s + 1],
            tables_l if s < 2 else None,
        )
        return y.reshape(cn, units, length, HEAD_DIM)

    def whole_units(x):
        return x.reshape(units, total, HEAD_DIM)

    def from_units(x):
        return exchange_ctx(x.reshape(units, cn, length, HEAD_DIM), False)

    def columns(x):
        x = x.reshape(fn * seqs, heads, length, HEAD_DIM)
        return x.transpose(0, 2, 1, 3).reshape(ntp, wcol)

    cols_of = [qkv_cols[:, s] for s in range(3)]
    g0, w0 = comm(9, gather_ctx(cols_of[0]), gather_fsdp(normed[0]))[::-1]
    p0 = projected(g0, w0, 0)
    q_u, w1, g1 = comm(4, exchange_ctx(p0, True), gather_ctx(cols_of[1]), gather_fsdp(normed[1]))
    p1 = projected(g1, w1, 1)
    p1, up_cols, out_rows, wdown = lax.optimization_barrier((p1, up_cols, out_weight, wdown))
    wout = lax.all_gather(out_rows, "ctx", axis=0, tiled=True)
    up_g = lax.all_gather(up_cols, "ctx", axis=0)
    k_u, w2, g2 = comm(4, exchange_ctx(p1, True), gather_ctx(cols_of[2]), gather_fsdp(normed[2]))
    p2 = projected(g2, w2, 2)
    (v_u,) = comm(5, exchange_ctx(p2, True))
    wqkv = [w.transpose(1, 0, 2, 3).reshape(width, wcol) for w in (w0, w1, w2)]
    q_u, k_u, v_u = whole_units(q_u), whole_units(k_u), whole_units(v_u)
    normed_g = [g.reshape(ntp, width) for g in (g0, g1, g2)]

    pos_all = jnp.arange(total, dtype=jnp.int32)
    unit_ids = ci * units + jnp.arange(units, dtype=jnp.int32)
    seq_ids = unit_ids // heads
    unit_starts = starts.reshape(fn * seqs, -1)[seq_ids]
    first_key = jnp.max(
        jnp.where(unit_starts[:, None, :] <= pos_all[None, :, None], unit_starts[:, None, :], 0),
        axis=-1,
    )[:, None, :]
    att_u, lse_u = attend(q_u, k_u, v_u, first_key)
    attended = columns(comm(6, from_units(att_u))[0])

    def scatter_tokens(x):
        return comm(10, scatter_fsdp(x.astype(BF16).reshape(fn, nloc, width)))[0]

    def gather_tokens(x):
        return comm(3, gather_fsdp(x))[0].reshape(ntp, width)

    hidden_res = streams[3] + scatter_tokens(dot("nd,de->ne", attended, wout)) + out_shift
    normed_mlp, mid_pull = jax.vjp(layer_norm, hidden_res, gain_all[3], shift_all[3])
    mlp_g = gather_tokens(normed_mlp.astype(BF16))
    up_bias_cols = lax.dynamic_slice_in_dim(up_shift, fi * fcol, fcol, 0)
    act_low, slope, wup = widen(mlp_g, up_g, up_bias_cols[None])
    result = hidden_res + scatter_tokens(dot("nf,fd->nd", act_low, wdown)) + down_shift
    block_out = result.astype(BF16).reshape(seqs, length, width)

    next_rows, mixer_pull = jax.vjp(
        mixer, result, root_full, mix_in_full, mix_out_weight, mix_out_bias
    )
    next_mix = next_rows.T.reshape(-1, seqs, length)
    grad_result, grad_root, grad_mix_in, grad_mix_out, grad_mix_bias = mixer_pull(
        mix_cotangent.reshape(-1, nloc).T
    )
    grad_result = grad_result + out_cotangent.reshape(nloc, width).astype(F32)

    grad_branch = grad_result.astype(BF16)
    branch_g = gather_tokens(grad_branch)
    grad_down_shift = jnp.sum(grad_branch.astype(F32), axis=0)

    low_bit = lax.rem(ci, 2)
    pairs = [(i, i ^ 1) for i in range(cn)]
    lines = [list(range(b, cn, 2)) for b in range(2)]

    def halves(x):
        x = x.reshape(cn // 2, 2, *x.shape[1:])
        away = lax.dynamic_index_in_dim(x, 1 - low_bit, 1, keepdims=False)
        kept = lax.dynamic_index_in_dim(x, low_bit, 1, keepdims=False)
        return away, kept

    def joined_half(kept, come):
        return (kept.astype(F32) + come.astype(F32)).astype(BF16)

    def line_scatter(x):
        y = lax.psum_scatter(
            x.reshape(-1, x.shape[-1]),
            "ctx",
            scatter_dimension=0,
            axis_index_groups=lines,
            tiled=True,
        )
        return y.reshape(x.shape[1:])

    down_part = dot("nf,nd->fd", act_low, branch_g).astype(BF16)
    down_part, wdown = lax.optimization_barrier((down_part, wdown))
    grad_down = lax.psum_scatter(down_part, "ctx", scatter_dimension=0, tiled=True)
    grad_active = dot("nd,fd->nf", branch_g, wdown)
    grad_upward = (grad_active * slope.astype(F32)).astype(BF16)
    grad_up_shift = jnp.sum(grad_upward.astype(F32), axis=0)
    up_part = dot("nd,nf->df", mlp_g, grad_upward).astype(BF16)
    up_part = up_part.reshape(fn, cn // 2, 2, rows, fcol)

    def up_rows(bit):
        x = lax.dynamic_index_in_dim(up_part, bit, 2, keepdims=False)
        return x.transpose(1, 0, 2, 3).reshape(cn // 2, -1, fcol)

    up_away, grad_upward = lax.optimization_barrier((up_rows(1 - low_bit), grad_upward))
    up_half = joined_half(up_rows(low_bit), lax.ppermute(up_away, "ctx", pairs))
    mlp_part = dot("nf,df->nd", grad_upward, wup).astype(BF16)
    grad_mlp = scatter_tokens(mlp_part)
    grad_hidden, grad_gain_mid, grad_shift_mid = mid_pull(grad_mlp)
    grad_hidden = grad_hidden + grad_result
    grad_attn = grad_hidden.astype(BF16)
    grad_out_shift = jnp.sum(grad_attn.astype(F32), axis=0)
    attn_g = gather_tokens(grad_attn)
    out_part = dot("nd,ne->de", attended, attn_g).astype(BF16)
    grad_att = dot("ne,de->nd", attn_g, wout).astype(BF16)
    grad_att = grad_att.reshape(fn * seqs, length, heads, HEAD_DIM).transpose(0, 2, 1, 3)
    out_away, out_kept = halves(out_part.reshape(cn, -1, width))
    (g_u,) = comm(5, exchange_ctx(grad_att.reshape(cn, units, length, HEAD_DIM), True))
    g_u, grad_down, up_half = lax.optimization_barrier((g_u, grad_down, up_half))
    grad_up = line_scatter(up_half)
    gq, gk, gv = attend_back(q_u, k_u, v_u, first_key, lse_u, att_u, whole_units(g_u), tables)

    def qkv_halves(p, s):
        x = dot("nd,nc->dc", normed_g[s], p).astype(BF16).reshape(fn, cn, rows, wcol)
        return halves(x.transpose(1, 0, 2, 3).reshape(cn, -1, wcol))

    def back_part(p, s):
        return dot("nc,dc->nd", p, wqkv[s]).astype(BF16).reshape(fn, nloc, width)

    gp0, out_come = comm(12, from_units(gq), exchange_pair(out_away))
    gp0 = columns(gp0)
    q_away, q_kept = qkv_halves(gp0, 0)
    gp1, q_come, gn0 = comm(
        8, from_units(gk), exchange_pair(q_away), scatter_fsdp(back_part(gp0, 0))
    )
    gp1 = columns(gp1)
    k_away, k_kept = qkv_halves(gp1, 1)
    gp2, k_come, gn1 = comm(
        8, from_units(gv), exchange_pair(k_away), scatter_fsdp(back_part(gp1, 1))
    )
    gp2, grad_up = lax.optimization_barrier((gp2, grad_up))
    out_half = joined_half(out_kept, out_come).reshape(cn // 2, -1, wcol)
    early = [joined_half(q_kept, q_come), joined_half(k_kept, k_come), out_half]
    early = line_scatter(jnp.concatenate(early, axis=1))
    grad_qk, grad_out = early[: 2 * fn * rows], early[2 * fn * rows :].reshape(rows, width)
    gp2 = columns(gp2)
    v_away, v_kept = qkv_halves(gp2, 2)
    gn2, v_come, grad_up = comm(
        7,
        scatter_fsdp(back_part(gp2, 2)),
        exchange_pair(v_away),
        exchange_fsdp(grad_up.reshape(fn, rows, fcol)),
    )
    grad_up = grad_up.transpose(1, 0, 2).reshape(rows, ff)
    grad_v = line_scatter(joined_half(v_kept, v_come))
    grad_proj = (gp0, gp1, gp2)
    grad_qkv = jnp.concatenate(
        [grad_qk.reshape(2, fn, rows, wcol), grad_v.reshape(1, fn, rows, wcol)], axis=0
    )
    grad_qkv = lax.all_to_all(grad_qkv.transpose(1, 0, 2, 3), "fsdp", 0, 0, tiled=True)
    grad_qkv = grad_qkv.transpose(2, 1, 0, 3).reshape(rows, 3, width).astype(F32)
    grad_qkv_shift = jnp.stack([jnp.sum(g.astype(F32), axis=0) for g in grad_proj])

    grad_history, grad_mix, grad_gain_front, grad_shift_front = last(
        hist2, mixes, streams, gain_all[:3], (gn0, gn1, gn2), grad_hidden
    )
    grad_history = grad_history.reshape(history.shape)
    grad_mix = grad_mix[:, : mix2.shape[0] * hist].T.reshape(dense_mix.shape)

    def own_columns(x, full):
        zero = jnp.zeros((x.shape[0], full), F32)
        return lax.dynamic_update_slice_in_dim(zero, x, fi * x.shape[1], 1)

    def parted(x):
        k = x.shape[0]
        return x.reshape(k, dn, -1).transpose(1, 0, 2).reshape(dn, -1)

    sums = [
        parted(jnp.concatenate([grad_gain_front, grad_gain_mid[None]], axis=0)),
        parted(jnp.concatenate([grad_shift_front, grad_shift_mid[None]], axis=0)),
        parted(own_columns(grad_qkv_shift, width)),
        parted(grad_out_shift[None]),
        parted(own_columns(grad_up_shift[None], ff)),
        parted(grad_down_shift[None]),
        parted(grad_root[None]),
        grad_mix_in.reshape(dn, -1),
    ]
    same = jnp.concatenate([grad_mix_out.reshape(-1), grad_mix_bias])
    sums.append(jnp.broadcast_to(same[None], (dn, same.size)))
    flat = jnp.concatenate(sums, axis=1)
    flat = jnp.pad(flat, ((0, 0), (0, -flat.shape[1] % 1024)))
    small = comm(2, scatter_small(flat.reshape(fn, cn, -1, 128)))[0].reshape(-1)
    out_small, at = [], 0
    for s, shape in zip(sums[:-1], [a.shape for a in parts[:-1]], strict=True):
        out_small.append(small[at : at + s.shape[1]].reshape(shape))
        at += s.shape[1]
    (g_gain, g_shift, g_qkv_b, g_out_b, g_up_b, g_down_b, g_root, g_mix_in) = out_small
    mix_sums = small[at : at + same.size]
    cut = grad_mix_out.size
    return (
        block_out,
        next_mix,
        grad_history,
        grad_mix,
        g_gain,
        g_shift,
        grad_qkv,
        g_qkv_b,
        grad_out.astype(F32),
        g_out_b,
        grad_up.astype(F32),
        g_up_b,
        grad_down.astype(F32),
        g_down_b,
        g_root,
        g_mix_in,
        mix_sums[:cut].reshape(grad_mix_out.shape),
        mix_sums[cut:],
    )


def solution(mesh):
    token = P(None, "fsdp", "ctx")
    both = P(BOTH)
    cols = P(None, BOTH)
    placed = (
        token,
        P(None, None, "fsdp", "ctx"),
        P("fsdp"),
        cols,
        cols,
        both,
        cols,
        both,
        both,
        both,
        both,
        both,
        both,
        both,
        both,
        P(),
        P(),
        P("fsdp", "ctx"),
        token,
    )
    outs = (
        P("fsdp", "ctx"),
        token,
        token,
        P(None, None, "fsdp", "ctx"),
        cols,
        cols,
        both,
        cols,
        both,
        both,
        both,
        both,
        both,
        both,
        both,
        both,
        P(),
        P(),
    )
    return jax.shard_map(body, mesh=mesh, in_specs=placed, out_specs=outs, check_vma=False)
```

```python
import math

import jax
import jax.numpy as jnp
import numpy as np
from jax import lax
from jax.experimental import pallas as pl
from jax.experimental.pallas import tpu as pltpu
from jax.sharding import PartitionSpec as P

HEAD_DIM = 128
ROT = 32
TOP_PRECISION = lax.Precision.HIGHEST
EPS_NORM = 1e-05
EPS_ROOT = 1e-06
NEG_BIG = -1e30
BOTH = ("fsdp", "ctx")
BF16 = jnp.bfloat16
F32 = jnp.float32
MESH = pl.DeviceIdType.MESH
ANY = pl.BlockSpec(memory_space=pl.ANY)
VMEM = pl.BlockSpec(memory_space=pltpu.VMEM)
LOG2E = 1.4426950408889634


def layer_norm(values, gain_row, shift_row):
    centre = values - jnp.mean(values, axis=-1, keepdims=True)
    spread = jnp.mean(centre * centre, axis=-1, keepdims=True)
    return centre * lax.rsqrt(spread + EPS_NORM) * gain_row + shift_row


def gelu(values):
    return jax.nn.gelu(values, approximate=False)


def rotary_tables(count):
    half = ROT // 2
    frequency = np.exp(np.arange(half, dtype=np.float32) * np.float32(-2.0 * math.log(10000.0) / ROT))
    angles = np.arange(count, dtype=np.float32)[:, None] * frequency.astype(np.float32)[None, :]
    cosine = jnp.asarray(np.cos(angles.astype(np.float64)), F32)
    sine = jnp.asarray(np.sin(angles.astype(np.float64)), F32)
    zero, rest = jnp.zeros_like(sine), HEAD_DIM - ROT
    return jnp.stack(
        [
            jnp.pad(jnp.concatenate([cosine, cosine], 1), ((0, 0), (0, rest)), constant_values=1.0),
            jnp.pad(jnp.concatenate([zero, sine], 1), ((0, 0), (0, rest))),
            jnp.pad(jnp.concatenate([-sine, zero], 1), ((0, 0), (0, rest))),
        ]
    )


def turn(x, straight, right, left):
    half = ROT // 2
    return (
        x * straight
        + pltpu.roll(x, half, axis=1) * right
        + pltpu.roll(x, HEAD_DIM - half, axis=1) * left
    )


def mixer(rows, gain_row, opening, closing, closing_bias):
    inverse_rms = lax.rsqrt(jnp.mean(rows * rows, axis=-1, keepdims=True) + EPS_ROOT)
    rooted = rows * inverse_rms * gain_row
    hidden = jnp.dot(rooted, opening, precision=TOP_PRECISION)
    return jnp.dot(gelu(hidden), closing, precision=TOP_PRECISION) + closing_bias


def dot(pattern, left, right):
    return jnp.einsum(pattern, left, right, preferred_element_type=F32)


def remote(src, dst, send_sem, recv_sem, target):
    return pltpu.make_async_remote_copy(
        src_ref=src,
        dst_ref=dst,
        send_sem=send_sem,
        recv_sem=recv_sem,
        device_id=target,
        device_id_type=MESH,
    )


def place():
    return lax.axis_index("fsdp"), lax.axis_index("ctx")


def links_and_twin():
    chips = lax.axis_size("fsdp") // 2
    f, c = place()
    chip, core = f // 2, lax.rem(f, 2)
    return [(lax.rem(chip + j, chips) * 2 + core, c) for j in range(1, chips)] + [
        (chip * 2 + 1 - core, c)
    ]


def along_ctx():
    cn = lax.axis_size("ctx")
    f, c = place()
    return [(f, lax.rem(c + j, cn)) for j in range(1, cn)]


def along_fsdp():
    fn = lax.axis_size("fsdp")
    f, c = place()
    return [(lax.rem(f + j, fn), c) for j in range(1, fn)]


def along_both():
    return along_ctx() + along_fsdp()


def comm(cid, *tasks):
    n = len(tasks)
    counts = [len(t[5]) for t in tasks]

    def kernel(*refs):
        targets, seen = [], []
        covered = [
            (along_fsdp, [along_both]),
            (the_pair, [along_ctx]),
            (the_pair, [plane_others]),
            (links_and_twin, [plane_others]),
            (along_fsdp, [plane_others]),
        ]
        for t in tasks:
            if t[0] not in seen and (t[0], seen[:1]) not in covered:
                seen.append(t[0])
                targets += t[0]()
        barrier = pltpu.get_barrier_semaphore()
        for t in targets:
            pl.semaphore_signal(barrier, inc=1, device_id=t, device_id_type=MESH)
        pl.semaphore_wait(barrier, len(targets))
        scratch = list(refs[2 * n :])
        phases = []
        for i, t in enumerate(tasks):
            mine, scratch = scratch[: counts[i]], scratch[counts[i] :]
            phases.append(t[6](refs[i], refs[n + i], *mine))
        for p in range(3):
            for ph in phases:
                ph[p]()

    out = pl.pallas_call(
        kernel,
        out_shape=[t[2] for t in tasks],
        in_specs=[t[3] for t in tasks],
        out_specs=[t[4] for t in tasks],
        scratch_shapes=[x for t in tasks for x in t[5]],
        compiler_params=pltpu.CompilerParams(
            collective_id=cid, has_side_effects=True, vmem_limit_bytes=56 * 2**20
        ),
        cost_estimate=pl.CostEstimate(flops=0, bytes_accessed=15_000_000, transcendentals=0),
    )(*[t[1] for t in tasks])
    return out


def dma(*shape):
    return pltpu.SemaphoreType.DMA(shape)


def gather_small(x):
    fn, cn = lax.axis_size("fsdp"), lax.axis_size("ctx")

    def body(x_ref, o_ref, s1, r1, s2, r2):
        f, c = place()

        def first(j):
            return remote(
                x_ref, o_ref.at[f, c], s1.at[j], r1.at[j], (f, lax.rem(c + j, cn))
            )

        def second(j):
            return remote(
                o_ref.at[f], o_ref.at[f], s2.at[j], r2.at[j], (lax.rem(f + j, fn), c)
            )

        def start():
            for j in range(1, cn):
                first(j).start()
            o_ref[f, c] = x_ref[...]

        def middle():
            for j in range(1, cn):
                there = o_ref.at[f, lax.rem(c + cn - j, cn)]
                remote(there, there, s1.at[j], r1.at[j], (f, lax.rem(c + j, cn))).wait_recv()
            for j in range(1, fn):
                second(j).start()

        def end():
            for j in range(1, fn):
                there = o_ref.at[lax.rem(f + fn - j, fn)]
                remote(there, there, s2.at[j], r2.at[j], (lax.rem(f + j, fn), c)).wait_recv()
            for j in range(1, cn):
                first(j).wait_send()
            for j in range(1, fn):
                second(j).wait_send()

        return start, middle, end

    shape = jax.ShapeDtypeStruct((fn, cn, *x.shape), x.dtype)
    return (along_both, x, shape, VMEM, VMEM, [dma(cn), dma(cn), dma(fn), dma(fn)], body)


def exchange_fsdp(x):
    fn = lax.axis_size("fsdp")

    def body(x_ref, o_ref, s, r, own):
        f, c = place()

        def copy(j, slot):
            t = lax.rem(f + j, fn)
            return remote(x_ref.at[t], o_ref.at[slot], s.at[j], r.at[j], (t, c))

        mine = pltpu.make_async_copy(x_ref.at[f], o_ref.at[f], own)

        def start():
            for j in range(1, fn):
                copy(j, f).start()
            mine.start()

        def end():
            mine.wait()
            for j in range(1, fn):
                copy(j, lax.rem(f + fn - j, fn)).wait_recv()
            for j in range(1, fn):
                copy(j, f).wait_send()

        return start, lambda: None, end

    shape = jax.ShapeDtypeStruct(x.shape, x.dtype)
    return (along_fsdp, x, shape, ANY, ANY, [dma(fn), dma(fn), dma()], body)


def exchange_ctx(x, to_units):
    cn = lax.axis_size("ctx")
    lead = x.shape[1] if to_units else x.shape[0]

    def body(x_ref, o_ref, s, r, own):
        f, c = place()

        def source(t):
            return x_ref.at[t] if to_units else x_ref.at[:, t]

        def target(slot):
            return o_ref.at[:, slot] if to_units else o_ref.at[slot]

        def copy(j, slot):
            t = lax.rem(c + j, cn)
            return remote(source(t), target(slot), s.at[j], r.at[j], (f, t))

        mine = pltpu.make_async_copy(source(c), target(c), own)

        def start():
            for j in range(1, cn):
                copy(j, c).start()
            mine.start()

        def end():
            mine.wait()
            for j in range(1, cn):
                copy(j, lax.rem(c + cn - j, cn)).wait_recv()
            for j in range(1, cn):
                copy(j, c).wait_send()

        return start, lambda: None, end

    dims = (lead, cn) if to_units else (cn, lead)
    shape = jax.ShapeDtypeStruct((*dims, *x.shape[2:]), x.dtype)
    return (along_ctx, x, shape, ANY, ANY, [dma(cn), dma(cn), dma()], body)


def the_pair():
    f, c = place()
    return [(f, c // 2 * 2 + 1 - lax.rem(c, 2))]


def exchange_pair(x):
    def body(x_ref, o_ref, s, r):
        (pair,) = the_pair()
        copy = remote(x_ref, o_ref, s, r, pair)
        return copy.start, lambda: None, copy.wait

    shape = jax.ShapeDtypeStruct(x.shape, x.dtype)
    return (the_pair, x, shape, ANY, ANY, [dma(), dma()], body)


def gather_fsdp(x, parts=4):
    fn = lax.axis_size("fsdp")
    chips = fn // 2
    n, d = x.shape
    step = n // parts
    pieces = [pl.ds(p * step, step) for p in range(parts)]

    def body(x_ref, o_ref, own_sem, s_link, r_link, s_core, r_core):
        f, c = place()
        chip, core = f // 2, lax.rem(f, 2)
        twin = (chip * 2 + 1 - core, c)
        links, cores = {}, {}

        def to(j):
            return (lax.rem(chip + j, chips) * 2 + core, c)

        def slot(j, core_id):
            return lax.rem(chip + chips - j, chips) * 2 + core_id

        own = pltpu.make_async_copy(x_ref, o_ref.at[f], own_sem)

        def start():
            for i, rows in enumerate(pieces):
                here, there = x_ref.at[rows], o_ref.at[f, rows]
                for j in range(1, chips):
                    links[i, j] = remote(here, there, s_link.at[j, i], r_link.at[j, i], to(j))
                    links[i, j].start()
            for i, rows in enumerate(pieces):
                here, there = x_ref.at[rows], o_ref.at[f, rows]
                cores[i, 0] = remote(here, there, s_core.at[0, i], r_core.at[0, i], twin)
                cores[i, 0].start()
            own.start()

        def middle():
            for i, rows in enumerate(pieces):
                for j in range(1, chips):
                    here = o_ref.at[slot(j, core), rows]
                    remote(here, here, s_link.at[j, i], r_link.at[j, i], to(j)).wait_recv()
                    cores[i, j] = remote(here, here, s_core.at[j, i], r_core.at[j, i], twin)
                    cores[i, j].start()

        def end():
            own.wait()
            for i, rows in enumerate(pieces):
                for j in range(chips):
                    there = o_ref.at[slot(j, 1 - core), rows]
                    cores[i, j].wait_send()
                    remote(there, there, s_core.at[j, i], r_core.at[j, i], twin).wait_recv()
                for j in range(1, chips):
                    links[i, j].wait_send()

        return start, middle, end

    shape = jax.ShapeDtypeStruct((fn, n, d), x.dtype)
    return (links_and_twin, x, shape, ANY, ANY, [dma()] + [dma(chips, parts)] * 4, body)


def gather_ctx(x):
    cn = lax.axis_size("ctx")
    count = cn // 2

    def body(x_ref, o_ref, own_sem, s_up, r_up, s_down, r_down, s_pair, r_pair):
        f, c = place()
        hi, lo = c // 2, lax.rem(c, 2)
        pair = (f, hi * 2 + 1 - lo)
        above = (f, lax.rem(hi + 1, count) * 2 + lo)
        below = (f, lax.rem(hi + count - 1, count) * 2 + lo)
        own = pltpu.make_async_copy(x_ref, o_ref.at[c], own_sem)

        def low(d):
            return lax.rem(hi + count - d, count)

        def high(d):
            return lax.rem(hi + d, count)

        def up(d):
            source = x_ref if d == 0 else o_ref.at[low(d) * 2 + lo]
            return remote(source, o_ref.at[low(d) * 2 + lo], s_up.at[d], r_up.at[d + 1], above)

        def down(d):
            source = x_ref if d == 0 else o_ref.at[high(d) * 2 + lo]
            return remote(
                source, o_ref.at[high(d) * 2 + lo], s_down.at[d], r_down.at[d + 1], below
            )

        def across(k, slot):
            source = x_ref if k == 0 else o_ref.at[slot * 2 + lo]
            return remote(source, o_ref.at[slot * 2 + lo], s_pair.at[k], r_pair.at[k], pair)

        def start():
            pl.when(hi < count - 1)(lambda: up(0).start())
            pl.when(hi > 0)(lambda: down(0).start())
            across(0, hi).start()
            own.start()

        def middle():
            for d in range(1, count):

                @pl.when(hi >= d)
                def _():
                    here = o_ref.at[low(d) * 2 + lo]
                    remote(here, here, s_up.at[d], r_up.at[d], above).wait_recv()
                    across(d, low(d)).start()
                    if d < count - 1:
                        pl.when(hi < count - 1)(lambda: up(d).start())

                @pl.when(hi + d < count)
                def _():
                    here = o_ref.at[high(d) * 2 + lo]
                    remote(here, here, s_down.at[d], r_down.at[d], below).wait_recv()
                    across(count - d, high(d)).start()
                    if d < count - 1:
                        pl.when(hi > 0)(lambda: down(d).start())

        def end():
            own.wait()
            across(0, hi).wait_send()
            for k in range(count):
                there = o_ref.at[low(k) * 2 + 1 - lo]
                remote(there, there, s_pair.at[k], r_pair.at[k], pair).wait_recv()
                if k > 0:
                    across(k, low(k)).wait_send()
            for d in range(count - 1):
                pl.when((hi >= d) & (hi < count - 1))(lambda d=d: up(d).wait_send())
                pl.when((hi + d < count) & (hi > 0))(lambda d=d: down(d).wait_send())

        return start, middle, end

    shape = jax.ShapeDtypeStruct((cn, *x.shape), x.dtype)
    scratch = [dma()] + [dma(count + 1)] * 4 + [dma(count)] * 2
    return (along_ctx, x, shape, ANY, ANY, scratch, body)


def scatter_fsdp(x, parts=4):
    fn = lax.axis_size("fsdp")
    chips = fn // 2
    _, n, d = x.shape
    step = n // parts

    def body(x_ref, o_ref, own, near, mine, far, ss, s_own, s_near, r_near, s_far, r_far):
        f, c = place()
        chip, core = f // 2, lax.rem(f, 2)
        twin = (chip * 2 + 1 - core, c)
        nears, owns, fars, outs = {}, {}, {}, {}

        def chip_at(j):
            return lax.rem(chip + j, chips)

        def start():
            for p in range(parts):
                rows = pl.ds(p * step, step)
                for j in list(range(1, chips)) + [0]:
                    at = chip_at(j) * 2
                    owns[p, j] = pltpu.make_async_copy(
                        x_ref.at[at + core, rows], own.at[j, p], s_own.at[j, p]
                    )
                    owns[p, j].start()
                    nears[p, j] = remote(
                        x_ref.at[at + 1 - core, rows],
                        near.at[j, p],
                        s_near.at[j, p],
                        r_near.at[j, p],
                        twin,
                    )
                    nears[p, j].start()

        def middle():
            for p in range(parts):
                for j in range(1, chips):
                    owns[p, j].wait()
                    nears[p, j].wait_recv()
                    mine[j, p] = (own[j, p].astype(F32) + near[j, p].astype(F32)).astype(BF16)
                    fars[p, j] = remote(
                        mine.at[j, p],
                        far.at[j, p],
                        s_far.at[j, p],
                        r_far.at[j, p],
                        (chip_at(j) * 2 + core, c),
                    )
                    fars[p, j].start()
            for p in range(parts):
                owns[p, 0].wait()
                nears[p, 0].wait_recv()
                ss[p] = own[0, p].astype(F32) + near[0, p].astype(F32)

        def end():
            for p in range(parts):
                for j in range(1, chips):
                    fars[p, j].wait_recv()
                    ss[p] += far[j, p].astype(F32)
                outs[p] = pltpu.make_async_copy(
                    ss.at[p], o_ref.at[pl.ds(p * step, step)], s_far.at[0, p]
                )
                outs[p].start()
            for p in range(parts):
                outs[p].wait()
                for j in range(chips):
                    nears[p, j].wait_send()
                for j in range(1, chips):
                    fars[p, j].wait_send()

        return start, middle, end

    block = pltpu.VMEM((chips, parts, step, d), BF16)
    scratch = [block] * 4 + [pltpu.VMEM((parts, step, d), F32)] + [dma(chips, parts)] * 5
    return (links_and_twin, x, jax.ShapeDtypeStruct((n, d), F32), ANY, ANY, scratch, body)


def plane_others():
    fn = lax.axis_size("fsdp")
    f, c = place()
    (pair,) = the_pair()
    return [(lax.rem(f + a, fn), (c, pair[1])[b]) for a in range(fn) for b in range(2) if a or b]


def plane_diagonals():
    fn = lax.axis_size("fsdp")
    f, _ = place()
    (pair,) = the_pair()
    return [(lax.rem(f + a, fn), pair[1]) for a in range(1, fn)]


def exchange_plane(x, peers):
    fn = lax.axis_size("fsdp")

    def body(x_ref, o_ref, s, r, own):
        f, c = place()
        lo = lax.rem(c, 2)
        (pair,) = the_pair()

        def index(a, b):
            return lax.rem(f + a + fn, fn), (lo if b == 0 else 1 - lo)

        def copy(a, b, slot):
            fa, lb = index(a, b)
            return remote(
                x_ref.at[fa, lb],
                o_ref.at[slot[0], slot[1]],
                s.at[a, b],
                r.at[a, b],
                (fa, c if b == 0 else pair[1]),
            )

        steps = [(a, b) for a in range(fn) for b in range(2) if a or b]
        mine = pltpu.make_async_copy(x_ref.at[f, lo], o_ref.at[f, lo], own)

        def start():
            for a, b in steps:
                copy(a, b, (f, lo)).start()
            mine.start()

        def end():
            mine.wait()
            for a, b in steps:
                copy(a, b, index(-a, b)).wait_recv()
            for a, b in steps:
                copy(a, b, (f, lo)).wait_send()

        return start, lambda: None, end

    shape = jax.ShapeDtypeStruct(x.shape, x.dtype)
    return (peers, x, shape, ANY, ANY, [dma(fn, 2), dma(fn, 2), dma()], body)


def links_twin_pair():
    return links_and_twin() + the_pair()


def gather_plane(x, parts=4):
    fn = lax.axis_size("fsdp")
    chips = fn // 2
    n, d = x.shape
    step = n // parts
    first, second = list(range(parts // 2)), list(range(parts // 2, parts))
    others = list(range(1, chips))

    def body(x_ref, o_ref, own_sem, sx, rx, sy, ry, st, rt):
        f, c = place()
        chip, core, lo = f // 2, lax.rem(f, 2), lax.rem(c, 2)
        twin = (chip * 2 + 1 - core, c)
        (pair,) = the_pair()

        def rows(p):
            return pl.ds(p * step, step)

        def block(j, core_id, kind, p):
            slot = lax.rem(chip + chips - j, chips) * 2 + core_id
            return o_ref.at[slot, lo if kind == 0 else 1 - lo, rows(p)]

        def source(j, kind, p):
            return x_ref.at[rows(p)] if j == 0 and kind == 0 else block(j, core, kind, p)

        def to(j):
            return (lax.rem(chip + j, chips) * 2 + core, c)

        def x_copy(j, kind, p):
            return remote(
                source(0, kind, p), block(0, core, kind, p), sx.at[j, kind, p], rx.at[j, kind, p], to(j)
            )

        def y_copy(j, p):
            return remote(source(j, 0, p), block(j, core, 0, p), sy.at[j, p], ry.at[j, p], pair)

        def t_copy(j, kind, p):
            return remote(
                source(j, kind, p), block(j, core, kind, p), st.at[j, kind, p], rt.at[j, kind, p], twin
            )

        def x_come(j, kind, p):
            here = block(j, core, kind, p)
            remote(here, here, sx.at[j, kind, p], rx.at[j, kind, p], to(j)).wait_recv()

        def y_come(j, p):
            here = block(j, core, 1, p)
            remote(here, here, sy.at[j, p], ry.at[j, p], pair).wait_recv()

        own = pltpu.make_async_copy(x_ref, o_ref.at[f, lo], own_sem)

        def start():
            for p in first:
                for j in others:
                    x_copy(j, 0, p).start()
            for p in second + first:
                y_copy(0, p).start()
            for p in second:
                for j in others:
                    x_copy(j, 0, p).start()
            for p in range(parts):
                t_copy(0, 0, p).start()
            own.start()

        def middle():
            for p, q in zip(first, second, strict=True):
                for j in others:
                    x_come(j, 0, p)
                    y_copy(j, p).start()
                    t_copy(j, 0, p).start()
                y_come(0, q)
                for j in others:
                    x_copy(j, 1, q).start()
                t_copy(0, 1, q).start()
            for p, q in zip(first, second, strict=True):
                y_come(0, p)
                t_copy(0, 1, p).start()
                for j in others:
                    x_come(j, 0, q)
                    t_copy(j, 0, q).start()

        def end():
            for p, q in zip(first, second, strict=True):
                for j in others:
                    y_come(j, p)
                    t_copy(j, 1, p).start()
                    x_come(j, 1, q)
                    t_copy(j, 1, q).start()
            own.wait()
            for p in range(parts):
                for j in range(chips):
                    for kind in range(2):
                        there = block(j, 1 - core, kind, p)
                        remote(
                            there, there, st.at[j, kind, p], rt.at[j, kind, p], twin
                        ).wait_recv()
                        t_copy(j, kind, p).wait_send()
                y_copy(0, p).wait_send()
                for j in others:
                    x_copy(j, 0, p).wait_send()
            for p, q in zip(first, second, strict=True):
                for j in others:
                    y_copy(j, p).wait_send()
                    x_copy(j, 1, q).wait_send()

        return start, middle, end

    shape = jax.ShapeDtypeStruct((fn, 2, n, d), x.dtype)
    scratch = [dma()] + [dma(chips, 2, parts)] * 2 + [dma(chips, parts)] * 2
    scratch = scratch + [dma(chips, 2, parts)] * 2
    return (links_twin_pair, x, shape, ANY, ANY, scratch, body)


def scatter_plane(x, parts=4):
    fn = lax.axis_size("fsdp")
    chips = fn // 2
    _, _, n, d = x.shape
    step = n // parts
    half = parts // 2
    others = list(range(1, chips))

    def body(
        x_ref, o_ref, own, near, send1, come_y, send_x, come_x, come_x2, send_y, come_y2, acc,
        s_own, s_near, r_near, s_1, r_y, r_x, s_2, r_x2, s_3, r_y2, s_out,
    ):
        f, c = place()
        chip, core, lo = f // 2, lax.rem(f, 2), lax.rem(c, 2)
        twin = (chip * 2 + 1 - core, c)
        (pair,) = the_pair()

        def chip_at(j):
            return lax.rem(chip + j, chips)

        def to(j):
            return (chip_at(j) * 2 + core, c)

        def part(j, core_id, kind, p):
            return x_ref.at[
                chip_at(j) * 2 + core_id, lo if kind == 0 else 1 - lo, pl.ds(p * step, step)
            ]

        def own_copy(j, k, p):
            return pltpu.make_async_copy(part(j, core, k, p), own.at[j, k, p], s_own.at[j, k, p])

        def near_copy(j, k, p):
            return remote(
                part(j, 1 - core, k, p), near.at[j, k, p], s_near.at[j, k, p], r_near.at[j, k, p], twin
            )

        def both(j, k, p):
            return own[j, k, p].astype(F32) + near[j, k, p].astype(F32)

        def ready(j, k, p):
            own_copy(j, k, p).wait()
            near_copy(j, k, p).wait_recv()

        def y_first(j, p):
            return remote(send1.at[j, 1, p], come_y.at[j, p], s_1.at[j, 1, p], r_y.at[j, p], pair)

        def x_first(j, k, p):
            q = p - half
            return remote(
                send1.at[j, k, p], come_x.at[j, k, q], s_1.at[j, k, p], r_x.at[j, k, q], to(j)
            )

        def x_then(j, p):
            return remote(send_x.at[j, p], come_x2.at[j, p], s_2.at[j, p], r_x2.at[j, p], to(j))

        def y_then(q):
            return remote(send_y.at[q], come_y2.at[q], s_3.at[q], r_y2.at[q], pair)

        def out(p):
            return pltpu.make_async_copy(acc.at[p], o_ref.at[pl.ds(p * step, step)], s_out.at[p])

        order = [(j, k, i) for i in range(half) for j in others + [0] for k in (1, 0)]

        def start():
            for j, k, i in order:
                for p in (i, i + half):
                    own_copy(j, k, p).start()
                    near_copy(j, k, p).start()

        def middle():
            for i in range(half):
                for j in range(chips):
                    ready(j, 1, i)
                    send1[j, 1, i] = both(j, 1, i).astype(BF16)
                    y_first(j, i).start()
                for j in others:
                    for k in (1, 0):
                        ready(j, k, i + half)
                        send1[j, k, i + half] = both(j, k, i + half).astype(BF16)
                        x_first(j, k, i + half).start()
            for i in range(half):
                for j in range(chips):
                    ready(j, 0, i)
                for k in range(2):
                    ready(0, k, i + half)

        def end():
            for i in range(half):
                for j in others:
                    y_first(j, i).wait_recv()
                    send_x[j, i] = (both(j, 0, i) + come_y[j, i].astype(F32)).astype(BF16)
                    x_then(j, i).start()
                total = both(0, 1, i + half)
                for j in others:
                    x_first(j, 1, i + half).wait_recv()
                    total += come_x[j, 1, i].astype(F32)
                send_y[i] = total.astype(BF16)
                y_then(i).start()
            for i in range(half):
                y_first(0, i).wait_recv()
                acc[i] = both(0, 0, i) + come_y[0, i].astype(F32)
                acc[i + half] = both(0, 0, i + half)
                for j in others:
                    x_first(j, 0, i + half).wait_recv()
                    acc[i + half] += come_x[j, 0, i].astype(F32)
            for i in range(half):
                for j in others:
                    x_then(j, i).wait_recv()
                    acc[i] += come_x2[j, i].astype(F32)
                out(i).start()
                y_then(i).wait_recv()
                acc[i + half] += come_y2[i].astype(F32)
                out(i + half).start()
            for i in range(half):
                out(i).wait()
                out(i + half).wait()
                y_then(i).wait_send()
                for j in others:
                    x_then(j, i).wait_send()
                    for k in range(2):
                        x_first(j, k, i + half).wait_send()
                for j in range(chips):
                    y_first(j, i).wait_send()
                    for k in range(2):
                        near_copy(j, k, i).wait_send()
                        near_copy(j, k, i + half).wait_send()

        return start, middle, end

    def buffer(*lead):
        return pltpu.VMEM((*lead, step, d), BF16)

    scratch = [
        buffer(chips, 2, parts),
        buffer(chips, 2, parts),
        buffer(chips, 2, parts),
        buffer(chips, half),
        buffer(chips, half),
        buffer(chips, 2, half),
        buffer(chips, half),
        buffer(half),
        buffer(half),
        pltpu.VMEM((parts, step, d), F32),
        dma(chips, 2, parts),
        dma(chips, 2, parts),
        dma(chips, 2, parts),
        dma(chips, 2, parts),
        dma(chips, half),
        dma(chips, 2, half),
        dma(chips, half),
        dma(chips, half),
        dma(half),
        dma(half),
        dma(parts),
    ]
    return (links_twin_pair, x, jax.ShapeDtypeStruct((n, d), F32), ANY, ANY, scratch, body)


def scatter_small(x):
    fn, cn = lax.axis_size("fsdp"), lax.axis_size("ctx")

    def body(x_ref, o_ref, got, sums, got2, s1, r1, s2, r2):
        f, c = place()

        def first(j):
            t = lax.rem(f + j, fn)
            return remote(x_ref.at[t], got.at[j], s1.at[j], r1.at[j], (t, c))

        def second(j):
            t = lax.rem(c + j, cn)
            return remote(sums.at[t], got2.at[j], s2.at[j], r2.at[j], (f, t))

        def start():
            for j in range(1, fn):
                first(j).start()
            sums[...] = x_ref[f]

        def middle():
            for j in range(1, fn):
                first(j).wait_recv()
                sums[...] += got[j]
            for j in range(1, cn):
                second(j).start()
            o_ref[...] = sums[c]

        def end():
            for j in range(1, cn):
                second(j).wait_recv()
                o_ref[...] += got2[j]
            for j in range(1, fn):
                first(j).wait_send()
            for j in range(1, cn):
                second(j).wait_send()

        return start, middle, end

    tail = x.shape[2:]
    scratch = [
        pltpu.VMEM(x.shape, x.dtype),
        pltpu.VMEM(x.shape[1:], x.dtype),
        pltpu.VMEM(x.shape[1:], x.dtype),
        dma(fn),
        dma(fn),
        dma(cn),
        dma(cn),
    ]
    return (along_both, x, jax.ShapeDtypeStruct(tail, x.dtype), VMEM, VMEM, scratch, body)


def nt(a, b):
    return lax.dot_general(a, b, (((1,), (1,)), ((), ())), preferred_element_type=F32)


def nn(a, b):
    return lax.dot_general(a, b, (((1,), (0,)), ((), ())), preferred_element_type=F32)


def attend(q, k, v, starts, block=512):
    u, t, _ = q.shape
    scale = HEAD_DIM**-0.5 * LOG2E

    def kernel(q_ref, k_ref, v_ref, s_ref, o_ref, l_ref, vt):
        i = pl.program_id(1)

        @pl.when(i == 0)
        def _():
            vt[...] = v_ref[0].T

        rows = q_ref[0]
        first = s_ref[0]
        base = lax.broadcasted_iota(jnp.int32, (block, block), 0)
        qpos = i * block + lax.broadcasted_iota(jnp.int32, (1, block), 1)

        def one(j, carry, diagonal):
            peak, total, acc = carry
            at = pl.multiple_of(j * block, block)
            s = nt(k_ref[0, pl.ds(at, block)], rows) * scale
            kpos = base + at
            keep = kpos >= first
            if diagonal:
                keep = keep & (kpos <= qpos)
            s = jnp.where(keep, s, NEG_BIG)
            new = jnp.maximum(peak, jnp.max(s, axis=0, keepdims=True))
            p = jnp.exp2(s - new)
            shrink = jnp.exp2(peak - new)
            total = total * shrink + jnp.sum(p, axis=0, keepdims=True)
            acc = acc * shrink + nn(vt[:, pl.ds(at, block)], p.astype(BF16))
            return new, total, acc

        start = (
            jnp.full((1, block), NEG_BIG, F32),
            jnp.zeros((1, block), F32),
            jnp.zeros((HEAD_DIM, block), F32),
        )
        start = one(i, start, True)
        peak, total, acc = lax.fori_loop(0, i, lambda j, c: one(j, c, False), start)
        o_ref[0] = (acc / total).T.astype(BF16)
        l_ref[0] = peak + jnp.log2(total)

    return pl.pallas_call(
        kernel,
        grid=(u, t // block),
        in_specs=[
            pl.BlockSpec((1, block, HEAD_DIM), lambda a, b: (a, b, 0)),
            pl.BlockSpec((1, t, HEAD_DIM), lambda a, b: (a, 0, 0)),
            pl.BlockSpec((1, t, HEAD_DIM), lambda a, b: (a, 0, 0)),
            pl.BlockSpec((1, 1, block), lambda a, b: (a, 0, b)),
        ],
        out_specs=[
            pl.BlockSpec((1, block, HEAD_DIM), lambda a, b: (a, b, 0)),
            pl.BlockSpec((1, 1, block), lambda a, b: (a, 0, b)),
        ],
        out_shape=[
            jax.ShapeDtypeStruct((u, t, HEAD_DIM), BF16),
            jax.ShapeDtypeStruct((u, 1, t), F32),
        ],
        scratch_shapes=[pltpu.VMEM((HEAD_DIM, t), BF16)],
        compiler_params=pltpu.CompilerParams(vmem_limit_bytes=32 * 2**20),
        cost_estimate=pl.CostEstimate(
            flops=2 * u * t * t * HEAD_DIM, bytes_accessed=8 * u * t * 256, transcendentals=u * t * t // 2
        ),
    )(q, k, v, starts)


def attend_back(q, k, v, starts, lse, o, g, tables, block=512):
    u, t, _ = q.shape
    scale = HEAD_DIM**-0.5

    def kernel(
        q_ref, k_ref, v_ref, s_ref, l_ref, o_ref, g_ref, t_ref, dq_ref, dk_ref, dv_ref, kt, dk, dv
    ):
        i = pl.program_id(1)

        @pl.when(i == 0)
        def _():
            kt[...] = k_ref[0].T
            dk[...] = jnp.zeros_like(dk)
            dv[...] = jnp.zeros_like(dv)

        rows, grows = q_ref[0], g_ref[0]
        first, logs = s_ref[0], l_ref[0]
        prod = o_ref[0].astype(F32) * grows.astype(F32)
        centre = jnp.sum(prod.T, axis=0, keepdims=True)
        base = lax.broadcasted_iota(jnp.int32, (block, block), 0)
        qpos = i * block + lax.broadcasted_iota(jnp.int32, (1, block), 1)

        def one(j, acc, diagonal):
            at = pl.multiple_of(j * block, block)
            here = pl.ds(at, block)
            p = jnp.exp2(nt(k_ref[0, here], rows) * (scale * LOG2E) - logs)
            kpos = base + at
            keep = kpos >= first
            if diagonal:
                keep = keep & (kpos <= qpos)
            p = jnp.where(keep, p, 0.0)
            gp = nt(v_ref[0, here], grows)
            ds = (p * (gp - centre)).astype(BF16)
            dv[here] += nn(p.astype(BF16), grows)
            dk[here] += nn(ds, rows)
            return acc + nn(kt[:, here], ds)

        acc = one(i, jnp.zeros((HEAD_DIM, block), F32), True)
        acc = lax.fori_loop(0, i, lambda j, a: one(j, a, False), acc)
        there = pl.ds(pl.multiple_of(i * block, block), block)
        straight, right, left = t_ref[0, there], t_ref[1, there], t_ref[2, there]
        dq_ref[0] = turn((acc * scale).T, straight, -right, -left).astype(BF16)

        @pl.when(i == t // block - 1)
        def _():
            for b in range(t // block):
                at = pl.ds(b * block, block)
                dk_ref[0, at] = turn(
                    dk[at] * scale, t_ref[0, at], -t_ref[1, at], -t_ref[2, at]
                ).astype(BF16)
                dv_ref[0, at] = dv[at].astype(BF16)

    def whole(a, b):
        return (a, 0, 0)

    def part(a, b):
        return (a, b, 0)

    def row(a, b):
        return (a, 0, b)

    spec, full, line = (1, block, HEAD_DIM), (1, t, HEAD_DIM), (1, 1, block)
    return pl.pallas_call(
        kernel,
        grid=(u, t // block),
        in_specs=[
            pl.BlockSpec(spec, part),
            pl.BlockSpec(full, whole),
            pl.BlockSpec(full, whole),
            pl.BlockSpec(line, row),
            pl.BlockSpec(line, row),
            pl.BlockSpec(spec, part),
            pl.BlockSpec(spec, part),
            pl.BlockSpec((3, t, HEAD_DIM), lambda a, b: (0, 0, 0)),
        ],
        out_specs=[
            pl.BlockSpec(spec, part),
            pl.BlockSpec(full, whole),
            pl.BlockSpec(full, whole),
        ],
        out_shape=[jax.ShapeDtypeStruct((u, t, HEAD_DIM), BF16)] * 3,
        scratch_shapes=[
            pltpu.VMEM((HEAD_DIM, t), BF16),
            pltpu.VMEM((t, HEAD_DIM), F32),
            pltpu.VMEM((t, HEAD_DIM), F32),
        ],
        compiler_params=pltpu.CompilerParams(vmem_limit_bytes=48 * 2**20),
        cost_estimate=pl.CostEstimate(
            flops=5 * u * t * t * HEAD_DIM, bytes_accessed=20 * u * t * 256, transcendentals=u * t * t // 2
        ),
    )(q, k, v, starts, lse, o, g, tables)


def project(x, w, stream, bias, tables):
    count, length, width = x.shape
    cn, fn, _, rows, cols = w.shape
    heads = cols // HEAD_DIM

    def kernel(*refs):
        x_ref, w_ref, b_ref = refs[:3]
        o_ref, held, sem = refs[-3:]

        @pl.when(pl.program_id(0) == 0)
        def _():
            copies = [
                pltpu.make_async_copy(w_ref.at[:, f, stream], held.at[f], sem.at[f])
                for f in range(fn)
            ]
            for c in copies:
                c.start()
            for c in copies:
                c.wait()

        y = nn(x_ref[0], held[...].reshape(width, cols)) + b_ref[...]
        for h in range(heads):
            part = y[:, h * HEAD_DIM : (h + 1) * HEAD_DIM]
            if tables is not None:
                t_ref = refs[3]
                part = turn(part, t_ref[0], t_ref[1], t_ref[2])
            o_ref[h] = part.astype(BF16)

    extra = [] if tables is None else [tables]
    return pl.pallas_call(
        kernel,
        grid=(count,),
        in_specs=[
            pl.BlockSpec((1, length, width), lambda i: (i, 0, 0)),
            ANY,
            pl.BlockSpec((1, cols), lambda i: (0, 0)),
        ]
        + [pl.BlockSpec((3, length, HEAD_DIM), lambda i: (0, 0, 0)) for _ in extra],
        out_specs=pl.BlockSpec((heads, length, HEAD_DIM), lambda i: (i, 0, 0)),
        out_shape=jax.ShapeDtypeStruct((count * heads, length, HEAD_DIM), BF16),
        scratch_shapes=[pltpu.VMEM((fn, cn, rows, cols), BF16), dma(fn)],
        compiler_params=pltpu.CompilerParams(vmem_limit_bytes=32 * 2**20),
        cost_estimate=pl.CostEstimate(
            flops=2 * count * length * width * cols,
            bytes_accessed=2 * (count * length * (width + cols) + width * cols),
            transcendentals=0,
        ),
    )(x, w, bias, *extra)


def widen(x, w, bias, tile=256, rows_at_once=512):
    n, d = x.shape
    cn, fn, rows, cols = w.shape
    tiles = cols // tile

    def kernel(x_ref, w_ref, b_ref, a_ref, g_ref, o_ref, held, sem):
        i = pl.program_id(0)

        def copy(j, f):
            at = pl.ds(pl.multiple_of(j * tile, tile), tile)
            return pltpu.make_async_copy(w_ref.at[:, f, :, at], held.at[j, f], sem.at[j, f])

        @pl.when(i == 0)
        def _():
            for j in range(tiles):
                for f in range(fn):
                    copy(j, f).start()

        for f in range(fn):
            copy(i, f).wait()
        w_tile = held[i].reshape(d, tile)
        o_ref[...] = w_tile
        for r in range(0, n, rows_at_once):
            part = pl.ds(r, rows_at_once)
            y = nn(x_ref[part], w_tile) + b_ref[...]
            t = y * math.sqrt(0.5)
            below = 0.5 + 0.5 * lax.erf(t)
            a_ref[part] = (y * below).astype(BF16)
            density = jnp.exp(-t * t) * (1.0 / math.sqrt(2.0 * math.pi))
            g_ref[part] = (below + y * density).astype(BF16)

    column = pl.BlockSpec((n, tile), lambda i: (0, i))
    return pl.pallas_call(
        kernel,
        grid=(tiles,),
        in_specs=[
            pl.BlockSpec((n, d), lambda i: (0, 0)),
            ANY,
            pl.BlockSpec((1, tile), lambda i: (0, i)),
        ],
        out_specs=[column, column, pl.BlockSpec((d, tile), lambda i: (0, i))],
        out_shape=[
            jax.ShapeDtypeStruct((n, cols), BF16),
            jax.ShapeDtypeStruct((n, cols), BF16),
            jax.ShapeDtypeStruct((d, cols), BF16),
        ],
        scratch_shapes=[pltpu.VMEM((tiles, fn, cn, rows, tile), BF16), dma(tiles, fn)],
        compiler_params=pltpu.CompilerParams(vmem_limit_bytes=48 * 2**20),
        cost_estimate=pl.CostEstimate(
            flops=2 * n * d * cols, bytes_accessed=60_000_000, transcendentals=0
        ),
    )(x, w, bias)


def halved_product(x, g, bit, groups, lines, tile=512, split=True):
    n, d = g.shape
    block = x.shape[1] // groups
    r = block // lines // 2
    tile = min(tile, d)

    def kernel(bit_ref, x_ref, g_ref, *refs):
        turned = refs[-1]

        @pl.when(pl.program_id(1) == 0)
        def _():
            turned[...] = x_ref[...].T

        y = nn(turned[...], g_ref[...]).astype(BF16)
        if not split:
            refs[0][:, 0] = y.reshape(lines, 2 * r, tile)
            return
        a_ref, k_ref = refs[:2]
        y = y.reshape(lines, 2, r, tile)
        first = bit_ref[0] == 0
        a_ref[:, 0] = jnp.where(first, y[:, 1], y[:, 0])
        k_ref[:, 0] = jnp.where(first, y[:, 0], y[:, 1])

    size = r if split else 2 * r
    half = pl.BlockSpec((lines, 1, size, tile), lambda i, j, b: (0, i, 0, j))
    shape = jax.ShapeDtypeStruct((lines, groups, size, d), BF16)
    outs = 2 if split else 1
    return pl.pallas_call(
        kernel,
        grid_spec=pltpu.PrefetchScalarGridSpec(
            num_scalar_prefetch=1,
            grid=(groups, d // tile),
            in_specs=[
                pl.BlockSpec((n, block), lambda i, j, b: (0, i)),
                pl.BlockSpec((n, tile), lambda i, j, b: (0, j)),
            ],
            out_specs=[half] * outs,
            scratch_shapes=[pltpu.VMEM((block, n), BF16)],
        ),
        out_shape=[shape] * outs,
        compiler_params=pltpu.CompilerParams(vmem_limit_bytes=48 * 2**20),
        cost_estimate=pl.CostEstimate(
            flops=2 * n * d * x.shape[1],
            bytes_accessed=2 * (n * d + n * x.shape[1] + d * x.shape[1]),
            transcendentals=0,
        ),
    )(bit, x, g)


def front(hist, mix, gain, shift, tokens=16, wide=256):
    h, n, d = hist.shape
    rest = gain.shape[0]

    def kernel(h_ref, m_ref, g_ref, b_ref, s_ref, n_ref):
        m = m_ref[...]
        for at in range(0, d, wide):
            cut = slice(at, at + wide)
            for s in range(4):
                acc = m[:, s * h : s * h + 1] * h_ref[0, :, cut].astype(F32)
                for j in range(1, h):
                    acc += m[:, s * h + j : s * h + j + 1] * h_ref[j, :, cut].astype(F32)
                s_ref[s, :, cut] = acc
        for s in range(rest):
            x = s_ref[s]
            centre = x - jnp.mean(x, axis=-1, keepdims=True)
            spread = jnp.mean(centre * centre, axis=-1, keepdims=True)
            y = centre * lax.rsqrt(spread + EPS_NORM) * g_ref[s : s + 1] + b_ref[s : s + 1]
            n_ref[s] = y.astype(BF16)

    return pl.pallas_call(
        kernel,
        grid=(n // tokens,),
        in_specs=[
            pl.BlockSpec((h, tokens, d), lambda i: (0, i, 0)),
            pl.BlockSpec((tokens, 128), lambda i: (i, 0)),
            pl.BlockSpec((rest, d), lambda i: (0, 0)),
            pl.BlockSpec((rest, d), lambda i: (0, 0)),
        ],
        out_specs=[
            pl.BlockSpec((4, tokens, d), lambda i: (0, i, 0)),
            pl.BlockSpec((rest, tokens, d), lambda i: (0, i, 0)),
        ],
        out_shape=[
            jax.ShapeDtypeStruct((4, n, d), F32),
            jax.ShapeDtypeStruct((rest, n, d), BF16),
        ],
        compiler_params=pltpu.CompilerParams(vmem_limit_bytes=60 * 2**20),
        cost_estimate=pl.CostEstimate(
            flops=2 * 4 * h * n * d, bytes_accessed=n * d * (2 * h + 22), transcendentals=0
        ),
    )(hist, mix, gain, shift)


def last(hist, mix, streams, gain, grads, grad_hidden, tokens=16, wide=256):
    h, n, d = hist.shape
    rest = gain.shape[0]

    def kernel(h_ref, m_ref, s_ref, g_ref, d0, d1, d2, r_ref, gh_ref, gm_ref, gg_ref, gb_ref, ds):
        @pl.when(pl.program_id(0) == 0)
        def _():
            gg_ref[...] = jnp.zeros_like(gg_ref)
            gb_ref[...] = jnp.zeros_like(gb_ref)

        for s, d_ref in enumerate((d0, d1, d2)):
            x = s_ref[s]
            centre = x - jnp.mean(x, axis=-1, keepdims=True)
            inverse = lax.rsqrt(jnp.mean(centre * centre, axis=-1, keepdims=True) + EPS_NORM)
            unit = centre * inverse
            dn = d_ref[...]
            gg_ref[s : s + 1] += jnp.sum(dn * unit, axis=0, keepdims=True)
            gb_ref[s : s + 1] += jnp.sum(dn, axis=0, keepdims=True)
            du = dn * g_ref[s : s + 1]
            ds[s] = inverse * (
                du
                - jnp.mean(du, axis=-1, keepdims=True)
                - unit * jnp.mean(du * unit, axis=-1, keepdims=True)
            )
        ds[rest] = r_ref[...]
        m = m_ref[...]
        sums = [[jnp.zeros((tokens, 128), F32) for _ in range(h)] for _ in range(4)]
        for at in range(0, d, wide):
            cut = slice(at, at + wide)
            parts = [ds[s, :, cut] for s in range(4)]
            for j in range(h):
                row = h_ref[j, :, cut].astype(F32)
                acc = m[:, j : j + 1] * parts[0]
                for s in range(1, 4):
                    acc += m[:, s * h + j : s * h + j + 1] * parts[s]
                gh_ref[j, :, cut] = acc
                for s in range(4):
                    prod = row * parts[s]
                    for b in range(0, wide, 128):
                        sums[s][j] += prod[:, b : b + 128]
        lane = lax.broadcasted_iota(jnp.int32, (tokens, 128), 1)
        total = jnp.zeros((tokens, 128), F32)
        for s in range(4):
            for j in range(h):
                value = jnp.sum(sums[s][j], axis=-1, keepdims=True)
                total = jnp.where(lane == s * h + j, value, total)
        gm_ref[...] = total

    row = pl.BlockSpec((tokens, d), lambda i: (i, 0))
    lines = pl.BlockSpec((rest, d), lambda i: (0, 0))
    return pl.pallas_call(
        kernel,
        grid=(n // tokens,),
        in_specs=[
            pl.BlockSpec((h, tokens, d), lambda i: (0, i, 0)),
            pl.BlockSpec((tokens, 128), lambda i: (i, 0)),
            pl.BlockSpec((4, tokens, d), lambda i: (0, i, 0)),
            lines,
            row,
            row,
            row,
            row,
        ],
        out_specs=[
            pl.BlockSpec((h, tokens, d), lambda i: (0, i, 0)),
            pl.BlockSpec((tokens, 128), lambda i: (i, 0)),
            lines,
            lines,
        ],
        out_shape=[
            jax.ShapeDtypeStruct((h, n, d), F32),
            jax.ShapeDtypeStruct((n, 128), F32),
            jax.ShapeDtypeStruct((rest, d), F32),
            jax.ShapeDtypeStruct((rest, d), F32),
        ],
        scratch_shapes=[pltpu.VMEM((4, tokens, d), F32)],
        compiler_params=pltpu.CompilerParams(vmem_limit_bytes=60 * 2**20),
        cost_estimate=pl.CostEstimate(
            flops=4 * 4 * h * n * d, bytes_accessed=n * d * (6 * h + 32), transcendentals=0
        ),
    )(hist, mix, streams, gain, *grads, grad_hidden)


def body(
    history,
    dense_mix,
    doc_starts,
    norm_gain,
    norm_bias,
    qkv_weight,
    qkv_bias,
    out_weight,
    out_bias,
    up_weight,
    up_bias,
    down_weight,
    down_bias,
    root_gain,
    mix_in_weight,
    mix_out_weight,
    mix_out_bias,
    out_cotangent,
    mix_cotangent,
):
    fn, cn = lax.axis_size("fsdp"), lax.axis_size("ctx")
    dn = fn * cn
    fi, ci = lax.axis_index("fsdp"), lax.axis_index("ctx")
    hist, seqs, length, width = history.shape
    nloc = seqs * length
    ntp = fn * nloc
    rows = qkv_weight.shape[0]
    ff = up_weight.shape[1]
    wcol, pcol = width // fn, ff // (2 * fn)
    count = cn // 2
    lo = lax.rem(ci, 2)
    lines = [list(range(b, cn, 2)) for b in range(2)]
    heads = wcol // HEAD_DIM
    units = fn * seqs * heads // cn
    total = cn * length
    mixn = mix_in_weight.shape[1]

    def line_gather(w):
        return lax.all_gather(w, "ctx", axis=0, axis_index_groups=lines)

    parts = [
        norm_gain,
        norm_bias,
        qkv_bias,
        out_bias,
        up_bias,
        down_bias,
        root_gain,
        mix_in_weight,
        doc_starts.astype(F32),
    ]
    flat = jnp.concatenate([a.reshape(-1) for a in parts])
    flat = jnp.pad(flat, (0, -flat.size % 1024)).reshape(-1, 128)
    flats, qkv_cols, up_cols = comm(
        1,
        gather_small(flat),
        exchange_fsdp(qkv_weight.reshape(rows, 3, fn, wcol).transpose(2, 1, 0, 3)),
        exchange_plane(
            up_weight.reshape(rows, fn, count, 2, -1).transpose(1, 3, 0, 2, 4).reshape(fn, 2, rows, pcol),
            plane_diagonals,
        ),
    )
    flats = flats.reshape(dn, -1)
    w12 = lax.all_gather(qkv_cols[:, 1:], "ctx", axis=0)
    pieces, at = [], 0
    for a in parts:
        pieces.append(flats[:, at : at + a.size])
        at += a.size

    def joined(piece, lead):
        return piece.reshape(dn, lead, -1).transpose(1, 0, 2).reshape(lead, -1)

    gain_all = joined(pieces[0], 4)
    shift_all = joined(pieces[1], 4)
    qkv_shift = joined(pieces[2], 3)
    out_shift = pieces[3].reshape(-1)
    up_shift = pieces[4].reshape(-1)
    down_shift = pieces[5].reshape(-1)
    root_full = pieces[6].reshape(-1)
    mix_in_full = pieces[7].reshape(width, mixn)
    starts = pieces[8].reshape(fn, cn, seqs, -1)[:, 0].astype(jnp.int32)

    hist2 = history.reshape(hist, nloc, width)
    mix2 = dense_mix.reshape(dense_mix.shape[0], hist, nloc)
    mixes = jnp.pad(mix2.reshape(-1, nloc).T, ((0, 0), (0, 128 - mix2.shape[0] * hist)))
    streams, normed = front(hist2, mixes, gain_all[:3], shift_all[:3])

    bias_cols = lax.dynamic_slice_in_dim(qkv_shift, fi * wcol, wcol, 1)
    tables = rotary_tables(total)
    tables_l = lax.dynamic_slice_in_dim(tables, ci * length, length, 1)

    def projected(x, w, at, s):
        y = project(
            x.reshape(fn * seqs, length, width),
            w,
            at,
            bias_cols[s : s + 1],
            tables_l if s < 2 else None,
        )
        return y.reshape(cn, units, length, HEAD_DIM)

    def whole_units(x):
        return x.reshape(units, total, HEAD_DIM)

    def from_units(x):
        return exchange_ctx(x.reshape(units, cn, length, HEAD_DIM), False)

    def columns(x):
        x = x.reshape(fn * seqs, heads, length, HEAD_DIM)
        return x.transpose(0, 2, 1, 3).reshape(ntp, wcol)

    w0, g0 = comm(9, gather_ctx(qkv_cols[:, 0]), gather_fsdp(normed[0]))
    p0 = projected(g0, w0[:, :, None], 0, 0)
    p0, w12, down_rows = lax.optimization_barrier((p0, w12, down_weight))
    wdown = line_gather(down_rows).reshape(pcol, width)
    q_u, g1 = comm(4, exchange_ctx(p0, True), gather_fsdp(normed[1]))
    p1 = projected(g1, w12, 0, 1)
    k_u, g2 = comm(4, exchange_ctx(p1, True), gather_fsdp(normed[2]))
    p2 = projected(g2, w12, 1, 2)
    p2, wdown, up_cols, out_rows = lax.optimization_barrier((p2, wdown, up_cols, out_weight))
    wout = lax.all_gather(out_rows, "ctx", axis=0, tiled=True)
    up_g = line_gather(up_cols).reshape(count, fn, 2 * rows, pcol)
    (v_u,) = comm(5, exchange_ctx(p2, True))
    wqkv = [w.transpose(1, 0, 2, 3).reshape(width, wcol) for w in (w0, w12[:, :, 0], w12[:, :, 1])]
    q_u, k_u, v_u = whole_units(q_u), whole_units(k_u), whole_units(v_u)
    normed_g = [g.reshape(ntp, width) for g in (g0, g1, g2)]

    pos_all = jnp.arange(total, dtype=jnp.int32)
    unit_ids = ci * units + jnp.arange(units, dtype=jnp.int32)
    seq_ids = unit_ids // heads
    unit_starts = starts.reshape(fn * seqs, -1)[seq_ids]
    first_key = jnp.max(
        jnp.where(unit_starts[:, None, :] <= pos_all[None, :, None], unit_starts[:, None, :], 0),
        axis=-1,
    )[:, None, :]
    att_u, lse_u = attend(q_u, k_u, v_u, first_key)
    attended = columns(comm(6, from_units(att_u))[0])

    def scatter_tokens(x):
        return comm(10, scatter_fsdp(x.astype(BF16).reshape(fn, nloc, width)))[0]

    def gather_tokens(x):
        return comm(3, gather_fsdp(x))[0].reshape(ntp, width)

    def scatter_plane_tokens(x):
        return comm(13, scatter_plane(x.astype(BF16).reshape(fn, 2, nloc, width)))[0]

    def gather_plane_tokens(x):
        return comm(14, gather_plane(x))[0].reshape(2 * ntp, width)

    hidden_res = streams[3] + scatter_tokens(dot("nd,de->ne", attended, wout)) + out_shift
    normed_mlp, mid_pull = jax.vjp(layer_norm, hidden_res, gain_all[3], shift_all[3])
    mlp_g = gather_plane_tokens(normed_mlp.astype(BF16))
    up_bias_cols = lax.dynamic_slice(
        up_shift.reshape(fn, count, 2, -1), (fi, 0, lo, 0), (1, count, 1, ff // dn)
    ).reshape(pcol)
    act_low, slope, wup = widen(mlp_g, up_g, up_bias_cols[None])
    result = hidden_res + scatter_plane_tokens(dot("nf,fd->nd", act_low, wdown)) + down_shift
    block_out = result.astype(BF16).reshape(seqs, length, width)

    next_rows, mixer_pull = jax.vjp(
        mixer, result, root_full, mix_in_full, mix_out_weight, mix_out_bias
    )
    next_mix = next_rows.T.reshape(-1, seqs, length)
    grad_result, grad_root, grad_mix_in, grad_mix_out, grad_mix_bias = mixer_pull(
        mix_cotangent.reshape(-1, nloc).T
    )
    grad_result = grad_result + out_cotangent.reshape(nloc, width).astype(F32)

    grad_branch = grad_result.astype(BF16)
    branch_g = gather_plane_tokens(grad_branch)
    grad_down_shift = jnp.sum(grad_branch.astype(F32), axis=0)

    bit = lo.reshape(1)

    def line_scatter(x):
        y = lax.psum_scatter(
            x.reshape(-1, x.shape[-1]),
            "ctx",
            scatter_dimension=0,
            axis_index_groups=lines,
            tiled=True,
        )
        return y.reshape(x.shape[1:])

    down_part = dot("nf,nd->fd", act_low, branch_g).astype(BF16)
    down_part, wdown = lax.optimization_barrier((down_part, wdown))
    grad_down = line_scatter(down_part.reshape(count, -1, width))
    grad_active = dot("nd,fd->nf", branch_g, wdown)
    grad_upward = (grad_active * slope.astype(F32)).astype(BF16)
    grad_up_shift = jnp.sum(grad_upward.astype(F32), axis=0)
    (up_part,) = halved_product(mlp_g, grad_upward, bit, fn, count, split=False)
    up_part, grad_upward = lax.optimization_barrier((up_part, grad_upward))
    grad_up = line_scatter(up_part.reshape(count, -1, pcol))
    mlp_part = dot("nf,df->nd", grad_upward, wup).astype(BF16)
    grad_mlp = scatter_plane_tokens(mlp_part)
    grad_hidden, grad_gain_mid, grad_shift_mid = mid_pull(grad_mlp)
    grad_hidden = grad_hidden + grad_result
    grad_attn = grad_hidden.astype(BF16)
    grad_out_shift = jnp.sum(grad_attn.astype(F32), axis=0)
    attn_g = gather_tokens(grad_attn)
    out_part = dot("nd,ne->de", attended, attn_g).astype(BF16)
    grad_att = dot("ne,de->nd", attn_g, wout).astype(BF16)
    grad_att = grad_att.reshape(fn * seqs, length, heads, HEAD_DIM).transpose(0, 2, 1, 3)
    out_part, grad_att = lax.optimization_barrier((out_part, grad_att))
    (g_u,) = comm(5, exchange_ctx(grad_att.reshape(cn, units, length, HEAD_DIM), True))
    g_u, grad_down, out_part = lax.optimization_barrier((g_u, grad_down, out_part))

    def ctx_scatter(x):
        return lax.psum_scatter(x, "ctx", scatter_dimension=0, tiled=True)

    grad_out = ctx_scatter(out_part)
    gq, gk, gv = attend_back(q_u, k_u, v_u, first_key, lse_u, att_u, whole_units(g_u), tables)

    def back_part(p, s):
        return dot("nc,dc->nd", p, wqkv[s]).astype(BF16).reshape(fn, nloc, width)

    def qkv_part(p, i):
        return halved_product(normed_g[i], p, bit, fn, cn, split=False)[0]

    gp0, grad_up = lax.optimization_barrier((comm(6, from_units(gq))[0], grad_up))
    gp0 = columns(gp0)
    q_part, gk = lax.optimization_barrier((qkv_part(gp0, 0), gk))
    grad_q = ctx_scatter(q_part.reshape(-1, wcol)).reshape(fn, rows, wcol)
    gp1, gn0 = comm(8, from_units(gk), scatter_fsdp(back_part(gp0, 0)))
    gp1, grad_out = lax.optimization_barrier((gp1, grad_out))
    gp1 = columns(gp1)
    gp2, gn1 = comm(8, from_units(gv), scatter_fsdp(back_part(gp1, 1)))
    gp2 = columns(gp2)
    kv_part = jnp.stack([qkv_part(gp1, 1), qkv_part(gp2, 2)], axis=1)
    kv_part, grad_up = lax.optimization_barrier((kv_part, grad_up))
    grad_kv = ctx_scatter(kv_part.reshape(-1, wcol)).reshape(2, fn, rows, wcol)
    grad_up, gn2, grad_q = comm(
        7,
        exchange_plane(grad_up.reshape(fn, 2, rows, pcol), plane_others),
        scatter_fsdp(back_part(gp2, 2)),
        exchange_fsdp(grad_q),
    )
    grad_up = grad_up.reshape(fn, 2, rows, count, -1).transpose(2, 0, 3, 1, 4).reshape(rows, ff)
    grad_proj = (gp0, gp1, gp2)
    grad_qkv_shift = jnp.stack([jnp.sum(g.astype(F32), axis=0) for g in grad_proj])

    grad_history, grad_mix, grad_gain_front, grad_shift_front = last(
        hist2, mixes, streams, gain_all[:3], (gn0, gn1, gn2), grad_hidden
    )
    grad_history = grad_history.reshape(history.shape)
    grad_mix = grad_mix[:, : mix2.shape[0] * hist].T.reshape(dense_mix.shape)

    def own_columns(x, full):
        zero = jnp.zeros((x.shape[0], full), F32)
        return lax.dynamic_update_slice_in_dim(zero, x, fi * x.shape[1], 1)

    lines_14 = [
        grad_gain_front,
        grad_gain_mid[None],
        grad_shift_front,
        grad_shift_mid[None],
        own_columns(grad_qkv_shift, width),
        grad_out_shift[None],
        grad_down_shift[None],
        grad_root[None],
    ]
    lines_14 = jnp.concatenate(lines_14, axis=0)
    up_lines = lax.dynamic_update_slice(
        jnp.zeros((fn, count, 2, ff // dn), F32),
        grad_up_shift.reshape(1, count, 1, -1),
        (fi, 0, lo, 0),
    ).reshape(dn, -1)
    same = jnp.concatenate([grad_mix_out.reshape(-1), grad_mix_bias])
    flat = jnp.concatenate(
        [
            lines_14.reshape(-1, dn, width // dn).transpose(1, 0, 2).reshape(dn, -1),
            up_lines,
            grad_mix_in.reshape(dn, -1),
            jnp.broadcast_to(same[None], (dn, same.size)),
        ],
        axis=1,
    )
    flat = jnp.pad(flat, ((0, 0), (0, -flat.shape[1] % 1024)))
    small, grad_k, grad_v = comm(
        2,
        scatter_small(flat.reshape(fn, cn, -1, 128)),
        exchange_fsdp(grad_kv[0]),
        exchange_fsdp(grad_kv[1]),
    )
    grad_qkv = jnp.stack([grad_q, grad_k, grad_v])
    grad_qkv = grad_qkv.transpose(2, 0, 1, 3).reshape(rows, 3, width).astype(F32)
    small = small.reshape(-1)
    out_small, at = [], 0
    order = [norm_gain, norm_bias, qkv_bias, out_bias, down_bias, root_gain, up_bias, mix_in_weight]
    for a in order:
        out_small.append(small[at : at + a.size].reshape(a.shape))
        at += a.size
    (g_gain, g_shift, g_qkv_b, g_out_b, g_down_b, g_root, g_up_b, g_mix_in) = out_small
    mix_sums = small[at : at + same.size]
    cut = grad_mix_out.size
    return (
        block_out,
        next_mix,
        grad_history,
        grad_mix,
        g_gain,
        g_shift,
        grad_qkv,
        g_qkv_b,
        grad_out.astype(F32),
        g_out_b,
        grad_up.astype(F32),
        g_up_b,
        grad_down.astype(F32),
        g_down_b,
        g_root,
        g_mix_in,
        mix_sums[:cut].reshape(grad_mix_out.shape),
        mix_sums[cut:],
    )


def solution(mesh):
    token = P(None, "fsdp", "ctx")
    both = P(BOTH)
    cols = P(None, BOTH)
    placed = (
        token,
        P(None, None, "fsdp", "ctx"),
        P("fsdp"),
        cols,
        cols,
        both,
        cols,
        both,
        both,
        both,
        both,
        both,
        both,
        both,
        both,
        P(),
        P(),
        P("fsdp", "ctx"),
        token,
    )
    outs = (
        P("fsdp", "ctx"),
        token,
        token,
        P(None, None, "fsdp", "ctx"),
        cols,
        cols,
        both,
        cols,
        both,
        both,
        both,
        both,
        both,
        both,
        both,
        both,
        P(),
        P(),
    )
    return jax.shard_map(body, mesh=mesh, in_specs=placed, out_specs=outs, check_vma=False)
```

```python
import math

import jax
import jax.numpy as jnp
import numpy as np
from jax import lax
from jax.experimental import pallas as pl
from jax.experimental.pallas import tpu as pltpu
from jax.sharding import PartitionSpec as P

HEAD_DIM = 128
ROT = 32
TOP_PRECISION = lax.Precision.HIGHEST
EPS_NORM = 1e-05
EPS_ROOT = 1e-06
NEG_BIG = -1e30
BOTH = ("fsdp", "ctx")
BF16 = jnp.bfloat16
F32 = jnp.float32
MESH = pl.DeviceIdType.MESH
ANY = pl.BlockSpec(memory_space=pl.ANY)
VMEM = pl.BlockSpec(memory_space=pltpu.VMEM)
LOG2E = 1.4426950408889634


def layer_norm(values, gain_row, shift_row):
    centre = values - jnp.mean(values, axis=-1, keepdims=True)
    spread = jnp.mean(centre * centre, axis=-1, keepdims=True)
    return centre * lax.rsqrt(spread + EPS_NORM) * gain_row + shift_row


def gelu(values):
    return jax.nn.gelu(values, approximate=False)


def rotary_tables(count):
    half = ROT // 2
    frequency = np.exp(np.arange(half, dtype=np.float32) * np.float32(-2.0 * math.log(10000.0) / ROT))
    angles = np.arange(count, dtype=np.float32)[:, None] * frequency.astype(np.float32)[None, :]
    cosine = jnp.asarray(np.cos(angles.astype(np.float64)), F32)
    sine = jnp.asarray(np.sin(angles.astype(np.float64)), F32)
    zero, rest = jnp.zeros_like(sine), HEAD_DIM - ROT
    return jnp.stack(
        [
            jnp.pad(jnp.concatenate([cosine, cosine], 1), ((0, 0), (0, rest)), constant_values=1.0),
            jnp.pad(jnp.concatenate([zero, sine], 1), ((0, 0), (0, rest))),
            jnp.pad(jnp.concatenate([-sine, zero], 1), ((0, 0), (0, rest))),
        ]
    )


def turn(x, straight, right, left):
    half = ROT // 2
    return (
        x * straight
        + pltpu.roll(x, half, axis=1) * right
        + pltpu.roll(x, HEAD_DIM - half, axis=1) * left
    )


def mixer(rows, gain_row, opening, closing, closing_bias):
    inverse_rms = lax.rsqrt(jnp.mean(rows * rows, axis=-1, keepdims=True) + EPS_ROOT)
    rooted = rows * inverse_rms * gain_row
    hidden = jnp.dot(rooted, opening, precision=TOP_PRECISION)
    return jnp.dot(gelu(hidden), closing, precision=TOP_PRECISION) + closing_bias


def dot(pattern, left, right):
    return jnp.einsum(pattern, left, right, preferred_element_type=F32)


def remote(src, dst, send_sem, recv_sem, target):
    return pltpu.make_async_remote_copy(
        src_ref=src,
        dst_ref=dst,
        send_sem=send_sem,
        recv_sem=recv_sem,
        device_id=target,
        device_id_type=MESH,
    )


def place():
    return lax.axis_index("fsdp"), lax.axis_index("ctx")


def links_and_twin():
    chips = lax.axis_size("fsdp") // 2
    f, c = place()
    chip, core = f // 2, lax.rem(f, 2)
    return [(lax.rem(chip + j, chips) * 2 + core, c) for j in range(1, chips)] + [
        (chip * 2 + 1 - core, c)
    ]


def along_ctx():
    cn = lax.axis_size("ctx")
    f, c = place()
    return [(f, lax.rem(c + j, cn)) for j in range(1, cn)]


def along_fsdp():
    fn = lax.axis_size("fsdp")
    f, c = place()
    return [(lax.rem(f + j, fn), c) for j in range(1, fn)]


def along_both():
    return along_ctx() + along_fsdp()


def comm(cid, *tasks):
    n = len(tasks)
    counts = [len(t[5]) for t in tasks]
    limit = 6 * 2**20
    for t in tasks:
        for x in t[5]:
            if x.dtype in (BF16, F32):
                limit += math.prod(x.shape) * jnp.dtype(x.dtype).itemsize

    def kernel(*refs):
        targets, seen = [], []
        covered = [
            (along_fsdp, [along_both]),
            (the_pair, [along_ctx]),
            (the_pair, [plane_others]),
            (links_and_twin, [plane_others]),
            (links_and_twin, [along_fsdp]),
        ]
        for t in tasks:
            if t[0] not in seen and (t[0], seen[:1]) not in covered:
                seen.append(t[0])
                targets += t[0]()
        barrier = pltpu.get_barrier_semaphore()
        for t in targets:
            pl.semaphore_signal(barrier, inc=1, device_id=t, device_id_type=MESH)
        pl.semaphore_wait(barrier, len(targets))
        scratch = list(refs[2 * n :])
        phases = []
        for i, t in enumerate(tasks):
            mine, scratch = scratch[: counts[i]], scratch[counts[i] :]
            phases.append(t[6](refs[i], refs[n + i], *mine))
        for p in range(3):
            for ph in phases:
                ph[p]()

    out = pl.pallas_call(
        kernel,
        out_shape=[t[2] for t in tasks],
        in_specs=[t[3] for t in tasks],
        out_specs=[t[4] for t in tasks],
        scratch_shapes=[x for t in tasks for x in t[5]],
        compiler_params=pltpu.CompilerParams(
            collective_id=cid, has_side_effects=True, vmem_limit_bytes=limit
        ),
        cost_estimate=pl.CostEstimate(flops=0, bytes_accessed=15_000_000, transcendentals=0),
    )(*[t[1] for t in tasks])
    return out


def dma(*shape):
    return pltpu.SemaphoreType.DMA(shape)


def gather_small(x):
    fn, cn = lax.axis_size("fsdp"), lax.axis_size("ctx")

    def body(x_ref, o_ref, s1, r1, s2, r2):
        f, c = place()

        def first(j):
            return remote(
                x_ref, o_ref.at[f, c], s1.at[j], r1.at[j], (f, lax.rem(c + j, cn))
            )

        def second(j):
            return remote(
                o_ref.at[f], o_ref.at[f], s2.at[j], r2.at[j], (lax.rem(f + j, fn), c)
            )

        def start():
            for j in range(1, cn):
                first(j).start()
            o_ref[f, c] = x_ref[...]

        def middle():
            for j in range(1, cn):
                there = o_ref.at[f, lax.rem(c + cn - j, cn)]
                remote(there, there, s1.at[j], r1.at[j], (f, lax.rem(c + j, cn))).wait_recv()
            for j in range(1, fn):
                second(j).start()

        def end():
            for j in range(1, fn):
                there = o_ref.at[lax.rem(f + fn - j, fn)]
                remote(there, there, s2.at[j], r2.at[j], (lax.rem(f + j, fn), c)).wait_recv()
            for j in range(1, cn):
                first(j).wait_send()
            for j in range(1, fn):
                second(j).wait_send()

        return start, middle, end

    shape = jax.ShapeDtypeStruct((fn, cn, *x.shape), x.dtype)
    return (along_both, x, shape, VMEM, VMEM, [dma(cn), dma(cn), dma(fn), dma(fn)], body)


def exchange_fsdp(x):
    fn = lax.axis_size("fsdp")

    def body(x_ref, o_ref, s, r, own):
        f, c = place()

        def copy(j, slot):
            t = lax.rem(f + j, fn)
            return remote(x_ref.at[t], o_ref.at[slot], s.at[j], r.at[j], (t, c))

        mine = pltpu.make_async_copy(x_ref.at[f], o_ref.at[f], own)

        def start():
            for j in range(1, fn):
                copy(j, f).start()
            mine.start()

        def end():
            mine.wait()
            for j in range(1, fn):
                copy(j, lax.rem(f + fn - j, fn)).wait_recv()
            for j in range(1, fn):
                copy(j, f).wait_send()

        return start, lambda: None, end

    shape = jax.ShapeDtypeStruct(x.shape, x.dtype)
    return (along_fsdp, x, shape, ANY, ANY, [dma(fn), dma(fn), dma()], body)


def exchange_ctx(x, to_units):
    cn = lax.axis_size("ctx")
    lead = x.shape[1] if to_units else x.shape[0]

    def body(x_ref, o_ref, s, r, own):
        f, c = place()

        def source(t):
            return x_ref.at[t] if to_units else x_ref.at[:, t]

        def target(slot):
            return o_ref.at[:, slot] if to_units else o_ref.at[slot]

        def copy(j, slot):
            t = lax.rem(c + j, cn)
            return remote(source(t), target(slot), s.at[j], r.at[j], (f, t))

        mine = pltpu.make_async_copy(source(c), target(c), own)

        def start():
            for j in range(1, cn):
                copy(j, c).start()
            mine.start()

        def end():
            mine.wait()
            for j in range(1, cn):
                copy(j, lax.rem(c + cn - j, cn)).wait_recv()
            for j in range(1, cn):
                copy(j, c).wait_send()

        return start, lambda: None, end

    dims = (lead, cn) if to_units else (cn, lead)
    shape = jax.ShapeDtypeStruct((*dims, *x.shape[2:]), x.dtype)
    return (along_ctx, x, shape, ANY, ANY, [dma(cn), dma(cn), dma()], body)


def the_pair():
    f, c = place()
    return [(f, c // 2 * 2 + 1 - lax.rem(c, 2))]


def exchange_pair(x):
    def body(x_ref, o_ref, s, r):
        (pair,) = the_pair()
        copy = remote(x_ref, o_ref, s, r, pair)
        return copy.start, lambda: None, copy.wait

    shape = jax.ShapeDtypeStruct(x.shape, x.dtype)
    return (the_pair, x, shape, ANY, ANY, [dma(), dma()], body)


def gather_fsdp(x, parts=4):
    fn = lax.axis_size("fsdp")
    chips = fn // 2
    n, d = x.shape
    step = n // parts
    pieces = [pl.ds(p * step, step) for p in range(parts)]

    def body(x_ref, o_ref, own_sem, s_link, r_link, s_core, r_core):
        f, c = place()
        chip, core = f // 2, lax.rem(f, 2)
        twin = (chip * 2 + 1 - core, c)
        links, cores = {}, {}

        def to(j):
            return (lax.rem(chip + j, chips) * 2 + core, c)

        def slot(j, core_id):
            return lax.rem(chip + chips - j, chips) * 2 + core_id

        own = pltpu.make_async_copy(x_ref, o_ref.at[f], own_sem)

        def start():
            for i, rows in enumerate(pieces):
                here, there = x_ref.at[rows], o_ref.at[f, rows]
                for j in range(1, chips):
                    links[i, j] = remote(here, there, s_link.at[j, i], r_link.at[j, i], to(j))
                    links[i, j].start()
            for i, rows in enumerate(pieces):
                here, there = x_ref.at[rows], o_ref.at[f, rows]
                cores[i, 0] = remote(here, there, s_core.at[0, i], r_core.at[0, i], twin)
                cores[i, 0].start()
            own.start()

        def middle():
            for i, rows in enumerate(pieces):
                for j in range(1, chips):
                    here = o_ref.at[slot(j, core), rows]
                    remote(here, here, s_link.at[j, i], r_link.at[j, i], to(j)).wait_recv()
                    cores[i, j] = remote(here, here, s_core.at[j, i], r_core.at[j, i], twin)
                    cores[i, j].start()

        def end():
            own.wait()
            for i, rows in enumerate(pieces):
                for j in range(chips):
                    there = o_ref.at[slot(j, 1 - core), rows]
                    cores[i, j].wait_send()
                    remote(there, there, s_core.at[j, i], r_core.at[j, i], twin).wait_recv()
                for j in range(1, chips):
                    links[i, j].wait_send()

        return start, middle, end

    shape = jax.ShapeDtypeStruct((fn, n, d), x.dtype)
    return (links_and_twin, x, shape, ANY, ANY, [dma()] + [dma(chips, parts)] * 4, body)


def gather_ctx(x):
    cn = lax.axis_size("ctx")
    count = cn // 2

    def body(x_ref, o_ref, own_sem, s_up, r_up, s_down, r_down, s_pair, r_pair):
        f, c = place()
        hi, lo = c // 2, lax.rem(c, 2)
        pair = (f, hi * 2 + 1 - lo)
        above = (f, lax.rem(hi + 1, count) * 2 + lo)
        below = (f, lax.rem(hi + count - 1, count) * 2 + lo)
        own = pltpu.make_async_copy(x_ref, o_ref.at[c], own_sem)

        def low(d):
            return lax.rem(hi + count - d, count)

        def high(d):
            return lax.rem(hi + d, count)

        def up(d):
            source = x_ref if d == 0 else o_ref.at[low(d) * 2 + lo]
            return remote(source, o_ref.at[low(d) * 2 + lo], s_up.at[d], r_up.at[d + 1], above)

        def down(d):
            source = x_ref if d == 0 else o_ref.at[high(d) * 2 + lo]
            return remote(
                source, o_ref.at[high(d) * 2 + lo], s_down.at[d], r_down.at[d + 1], below
            )

        def across(k, slot):
            source = x_ref if k == 0 else o_ref.at[slot * 2 + lo]
            return remote(source, o_ref.at[slot * 2 + lo], s_pair.at[k], r_pair.at[k], pair)

        def start():
            pl.when(hi < count - 1)(lambda: up(0).start())
            pl.when(hi > 0)(lambda: down(0).start())
            across(0, hi).start()
            own.start()

        def middle():
            for d in range(1, count):

                @pl.when(hi >= d)
                def _():
                    here = o_ref.at[low(d) * 2 + lo]
                    remote(here, here, s_up.at[d], r_up.at[d], above).wait_recv()
                    across(d, low(d)).start()
                    if d < count - 1:
                        pl.when(hi < count - 1)(lambda: up(d).start())

                @pl.when(hi + d < count)
                def _():
                    here = o_ref.at[high(d) * 2 + lo]
                    remote(here, here, s_down.at[d], r_down.at[d], below).wait_recv()
                    across(count - d, high(d)).start()
                    if d < count - 1:
                        pl.when(hi > 0)(lambda: down(d).start())

        def end():
            own.wait()
            across(0, hi).wait_send()
            for k in range(count):
                there = o_ref.at[low(k) * 2 + 1 - lo]
                remote(there, there, s_pair.at[k], r_pair.at[k], pair).wait_recv()
                if k > 0:
                    across(k, low(k)).wait_send()
            for d in range(count - 1):
                pl.when((hi >= d) & (hi < count - 1))(lambda d=d: up(d).wait_send())
                pl.when((hi + d < count) & (hi > 0))(lambda d=d: down(d).wait_send())

        return start, middle, end

    shape = jax.ShapeDtypeStruct((cn, *x.shape), x.dtype)
    scratch = [dma()] + [dma(count + 1)] * 4 + [dma(count)] * 2
    return (along_ctx, x, shape, ANY, ANY, scratch, body)


def scatter_fsdp(x, parts=4):
    fn = lax.axis_size("fsdp")
    chips = fn // 2
    _, n, d = x.shape
    step = n // parts

    def body(x_ref, o_ref, own, near, mine, far, ss, s_own, s_near, r_near, s_far, r_far):
        f, c = place()
        chip, core = f // 2, lax.rem(f, 2)
        twin = (chip * 2 + 1 - core, c)
        nears, owns, fars, outs = {}, {}, {}, {}

        def chip_at(j):
            return lax.rem(chip + j, chips)

        def start():
            for p in range(parts):
                rows = pl.ds(p * step, step)
                for j in list(range(1, chips)) + [0]:
                    at = chip_at(j) * 2
                    owns[p, j] = pltpu.make_async_copy(
                        x_ref.at[at + core, rows], own.at[j, p], s_own.at[j, p]
                    )
                    owns[p, j].start()
                    nears[p, j] = remote(
                        x_ref.at[at + 1 - core, rows],
                        near.at[j, p],
                        s_near.at[j, p],
                        r_near.at[j, p],
                        twin,
                    )
                    nears[p, j].start()

        def middle():
            for p in range(parts):
                for j in range(1, chips):
                    owns[p, j].wait()
                    nears[p, j].wait_recv()
                    mine[j, p] = (own[j, p].astype(F32) + near[j, p].astype(F32)).astype(BF16)
                    fars[p, j] = remote(
                        mine.at[j, p],
                        far.at[j, p],
                        s_far.at[j, p],
                        r_far.at[j, p],
                        (chip_at(j) * 2 + core, c),
                    )
                    fars[p, j].start()
            for p in range(parts):
                owns[p, 0].wait()
                nears[p, 0].wait_recv()
                ss[p] = own[0, p].astype(F32) + near[0, p].astype(F32)

        def end():
            for p in range(parts):
                for j in range(1, chips):
                    fars[p, j].wait_recv()
                    ss[p] += far[j, p].astype(F32)
                outs[p] = pltpu.make_async_copy(
                    ss.at[p], o_ref.at[pl.ds(p * step, step)], s_far.at[0, p]
                )
                outs[p].start()
            for p in range(parts):
                outs[p].wait()
                for j in range(chips):
                    nears[p, j].wait_send()
                for j in range(1, chips):
                    fars[p, j].wait_send()

        return start, middle, end

    block = pltpu.VMEM((chips, parts, step, d), BF16)
    scratch = [block] * 4 + [pltpu.VMEM((parts, step, d), F32)] + [dma(chips, parts)] * 5
    return (links_and_twin, x, jax.ShapeDtypeStruct((n, d), F32), ANY, ANY, scratch, body)


def plane_others():
    fn = lax.axis_size("fsdp")
    f, c = place()
    (pair,) = the_pair()
    return [(lax.rem(f + a, fn), (c, pair[1])[b]) for a in range(fn) for b in range(2) if a or b]


def plane_sides():
    return [t for i, t in enumerate(plane_others()) if i > 0]


def exchange_plane(x, peers):
    fn = lax.axis_size("fsdp")

    def body(x_ref, o_ref, s, r, own):
        f, c = place()
        lo = lax.rem(c, 2)
        (pair,) = the_pair()

        def index(a, b):
            return lax.rem(f + a + fn, fn), (lo if b == 0 else 1 - lo)

        def copy(a, b, slot):
            fa, lb = index(a, b)
            return remote(
                x_ref.at[fa, lb],
                o_ref.at[slot[0], slot[1]],
                s.at[a, b],
                r.at[a, b],
                (fa, c if b == 0 else pair[1]),
            )

        steps = [(a, b) for a in range(fn) for b in range(2) if a or b]
        mine = pltpu.make_async_copy(x_ref.at[f, lo], o_ref.at[f, lo], own)

        def start():
            for a, b in steps:
                copy(a, b, (f, lo)).start()
            mine.start()

        def end():
            mine.wait()
            for a, b in steps:
                copy(a, b, index(-a, b)).wait_recv()
            for a, b in steps:
                copy(a, b, (f, lo)).wait_send()

        return start, lambda: None, end

    shape = jax.ShapeDtypeStruct(x.shape, x.dtype)
    return (peers, x, shape, ANY, ANY, [dma(fn, 2), dma(fn, 2), dma()], body)


def exchange_columns(x, wide, peers):
    fn = lax.axis_size("fsdp")
    _, _, rows, cols = x.shape
    count = cols // wide

    def body(x_ref, o_ref, s, r, own):
        f, c = place()
        lo = lax.rem(c, 2)
        (pair,) = the_pair()

        def index(a, b):
            return lax.rem(f + a + fn, fn), (lo if b == 0 else 1 - lo)

        def target(slot, h):
            at = ((slot[0] * count + h) * 2 + slot[1]) * wide
            return o_ref.at[:, pl.ds(pl.multiple_of(at, wide), wide)]

        def copy(a, b, h, slot):
            fa, lb = index(a, b)
            return remote(
                x_ref.at[fa, lb, :, pl.ds(h * wide, wide)],
                target(slot, h),
                s.at[a, b, h],
                r.at[a, b, h],
                (fa, c if b == 0 else pair[1]),
            )

        steps = [
            (a, b, h) for a in range(fn) for b in range(2) for h in range(count) if a or b
        ]
        mine = [
            pltpu.make_async_copy(
                x_ref.at[f, lo, :, pl.ds(h * wide, wide)], target((f, lo), h), own.at[h]
            )
            for h in range(count)
        ]

        def start():
            for a, b, h in steps:
                copy(a, b, h, (f, lo)).start()
            for m in mine:
                m.start()

        def end():
            for m in mine:
                m.wait()
            for a, b, h in steps:
                copy(a, b, h, index(-a, b)).wait_recv()
            for a, b, h in steps:
                copy(a, b, h, (f, lo)).wait_send()

        return start, lambda: None, end

    shape = jax.ShapeDtypeStruct((rows, fn * 2 * cols), x.dtype)
    scratch = [dma(fn, 2, count), dma(fn, 2, count), dma(count)]
    return (peers, x, shape, ANY, ANY, scratch, body)


def links_twin_pair():
    return links_and_twin() + the_pair()


def gather_plane(x, parts=8):
    fn = lax.axis_size("fsdp")
    chips = fn // 2
    n, d = x.shape
    step = n // parts
    first, second = list(range(parts // 2)), list(range(parts // 2, parts))
    others = list(range(1, chips))

    def body(x_ref, o_ref, own_sem, sx, rx, sy, ry, st, rt):
        f, c = place()
        chip, core, lo = f // 2, lax.rem(f, 2), lax.rem(c, 2)
        twin = (chip * 2 + 1 - core, c)
        (pair,) = the_pair()

        def rows(p):
            return pl.ds(p * step, step)

        def block(j, core_id, kind, p):
            slot = lax.rem(chip + chips - j, chips) * 2 + core_id
            return o_ref.at[slot, lo if kind == 0 else 1 - lo, rows(p)]

        def source(j, kind, p):
            return x_ref.at[rows(p)] if j == 0 and kind == 0 else block(j, core, kind, p)

        def to(j):
            return (lax.rem(chip + j, chips) * 2 + core, c)

        def x_copy(j, kind, p):
            return remote(
                source(0, kind, p), block(0, core, kind, p), sx.at[j, kind, p], rx.at[j, kind, p], to(j)
            )

        def y_copy(j, p):
            return remote(source(j, 0, p), block(j, core, 0, p), sy.at[j, p], ry.at[j, p], pair)

        def t_copy(j, kind, p):
            return remote(
                source(j, kind, p), block(j, core, kind, p), st.at[j, kind, p], rt.at[j, kind, p], twin
            )

        def x_come(j, kind, p):
            here = block(j, core, kind, p)
            remote(here, here, sx.at[j, kind, p], rx.at[j, kind, p], to(j)).wait_recv()

        def y_come(j, p):
            here = block(j, core, 1, p)
            remote(here, here, sy.at[j, p], ry.at[j, p], pair).wait_recv()

        own = pltpu.make_async_copy(x_ref, o_ref.at[f, lo], own_sem)

        def start():
            for p in first:
                for j in others:
                    x_copy(j, 0, p).start()
            for p in second + first:
                y_copy(0, p).start()
            for p in second:
                for j in others:
                    x_copy(j, 0, p).start()
            for p in range(parts):
                t_copy(0, 0, p).start()
            own.start()

        def middle():
            for p, q in zip(first, second, strict=True):
                for j in others:
                    x_come(j, 0, p)
                    y_copy(j, p).start()
                    t_copy(j, 0, p).start()
                y_come(0, q)
                for j in others:
                    x_copy(j, 1, q).start()
                t_copy(0, 1, q).start()
            for p, q in zip(first, second, strict=True):
                y_come(0, p)
                t_copy(0, 1, p).start()
                for j in others:
                    x_come(j, 0, q)
                    t_copy(j, 0, q).start()

        def end():
            for p, q in zip(first, second, strict=True):
                for j in others:
                    y_come(j, p)
                    t_copy(j, 1, p).start()
                    x_come(j, 1, q)
                    t_copy(j, 1, q).start()
            own.wait()
            for p in range(parts):
                for j in range(chips):
                    for kind in range(2):
                        there = block(j, 1 - core, kind, p)
                        remote(
                            there, there, st.at[j, kind, p], rt.at[j, kind, p], twin
                        ).wait_recv()
                        t_copy(j, kind, p).wait_send()
                y_copy(0, p).wait_send()
                for j in others:
                    x_copy(j, 0, p).wait_send()
            for p, q in zip(first, second, strict=True):
                for j in others:
                    y_copy(j, p).wait_send()
                    x_copy(j, 1, q).wait_send()

        return start, middle, end

    shape = jax.ShapeDtypeStruct((fn, 2, n, d), x.dtype)
    scratch = [dma()] + [dma(chips, 2, parts)] * 2 + [dma(chips, parts)] * 2
    scratch = scratch + [dma(chips, 2, parts)] * 2
    return (links_twin_pair, x, shape, ANY, ANY, scratch, body)


def scatter_plane(x, parts=4):
    fn = lax.axis_size("fsdp")
    chips = fn // 2
    _, _, n, d = x.shape
    step = n // parts
    half = parts // 2
    others = list(range(1, chips))

    def body(
        x_ref, o_ref, own, near, send1, come_y, send_x, come_x, come_x2, send_y, come_y2, acc,
        s_own, s_near, r_near, s_1, r_y, r_x, s_2, r_x2, s_3, r_y2, s_out,
    ):
        f, c = place()
        chip, core, lo = f // 2, lax.rem(f, 2), lax.rem(c, 2)
        twin = (chip * 2 + 1 - core, c)
        (pair,) = the_pair()

        def chip_at(j):
            return lax.rem(chip + j, chips)

        def to(j):
            return (chip_at(j) * 2 + core, c)

        def part(j, core_id, kind, p):
            return x_ref.at[
                chip_at(j) * 2 + core_id, lo if kind == 0 else 1 - lo, pl.ds(p * step, step)
            ]

        def own_copy(j, k, p):
            return pltpu.make_async_copy(part(j, core, k, p), own.at[j, k, p], s_own.at[j, k, p])

        def near_copy(j, k, p):
            return remote(
                part(j, 1 - core, k, p), near.at[j, k, p], s_near.at[j, k, p], r_near.at[j, k, p], twin
            )

        def both(j, k, p):
            return own[j, k, p].astype(F32) + near[j, k, p].astype(F32)

        def ready(j, k, p):
            own_copy(j, k, p).wait()
            near_copy(j, k, p).wait_recv()

        def y_first(j, p):
            return remote(send1.at[j, 1, p], come_y.at[j, p], s_1.at[j, 1, p], r_y.at[j, p], pair)

        def x_first(j, k, p):
            q = p - half
            return remote(
                send1.at[j, k, p], come_x.at[j, k, q], s_1.at[j, k, p], r_x.at[j, k, q], to(j)
            )

        def x_then(j, p):
            return remote(send_x.at[j, p], come_x2.at[j, p], s_2.at[j, p], r_x2.at[j, p], to(j))

        def y_then(q):
            return remote(send_y.at[q], come_y2.at[q], s_3.at[q], r_y2.at[q], pair)

        def out(p):
            return pltpu.make_async_copy(acc.at[p], o_ref.at[pl.ds(p * step, step)], s_out.at[p])

        order = [(j, k, i) for i in range(half) for j in others + [0] for k in (1, 0)]

        def start():
            for j, k, i in order:
                for p in (i, i + half):
                    own_copy(j, k, p).start()
                    near_copy(j, k, p).start()

        def middle():
            for i in range(half):
                for j in range(chips):
                    ready(j, 1, i)
                    send1[j, 1, i] = both(j, 1, i).astype(BF16)
                    y_first(j, i).start()
                for j in others:
                    for k in (1, 0):
                        ready(j, k, i + half)
                        send1[j, k, i + half] = both(j, k, i + half).astype(BF16)
                        x_first(j, k, i + half).start()
            for i in range(half):
                for j in range(chips):
                    ready(j, 0, i)
                for k in range(2):
                    ready(0, k, i + half)

        def end():
            for i in range(half):
                for j in others:
                    y_first(j, i).wait_recv()
                    send_x[j, i] = (both(j, 0, i) + come_y[j, i].astype(F32)).astype(BF16)
                    x_then(j, i).start()
                total = both(0, 1, i + half)
                for j in others:
                    x_first(j, 1, i + half).wait_recv()
                    total += come_x[j, 1, i].astype(F32)
                send_y[i] = total.astype(BF16)
                y_then(i).start()
            for i in range(half):
                y_first(0, i).wait_recv()
                acc[i] = both(0, 0, i) + come_y[0, i].astype(F32)
                acc[i + half] = both(0, 0, i + half)
                for j in others:
                    x_first(j, 0, i + half).wait_recv()
                    acc[i + half] += come_x[j, 0, i].astype(F32)
            for i in range(half):
                for j in others:
                    x_then(j, i).wait_recv()
                    acc[i] += come_x2[j, i].astype(F32)
                out(i).start()
                y_then(i).wait_recv()
                acc[i + half] += come_y2[i].astype(F32)
                out(i + half).start()
            for i in range(half):
                out(i).wait()
                out(i + half).wait()
                y_then(i).wait_send()
                for j in others:
                    x_then(j, i).wait_send()
                    for k in range(2):
                        x_first(j, k, i + half).wait_send()
                for j in range(chips):
                    y_first(j, i).wait_send()
                    for k in range(2):
                        near_copy(j, k, i).wait_send()
                        near_copy(j, k, i + half).wait_send()

        return start, middle, end

    def buffer(*lead):
        return pltpu.VMEM((*lead, step, d), BF16)

    scratch = [
        buffer(chips, 2, parts),
        buffer(chips, 2, parts),
        buffer(chips, 2, parts),
        buffer(chips, half),
        buffer(chips, half),
        buffer(chips, 2, half),
        buffer(chips, half),
        buffer(half),
        buffer(half),
        pltpu.VMEM((parts, step, d), F32),
        dma(chips, 2, parts),
        dma(chips, 2, parts),
        dma(chips, 2, parts),
        dma(chips, 2, parts),
        dma(chips, half),
        dma(chips, 2, half),
        dma(chips, half),
        dma(chips, half),
        dma(half),
        dma(half),
        dma(parts),
    ]
    return (links_twin_pair, x, jax.ShapeDtypeStruct((n, d), F32), ANY, ANY, scratch, body)


def scatter_small(x):
    fn, cn = lax.axis_size("fsdp"), lax.axis_size("ctx")

    def body(x_ref, o_ref, got, sums, got2, s1, r1, s2, r2):
        f, c = place()

        def first(j):
            t = lax.rem(f + j, fn)
            return remote(x_ref.at[t], got.at[j], s1.at[j], r1.at[j], (t, c))

        def second(j):
            t = lax.rem(c + j, cn)
            return remote(sums.at[t], got2.at[j], s2.at[j], r2.at[j], (f, t))

        def start():
            for j in range(1, fn):
                first(j).start()
            sums[...] = x_ref[f]

        def middle():
            for j in range(1, fn):
                first(j).wait_recv()
                sums[...] += got[j]
            for j in range(1, cn):
                second(j).start()
            o_ref[...] = sums[c]

        def end():
            for j in range(1, cn):
                second(j).wait_recv()
                o_ref[...] += got2[j]
            for j in range(1, fn):
                first(j).wait_send()
            for j in range(1, cn):
                second(j).wait_send()

        return start, middle, end

    tail = x.shape[2:]
    scratch = [
        pltpu.VMEM(x.shape, x.dtype),
        pltpu.VMEM(x.shape[1:], x.dtype),
        pltpu.VMEM(x.shape[1:], x.dtype),
        dma(fn),
        dma(fn),
        dma(cn),
        dma(cn),
    ]
    return (along_both, x, jax.ShapeDtypeStruct(tail, x.dtype), VMEM, VMEM, scratch, body)


def nt(a, b):
    return lax.dot_general(a, b, (((1,), (1,)), ((), ())), preferred_element_type=F32)


def nn(a, b):
    return lax.dot_general(a, b, (((1,), (0,)), ((), ())), preferred_element_type=F32)


def attend(q, k, v, starts, block=512):
    u, t, _ = q.shape
    scale = HEAD_DIM**-0.5 * LOG2E

    def kernel(q_ref, k_ref, v_ref, s_ref, o_ref, l_ref, vt):
        i = pl.program_id(1)

        @pl.when(i == 0)
        def _():
            vt[...] = v_ref[0].T

        rows = q_ref[0]
        first = s_ref[0]
        base = lax.broadcasted_iota(jnp.int32, (block, block), 0)
        qpos = i * block + lax.broadcasted_iota(jnp.int32, (1, block), 1)

        def one(j, carry, diagonal):
            peak, total, acc = carry
            at = pl.multiple_of(j * block, block)
            s = nt(k_ref[0, pl.ds(at, block)], rows) * scale
            kpos = base + at
            keep = kpos >= first
            if diagonal:
                keep = keep & (kpos <= qpos)
            s = jnp.where(keep, s, NEG_BIG)
            new = jnp.maximum(peak, jnp.max(s, axis=0, keepdims=True))
            p = jnp.exp2(s - new)
            shrink = jnp.exp2(peak - new)
            total = total * shrink + jnp.sum(p, axis=0, keepdims=True)
            acc = acc * shrink + nn(vt[:, pl.ds(at, block)], p.astype(BF16))
            return new, total, acc

        start = (
            jnp.full((1, block), NEG_BIG, F32),
            jnp.zeros((1, block), F32),
            jnp.zeros((HEAD_DIM, block), F32),
        )
        start = one(i, start, True)
        peak, total, acc = lax.fori_loop(0, i, lambda j, c: one(j, c, False), start)
        o_ref[0] = (acc / total).T.astype(BF16)
        l_ref[0] = peak + jnp.log2(total)

    return pl.pallas_call(
        kernel,
        grid=(u, t // block),
        in_specs=[
            pl.BlockSpec((1, block, HEAD_DIM), lambda a, b: (a, b, 0)),
            pl.BlockSpec((1, t, HEAD_DIM), lambda a, b: (a, 0, 0)),
            pl.BlockSpec((1, t, HEAD_DIM), lambda a, b: (a, 0, 0)),
            pl.BlockSpec((1, 1, block), lambda a, b: (a, 0, b)),
        ],
        out_specs=[
            pl.BlockSpec((1, block, HEAD_DIM), lambda a, b: (a, b, 0)),
            pl.BlockSpec((1, 1, block), lambda a, b: (a, 0, b)),
        ],
        out_shape=[
            jax.ShapeDtypeStruct((u, t, HEAD_DIM), BF16),
            jax.ShapeDtypeStruct((u, 1, t), F32),
        ],
        scratch_shapes=[pltpu.VMEM((HEAD_DIM, t), BF16)],
        compiler_params=pltpu.CompilerParams(vmem_limit_bytes=32 * 2**20),
        cost_estimate=pl.CostEstimate(
            flops=2 * u * t * t * HEAD_DIM, bytes_accessed=8 * u * t * 256, transcendentals=u * t * t // 2
        ),
    )(q, k, v, starts)


def attend_back(q, k, v, starts, lse, o, g, tables, block=512):
    u, t, _ = q.shape
    scale = HEAD_DIM**-0.5

    def kernel(
        q_ref, k_ref, v_ref, s_ref, l_ref, o_ref, g_ref, t_ref, dq_ref, dk_ref, dv_ref, kt, dk, dv
    ):
        i = pl.program_id(1)

        @pl.when(i == 0)
        def _():
            kt[...] = k_ref[0].T
            dk[...] = jnp.zeros_like(dk)
            dv[...] = jnp.zeros_like(dv)

        rows, grows = q_ref[0], g_ref[0]
        first, logs = s_ref[0], l_ref[0]
        prod = o_ref[0].astype(F32) * grows.astype(F32)
        centre = jnp.sum(prod.T, axis=0, keepdims=True)
        base = lax.broadcasted_iota(jnp.int32, (block, block), 0)
        qpos = i * block + lax.broadcasted_iota(jnp.int32, (1, block), 1)

        def one(j, acc, diagonal):
            at = pl.multiple_of(j * block, block)
            here = pl.ds(at, block)
            p = jnp.exp2(nt(k_ref[0, here], rows) * (scale * LOG2E) - logs)
            kpos = base + at
            keep = kpos >= first
            if diagonal:
                keep = keep & (kpos <= qpos)
            p = jnp.where(keep, p, 0.0)
            gp = nt(v_ref[0, here], grows)
            ds = (p * (gp - centre)).astype(BF16)
            dv[here] += nn(p.astype(BF16), grows)
            dk[here] += nn(ds, rows)
            return acc + nn(kt[:, here], ds)

        acc = one(i, jnp.zeros((HEAD_DIM, block), F32), True)
        acc = lax.fori_loop(0, i, lambda j, a: one(j, a, False), acc)
        there = pl.ds(pl.multiple_of(i * block, block), block)
        straight, right, left = t_ref[0, there], t_ref[1, there], t_ref[2, there]
        dq_ref[0] = turn((acc * scale).T, straight, -right, -left).astype(BF16)

        @pl.when(i == t // block - 1)
        def _():
            for b in range(t // block):
                at = pl.ds(b * block, block)
                dk_ref[0, at] = turn(
                    dk[at] * scale, t_ref[0, at], -t_ref[1, at], -t_ref[2, at]
                ).astype(BF16)
                dv_ref[0, at] = dv[at].astype(BF16)

    def whole(a, b):
        return (a, 0, 0)

    def part(a, b):
        return (a, b, 0)

    def row(a, b):
        return (a, 0, b)

    spec, full, line = (1, block, HEAD_DIM), (1, t, HEAD_DIM), (1, 1, block)
    return pl.pallas_call(
        kernel,
        grid=(u, t // block),
        in_specs=[
            pl.BlockSpec(spec, part),
            pl.BlockSpec(full, whole),
            pl.BlockSpec(full, whole),
            pl.BlockSpec(line, row),
            pl.BlockSpec(line, row),
            pl.BlockSpec(spec, part),
            pl.BlockSpec(spec, part),
            pl.BlockSpec((3, t, HEAD_DIM), lambda a, b: (0, 0, 0)),
        ],
        out_specs=[
            pl.BlockSpec(spec, part),
            pl.BlockSpec(full, whole),
            pl.BlockSpec(full, whole),
        ],
        out_shape=[jax.ShapeDtypeStruct((u, t, HEAD_DIM), BF16)] * 3,
        scratch_shapes=[
            pltpu.VMEM((HEAD_DIM, t), BF16),
            pltpu.VMEM((t, HEAD_DIM), F32),
            pltpu.VMEM((t, HEAD_DIM), F32),
        ],
        compiler_params=pltpu.CompilerParams(vmem_limit_bytes=48 * 2**20),
        cost_estimate=pl.CostEstimate(
            flops=5 * u * t * t * HEAD_DIM, bytes_accessed=20 * u * t * 256, transcendentals=u * t * t // 2
        ),
    )(q, k, v, starts, lse, o, g, tables)


def project(x, w, stream, bias, tables):
    count, length, width = x.shape
    cn, fn, _, rows, cols = w.shape
    heads = cols // HEAD_DIM

    def kernel(*refs):
        x_ref, w_ref, b_ref = refs[:3]
        o_ref, held, sem = refs[-3:]

        @pl.when(pl.program_id(0) == 0)
        def _():
            copies = [
                pltpu.make_async_copy(w_ref.at[:, f, stream], held.at[f], sem.at[f])
                for f in range(fn)
            ]
            for c in copies:
                c.start()
            for c in copies:
                c.wait()

        y = nn(x_ref[0], held[...].reshape(width, cols)) + b_ref[...]
        for h in range(heads):
            part = y[:, h * HEAD_DIM : (h + 1) * HEAD_DIM]
            if tables is not None:
                t_ref = refs[3]
                part = turn(part, t_ref[0], t_ref[1], t_ref[2])
            o_ref[h] = part.astype(BF16)

    extra = [] if tables is None else [tables]
    return pl.pallas_call(
        kernel,
        grid=(count,),
        in_specs=[
            pl.BlockSpec((1, length, width), lambda i: (i, 0, 0)),
            ANY,
            pl.BlockSpec((1, cols), lambda i: (0, 0)),
        ]
        + [pl.BlockSpec((3, length, HEAD_DIM), lambda i: (0, 0, 0)) for _ in extra],
        out_specs=pl.BlockSpec((heads, length, HEAD_DIM), lambda i: (i, 0, 0)),
        out_shape=jax.ShapeDtypeStruct((count * heads, length, HEAD_DIM), BF16),
        scratch_shapes=[pltpu.VMEM((fn, cn, rows, cols), BF16), dma(fn)],
        compiler_params=pltpu.CompilerParams(vmem_limit_bytes=32 * 2**20),
        cost_estimate=pl.CostEstimate(
            flops=2 * count * length * width * cols,
            bytes_accessed=2 * (count * length * (width + cols) + width * cols),
            transcendentals=0,
        ),
    )(x, w, bias, *extra)


def widen(x, w, bias, tile=256, rows_at_once=512):
    n, d = x.shape
    cn, fn, rows, cols = w.shape
    tiles = cols // tile

    def kernel(x_ref, w_ref, b_ref, a_ref, g_ref, o_ref, held, sem):
        i = pl.program_id(0)

        def copy(j, f):
            at = pl.ds(pl.multiple_of(j * tile, tile), tile)
            return pltpu.make_async_copy(w_ref.at[:, f, :, at], held.at[j, f], sem.at[j, f])

        @pl.when(i == 0)
        def _():
            for j in range(tiles):
                for f in range(fn):
                    copy(j, f).start()

        for f in range(fn):
            copy(i, f).wait()
        w_tile = held[i].reshape(d, tile)
        o_ref[...] = w_tile
        for r in range(0, n, rows_at_once):
            part = pl.ds(r, rows_at_once)
            y = nn(x_ref[part], w_tile) + b_ref[...]
            t = y * math.sqrt(0.5)
            below = 0.5 + 0.5 * lax.erf(t)
            a_ref[part] = (y * below).astype(BF16)
            density = jnp.exp(-t * t) * (1.0 / math.sqrt(2.0 * math.pi))
            g_ref[part] = (below + y * density).astype(BF16)

    column = pl.BlockSpec((n, tile), lambda i: (0, i))
    return pl.pallas_call(
        kernel,
        grid=(tiles,),
        in_specs=[
            pl.BlockSpec((n, d), lambda i: (0, 0)),
            ANY,
            pl.BlockSpec((1, tile), lambda i: (0, i)),
        ],
        out_specs=[column, column, pl.BlockSpec((d, tile), lambda i: (0, i))],
        out_shape=[
            jax.ShapeDtypeStruct((n, cols), BF16),
            jax.ShapeDtypeStruct((n, cols), BF16),
            jax.ShapeDtypeStruct((d, cols), BF16),
        ],
        scratch_shapes=[pltpu.VMEM((tiles, fn, cn, rows, tile), BF16), dma(tiles, fn)],
        compiler_params=pltpu.CompilerParams(vmem_limit_bytes=48 * 2**20),
        cost_estimate=pl.CostEstimate(
            flops=2 * n * d * cols, bytes_accessed=60_000_000, transcendentals=0
        ),
    )(x, w, bias)


def halved_product(x, g, bit, groups, lines, tile=512, split=True):
    n, d = g.shape
    block = x.shape[1] // groups
    r = block // lines // 2
    tile = min(tile, d)

    def kernel(bit_ref, x_ref, g_ref, *refs):
        turned = refs[-1]

        @pl.when(pl.program_id(1) == 0)
        def _():
            turned[...] = x_ref[...].T

        y = nn(turned[...], g_ref[...]).astype(BF16)
        if not split:
            refs[0][:, 0] = y.reshape(lines, 2 * r, tile)
            return
        a_ref, k_ref = refs[:2]
        y = y.reshape(lines, 2, r, tile)
        first = bit_ref[0] == 0
        a_ref[:, 0] = jnp.where(first, y[:, 1], y[:, 0])
        k_ref[:, 0] = jnp.where(first, y[:, 0], y[:, 1])

    size = r if split else 2 * r
    half = pl.BlockSpec((lines, 1, size, tile), lambda i, j, b: (0, i, 0, j))
    shape = jax.ShapeDtypeStruct((lines, groups, size, d), BF16)
    outs = 2 if split else 1
    return pl.pallas_call(
        kernel,
        grid_spec=pltpu.PrefetchScalarGridSpec(
            num_scalar_prefetch=1,
            grid=(groups, d // tile),
            in_specs=[
                pl.BlockSpec((n, block), lambda i, j, b: (0, i)),
                pl.BlockSpec((n, tile), lambda i, j, b: (0, j)),
            ],
            out_specs=[half] * outs,
            scratch_shapes=[pltpu.VMEM((block, n), BF16)],
        ),
        out_shape=[shape] * outs,
        compiler_params=pltpu.CompilerParams(vmem_limit_bytes=48 * 2**20),
        cost_estimate=pl.CostEstimate(
            flops=2 * n * d * x.shape[1],
            bytes_accessed=2 * (n * d + n * x.shape[1] + d * x.shape[1]),
            transcendentals=0,
        ),
    )(bit, x, g)


def front(hist, mix, gain, shift, tokens=16, wide=128):
    h, n, d = hist.shape
    rest = gain.shape[0]

    def kernel(h_ref, m_ref, g_ref, b_ref, s_ref, *n_refs):
        m = m_ref[...]
        across = [jnp.broadcast_to(m[:, i : i + 1], (tokens, wide)) for i in range(4 * h)]
        for at in range(0, d, wide):
            cut = slice(at, at + wide)
            rows = [h_ref[j, :, cut].astype(F32) for j in range(h)]
            for s in range(4):
                acc = across[s * h] * rows[0]
                for j in range(1, h):
                    acc += across[s * h + j] * rows[j]
                s_ref[s, :, cut] = acc
        for s in range(rest):
            x = s_ref[s]
            centre = x - jnp.mean(x, axis=-1, keepdims=True)
            spread = jnp.mean(centre * centre, axis=-1, keepdims=True)
            y = centre * lax.rsqrt(spread + EPS_NORM) * g_ref[s : s + 1] + b_ref[s : s + 1]
            n_refs[s][...] = y.astype(BF16)

    return pl.pallas_call(
        kernel,
        grid=(n // tokens,),
        in_specs=[
            pl.BlockSpec((h, tokens, d), lambda i: (0, i, 0)),
            pl.BlockSpec((tokens, 128), lambda i: (i, 0)),
            pl.BlockSpec((rest, d), lambda i: (0, 0)),
            pl.BlockSpec((rest, d), lambda i: (0, 0)),
        ],
        out_specs=[
            pl.BlockSpec((4, tokens, d), lambda i: (0, i, 0)),
        ]
        + [pl.BlockSpec((tokens, d), lambda i: (i, 0))] * rest,
        out_shape=[jax.ShapeDtypeStruct((4, n, d), F32)]
        + [jax.ShapeDtypeStruct((n, d), BF16)] * rest,
        compiler_params=pltpu.CompilerParams(vmem_limit_bytes=60 * 2**20),
        cost_estimate=pl.CostEstimate(
            flops=2 * 4 * h * n * d, bytes_accessed=n * d * (2 * h + 22), transcendentals=0
        ),
    )(hist, mix, gain, shift)


def last(hist, mix, streams, gain, grads, grad_hidden, tokens=16, wide=256):
    h, n, d = hist.shape
    rest = gain.shape[0]

    def kernel(h_ref, m_ref, s_ref, g_ref, d0, d1, d2, r_ref, gh_ref, gm_ref, gg_ref, gb_ref, ds):
        @pl.when(pl.program_id(0) == 0)
        def _():
            gg_ref[...] = jnp.zeros_like(gg_ref)
            gb_ref[...] = jnp.zeros_like(gb_ref)

        for s, d_ref in enumerate((d0, d1, d2)):
            x = s_ref[s]
            centre = x - jnp.mean(x, axis=-1, keepdims=True)
            inverse = lax.rsqrt(jnp.mean(centre * centre, axis=-1, keepdims=True) + EPS_NORM)
            unit = centre * inverse
            dn = d_ref[...]
            gg_ref[s : s + 1] += jnp.sum(dn * unit, axis=0, keepdims=True)
            gb_ref[s : s + 1] += jnp.sum(dn, axis=0, keepdims=True)
            du = dn * g_ref[s : s + 1]
            ds[s] = inverse * (
                du
                - jnp.mean(du, axis=-1, keepdims=True)
                - unit * jnp.mean(du * unit, axis=-1, keepdims=True)
            )
        ds[rest] = r_ref[...]
        m = m_ref[...]
        across = [jnp.broadcast_to(m[:, i : i + 1], (tokens, 128)) for i in range(4 * h)]
        sums = [[jnp.zeros((tokens, 128), F32) for _ in range(h)] for _ in range(4)]
        for at in range(0, d, wide):
            cuts = [slice(b, b + 128) for b in range(at, at + wide, 128)]
            parts = [[ds[s, :, cut] for cut in cuts] for s in range(4)]
            for j in range(h):
                for i, cut in enumerate(cuts):
                    acc = across[j] * parts[0][i]
                    for s in range(1, 4):
                        acc += across[s * h + j] * parts[s][i]
                    gh_ref[j, :, cut] = acc
                rows = [h_ref[j, :, cut].astype(F32) for cut in cuts]
                for s in range(4):
                    prod = rows[0] * parts[s][0]
                    for i in range(1, len(cuts)):
                        prod += rows[i] * parts[s][i]
                    sums[s][j] += prod
        lane = lax.broadcasted_iota(jnp.int32, (tokens, 128), 1)
        total = jnp.zeros((tokens, 128), F32)
        for s in range(4):
            for j in range(h):
                value = jnp.sum(sums[s][j], axis=-1, keepdims=True)
                total = jnp.where(lane == s * h + j, value, total)
        gm_ref[...] = total

    row = pl.BlockSpec((tokens, d), lambda i: (i, 0))
    lines = pl.BlockSpec((rest, d), lambda i: (0, 0))
    return pl.pallas_call(
        kernel,
        grid=(n // tokens,),
        in_specs=[
            pl.BlockSpec((h, tokens, d), lambda i: (0, i, 0)),
            pl.BlockSpec((tokens, 128), lambda i: (i, 0)),
            pl.BlockSpec((4, tokens, d), lambda i: (0, i, 0)),
            lines,
            row,
            row,
            row,
            row,
        ],
        out_specs=[
            pl.BlockSpec((h, tokens, d), lambda i: (0, i, 0)),
            pl.BlockSpec((tokens, 128), lambda i: (i, 0)),
            lines,
            lines,
        ],
        out_shape=[
            jax.ShapeDtypeStruct((h, n, d), F32),
            jax.ShapeDtypeStruct((n, 128), F32),
            jax.ShapeDtypeStruct((rest, d), F32),
            jax.ShapeDtypeStruct((rest, d), F32),
        ],
        scratch_shapes=[pltpu.VMEM((4, tokens, d), F32)],
        compiler_params=pltpu.CompilerParams(vmem_limit_bytes=60 * 2**20),
        cost_estimate=pl.CostEstimate(
            flops=4 * 4 * h * n * d, bytes_accessed=n * d * (6 * h + 32), transcendentals=0
        ),
    )(hist, mix, streams, gain, *grads, grad_hidden)


def body(
    history,
    dense_mix,
    doc_starts,
    norm_gain,
    norm_bias,
    qkv_weight,
    qkv_bias,
    out_weight,
    out_bias,
    up_weight,
    up_bias,
    down_weight,
    down_bias,
    root_gain,
    mix_in_weight,
    mix_out_weight,
    mix_out_bias,
    out_cotangent,
    mix_cotangent,
):
    fn, cn = lax.axis_size("fsdp"), lax.axis_size("ctx")
    dn = fn * cn
    fi, ci = lax.axis_index("fsdp"), lax.axis_index("ctx")
    hist, seqs, length, width = history.shape
    nloc = seqs * length
    ntp = fn * nloc
    rows = qkv_weight.shape[0]
    ff = up_weight.shape[1]
    wcol, pcol = width // fn, ff // (2 * fn)
    count = cn // 2
    lo = lax.rem(ci, 2)
    lines = [list(range(b, cn, 2)) for b in range(2)]
    heads = wcol // HEAD_DIM
    units = fn * seqs * heads // cn
    total = cn * length
    mixn = mix_in_weight.shape[1]

    def line_gather(w):
        return lax.all_gather(w, "ctx", axis=0, axis_index_groups=lines)

    parts = [
        norm_gain,
        norm_bias,
        qkv_bias,
        out_bias,
        up_bias,
        down_bias,
        root_gain,
        mix_in_weight,
        doc_starts.astype(F32),
    ]
    flat = jnp.concatenate([a.reshape(-1) for a in parts])
    flat = jnp.pad(flat, (0, -flat.size % 1024)).reshape(-1, 128)
    wout = lax.all_gather(out_weight, "ctx", axis=0, tiled=True)
    flats, qkv_cols = comm(
        1,
        gather_small(flat),
        exchange_fsdp(qkv_weight.reshape(rows, 3, fn, wcol).transpose(2, 1, 0, 3)),
    )
    flats = flats.reshape(dn, -1)
    pieces, at = [], 0
    for a in parts:
        pieces.append(flats[:, at : at + a.size])
        at += a.size

    def joined(piece, lead):
        return piece.reshape(dn, lead, -1).transpose(1, 0, 2).reshape(lead, -1)

    gain_all = joined(pieces[0], 4)
    shift_all = joined(pieces[1], 4)
    qkv_shift = joined(pieces[2], 3)
    out_shift = pieces[3].reshape(-1)
    up_shift = pieces[4].reshape(-1)
    down_shift = pieces[5].reshape(-1)
    root_full = pieces[6].reshape(-1)
    mix_in_full = pieces[7].reshape(width, mixn)
    starts = pieces[8].reshape(fn, cn, seqs, -1)[:, 0].astype(jnp.int32)

    hist2 = history.reshape(hist, nloc, width)
    mix2 = dense_mix.reshape(dense_mix.shape[0], hist, nloc)
    mixes = jnp.pad(mix2.reshape(-1, nloc).T, ((0, 0), (0, 128 - mix2.shape[0] * hist)))
    streams, *normed = front(hist2, mixes, gain_all[:3], shift_all[:3])

    bias_cols = lax.dynamic_slice_in_dim(qkv_shift, fi * wcol, wcol, 1)
    tables = rotary_tables(total)
    tables_l = lax.dynamic_slice_in_dim(tables, ci * length, length, 1)

    def projected(x, w, at, s):
        y = project(
            x.reshape(fn * seqs, length, width),
            w,
            at,
            bias_cols[s : s + 1],
            tables_l if s < 2 else None,
        )
        return y.reshape(cn, units, length, HEAD_DIM)

    def whole_units(x):
        return x.reshape(units, total, HEAD_DIM)

    def from_units(x):
        return exchange_ctx(x.reshape(units, cn, length, HEAD_DIM), False)

    def columns(x):
        x = x.reshape(fn * seqs, heads, length, HEAD_DIM)
        return x.transpose(0, 2, 1, 3).reshape(ntp, wcol)

    w01, g0 = comm(9, gather_ctx(qkv_cols[:, :2]), gather_fsdp(normed[0]))
    g0, cols_2, wout = lax.optimization_barrier((g0, qkv_cols[:, 2], wout))
    w2 = lax.all_gather(cols_2, "ctx", axis=0)
    p0 = projected(g0, w01, 0, 0)
    q_u, g1 = comm(4, exchange_ctx(p0, True), gather_fsdp(normed[1]))
    p1 = projected(g1, w01, 1, 1)
    p1, down_rows = lax.optimization_barrier((p1, down_weight))
    wdown = line_gather(down_rows).reshape(pcol, width)
    k_u, g2 = comm(4, exchange_ctx(p1, True), gather_fsdp(normed[2]))
    p2 = projected(g2, w2[:, :, None], 0, 2)
    v_u, up_cols = comm(
        11,
        exchange_ctx(p2, True),
        exchange_plane(
            up_weight.reshape(rows, fn, count, 2, -1).transpose(1, 3, 0, 2, 4).reshape(fn, 2, rows, pcol),
            plane_sides,
        ),
    )
    up_g = line_gather(up_cols).reshape(count, fn, 2 * rows, pcol)
    wqkv = [w.transpose(1, 0, 2, 3).reshape(width, wcol) for w in (w01[:, :, 0], w01[:, :, 1], w2)]
    q_u, k_u, v_u = whole_units(q_u), whole_units(k_u), whole_units(v_u)
    normed_g = [g.reshape(ntp, width) for g in (g0, g1, g2)]

    pos_all = jnp.arange(total, dtype=jnp.int32)
    unit_ids = ci * units + jnp.arange(units, dtype=jnp.int32)
    seq_ids = unit_ids // heads
    unit_starts = starts.reshape(fn * seqs, -1)[seq_ids]
    first_key = jnp.max(
        jnp.where(unit_starts[:, None, :] <= pos_all[None, :, None], unit_starts[:, None, :], 0),
        axis=-1,
    )[:, None, :]
    att_u, lse_u = attend(q_u, k_u, v_u, first_key)
    attended = columns(comm(6, from_units(att_u))[0])
    attended, wdown = lax.optimization_barrier((attended, wdown))

    def scatter_tokens(x):
        return comm(10, scatter_fsdp(x.astype(BF16).reshape(fn, nloc, width)))[0]

    def gather_tokens(x):
        return comm(3, gather_fsdp(x))[0].reshape(ntp, width)

    def scatter_plane_tokens(x):
        return comm(13, scatter_plane(x.astype(BF16).reshape(fn, 2, nloc, width)))[0]

    def gather_plane_tokens(x):
        return comm(14, gather_plane(x))[0].reshape(2 * ntp, width)

    hidden_res = streams[3] + scatter_tokens(dot("nd,de->ne", attended, wout)) + out_shift
    normed_mlp, mid_pull = jax.vjp(layer_norm, hidden_res, gain_all[3], shift_all[3])
    mlp_g = gather_plane_tokens(normed_mlp.astype(BF16))
    up_bias_cols = lax.dynamic_slice(
        up_shift.reshape(fn, count, 2, -1), (fi, 0, lo, 0), (1, count, 1, ff // dn)
    ).reshape(pcol)
    act_low, slope, wup = widen(mlp_g, up_g, up_bias_cols[None])
    result = hidden_res + scatter_plane_tokens(dot("nf,fd->nd", act_low, wdown)) + down_shift
    block_out = result.astype(BF16).reshape(seqs, length, width)

    next_rows, mixer_pull = jax.vjp(
        mixer, result, root_full, mix_in_full, mix_out_weight, mix_out_bias
    )
    next_mix = next_rows.T.reshape(-1, seqs, length)
    grad_result, grad_root, grad_mix_in, grad_mix_out, grad_mix_bias = mixer_pull(
        mix_cotangent.reshape(-1, nloc).T
    )
    grad_result = grad_result + out_cotangent.reshape(nloc, width).astype(F32)

    grad_branch = grad_result.astype(BF16)
    branch_g = gather_plane_tokens(grad_branch)
    grad_down_shift = jnp.sum(grad_branch.astype(F32), axis=0)

    bit = lo.reshape(1)

    def line_scatter(x):
        y = lax.psum_scatter(
            x.reshape(-1, x.shape[-1]),
            "ctx",
            scatter_dimension=0,
            axis_index_groups=lines,
            tiled=True,
        )
        return y.reshape(x.shape[1:])

    down_part = dot("nf,nd->fd", act_low, branch_g).astype(BF16)
    down_part, wdown = lax.optimization_barrier((down_part, wdown))
    grad_down = line_scatter(down_part.reshape(count, -1, width))
    grad_active = dot("nd,fd->nf", branch_g, wdown)
    grad_upward = (grad_active * slope.astype(F32)).astype(BF16)
    grad_up_shift = jnp.sum(grad_upward.astype(F32), axis=0)
    (up_part,) = halved_product(mlp_g, grad_upward, bit, fn, count, split=False)
    up_part, grad_upward = lax.optimization_barrier((up_part, grad_upward))
    grad_up = line_scatter(up_part.reshape(count, -1, pcol))
    mlp_part = dot("nf,df->nd", grad_upward, wup).astype(BF16)
    grad_mlp = scatter_plane_tokens(mlp_part)
    grad_hidden, grad_gain_mid, grad_shift_mid = mid_pull(grad_mlp)
    grad_hidden = grad_hidden + grad_result
    grad_attn = grad_hidden.astype(BF16)
    grad_out_shift = jnp.sum(grad_attn.astype(F32), axis=0)
    attn_g = gather_tokens(grad_attn)
    out_part = dot("nd,ne->de", attended, attn_g).astype(BF16)
    grad_att = dot("ne,de->nd", attn_g, wout).astype(BF16)
    grad_att = grad_att.reshape(fn * seqs, length, heads, HEAD_DIM).transpose(0, 2, 1, 3)
    out_part, grad_att = lax.optimization_barrier((out_part, grad_att))
    (g_u,) = comm(5, exchange_ctx(grad_att.reshape(cn, units, length, HEAD_DIM), True))
    g_u, grad_down, out_part = lax.optimization_barrier((g_u, grad_down, out_part))

    def ctx_scatter(x):
        return lax.psum_scatter(x, "ctx", scatter_dimension=0, tiled=True)

    grad_out = ctx_scatter(out_part)
    gq, gk, gv = attend_back(q_u, k_u, v_u, first_key, lse_u, att_u, whole_units(g_u), tables)

    def back_part(p, s):
        return dot("nc,dc->nd", p, wqkv[s]).astype(BF16).reshape(fn, nloc, width)

    def qkv_part(p, i):
        return halved_product(normed_g[i], p, bit, fn, cn, split=False)[0]

    grad_up = grad_up.reshape(fn, 2, rows, pcol)
    if ff // dn % 128 == 0:
        gp0, grad_up = comm(12, from_units(gq), exchange_columns(grad_up, ff // dn, plane_sides))
    else:
        gp0, grad_up = comm(12, from_units(gq), exchange_plane(grad_up, plane_sides))
        grad_up = grad_up.reshape(fn, 2, rows, count, -1).transpose(2, 0, 3, 1, 4)
        grad_up = grad_up.reshape(rows, ff)
    gp0 = columns(gp0)
    q_part, gk = lax.optimization_barrier((qkv_part(gp0, 0), gk))
    grad_q = ctx_scatter(q_part.reshape(-1, wcol)).reshape(fn, rows, wcol)
    gp1, gn0 = comm(8, from_units(gk), scatter_fsdp(back_part(gp0, 0)))
    gp1, grad_out = lax.optimization_barrier((gp1, grad_out))
    gp1 = columns(gp1)
    gp2, gn1 = comm(8, from_units(gv), scatter_fsdp(back_part(gp1, 1)))
    gp2 = columns(gp2)
    kv_part = jnp.stack([qkv_part(gp1, 1), qkv_part(gp2, 2)], axis=1)
    kv_part, gp2 = lax.optimization_barrier((kv_part, gp2))
    grad_kv = ctx_scatter(kv_part.reshape(-1, wcol)).reshape(2, fn, rows, wcol)
    grad_q, gn2 = comm(
        7,
        exchange_fsdp(grad_q),
        scatter_fsdp(back_part(gp2, 2)),
    )
    grad_proj = (gp0, gp1, gp2)
    grad_qkv_shift = jnp.stack([jnp.sum(g.astype(F32), axis=0) for g in grad_proj])

    grad_history, grad_mix, grad_gain_front, grad_shift_front = last(
        hist2, mixes, streams, gain_all[:3], (gn0, gn1, gn2), grad_hidden
    )
    grad_history = grad_history.reshape(history.shape)
    grad_mix = grad_mix[:, : mix2.shape[0] * hist].T.reshape(dense_mix.shape)

    def own_columns(x, full):
        zero = jnp.zeros((x.shape[0], full), F32)
        return lax.dynamic_update_slice_in_dim(zero, x, fi * x.shape[1], 1)

    lines_14 = [
        grad_gain_front,
        grad_gain_mid[None],
        grad_shift_front,
        grad_shift_mid[None],
        own_columns(grad_qkv_shift, width),
        grad_out_shift[None],
        grad_down_shift[None],
        grad_root[None],
    ]
    lines_14 = jnp.concatenate(lines_14, axis=0)
    up_lines = lax.dynamic_update_slice(
        jnp.zeros((fn, count, 2, ff // dn), F32),
        grad_up_shift.reshape(1, count, 1, -1),
        (fi, 0, lo, 0),
    ).reshape(dn, -1)
    same = jnp.concatenate([grad_mix_out.reshape(-1), grad_mix_bias])
    flat = jnp.concatenate(
        [
            lines_14.reshape(-1, dn, width // dn).transpose(1, 0, 2).reshape(dn, -1),
            up_lines,
            grad_mix_in.reshape(dn, -1),
            jnp.broadcast_to(same[None], (dn, same.size)),
        ],
        axis=1,
    )
    flat = jnp.pad(flat, ((0, 0), (0, -flat.shape[1] % 1024)))
    small, grad_k, grad_v = comm(
        2,
        scatter_small(flat.reshape(fn, cn, -1, 128)),
        exchange_fsdp(grad_kv[0]),
        exchange_fsdp(grad_kv[1]),
    )
    grad_qkv = jnp.stack([grad_q, grad_k, grad_v])
    grad_qkv = grad_qkv.transpose(2, 0, 1, 3).reshape(rows, 3, width).astype(F32)
    small = small.reshape(-1)
    out_small, at = [], 0
    order = [norm_gain, norm_bias, qkv_bias, out_bias, down_bias, root_gain, up_bias, mix_in_weight]
    for a in order:
        out_small.append(small[at : at + a.size].reshape(a.shape))
        at += a.size
    (g_gain, g_shift, g_qkv_b, g_out_b, g_down_b, g_root, g_up_b, g_mix_in) = out_small
    mix_sums = small[at : at + same.size]
    cut = grad_mix_out.size
    return (
        block_out,
        next_mix,
        grad_history,
        grad_mix,
        g_gain,
        g_shift,
        grad_qkv,
        g_qkv_b,
        grad_out.astype(F32),
        g_out_b,
        grad_up.astype(F32),
        g_up_b,
        grad_down.astype(F32),
        g_down_b,
        g_root,
        g_mix_in,
        mix_sums[:cut].reshape(grad_mix_out.shape),
        mix_sums[cut:],
    )


def solution(mesh):
    token = P(None, "fsdp", "ctx")
    both = P(BOTH)
    cols = P(None, BOTH)
    placed = (
        token,
        P(None, None, "fsdp", "ctx"),
        P("fsdp"),
        cols,
        cols,
        both,
        cols,
        both,
        both,
        both,
        both,
        both,
        both,
        both,
        both,
        P(),
        P(),
        P("fsdp", "ctx"),
        token,
    )
    outs = (
        P("fsdp", "ctx"),
        token,
        token,
        P(None, None, "fsdp", "ctx"),
        cols,
        cols,
        both,
        cols,
        both,
        both,
        both,
        both,
        both,
        both,
        both,
        both,
        P(),
        P(),
    )
    return jax.shard_map(body, mesh=mesh, in_specs=placed, out_specs=outs, check_vma=False)
```

```python
import math

import jax
import jax.numpy as jnp
import numpy as np
from jax import lax
from jax.experimental import pallas as pl
from jax.experimental.pallas import tpu as pltpu
from jax.sharding import PartitionSpec as P

HEAD_DIM = 128
ROT = 32
TOP_PRECISION = lax.Precision.HIGHEST
EPS_NORM = 1e-05
EPS_ROOT = 1e-06
NEG_BIG = -1e30
BOTH = ("fsdp", "ctx")
BF16 = jnp.bfloat16
F32 = jnp.float32
MESH = pl.DeviceIdType.MESH
ANY = pl.BlockSpec(memory_space=pl.ANY)
VMEM = pl.BlockSpec(memory_space=pltpu.VMEM)
LOG2E = 1.4426950408889634


def layer_norm(values, gain_row, shift_row):
    centre = values - jnp.mean(values, axis=-1, keepdims=True)
    spread = jnp.mean(centre * centre, axis=-1, keepdims=True)
    return centre * lax.rsqrt(spread + EPS_NORM) * gain_row + shift_row


def gelu(values):
    return jax.nn.gelu(values, approximate=False)


def rotary_tables(count):
    half = ROT // 2
    frequency = np.exp(np.arange(half, dtype=np.float32) * np.float32(-2.0 * math.log(10000.0) / ROT))
    angles = np.arange(count, dtype=np.float32)[:, None] * frequency.astype(np.float32)[None, :]
    cosine = jnp.asarray(np.cos(angles.astype(np.float64)), F32)
    sine = jnp.asarray(np.sin(angles.astype(np.float64)), F32)
    zero, rest = jnp.zeros_like(sine), HEAD_DIM - ROT
    return jnp.stack(
        [
            jnp.pad(jnp.concatenate([cosine, cosine], 1), ((0, 0), (0, rest)), constant_values=1.0),
            jnp.pad(jnp.concatenate([zero, sine], 1), ((0, 0), (0, rest))),
            jnp.pad(jnp.concatenate([-sine, zero], 1), ((0, 0), (0, rest))),
        ]
    )


def turn(x, straight, right, left):
    half = ROT // 2
    return (
        x * straight
        + pltpu.roll(x, half, axis=1) * right
        + pltpu.roll(x, HEAD_DIM - half, axis=1) * left
    )


def mixer(rows, gain_row, opening, closing, closing_bias):
    inverse_rms = lax.rsqrt(jnp.mean(rows * rows, axis=-1, keepdims=True) + EPS_ROOT)
    rooted = rows * inverse_rms * gain_row
    hidden = jnp.dot(rooted, opening, precision=TOP_PRECISION)
    return jnp.dot(gelu(hidden), closing, precision=TOP_PRECISION) + closing_bias


def dot(pattern, left, right):
    return jnp.einsum(pattern, left, right, preferred_element_type=F32)


def remote(src, dst, send_sem, recv_sem, target):
    return pltpu.make_async_remote_copy(
        src_ref=src,
        dst_ref=dst,
        send_sem=send_sem,
        recv_sem=recv_sem,
        device_id=target,
        device_id_type=MESH,
    )


def place():
    return lax.axis_index("fsdp"), lax.axis_index("ctx")


def links_and_twin():
    chips = lax.axis_size("fsdp") // 2
    f, c = place()
    chip, core = f // 2, lax.rem(f, 2)
    return [(lax.rem(chip + j, chips) * 2 + core, c) for j in range(1, chips)] + [
        (chip * 2 + 1 - core, c)
    ]


def along_ctx():
    cn = lax.axis_size("ctx")
    f, c = place()
    return [(f, lax.rem(c + j, cn)) for j in range(1, cn)]


def along_fsdp():
    fn = lax.axis_size("fsdp")
    f, c = place()
    return [(lax.rem(f + j, fn), c) for j in range(1, fn)]


def along_both():
    return along_ctx() + along_fsdp()


def comm(cid, *tasks):
    n = len(tasks)
    counts = [len(t[5]) for t in tasks]
    limit = 6 * 2**20
    for t in tasks:
        for x in t[5]:
            if x.dtype in (BF16, F32):
                limit += math.prod(x.shape) * jnp.dtype(x.dtype).itemsize

    def kernel(*refs):
        targets, seen = [], []
        covered = [
            (along_fsdp, [along_both]),
            (the_pair, [along_ctx]),
            (the_pair, [plane_others]),
            (links_and_twin, [plane_others]),
            (links_and_twin, [along_fsdp]),
        ]
        for t in tasks:
            if t[0] not in seen and (t[0], seen[:1]) not in covered:
                seen.append(t[0])
                targets += t[0]()
        barrier = pltpu.get_barrier_semaphore()
        for t in targets:
            pl.semaphore_signal(barrier, inc=1, device_id=t, device_id_type=MESH)
        pl.semaphore_wait(barrier, len(targets))
        scratch = list(refs[2 * n :])
        phases = []
        for i, t in enumerate(tasks):
            mine, scratch = scratch[: counts[i]], scratch[counts[i] :]
            phases.append(t[6](refs[i], refs[n + i], *mine))
        for p in range(3):
            for ph in phases:
                ph[p]()

    out = pl.pallas_call(
        kernel,
        out_shape=[t[2] for t in tasks],
        in_specs=[t[3] for t in tasks],
        out_specs=[t[4] for t in tasks],
        scratch_shapes=[x for t in tasks for x in t[5]],
        compiler_params=pltpu.CompilerParams(
            collective_id=cid, has_side_effects=True, vmem_limit_bytes=limit
        ),
        cost_estimate=pl.CostEstimate(flops=0, bytes_accessed=15_000_000, transcendentals=0),
    )(*[t[1] for t in tasks])
    return out


def dma(*shape):
    return pltpu.SemaphoreType.DMA(shape)


def gather_small(x):
    fn, cn = lax.axis_size("fsdp"), lax.axis_size("ctx")

    def body(x_ref, o_ref, s1, r1, s2, r2):
        f, c = place()

        def first(j):
            return remote(
                x_ref, o_ref.at[f, c], s1.at[j], r1.at[j], (f, lax.rem(c + j, cn))
            )

        def second(j):
            return remote(
                o_ref.at[f], o_ref.at[f], s2.at[j], r2.at[j], (lax.rem(f + j, fn), c)
            )

        def start():
            for j in range(1, cn):
                first(j).start()
            o_ref[f, c] = x_ref[...]

        def middle():
            for j in range(1, cn):
                there = o_ref.at[f, lax.rem(c + cn - j, cn)]
                remote(there, there, s1.at[j], r1.at[j], (f, lax.rem(c + j, cn))).wait_recv()
            for j in range(1, fn):
                second(j).start()

        def end():
            for j in range(1, fn):
                there = o_ref.at[lax.rem(f + fn - j, fn)]
                remote(there, there, s2.at[j], r2.at[j], (lax.rem(f + j, fn), c)).wait_recv()
            for j in range(1, cn):
                first(j).wait_send()
            for j in range(1, fn):
                second(j).wait_send()

        return start, middle, end

    shape = jax.ShapeDtypeStruct((fn, cn, *x.shape), x.dtype)
    return (along_both, x, shape, VMEM, VMEM, [dma(cn), dma(cn), dma(fn), dma(fn)], body)


def exchange_fsdp(x):
    fn = lax.axis_size("fsdp")

    def body(x_ref, o_ref, s, r, own):
        f, c = place()

        def copy(j, slot):
            t = lax.rem(f + j, fn)
            return remote(x_ref.at[t], o_ref.at[slot], s.at[j], r.at[j], (t, c))

        mine = pltpu.make_async_copy(x_ref.at[f], o_ref.at[f], own)

        def start():
            for j in range(1, fn):
                copy(j, f).start()
            mine.start()

        def end():
            mine.wait()
            for j in range(1, fn):
                copy(j, lax.rem(f + fn - j, fn)).wait_recv()
            for j in range(1, fn):
                copy(j, f).wait_send()

        return start, lambda: None, end

    shape = jax.ShapeDtypeStruct(x.shape, x.dtype)
    return (along_fsdp, x, shape, ANY, ANY, [dma(fn), dma(fn), dma()], body)


def exchange_ctx(x, to_units):
    cn = lax.axis_size("ctx")
    lead = x.shape[1] if to_units else x.shape[0]

    def body(x_ref, o_ref, s, r, own):
        f, c = place()

        def source(t):
            return x_ref.at[t] if to_units else x_ref.at[:, t]

        def target(slot):
            return o_ref.at[:, slot] if to_units else o_ref.at[slot]

        def copy(j, slot):
            t = lax.rem(c + j, cn)
            return remote(source(t), target(slot), s.at[j], r.at[j], (f, t))

        mine = pltpu.make_async_copy(source(c), target(c), own)

        def start():
            for j in range(1, cn):
                copy(j, c).start()
            mine.start()

        def end():
            mine.wait()
            for j in range(1, cn):
                copy(j, lax.rem(c + cn - j, cn)).wait_recv()
            for j in range(1, cn):
                copy(j, c).wait_send()

        return start, lambda: None, end

    dims = (lead, cn) if to_units else (cn, lead)
    shape = jax.ShapeDtypeStruct((*dims, *x.shape[2:]), x.dtype)
    return (along_ctx, x, shape, ANY, ANY, [dma(cn), dma(cn), dma()], body)


def the_pair():
    f, c = place()
    return [(f, c // 2 * 2 + 1 - lax.rem(c, 2))]


def exchange_pair(x):
    def body(x_ref, o_ref, s, r):
        (pair,) = the_pair()
        copy = remote(x_ref, o_ref, s, r, pair)
        return copy.start, lambda: None, copy.wait

    shape = jax.ShapeDtypeStruct(x.shape, x.dtype)
    return (the_pair, x, shape, ANY, ANY, [dma(), dma()], body)


def gather_fsdp(x, parts=4):
    fn = lax.axis_size("fsdp")
    chips = fn // 2
    n, d = x.shape
    step = n // parts
    pieces = [pl.ds(p * step, step) for p in range(parts)]

    def body(x_ref, o_ref, own_sem, s_link, r_link, s_core, r_core):
        f, c = place()
        chip, core = f // 2, lax.rem(f, 2)
        twin = (chip * 2 + 1 - core, c)
        links, cores = {}, {}

        def to(j):
            return (lax.rem(chip + j, chips) * 2 + core, c)

        def slot(j, core_id):
            return lax.rem(chip + chips - j, chips) * 2 + core_id

        own = pltpu.make_async_copy(x_ref, o_ref.at[f], own_sem)

        def start():
            for i, rows in enumerate(pieces):
                here, there = x_ref.at[rows], o_ref.at[f, rows]
                for j in range(1, chips):
                    links[i, j] = remote(here, there, s_link.at[j, i], r_link.at[j, i], to(j))
                    links[i, j].start()
            for i, rows in enumerate(pieces):
                here, there = x_ref.at[rows], o_ref.at[f, rows]
                cores[i, 0] = remote(here, there, s_core.at[0, i], r_core.at[0, i], twin)
                cores[i, 0].start()
            own.start()

        def middle():
            for i, rows in enumerate(pieces):
                for j in range(1, chips):
                    here = o_ref.at[slot(j, core), rows]
                    remote(here, here, s_link.at[j, i], r_link.at[j, i], to(j)).wait_recv()
                    cores[i, j] = remote(here, here, s_core.at[j, i], r_core.at[j, i], twin)
                    cores[i, j].start()

        def end():
            own.wait()
            for i, rows in enumerate(pieces):
                for j in range(chips):
                    there = o_ref.at[slot(j, 1 - core), rows]
                    cores[i, j].wait_send()
                    remote(there, there, s_core.at[j, i], r_core.at[j, i], twin).wait_recv()
                for j in range(1, chips):
                    links[i, j].wait_send()

        return start, middle, end

    shape = jax.ShapeDtypeStruct((fn, n, d), x.dtype)
    return (links_and_twin, x, shape, ANY, ANY, [dma()] + [dma(chips, parts)] * 4, body)


def gather_ctx(x):
    cn = lax.axis_size("ctx")
    count = cn // 2

    def body(x_ref, o_ref, own_sem, s_up, r_up, s_down, r_down, s_pair, r_pair):
        f, c = place()
        hi, lo = c // 2, lax.rem(c, 2)
        pair = (f, hi * 2 + 1 - lo)
        above = (f, lax.rem(hi + 1, count) * 2 + lo)
        below = (f, lax.rem(hi + count - 1, count) * 2 + lo)
        own = pltpu.make_async_copy(x_ref, o_ref.at[c], own_sem)

        def low(d):
            return lax.rem(hi + count - d, count)

        def high(d):
            return lax.rem(hi + d, count)

        def up(d):
            source = x_ref if d == 0 else o_ref.at[low(d) * 2 + lo]
            return remote(source, o_ref.at[low(d) * 2 + lo], s_up.at[d], r_up.at[d + 1], above)

        def down(d):
            source = x_ref if d == 0 else o_ref.at[high(d) * 2 + lo]
            return remote(
                source, o_ref.at[high(d) * 2 + lo], s_down.at[d], r_down.at[d + 1], below
            )

        def across(k, slot):
            source = x_ref if k == 0 else o_ref.at[slot * 2 + lo]
            return remote(source, o_ref.at[slot * 2 + lo], s_pair.at[k], r_pair.at[k], pair)

        def start():
            pl.when(hi < count - 1)(lambda: up(0).start())
            pl.when(hi > 0)(lambda: down(0).start())
            across(0, hi).start()
            own.start()

        def middle():
            for d in range(1, count):

                @pl.when(hi >= d)
                def _():
                    here = o_ref.at[low(d) * 2 + lo]
                    remote(here, here, s_up.at[d], r_up.at[d], above).wait_recv()
                    across(d, low(d)).start()
                    if d < count - 1:
                        pl.when(hi < count - 1)(lambda: up(d).start())

                @pl.when(hi + d < count)
                def _():
                    here = o_ref.at[high(d) * 2 + lo]
                    remote(here, here, s_down.at[d], r_down.at[d], below).wait_recv()
                    across(count - d, high(d)).start()
                    if d < count - 1:
                        pl.when(hi > 0)(lambda: down(d).start())

        def end():
            own.wait()
            across(0, hi).wait_send()
            for k in range(count):
                there = o_ref.at[low(k) * 2 + 1 - lo]
                remote(there, there, s_pair.at[k], r_pair.at[k], pair).wait_recv()
                if k > 0:
                    across(k, low(k)).wait_send()
            for d in range(count - 1):
                pl.when((hi >= d) & (hi < count - 1))(lambda d=d: up(d).wait_send())
                pl.when((hi + d < count) & (hi > 0))(lambda d=d: down(d).wait_send())

        return start, middle, end

    shape = jax.ShapeDtypeStruct((cn, *x.shape), x.dtype)
    scratch = [dma()] + [dma(count + 1)] * 4 + [dma(count)] * 2
    return (along_ctx, x, shape, ANY, ANY, scratch, body)


def scatter_fsdp(x, parts=4):
    fn = lax.axis_size("fsdp")
    chips = fn // 2
    _, n, d = x.shape
    step = n // parts

    def body(x_ref, o_ref, own, near, mine, far, ss, s_own, s_near, r_near, s_far, r_far):
        f, c = place()
        chip, core = f // 2, lax.rem(f, 2)
        twin = (chip * 2 + 1 - core, c)
        nears, owns, fars, outs = {}, {}, {}, {}

        def chip_at(j):
            return lax.rem(chip + j, chips)

        def start():
            for p in range(parts):
                rows = pl.ds(p * step, step)
                for j in list(range(1, chips)) + [0]:
                    at = chip_at(j) * 2
                    owns[p, j] = pltpu.make_async_copy(
                        x_ref.at[at + core, rows], own.at[j, p], s_own.at[j, p]
                    )
                    owns[p, j].start()
                    nears[p, j] = remote(
                        x_ref.at[at + 1 - core, rows],
                        near.at[j, p],
                        s_near.at[j, p],
                        r_near.at[j, p],
                        twin,
                    )
                    nears[p, j].start()

        def middle():
            for p in range(parts):
                for j in range(1, chips):
                    owns[p, j].wait()
                    nears[p, j].wait_recv()
                    mine[j, p] = (own[j, p].astype(F32) + near[j, p].astype(F32)).astype(BF16)
                    fars[p, j] = remote(
                        mine.at[j, p],
                        far.at[j, p],
                        s_far.at[j, p],
                        r_far.at[j, p],
                        (chip_at(j) * 2 + core, c),
                    )
                    fars[p, j].start()
            for p in range(parts):
                owns[p, 0].wait()
                nears[p, 0].wait_recv()
                ss[p] = own[0, p].astype(F32) + near[0, p].astype(F32)

        def end():
            for p in range(parts):
                for j in range(1, chips):
                    fars[p, j].wait_recv()
                    ss[p] += far[j, p].astype(F32)
                outs[p] = pltpu.make_async_copy(
                    ss.at[p], o_ref.at[pl.ds(p * step, step)], s_far.at[0, p]
                )
                outs[p].start()
            for p in range(parts):
                outs[p].wait()
                for j in range(chips):
                    nears[p, j].wait_send()
                for j in range(1, chips):
                    fars[p, j].wait_send()

        return start, middle, end

    block = pltpu.VMEM((chips, parts, step, d), BF16)
    scratch = [block] * 4 + [pltpu.VMEM((parts, step, d), F32)] + [dma(chips, parts)] * 5
    return (links_and_twin, x, jax.ShapeDtypeStruct((n, d), F32), ANY, ANY, scratch, body)


def plane_others():
    fn = lax.axis_size("fsdp")
    f, c = place()
    (pair,) = the_pair()
    return [(lax.rem(f + a, fn), (c, pair[1])[b]) for a in range(fn) for b in range(2) if a or b]


def plane_sides():
    return [t for i, t in enumerate(plane_others()) if i > 0]


def exchange_plane(x, peers):
    fn = lax.axis_size("fsdp")

    def body(x_ref, o_ref, s, r, own):
        f, c = place()
        lo = lax.rem(c, 2)
        (pair,) = the_pair()

        def index(a, b):
            return lax.rem(f + a + fn, fn), (lo if b == 0 else 1 - lo)

        def copy(a, b, slot):
            fa, lb = index(a, b)
            return remote(
                x_ref.at[fa, lb],
                o_ref.at[slot[0], slot[1]],
                s.at[a, b],
                r.at[a, b],
                (fa, c if b == 0 else pair[1]),
            )

        steps = [(a, b) for a in range(fn) for b in range(2) if a or b]
        mine = pltpu.make_async_copy(x_ref.at[f, lo], o_ref.at[f, lo], own)

        def start():
            for a, b in steps:
                copy(a, b, (f, lo)).start()
            mine.start()

        def end():
            mine.wait()
            for a, b in steps:
                copy(a, b, index(-a, b)).wait_recv()
            for a, b in steps:
                copy(a, b, (f, lo)).wait_send()

        return start, lambda: None, end

    shape = jax.ShapeDtypeStruct(x.shape, x.dtype)
    return (peers, x, shape, ANY, ANY, [dma(fn, 2), dma(fn, 2), dma()], body)


def exchange_columns(x, wide, peers):
    fn = lax.axis_size("fsdp")
    _, _, rows, cols = x.shape
    count = cols // wide

    def body(x_ref, o_ref, s, r, own):
        f, c = place()
        lo = lax.rem(c, 2)
        (pair,) = the_pair()

        def index(a, b):
            return lax.rem(f + a + fn, fn), (lo if b == 0 else 1 - lo)

        def target(slot, h):
            at = ((slot[0] * count + h) * 2 + slot[1]) * wide
            return o_ref.at[:, pl.ds(pl.multiple_of(at, wide), wide)]

        def copy(a, b, h, slot):
            fa, lb = index(a, b)
            return remote(
                x_ref.at[fa, lb, :, pl.ds(h * wide, wide)],
                target(slot, h),
                s.at[a, b, h],
                r.at[a, b, h],
                (fa, c if b == 0 else pair[1]),
            )

        steps = [
            (a, b, h) for a in range(fn) for b in range(2) for h in range(count) if a or b
        ]
        mine = [
            pltpu.make_async_copy(
                x_ref.at[f, lo, :, pl.ds(h * wide, wide)], target((f, lo), h), own.at[h]
            )
            for h in range(count)
        ]

        def start():
            for a, b, h in steps:
                copy(a, b, h, (f, lo)).start()
            for m in mine:
                m.start()

        def end():
            for m in mine:
                m.wait()
            for a, b, h in steps:
                copy(a, b, h, index(-a, b)).wait_recv()
            for a, b, h in steps:
                copy(a, b, h, (f, lo)).wait_send()

        return start, lambda: None, end

    shape = jax.ShapeDtypeStruct((rows, fn * 2 * cols), x.dtype)
    scratch = [dma(fn, 2, count), dma(fn, 2, count), dma(count)]
    return (peers, x, shape, ANY, ANY, scratch, body)


def links_twin_pair():
    return links_and_twin() + the_pair()


def gather_plane(x, parts=8):
    fn = lax.axis_size("fsdp")
    chips = fn // 2
    n, d = x.shape
    step = n // parts
    first, second = list(range(parts // 2)), list(range(parts // 2, parts))
    others = list(range(1, chips))

    def body(x_ref, o_ref, own_sem, sx, rx, sy, ry, st, rt):
        f, c = place()
        chip, core, lo = f // 2, lax.rem(f, 2), lax.rem(c, 2)
        twin = (chip * 2 + 1 - core, c)
        (pair,) = the_pair()

        def rows(p):
            return pl.ds(p * step, step)

        def block(j, core_id, kind, p):
            slot = lax.rem(chip + chips - j, chips) * 2 + core_id
            return o_ref.at[slot, lo if kind == 0 else 1 - lo, rows(p)]

        def source(j, kind, p):
            return x_ref.at[rows(p)] if j == 0 and kind == 0 else block(j, core, kind, p)

        def to(j):
            return (lax.rem(chip + j, chips) * 2 + core, c)

        def x_copy(j, kind, p):
            return remote(
                source(0, kind, p), block(0, core, kind, p), sx.at[j, kind, p], rx.at[j, kind, p], to(j)
            )

        def y_copy(j, p):
            return remote(source(j, 0, p), block(j, core, 0, p), sy.at[j, p], ry.at[j, p], pair)

        def t_copy(j, kind, p):
            return remote(
                source(j, kind, p), block(j, core, kind, p), st.at[j, kind, p], rt.at[j, kind, p], twin
            )

        def x_come(j, kind, p):
            here = block(j, core, kind, p)
            remote(here, here, sx.at[j, kind, p], rx.at[j, kind, p], to(j)).wait_recv()

        def y_come(j, p):
            here = block(j, core, 1, p)
            remote(here, here, sy.at[j, p], ry.at[j, p], pair).wait_recv()

        own = pltpu.make_async_copy(x_ref, o_ref.at[f, lo], own_sem)

        def start():
            for p in first:
                for j in others:
                    x_copy(j, 0, p).start()
            for p in second + first:
                y_copy(0, p).start()
            for p in second:
                for j in others:
                    x_copy(j, 0, p).start()
            for p in range(parts):
                t_copy(0, 0, p).start()
            own.start()

        def middle():
            for p, q in zip(first, second, strict=True):
                for j in others:
                    x_come(j, 0, p)
                    y_copy(j, p).start()
                    t_copy(j, 0, p).start()
                y_come(0, q)
                for j in others:
                    x_copy(j, 1, q).start()
                t_copy(0, 1, q).start()
            for p, q in zip(first, second, strict=True):
                y_come(0, p)
                t_copy(0, 1, p).start()
                for j in others:
                    x_come(j, 0, q)
                    t_copy(j, 0, q).start()

        def end():
            for p, q in zip(first, second, strict=True):
                for j in others:
                    y_come(j, p)
                    t_copy(j, 1, p).start()
                    x_come(j, 1, q)
                    t_copy(j, 1, q).start()
            own.wait()
            for p in range(parts):
                for j in range(chips):
                    for kind in range(2):
                        there = block(j, 1 - core, kind, p)
                        remote(
                            there, there, st.at[j, kind, p], rt.at[j, kind, p], twin
                        ).wait_recv()
                        t_copy(j, kind, p).wait_send()
                y_copy(0, p).wait_send()
                for j in others:
                    x_copy(j, 0, p).wait_send()
            for p, q in zip(first, second, strict=True):
                for j in others:
                    y_copy(j, p).wait_send()
                    x_copy(j, 1, q).wait_send()

        return start, middle, end

    shape = jax.ShapeDtypeStruct((fn, 2, n, d), x.dtype)
    scratch = [dma()] + [dma(chips, 2, parts)] * 2 + [dma(chips, parts)] * 2
    scratch = scratch + [dma(chips, 2, parts)] * 2
    return (links_twin_pair, x, shape, ANY, ANY, scratch, body)


def scatter_plane(x, parts=4):
    fn = lax.axis_size("fsdp")
    chips = fn // 2
    _, _, n, d = x.shape
    step = n // parts
    half = parts // 2
    others = list(range(1, chips))

    def body(
        x_ref, o_ref, own, near, send1, come_y, send_x, come_x, come_x2, send_y, come_y2, acc,
        s_own, s_near, r_near, s_1, r_y, r_x, s_2, r_x2, s_3, r_y2, s_out,
    ):
        f, c = place()
        chip, core, lo = f // 2, lax.rem(f, 2), lax.rem(c, 2)
        twin = (chip * 2 + 1 - core, c)
        (pair,) = the_pair()

        def chip_at(j):
            return lax.rem(chip + j, chips)

        def to(j):
            return (chip_at(j) * 2 + core, c)

        def part(j, core_id, kind, p):
            return x_ref.at[
                chip_at(j) * 2 + core_id, lo if kind == 0 else 1 - lo, pl.ds(p * step, step)
            ]

        def own_copy(j, k, p):
            return pltpu.make_async_copy(part(j, core, k, p), own.at[j, k, p], s_own.at[j, k, p])

        def near_copy(j, k, p):
            return remote(
                part(j, 1 - core, k, p), near.at[j, k, p], s_near.at[j, k, p], r_near.at[j, k, p], twin
            )

        def both(j, k, p):
            return own[j, k, p].astype(F32) + near[j, k, p].astype(F32)

        def ready(j, k, p):
            own_copy(j, k, p).wait()
            near_copy(j, k, p).wait_recv()

        def y_first(j, p):
            return remote(send1.at[j, 1, p], come_y.at[j, p], s_1.at[j, 1, p], r_y.at[j, p], pair)

        def x_first(j, k, p):
            q = p - half
            return remote(
                send1.at[j, k, p], come_x.at[j, k, q], s_1.at[j, k, p], r_x.at[j, k, q], to(j)
            )

        def x_then(j, p):
            return remote(send_x.at[j, p], come_x2.at[j, p], s_2.at[j, p], r_x2.at[j, p], to(j))

        def y_then(q):
            return remote(send_y.at[q], come_y2.at[q], s_3.at[q], r_y2.at[q], pair)

        def out(p):
            return pltpu.make_async_copy(acc.at[p], o_ref.at[pl.ds(p * step, step)], s_out.at[p])

        order = [(j, k, i) for i in range(half) for j in others + [0] for k in (1, 0)]

        def start():
            for j, k, i in order:
                for p in (i, i + half):
                    own_copy(j, k, p).start()
                    near_copy(j, k, p).start()

        def middle():
            for i in range(half):
                for j in range(chips):
                    ready(j, 1, i)
                    send1[j, 1, i] = both(j, 1, i).astype(BF16)
                    y_first(j, i).start()
                for j in others:
                    for k in (1, 0):
                        ready(j, k, i + half)
                        send1[j, k, i + half] = both(j, k, i + half).astype(BF16)
                        x_first(j, k, i + half).start()
            for i in range(half):
                for j in range(chips):
                    ready(j, 0, i)
                for k in range(2):
                    ready(0, k, i + half)

        def end():
            for i in range(half):
                for j in others:
                    y_first(j, i).wait_recv()
                    send_x[j, i] = (both(j, 0, i) + come_y[j, i].astype(F32)).astype(BF16)
                    x_then(j, i).start()
                total = both(0, 1, i + half)
                for j in others:
                    x_first(j, 1, i + half).wait_recv()
                    total += come_x[j, 1, i].astype(F32)
                send_y[i] = total.astype(BF16)
                y_then(i).start()
            for i in range(half):
                y_first(0, i).wait_recv()
                acc[i] = both(0, 0, i) + come_y[0, i].astype(F32)
                acc[i + half] = both(0, 0, i + half)
                for j in others:
                    x_first(j, 0, i + half).wait_recv()
                    acc[i + half] += come_x[j, 0, i].astype(F32)
            for i in range(half):
                for j in others:
                    x_then(j, i).wait_recv()
                    acc[i] += come_x2[j, i].astype(F32)
                out(i).start()
                y_then(i).wait_recv()
                acc[i + half] += come_y2[i].astype(F32)
                out(i + half).start()
            for i in range(half):
                out(i).wait()
                out(i + half).wait()
                y_then(i).wait_send()
                for j in others:
                    x_then(j, i).wait_send()
                    for k in range(2):
                        x_first(j, k, i + half).wait_send()
                for j in range(chips):
                    y_first(j, i).wait_send()
                    for k in range(2):
                        near_copy(j, k, i).wait_send()
                        near_copy(j, k, i + half).wait_send()

        return start, middle, end

    def buffer(*lead):
        return pltpu.VMEM((*lead, step, d), BF16)

    scratch = [
        buffer(chips, 2, parts),
        buffer(chips, 2, parts),
        buffer(chips, 2, parts),
        buffer(chips, half),
        buffer(chips, half),
        buffer(chips, 2, half),
        buffer(chips, half),
        buffer(half),
        buffer(half),
        pltpu.VMEM((parts, step, d), F32),
        dma(chips, 2, parts),
        dma(chips, 2, parts),
        dma(chips, 2, parts),
        dma(chips, 2, parts),
        dma(chips, half),
        dma(chips, 2, half),
        dma(chips, half),
        dma(chips, half),
        dma(half),
        dma(half),
        dma(parts),
    ]
    return (links_twin_pair, x, jax.ShapeDtypeStruct((n, d), F32), ANY, ANY, scratch, body)


def scatter_small(x):
    fn, cn = lax.axis_size("fsdp"), lax.axis_size("ctx")

    def body(x_ref, o_ref, got, sums, got2, s1, r1, s2, r2):
        f, c = place()

        def first(j):
            t = lax.rem(f + j, fn)
            return remote(x_ref.at[t], got.at[j], s1.at[j], r1.at[j], (t, c))

        def second(j):
            t = lax.rem(c + j, cn)
            return remote(sums.at[t], got2.at[j], s2.at[j], r2.at[j], (f, t))

        def start():
            for j in range(1, fn):
                first(j).start()
            sums[...] = x_ref[f]

        def middle():
            for j in range(1, fn):
                first(j).wait_recv()
                sums[...] += got[j]
            for j in range(1, cn):
                second(j).start()
            o_ref[...] = sums[c]

        def end():
            for j in range(1, cn):
                second(j).wait_recv()
                o_ref[...] += got2[j]
            for j in range(1, fn):
                first(j).wait_send()
            for j in range(1, cn):
                second(j).wait_send()

        return start, middle, end

    tail = x.shape[2:]
    scratch = [
        pltpu.VMEM(x.shape, x.dtype),
        pltpu.VMEM(x.shape[1:], x.dtype),
        pltpu.VMEM(x.shape[1:], x.dtype),
        dma(fn),
        dma(fn),
        dma(cn),
        dma(cn),
    ]
    return (along_both, x, jax.ShapeDtypeStruct(tail, x.dtype), VMEM, VMEM, scratch, body)


def nt(a, b):
    return lax.dot_general(a, b, (((1,), (1,)), ((), ())), preferred_element_type=F32)


def nn(a, b):
    return lax.dot_general(a, b, (((1,), (0,)), ((), ())), preferred_element_type=F32)


def attend(q, k, v, starts, block=512):
    u, t, _ = q.shape
    scale = HEAD_DIM**-0.5 * LOG2E

    def kernel(q_ref, k_ref, v_ref, s_ref, o_ref, l_ref, vt):
        i = pl.program_id(1)

        @pl.when(i == 0)
        def _():
            vt[...] = v_ref[0].T

        rows = q_ref[0]
        first = s_ref[0]
        base = lax.broadcasted_iota(jnp.int32, (block, block), 0)
        qpos = i * block + lax.broadcasted_iota(jnp.int32, (1, block), 1)

        def one(j, carry, diagonal):
            peak, total, acc = carry
            at = pl.multiple_of(j * block, block)
            s = nt(k_ref[0, pl.ds(at, block)], rows) * scale
            kpos = base + at
            keep = kpos >= first
            if diagonal:
                keep = keep & (kpos <= qpos)
            s = jnp.where(keep, s, NEG_BIG)
            new = jnp.maximum(peak, jnp.max(s, axis=0, keepdims=True))
            p = jnp.exp2(s - new)
            shrink = jnp.exp2(peak - new)
            total = total * shrink + jnp.sum(p, axis=0, keepdims=True)
            acc = acc * shrink + nn(vt[:, pl.ds(at, block)], p.astype(BF16))
            return new, total, acc

        start = (
            jnp.full((1, block), NEG_BIG, F32),
            jnp.zeros((1, block), F32),
            jnp.zeros((HEAD_DIM, block), F32),
        )
        start = one(i, start, True)
        peak, total, acc = lax.fori_loop(0, i, lambda j, c: one(j, c, False), start)
        o_ref[0] = (acc / total).T.astype(BF16)
        l_ref[0] = peak + jnp.log2(total)

    return pl.pallas_call(
        kernel,
        grid=(u, t // block),
        in_specs=[
            pl.BlockSpec((1, block, HEAD_DIM), lambda a, b: (a, b, 0)),
            pl.BlockSpec((1, t, HEAD_DIM), lambda a, b: (a, 0, 0)),
            pl.BlockSpec((1, t, HEAD_DIM), lambda a, b: (a, 0, 0)),
            pl.BlockSpec((1, 1, block), lambda a, b: (a, 0, b)),
        ],
        out_specs=[
            pl.BlockSpec((1, block, HEAD_DIM), lambda a, b: (a, b, 0)),
            pl.BlockSpec((1, 1, block), lambda a, b: (a, 0, b)),
        ],
        out_shape=[
            jax.ShapeDtypeStruct((u, t, HEAD_DIM), BF16),
            jax.ShapeDtypeStruct((u, 1, t), F32),
        ],
        scratch_shapes=[pltpu.VMEM((HEAD_DIM, t), BF16)],
        compiler_params=pltpu.CompilerParams(vmem_limit_bytes=32 * 2**20),
        cost_estimate=pl.CostEstimate(
            flops=2 * u * t * t * HEAD_DIM, bytes_accessed=8 * u * t * 256, transcendentals=u * t * t // 2
        ),
    )(q, k, v, starts)


def attend_back(q, k, v, starts, lse, o, g, tables, block=512):
    u, t, _ = q.shape
    scale = HEAD_DIM**-0.5

    def kernel(
        q_ref, k_ref, v_ref, s_ref, l_ref, o_ref, g_ref, t_ref, dq_ref, dk_ref, dv_ref, kt, dk, dv
    ):
        i = pl.program_id(1)

        @pl.when(i == 0)
        def _():
            kt[...] = k_ref[0].T
            dk[...] = jnp.zeros_like(dk)
            dv[...] = jnp.zeros_like(dv)

        rows, grows = q_ref[0], g_ref[0]
        first, logs = s_ref[0], l_ref[0]
        prod = o_ref[0].astype(F32) * grows.astype(F32)
        centre = jnp.sum(prod.T, axis=0, keepdims=True)
        base = lax.broadcasted_iota(jnp.int32, (block, block), 0)
        qpos = i * block + lax.broadcasted_iota(jnp.int32, (1, block), 1)

        def one(j, acc, diagonal):
            at = pl.multiple_of(j * block, block)
            here = pl.ds(at, block)
            p = jnp.exp2(nt(k_ref[0, here], rows) * (scale * LOG2E) - logs)
            kpos = base + at
            keep = kpos >= first
            if diagonal:
                keep = keep & (kpos <= qpos)
            p = jnp.where(keep, p, 0.0)
            gp = nt(v_ref[0, here], grows)
            ds = (p * (gp - centre)).astype(BF16)
            dv[here] += nn(p.astype(BF16), grows)
            dk[here] += nn(ds, rows)
            return acc + nn(kt[:, here], ds)

        acc = one(i, jnp.zeros((HEAD_DIM, block), F32), True)
        acc = lax.fori_loop(0, i, lambda j, a: one(j, a, False), acc)
        there = pl.ds(pl.multiple_of(i * block, block), block)
        straight, right, left = t_ref[0, there], t_ref[1, there], t_ref[2, there]
        dq_ref[0] = turn((acc * scale).T, straight, -right, -left).astype(BF16)

        @pl.when(i == t // block - 1)
        def _():
            for b in range(t // block):
                at = pl.ds(b * block, block)
                dk_ref[0, at] = turn(
                    dk[at] * scale, t_ref[0, at], -t_ref[1, at], -t_ref[2, at]
                ).astype(BF16)
                dv_ref[0, at] = dv[at].astype(BF16)

    def whole(a, b):
        return (a, 0, 0)

    def part(a, b):
        return (a, b, 0)

    def row(a, b):
        return (a, 0, b)

    spec, full, line = (1, block, HEAD_DIM), (1, t, HEAD_DIM), (1, 1, block)
    return pl.pallas_call(
        kernel,
        grid=(u, t // block),
        in_specs=[
            pl.BlockSpec(spec, part),
            pl.BlockSpec(full, whole),
            pl.BlockSpec(full, whole),
            pl.BlockSpec(line, row),
            pl.BlockSpec(line, row),
            pl.BlockSpec(spec, part),
            pl.BlockSpec(spec, part),
            pl.BlockSpec((3, t, HEAD_DIM), lambda a, b: (0, 0, 0)),
        ],
        out_specs=[
            pl.BlockSpec(spec, part),
            pl.BlockSpec(full, whole),
            pl.BlockSpec(full, whole),
        ],
        out_shape=[jax.ShapeDtypeStruct((u, t, HEAD_DIM), BF16)] * 3,
        scratch_shapes=[
            pltpu.VMEM((HEAD_DIM, t), BF16),
            pltpu.VMEM((t, HEAD_DIM), F32),
            pltpu.VMEM((t, HEAD_DIM), F32),
        ],
        compiler_params=pltpu.CompilerParams(vmem_limit_bytes=48 * 2**20),
        cost_estimate=pl.CostEstimate(
            flops=5 * u * t * t * HEAD_DIM, bytes_accessed=20 * u * t * 256, transcendentals=u * t * t // 2
        ),
    )(q, k, v, starts, lse, o, g, tables)


def project(x, w, stream, bias, tables):
    count, length, width = x.shape
    cn, fn, _, rows, cols = w.shape
    heads = cols // HEAD_DIM

    def kernel(*refs):
        x_ref, w_ref, b_ref = refs[:3]
        o_ref, held, sem = refs[-3:]

        @pl.when(pl.program_id(0) == 0)
        def _():
            copies = [
                pltpu.make_async_copy(w_ref.at[:, f, stream], held.at[f], sem.at[f])
                for f in range(fn)
            ]
            for c in copies:
                c.start()
            for c in copies:
                c.wait()

        y = nn(x_ref[0], held[...].reshape(width, cols)) + b_ref[...]
        for h in range(heads):
            part = y[:, h * HEAD_DIM : (h + 1) * HEAD_DIM]
            if tables is not None:
                t_ref = refs[3]
                part = turn(part, t_ref[0], t_ref[1], t_ref[2])
            o_ref[h] = part.astype(BF16)

    extra = [] if tables is None else [tables]
    return pl.pallas_call(
        kernel,
        grid=(count,),
        in_specs=[
            pl.BlockSpec((1, length, width), lambda i: (i, 0, 0)),
            ANY,
            pl.BlockSpec((1, cols), lambda i: (0, 0)),
        ]
        + [pl.BlockSpec((3, length, HEAD_DIM), lambda i: (0, 0, 0)) for _ in extra],
        out_specs=pl.BlockSpec((heads, length, HEAD_DIM), lambda i: (i, 0, 0)),
        out_shape=jax.ShapeDtypeStruct((count * heads, length, HEAD_DIM), BF16),
        scratch_shapes=[pltpu.VMEM((fn, cn, rows, cols), BF16), dma(fn)],
        compiler_params=pltpu.CompilerParams(vmem_limit_bytes=32 * 2**20),
        cost_estimate=pl.CostEstimate(
            flops=2 * count * length * width * cols,
            bytes_accessed=2 * (count * length * (width + cols) + width * cols),
            transcendentals=0,
        ),
    )(x, w, bias, *extra)


def widen(x, w, bias, tile=256, rows_at_once=512):
    n, d = x.shape
    cn, fn, rows, cols = w.shape
    tiles = cols // tile

    def kernel(x_ref, w_ref, b_ref, a_ref, g_ref, o_ref, held, sem):
        i = pl.program_id(0)

        def copy(j, f):
            at = pl.ds(pl.multiple_of(j * tile, tile), tile)
            return pltpu.make_async_copy(w_ref.at[:, f, :, at], held.at[j, f], sem.at[j, f])

        @pl.when(i == 0)
        def _():
            for j in range(tiles):
                for f in range(fn):
                    copy(j, f).start()

        for f in range(fn):
            copy(i, f).wait()
        w_tile = held[i].reshape(d, tile)
        o_ref[...] = w_tile
        for r in range(0, n, rows_at_once):
            part = pl.ds(r, rows_at_once)
            y = nn(x_ref[part], w_tile) + b_ref[...]
            t = y * math.sqrt(0.5)
            below = 0.5 + 0.5 * lax.erf(t)
            a_ref[part] = (y * below).astype(BF16)
            density = jnp.exp(-t * t) * (1.0 / math.sqrt(2.0 * math.pi))
            g_ref[part] = (below + y * density).astype(BF16)

    column = pl.BlockSpec((n, tile), lambda i: (0, i))
    return pl.pallas_call(
        kernel,
        grid=(tiles,),
        in_specs=[
            pl.BlockSpec((n, d), lambda i: (0, 0)),
            ANY,
            pl.BlockSpec((1, tile), lambda i: (0, i)),
        ],
        out_specs=[column, column, pl.BlockSpec((d, tile), lambda i: (0, i))],
        out_shape=[
            jax.ShapeDtypeStruct((n, cols), BF16),
            jax.ShapeDtypeStruct((n, cols), BF16),
            jax.ShapeDtypeStruct((d, cols), BF16),
        ],
        scratch_shapes=[pltpu.VMEM((tiles, fn, cn, rows, tile), BF16), dma(tiles, fn)],
        compiler_params=pltpu.CompilerParams(vmem_limit_bytes=48 * 2**20),
        cost_estimate=pl.CostEstimate(
            flops=2 * n * d * cols, bytes_accessed=60_000_000, transcendentals=0
        ),
    )(x, w, bias)


def line_product(x, g, groups, lines, tile=512, shelf=None):
    n, d = g.shape
    block = x.shape[1] // groups
    r = block // lines
    tile = min(tile, d)
    held, first, count = shelf or (None, 0, groups)

    def kernel(x_ref, g_ref, *refs):
        o_ref, turned = refs[-2:]

        @pl.when(pl.program_id(1) == 0)
        def _():
            turned[...] = x_ref[...].T

        y = nn(turned[...], g_ref[...]).astype(BF16)
        o_ref[:, 0] = y.reshape(lines, r, tile)

    extra = [] if held is None else [held]
    return pl.pallas_call(
        kernel,
        grid=(groups, d // tile),
        in_specs=[
            pl.BlockSpec((n, block), lambda i, j: (0, i)),
            pl.BlockSpec((n, tile), lambda i, j: (0, j)),
        ]
        + [ANY] * len(extra),
        out_specs=pl.BlockSpec((lines, 1, r, tile), lambda i, j: (0, first + i, 0, j)),
        out_shape=jax.ShapeDtypeStruct((lines, count, r, d), BF16),
        scratch_shapes=[pltpu.VMEM((block, n), BF16)],
        input_output_aliases={2: 0} if extra else {},
        compiler_params=pltpu.CompilerParams(vmem_limit_bytes=48 * 2**20),
        cost_estimate=pl.CostEstimate(
            flops=2 * n * d * x.shape[1],
            bytes_accessed=2 * (n * d + n * x.shape[1] + d * x.shape[1]),
            transcendentals=0,
        ),
    )(x, g, *extra)


def front(hist, mix, gain, shift, tokens=32, wide=128):
    h, n, d = hist.shape
    rest = gain.shape[0]

    def kernel(h_ref, m_ref, g_ref, b_ref, s_ref, *n_refs):
        for start in range(0, tokens, 16):
            t = slice(start, start + 16)
            m = m_ref[t]
            across = [jnp.broadcast_to(m[:, i : i + 1], (16, wide)) for i in range(4 * h)]
            for at in range(0, d, wide):
                cut = slice(at, at + wide)
                rows = [h_ref[j, t, cut].astype(F32) for j in range(h)]
                for s in range(4):
                    acc = across[s * h] * rows[0]
                    for j in range(1, h):
                        acc += across[s * h + j] * rows[j]
                    s_ref[s, t, cut] = acc
            for s in range(rest):
                x = s_ref[s, t]
                centre = x - jnp.mean(x, axis=-1, keepdims=True)
                spread = jnp.mean(centre * centre, axis=-1, keepdims=True)
                y = centre * lax.rsqrt(spread + EPS_NORM) * g_ref[s : s + 1] + b_ref[s : s + 1]
                n_refs[s][t] = y.astype(BF16)

    return pl.pallas_call(
        kernel,
        grid=(n // tokens,),
        in_specs=[
            pl.BlockSpec((h, tokens, d), lambda i: (0, i, 0)),
            pl.BlockSpec((tokens, 128), lambda i: (i, 0)),
            pl.BlockSpec((rest, d), lambda i: (0, 0)),
            pl.BlockSpec((rest, d), lambda i: (0, 0)),
        ],
        out_specs=[
            pl.BlockSpec((4, tokens, d), lambda i: (0, i, 0)),
        ]
        + [pl.BlockSpec((tokens, d), lambda i: (i, 0))] * rest,
        out_shape=[jax.ShapeDtypeStruct((4, n, d), F32)]
        + [jax.ShapeDtypeStruct((n, d), BF16)] * rest,
        compiler_params=pltpu.CompilerParams(vmem_limit_bytes=60 * 2**20),
        cost_estimate=pl.CostEstimate(
            flops=2 * 4 * h * n * d, bytes_accessed=n * d * (2 * h + 22), transcendentals=0
        ),
    )(hist, mix, gain, shift)


def last(hist, mix, streams, gain, grads, grad_hidden, tokens=32, wide=256):
    h, n, d = hist.shape
    rest = gain.shape[0]

    def kernel(h_ref, m_ref, s_ref, g_ref, d0, d1, d2, r_ref, gh_ref, gm_ref, gg_ref, gb_ref, ds):
        @pl.when(pl.program_id(0) == 0)
        def _():
            gg_ref[...] = jnp.zeros_like(gg_ref)
            gb_ref[...] = jnp.zeros_like(gb_ref)

        for start in range(0, tokens, 16):
            t = slice(start, start + 16)
            for s, d_ref in enumerate((d0, d1, d2)):
                x = s_ref[s, t]
                centre = x - jnp.mean(x, axis=-1, keepdims=True)
                inverse = lax.rsqrt(jnp.mean(centre * centre, axis=-1, keepdims=True) + EPS_NORM)
                unit = centre * inverse
                dn = d_ref[t]
                gg_ref[s : s + 1] += jnp.sum(dn * unit, axis=0, keepdims=True)
                gb_ref[s : s + 1] += jnp.sum(dn, axis=0, keepdims=True)
                du = dn * g_ref[s : s + 1]
                ds[s] = inverse * (
                    du
                    - jnp.mean(du, axis=-1, keepdims=True)
                    - unit * jnp.mean(du * unit, axis=-1, keepdims=True)
                )
            ds[rest] = r_ref[t]
            m = m_ref[t]
            across = [jnp.broadcast_to(m[:, i : i + 1], (16, 128)) for i in range(4 * h)]
            sums = [[jnp.zeros((16, 128), F32) for _ in range(h)] for _ in range(4)]
            for at in range(0, d, wide):
                cuts = [slice(b, b + 128) for b in range(at, at + wide, 128)]
                parts = [[ds[s, :, cut] for cut in cuts] for s in range(4)]
                for j in range(h):
                    for i, cut in enumerate(cuts):
                        acc = across[j] * parts[0][i]
                        for s in range(1, 4):
                            acc += across[s * h + j] * parts[s][i]
                        gh_ref[j, t, cut] = acc
                    rows = [h_ref[j, t, cut].astype(F32) for cut in cuts]
                    for s in range(4):
                        prod = rows[0] * parts[s][0]
                        for i in range(1, len(cuts)):
                            prod += rows[i] * parts[s][i]
                        sums[s][j] += prod
            lane = lax.broadcasted_iota(jnp.int32, (16, 128), 1)
            total = jnp.zeros((16, 128), F32)
            for s in range(4):
                for j in range(h):
                    value = jnp.sum(sums[s][j], axis=-1, keepdims=True)
                    total = jnp.where(lane == s * h + j, value, total)
            gm_ref[t] = total

    row = pl.BlockSpec((tokens, d), lambda i: (i, 0))
    lines = pl.BlockSpec((rest, d), lambda i: (0, 0))
    return pl.pallas_call(
        kernel,
        grid=(n // tokens,),
        in_specs=[
            pl.BlockSpec((h, tokens, d), lambda i: (0, i, 0)),
            pl.BlockSpec((tokens, 128), lambda i: (i, 0)),
            pl.BlockSpec((rest, tokens, d), lambda i: (0, i, 0)),
            lines,
            row,
            row,
            row,
            row,
        ],
        out_specs=[
            pl.BlockSpec((h, tokens, d), lambda i: (0, i, 0)),
            pl.BlockSpec((tokens, 128), lambda i: (i, 0)),
            lines,
            lines,
        ],
        out_shape=[
            jax.ShapeDtypeStruct((h, n, d), F32),
            jax.ShapeDtypeStruct((n, 128), F32),
            jax.ShapeDtypeStruct((rest, d), F32),
            jax.ShapeDtypeStruct((rest, d), F32),
        ],
        scratch_shapes=[pltpu.VMEM((4, 16, d), F32)],
        compiler_params=pltpu.CompilerParams(vmem_limit_bytes=60 * 2**20),
        cost_estimate=pl.CostEstimate(
            flops=4 * 4 * h * n * d, bytes_accessed=n * d * (6 * h + 32), transcendentals=0
        ),
    )(hist, mix, streams, gain, *grads, grad_hidden)


def body(
    history,
    dense_mix,
    doc_starts,
    norm_gain,
    norm_bias,
    qkv_weight,
    qkv_bias,
    out_weight,
    out_bias,
    up_weight,
    up_bias,
    down_weight,
    down_bias,
    root_gain,
    mix_in_weight,
    mix_out_weight,
    mix_out_bias,
    out_cotangent,
    mix_cotangent,
):
    fn, cn = lax.axis_size("fsdp"), lax.axis_size("ctx")
    dn = fn * cn
    fi, ci = lax.axis_index("fsdp"), lax.axis_index("ctx")
    hist, seqs, length, width = history.shape
    nloc = seqs * length
    ntp = fn * nloc
    rows = qkv_weight.shape[0]
    ff = up_weight.shape[1]
    wcol, pcol = width // fn, ff // (2 * fn)
    count = cn // 2
    lo = lax.rem(ci, 2)
    lines = [list(range(b, cn, 2)) for b in range(2)]
    heads = wcol // HEAD_DIM
    units = fn * seqs * heads // cn
    total = cn * length
    mixn = mix_in_weight.shape[1]

    def line_gather(w):
        return lax.all_gather(w, "ctx", axis=0, axis_index_groups=lines)

    parts = [
        norm_gain,
        norm_bias,
        qkv_bias,
        out_bias,
        up_bias,
        down_bias,
        root_gain,
        mix_in_weight,
        doc_starts.astype(F32),
    ]
    flat = jnp.concatenate([a.reshape(-1) for a in parts])
    flat = jnp.pad(flat, (0, -flat.size % 1024)).reshape(-1, 128)
    wout = lax.all_gather(out_weight, "ctx", axis=0, tiled=True)
    flats, qkv_cols = comm(
        1,
        gather_small(flat),
        exchange_fsdp(qkv_weight.reshape(rows, 3, fn, wcol).transpose(2, 1, 0, 3)),
    )
    flats = flats.reshape(dn, -1)
    pieces, at = [], 0
    for a in parts:
        pieces.append(flats[:, at : at + a.size])
        at += a.size

    def joined(piece, lead):
        return piece.reshape(dn, lead, -1).transpose(1, 0, 2).reshape(lead, -1)

    gain_all = joined(pieces[0], 4)
    shift_all = joined(pieces[1], 4)
    qkv_shift = joined(pieces[2], 3)
    out_shift = pieces[3].reshape(-1)
    up_shift = pieces[4].reshape(-1)
    down_shift = pieces[5].reshape(-1)
    root_full = pieces[6].reshape(-1)
    mix_in_full = pieces[7].reshape(width, mixn)
    starts = pieces[8].reshape(fn, cn, seqs, -1)[:, 0].astype(jnp.int32)

    hist2 = history.reshape(hist, nloc, width)
    mix2 = dense_mix.reshape(dense_mix.shape[0], hist, nloc)
    mixes = jnp.pad(mix2.reshape(-1, nloc).T, ((0, 0), (0, 128 - mix2.shape[0] * hist)))
    streams, *normed = front(hist2, mixes, gain_all[:3], shift_all[:3])

    bias_cols = lax.dynamic_slice_in_dim(qkv_shift, fi * wcol, wcol, 1)
    tables = rotary_tables(total)
    tables_l = lax.dynamic_slice_in_dim(tables, ci * length, length, 1)

    def projected(x, w, at, s):
        y = project(
            x.reshape(fn * seqs, length, width),
            w,
            at,
            bias_cols[s : s + 1],
            tables_l if s < 2 else None,
        )
        return y.reshape(cn, units, length, HEAD_DIM)

    def whole_units(x):
        return x.reshape(units, total, HEAD_DIM)

    def from_units(x):
        return exchange_ctx(x.reshape(units, cn, length, HEAD_DIM), False)

    def columns(x):
        x = x.reshape(fn * seqs, heads, length, HEAD_DIM)
        return x.transpose(0, 2, 1, 3).reshape(ntp, wcol)

    w01, g0 = comm(9, gather_ctx(qkv_cols[:, :2]), gather_fsdp(normed[0]))
    g0, cols_2, wout = lax.optimization_barrier((g0, qkv_cols[:, 2], wout))
    w2 = lax.all_gather(cols_2, "ctx", axis=0)
    p0 = projected(g0, w01, 0, 0)
    q_u, g1 = comm(4, exchange_ctx(p0, True), gather_fsdp(normed[1]))
    p1 = projected(g1, w01, 1, 1)
    p1, down_rows = lax.optimization_barrier((p1, down_weight))
    wdown = line_gather(down_rows).reshape(pcol, width)
    k_u, g2 = comm(4, exchange_ctx(p1, True), gather_fsdp(normed[2]))
    p2 = projected(g2, w2[:, :, None], 0, 2)
    v_u, up_cols = comm(
        11,
        exchange_ctx(p2, True),
        exchange_plane(
            up_weight.reshape(rows, fn, count, 2, -1).transpose(1, 3, 0, 2, 4).reshape(fn, 2, rows, pcol),
            plane_sides,
        ),
    )
    up_g = line_gather(up_cols).reshape(count, fn, 2 * rows, pcol)
    wqkv = [w.transpose(1, 0, 2, 3).reshape(width, wcol) for w in (w01[:, :, 0], w01[:, :, 1], w2)]
    q_u, k_u, v_u = whole_units(q_u), whole_units(k_u), whole_units(v_u)
    normed_g = [g.reshape(ntp, width) for g in (g0, g1, g2)]

    pos_all = jnp.arange(total, dtype=jnp.int32)
    unit_ids = ci * units + jnp.arange(units, dtype=jnp.int32)
    seq_ids = unit_ids // heads
    unit_starts = starts.reshape(fn * seqs, -1)[seq_ids]
    first_key = jnp.max(
        jnp.where(unit_starts[:, None, :] <= pos_all[None, :, None], unit_starts[:, None, :], 0),
        axis=-1,
    )[:, None, :]
    att_u, lse_u = attend(q_u, k_u, v_u, first_key)
    attended = columns(comm(6, from_units(att_u))[0])
    attended, wdown = lax.optimization_barrier((attended, wdown))

    def scatter_tokens(x):
        return comm(10, scatter_fsdp(x.astype(BF16).reshape(fn, nloc, width)))[0]

    def gather_tokens(x):
        return comm(3, gather_fsdp(x))[0].reshape(ntp, width)

    def scatter_plane_tokens(x):
        return comm(13, scatter_plane(x.astype(BF16).reshape(fn, 2, nloc, width)))[0]

    def gather_plane_tokens(x):
        return comm(14, gather_plane(x))[0].reshape(2 * ntp, width)

    hidden_res = streams[3] + scatter_tokens(dot("nd,de->ne", attended, wout)) + out_shift
    normed_mlp, mid_pull = jax.vjp(layer_norm, hidden_res, gain_all[3], shift_all[3])
    mlp_g = gather_plane_tokens(normed_mlp.astype(BF16))
    up_bias_cols = lax.dynamic_slice(
        up_shift.reshape(fn, count, 2, -1), (fi, 0, lo, 0), (1, count, 1, ff // dn)
    ).reshape(pcol)
    act_low, slope, wup = widen(mlp_g, up_g, up_bias_cols[None])
    result = hidden_res + scatter_plane_tokens(dot("nf,fd->nd", act_low, wdown)) + down_shift
    block_out = result.astype(BF16).reshape(seqs, length, width)

    next_rows, mixer_pull = jax.vjp(
        mixer, result, root_full, mix_in_full, mix_out_weight, mix_out_bias
    )
    next_mix = next_rows.T.reshape(-1, seqs, length)
    grad_result, grad_root, grad_mix_in, grad_mix_out, grad_mix_bias = mixer_pull(
        mix_cotangent.reshape(-1, nloc).T
    )
    grad_result = grad_result + out_cotangent.reshape(nloc, width).astype(F32)

    grad_branch = grad_result.astype(BF16)
    branch_g = gather_plane_tokens(grad_branch)
    grad_down_shift = jnp.sum(grad_branch.astype(F32), axis=0)

    def line_scatter(x):
        y = lax.psum_scatter(
            x.reshape(-1, x.shape[-1]),
            "ctx",
            scatter_dimension=0,
            axis_index_groups=lines,
            tiled=True,
        )
        return y.reshape(x.shape[1:])

    down_part = dot("nf,nd->fd", act_low, branch_g).astype(BF16)
    down_part, wdown = lax.optimization_barrier((down_part, wdown))
    grad_down = line_scatter(down_part.reshape(count, -1, width))
    grad_active = dot("nd,fd->nf", branch_g, wdown)
    grad_upward = (grad_active * slope.astype(F32)).astype(BF16)
    grad_up_shift = jnp.sum(grad_upward.astype(F32), axis=0)
    up_part = line_product(mlp_g, grad_upward, fn, count)
    up_part, grad_upward = lax.optimization_barrier((up_part, grad_upward))
    grad_up = line_scatter(up_part.reshape(count, -1, pcol))
    mlp_part = dot("nf,df->nd", grad_upward, wup).astype(BF16)
    grad_mlp = scatter_plane_tokens(mlp_part)
    grad_hidden, grad_gain_mid, grad_shift_mid = mid_pull(grad_mlp)
    grad_hidden = grad_hidden + grad_result
    grad_attn = grad_hidden.astype(BF16)
    grad_out_shift = jnp.sum(grad_attn.astype(F32), axis=0)
    attn_g = gather_tokens(grad_attn)
    out_part = dot("nd,ne->de", attended, attn_g).astype(BF16)
    grad_att = dot("ne,de->nd", attn_g, wout).astype(BF16)
    grad_att = grad_att.reshape(fn * seqs, length, heads, HEAD_DIM).transpose(0, 2, 1, 3)
    out_part, grad_att = lax.optimization_barrier((out_part, grad_att))
    (g_u,) = comm(5, exchange_ctx(grad_att.reshape(cn, units, length, HEAD_DIM), True))
    g_u, grad_down, out_part = lax.optimization_barrier((g_u, grad_down, out_part))

    def ctx_scatter(x):
        return lax.psum_scatter(x, "ctx", scatter_dimension=0, tiled=True)

    grad_out = ctx_scatter(out_part)

    gq, gk, gv = attend_back(q_u, k_u, v_u, first_key, lse_u, att_u, whole_units(g_u), tables)

    def back_part(p, s):
        return dot("nc,dc->nd", p, wqkv[s]).astype(BF16).reshape(fn, nloc, width)

    grad_up = grad_up.reshape(fn, 2, rows, pcol)
    if ff // dn % 128 == 0:
        gp0, grad_up = comm(12, from_units(gq), exchange_columns(grad_up, ff // dn, plane_sides))
    else:
        gp0, grad_up = comm(12, from_units(gq), exchange_plane(grad_up, plane_sides))
        grad_up = grad_up.reshape(fn, 2, rows, count, -1).transpose(2, 0, 3, 1, 4)
        grad_up = grad_up.reshape(rows, ff)
    gp0 = columns(gp0)
    q_part = line_product(normed_g[0], gp0, fn, cn)
    q_part, gk = lax.optimization_barrier((q_part, gk))
    grad_q = ctx_scatter(q_part.reshape(-1, wcol)).reshape(fn, rows, wcol)
    gp1, gn0 = comm(8, from_units(gk), scatter_fsdp(back_part(gp0, 0)))
    gp1, grad_out = lax.optimization_barrier((gp1, grad_out))
    gp1 = columns(gp1)
    gp2, gn1 = comm(8, from_units(gv), scatter_fsdp(back_part(gp1, 1)))
    gp2 = columns(gp2)
    kv_part = line_product(normed_g[1], gp1, fn, cn, shelf=(None, 0, 2 * fn))
    kv_part = line_product(normed_g[2], gp2, fn, cn, shelf=(kv_part, fn, 2 * fn))
    kv_part, gp2 = lax.optimization_barrier((kv_part, gp2))
    grad_kv = ctx_scatter(kv_part.reshape(-1, wcol)).reshape(2, fn, rows, wcol)
    grad_q, gn2 = comm(
        7,
        exchange_fsdp(grad_q),
        scatter_fsdp(back_part(gp2, 2)),
    )
    grad_proj = (gp0, gp1, gp2)
    grad_qkv_shift = jnp.stack([jnp.sum(g.astype(F32), axis=0) for g in grad_proj])

    grad_history, grad_mix, grad_gain_front, grad_shift_front = last(
        hist2, mixes, streams, gain_all[:3], (gn0, gn1, gn2), grad_hidden
    )
    grad_history = grad_history.reshape(history.shape)
    grad_mix = grad_mix[:, : mix2.shape[0] * hist].T.reshape(dense_mix.shape)

    def own_columns(x, full):
        zero = jnp.zeros((x.shape[0], full), F32)
        return lax.dynamic_update_slice_in_dim(zero, x, fi * x.shape[1], 1)

    lines_14 = [
        grad_gain_front,
        grad_gain_mid[None],
        grad_shift_front,
        grad_shift_mid[None],
        own_columns(grad_qkv_shift, width),
        grad_out_shift[None],
        grad_down_shift[None],
        grad_root[None],
    ]
    lines_14 = jnp.concatenate(lines_14, axis=0)
    up_lines = lax.dynamic_update_slice(
        jnp.zeros((fn, count, 2, ff // dn), F32),
        grad_up_shift.reshape(1, count, 1, -1),
        (fi, 0, lo, 0),
    ).reshape(dn, -1)
    same = jnp.concatenate([grad_mix_out.reshape(-1), grad_mix_bias])
    flat = jnp.concatenate(
        [
            lines_14.reshape(-1, dn, width // dn).transpose(1, 0, 2).reshape(dn, -1),
            up_lines,
            grad_mix_in.reshape(dn, -1),
            jnp.broadcast_to(same[None], (dn, same.size)),
        ],
        axis=1,
    )
    flat = jnp.pad(flat, ((0, 0), (0, -flat.shape[1] % 1024)))
    (small,) = comm(2, scatter_small(flat.reshape(fn, cn, -1, 128)))
    small = small.reshape(-1)
    out_small, at = [], 0
    order = [norm_gain, norm_bias, qkv_bias, out_bias, down_bias, root_gain, up_bias, mix_in_weight]
    for a in order:
        out_small.append(small[at : at + a.size].reshape(a.shape))
        at += a.size
    mix_sums = small[at : at + same.size]
    cut = grad_mix_out.size
    out_small += [mix_sums[:cut].reshape(grad_mix_out.shape), mix_sums[cut:]]
    out_small, grad_kv = lax.optimization_barrier((out_small, grad_kv))
    (g_gain, g_shift, g_qkv_b, g_out_b, g_down_b, g_root, g_up_b, g_mix_in) = out_small[:-2]
    grad_k, grad_v = comm(15, exchange_fsdp(grad_kv[0]), exchange_fsdp(grad_kv[1]))
    grad_qkv = jnp.stack([grad_q, grad_k, grad_v])
    grad_qkv = grad_qkv.transpose(2, 0, 1, 3).reshape(rows, 3, width).astype(F32)
    return (
        block_out,
        next_mix,
        grad_history,
        grad_mix,
        g_gain,
        g_shift,
        grad_qkv,
        g_qkv_b,
        grad_out.astype(F32),
        g_out_b,
        grad_up.astype(F32),
        g_up_b,
        grad_down.astype(F32),
        g_down_b,
        g_root,
        g_mix_in,
        out_small[-2],
        out_small[-1],
    )


def solution(mesh):
    token = P(None, "fsdp", "ctx")
    both = P(BOTH)
    cols = P(None, BOTH)
    placed = (
        token,
        P(None, None, "fsdp", "ctx"),
        P("fsdp"),
        cols,
        cols,
        both,
        cols,
        both,
        both,
        both,
        both,
        both,
        both,
        both,
        both,
        P(),
        P(),
        P("fsdp", "ctx"),
        token,
    )
    outs = (
        P("fsdp", "ctx"),
        token,
        token,
        P(None, None, "fsdp", "ctx"),
        cols,
        cols,
        both,
        cols,
        both,
        both,
        both,
        both,
        both,
        both,
        both,
        both,
        P(),
        P(),
    )
    return jax.shard_map(body, mesh=mesh, in_specs=placed, out_specs=outs, check_vma=False)
```

```python
import math

import jax
import jax.numpy as jnp
import numpy as np
from jax import lax
from jax.experimental import pallas as pl
from jax.experimental.pallas import tpu as pltpu
from jax.sharding import PartitionSpec as P

HEAD_DIM = 128
ROT = 32
TOP_PRECISION = lax.Precision.HIGHEST
EPS_NORM = 1e-05
EPS_ROOT = 1e-06
NEG_BIG = -1e30
BOTH = ("fsdp", "ctx")
BF16 = jnp.bfloat16
F32 = jnp.float32
MESH = pl.DeviceIdType.MESH
ANY = pl.BlockSpec(memory_space=pl.ANY)
VMEM = pl.BlockSpec(memory_space=pltpu.VMEM)
LOG2E = 1.4426950408889634


def layer_norm(values, gain_row, shift_row):
    centre = values - jnp.mean(values, axis=-1, keepdims=True)
    spread = jnp.mean(centre * centre, axis=-1, keepdims=True)
    return centre * lax.rsqrt(spread + EPS_NORM) * gain_row + shift_row


def gelu(values):
    return jax.nn.gelu(values, approximate=False)


def rotary_tables(count):
    half = ROT // 2
    frequency = np.exp(np.arange(half, dtype=np.float32) * np.float32(-2.0 * math.log(10000.0) / ROT))
    angles = np.arange(count, dtype=np.float32)[:, None] * frequency.astype(np.float32)[None, :]
    cosine = jnp.asarray(np.cos(angles.astype(np.float64)), F32)
    sine = jnp.asarray(np.sin(angles.astype(np.float64)), F32)
    zero, rest = jnp.zeros_like(sine), HEAD_DIM - ROT
    return jnp.stack(
        [
            jnp.pad(jnp.concatenate([cosine, cosine], 1), ((0, 0), (0, rest)), constant_values=1.0),
            jnp.pad(jnp.concatenate([zero, sine], 1), ((0, 0), (0, rest))),
            jnp.pad(jnp.concatenate([-sine, zero], 1), ((0, 0), (0, rest))),
        ]
    )


def turn(x, straight, right, left):
    half = ROT // 2
    return (
        x * straight
        + pltpu.roll(x, half, axis=1) * right
        + pltpu.roll(x, HEAD_DIM - half, axis=1) * left
    )


def mixer(rows, gain_row, opening, closing, closing_bias):
    inverse_rms = lax.rsqrt(jnp.mean(rows * rows, axis=-1, keepdims=True) + EPS_ROOT)
    rooted = rows * inverse_rms * gain_row
    hidden = jnp.dot(rooted, opening, precision=TOP_PRECISION)
    return jnp.dot(gelu(hidden), closing, precision=TOP_PRECISION) + closing_bias


def dot(pattern, left, right):
    return jnp.einsum(pattern, left, right, preferred_element_type=F32)


def remote(src, dst, send_sem, recv_sem, target):
    return pltpu.make_async_remote_copy(
        src_ref=src,
        dst_ref=dst,
        send_sem=send_sem,
        recv_sem=recv_sem,
        device_id=target,
        device_id_type=MESH,
    )


def place():
    return lax.axis_index("fsdp"), lax.axis_index("ctx")


def links_and_twin():
    chips = lax.axis_size("fsdp") // 2
    f, c = place()
    chip, core = f // 2, lax.rem(f, 2)
    return [(lax.rem(chip + j, chips) * 2 + core, c) for j in range(1, chips)] + [
        (chip * 2 + 1 - core, c)
    ]


def along_ctx():
    cn = lax.axis_size("ctx")
    f, c = place()
    return [(f, lax.rem(c + j, cn)) for j in range(1, cn)]


def along_fsdp():
    fn = lax.axis_size("fsdp")
    f, c = place()
    return [(lax.rem(f + j, fn), c) for j in range(1, fn)]


def along_both():
    return along_ctx() + along_fsdp()


def comm(cid, *tasks):
    n = len(tasks)
    counts = [len(t[5]) for t in tasks]
    given = [t[1] if isinstance(t[1], tuple) else (t[1],) for t in tasks]
    many = sum(len(g) for g in given)
    limit = 6 * 2**20
    for t in tasks:
        for x in t[5]:
            if x.dtype in (BF16, F32):
                limit += math.prod(x.shape) * jnp.dtype(x.dtype).itemsize

    def kernel(*refs):
        targets, seen = [], []
        covered = [
            (along_fsdp, [along_both]),
            (the_pair, [along_ctx]),
            (the_pair, [plane_others]),
            (links_and_twin, [plane_others]),
            (links_and_twin, [along_fsdp]),
        ]
        for t in tasks:
            if t[0] not in seen and (t[0], seen[:1]) not in covered:
                seen.append(t[0])
                targets += t[0]()
        barrier = pltpu.get_barrier_semaphore()
        for t in targets:
            pl.semaphore_signal(barrier, inc=1, device_id=t, device_id_type=MESH)
        pl.semaphore_wait(barrier, len(targets))
        inputs, scratch = list(refs[:many]), list(refs[many + n :])
        phases = []
        for i, t in enumerate(tasks):
            mine, scratch = scratch[: counts[i]], scratch[counts[i] :]
            own, inputs = inputs[: len(given[i])], inputs[len(given[i]) :]
            phases.append(t[6](*own, refs[many + i], *mine))
        for p in range(3):
            for ph in phases:
                ph[p]()

    out = pl.pallas_call(
        kernel,
        out_shape=[t[2] for t in tasks],
        in_specs=[t[3] for t, g in zip(tasks, given, strict=True) for _ in g],
        out_specs=[t[4] for t in tasks],
        scratch_shapes=[x for t in tasks for x in t[5]],
        compiler_params=pltpu.CompilerParams(
            collective_id=cid, has_side_effects=True, vmem_limit_bytes=limit
        ),
        cost_estimate=pl.CostEstimate(flops=0, bytes_accessed=15_000_000, transcendentals=0),
    )(*[x for g in given for x in g])
    return out


def dma(*shape):
    return pltpu.SemaphoreType.DMA(shape)


def gather_small(x):
    fn, cn = lax.axis_size("fsdp"), lax.axis_size("ctx")

    def body(x_ref, o_ref, s1, r1, s2, r2):
        f, c = place()

        def first(j):
            return remote(
                x_ref, o_ref.at[f, c], s1.at[j], r1.at[j], (f, lax.rem(c + j, cn))
            )

        def second(j):
            return remote(
                o_ref.at[f], o_ref.at[f], s2.at[j], r2.at[j], (lax.rem(f + j, fn), c)
            )

        def start():
            for j in range(1, cn):
                first(j).start()
            o_ref[f, c] = x_ref[...]

        def middle():
            for j in range(1, cn):
                there = o_ref.at[f, lax.rem(c + cn - j, cn)]
                remote(there, there, s1.at[j], r1.at[j], (f, lax.rem(c + j, cn))).wait_recv()
            for j in range(1, fn):
                second(j).start()

        def end():
            for j in range(1, fn):
                there = o_ref.at[lax.rem(f + fn - j, fn)]
                remote(there, there, s2.at[j], r2.at[j], (lax.rem(f + j, fn), c)).wait_recv()
            for j in range(1, cn):
                first(j).wait_send()
            for j in range(1, fn):
                second(j).wait_send()

        return start, middle, end

    shape = jax.ShapeDtypeStruct((fn, cn, *x.shape), x.dtype)
    return (along_both, x, shape, VMEM, VMEM, [dma(cn), dma(cn), dma(fn), dma(fn)], body)


def exchange_fsdp(x):
    fn = lax.axis_size("fsdp")

    def body(x_ref, o_ref, s, r, own):
        f, c = place()

        def copy(j, slot):
            t = lax.rem(f + j, fn)
            return remote(x_ref.at[t], o_ref.at[slot], s.at[j], r.at[j], (t, c))

        mine = pltpu.make_async_copy(x_ref.at[f], o_ref.at[f], own)

        def start():
            for j in range(1, fn):
                copy(j, f).start()
            mine.start()

        def end():
            mine.wait()
            for j in range(1, fn):
                copy(j, lax.rem(f + fn - j, fn)).wait_recv()
            for j in range(1, fn):
                copy(j, f).wait_send()

        return start, lambda: None, end

    shape = jax.ShapeDtypeStruct(x.shape, x.dtype)
    return (along_fsdp, x, shape, ANY, ANY, [dma(fn), dma(fn), dma()], body)


def exchange_ctx(x, to_units):
    cn = lax.axis_size("ctx")
    lead = x.shape[1] if to_units else x.shape[0]

    def body(x_ref, o_ref, s, r, own):
        f, c = place()

        def source(t):
            return x_ref.at[t] if to_units else x_ref.at[:, t]

        def target(slot):
            return o_ref.at[:, slot] if to_units else o_ref.at[slot]

        def copy(j, slot):
            t = lax.rem(c + j, cn)
            return remote(source(t), target(slot), s.at[j], r.at[j], (f, t))

        mine = pltpu.make_async_copy(source(c), target(c), own)

        def start():
            for j in range(1, cn):
                copy(j, c).start()
            mine.start()

        def end():
            mine.wait()
            for j in range(1, cn):
                copy(j, lax.rem(c + cn - j, cn)).wait_recv()
            for j in range(1, cn):
                copy(j, c).wait_send()

        return start, lambda: None, end

    dims = (lead, cn) if to_units else (cn, lead)
    shape = jax.ShapeDtypeStruct((*dims, *x.shape[2:]), x.dtype)
    return (along_ctx, x, shape, ANY, ANY, [dma(cn), dma(cn), dma()], body)


def the_pair():
    f, c = place()
    return [(f, c // 2 * 2 + 1 - lax.rem(c, 2))]


def exchange_pair(x):
    def body(x_ref, o_ref, s, r):
        (pair,) = the_pair()
        copy = remote(x_ref, o_ref, s, r, pair)
        return copy.start, lambda: None, copy.wait

    shape = jax.ShapeDtypeStruct(x.shape, x.dtype)
    return (the_pair, x, shape, ANY, ANY, [dma(), dma()], body)


def gather_fsdp(x, parts=4):
    fn = lax.axis_size("fsdp")
    chips = fn // 2
    n, d = x.shape
    step = n // parts
    pieces = [pl.ds(p * step, step) for p in range(parts)]

    def body(x_ref, o_ref, own_sem, s_link, r_link, s_core, r_core):
        f, c = place()
        chip, core = f // 2, lax.rem(f, 2)
        twin = (chip * 2 + 1 - core, c)
        links, cores = {}, {}

        def to(j):
            return (lax.rem(chip + j, chips) * 2 + core, c)

        def slot(j, core_id):
            return lax.rem(chip + chips - j, chips) * 2 + core_id

        own = pltpu.make_async_copy(x_ref, o_ref.at[f], own_sem)

        def start():
            for i, rows in enumerate(pieces):
                here, there = x_ref.at[rows], o_ref.at[f, rows]
                for j in range(1, chips):
                    links[i, j] = remote(here, there, s_link.at[j, i], r_link.at[j, i], to(j))
                    links[i, j].start()
            for i, rows in enumerate(pieces):
                here, there = x_ref.at[rows], o_ref.at[f, rows]
                cores[i, 0] = remote(here, there, s_core.at[0, i], r_core.at[0, i], twin)
                cores[i, 0].start()
            own.start()

        def middle():
            for i, rows in enumerate(pieces):
                for j in range(1, chips):
                    here = o_ref.at[slot(j, core), rows]
                    remote(here, here, s_link.at[j, i], r_link.at[j, i], to(j)).wait_recv()
                    cores[i, j] = remote(here, here, s_core.at[j, i], r_core.at[j, i], twin)
                    cores[i, j].start()

        def end():
            own.wait()
            for i, rows in enumerate(pieces):
                for j in range(chips):
                    there = o_ref.at[slot(j, 1 - core), rows]
                    cores[i, j].wait_send()
                    remote(there, there, s_core.at[j, i], r_core.at[j, i], twin).wait_recv()
                for j in range(1, chips):
                    links[i, j].wait_send()

        return start, middle, end

    shape = jax.ShapeDtypeStruct((fn, n, d), x.dtype)
    return (links_and_twin, x, shape, ANY, ANY, [dma()] + [dma(chips, parts)] * 4, body)


def gather_ctx(x):
    cn = lax.axis_size("ctx")
    count = cn // 2

    def body(x_ref, o_ref, own_sem, s_up, r_up, s_down, r_down, s_pair, r_pair):
        f, c = place()
        hi, lo = c // 2, lax.rem(c, 2)
        pair = (f, hi * 2 + 1 - lo)
        above = (f, lax.rem(hi + 1, count) * 2 + lo)
        below = (f, lax.rem(hi + count - 1, count) * 2 + lo)
        own = pltpu.make_async_copy(x_ref, o_ref.at[c], own_sem)

        def low(d):
            return lax.rem(hi + count - d, count)

        def high(d):
            return lax.rem(hi + d, count)

        def up(d):
            source = x_ref if d == 0 else o_ref.at[low(d) * 2 + lo]
            return remote(source, o_ref.at[low(d) * 2 + lo], s_up.at[d], r_up.at[d + 1], above)

        def down(d):
            source = x_ref if d == 0 else o_ref.at[high(d) * 2 + lo]
            return remote(
                source, o_ref.at[high(d) * 2 + lo], s_down.at[d], r_down.at[d + 1], below
            )

        def across(k, slot):
            source = x_ref if k == 0 else o_ref.at[slot * 2 + lo]
            return remote(source, o_ref.at[slot * 2 + lo], s_pair.at[k], r_pair.at[k], pair)

        def start():
            pl.when(hi < count - 1)(lambda: up(0).start())
            pl.when(hi > 0)(lambda: down(0).start())
            across(0, hi).start()
            own.start()

        def middle():
            for d in range(1, count):

                @pl.when(hi >= d)
                def _():
                    here = o_ref.at[low(d) * 2 + lo]
                    remote(here, here, s_up.at[d], r_up.at[d], above).wait_recv()
                    across(d, low(d)).start()
                    if d < count - 1:
                        pl.when(hi < count - 1)(lambda: up(d).start())

                @pl.when(hi + d < count)
                def _():
                    here = o_ref.at[high(d) * 2 + lo]
                    remote(here, here, s_down.at[d], r_down.at[d], below).wait_recv()
                    across(count - d, high(d)).start()
                    if d < count - 1:
                        pl.when(hi > 0)(lambda: down(d).start())

        def end():
            own.wait()
            across(0, hi).wait_send()
            for k in range(count):
                there = o_ref.at[low(k) * 2 + 1 - lo]
                remote(there, there, s_pair.at[k], r_pair.at[k], pair).wait_recv()
                if k > 0:
                    across(k, low(k)).wait_send()
            for d in range(count - 1):
                pl.when((hi >= d) & (hi < count - 1))(lambda d=d: up(d).wait_send())
                pl.when((hi + d < count) & (hi > 0))(lambda d=d: down(d).wait_send())

        return start, middle, end

    shape = jax.ShapeDtypeStruct((cn, *x.shape), x.dtype)
    scratch = [dma()] + [dma(count + 1)] * 4 + [dma(count)] * 2
    return (along_ctx, x, shape, ANY, ANY, scratch, body)


def scatter_fsdp(x, parts=4):
    fn = lax.axis_size("fsdp")
    chips = fn // 2
    _, n, d = x.shape
    step = n // parts

    def body(x_ref, o_ref, own, near, mine, far, ss, s_own, s_near, r_near, s_far, r_far):
        f, c = place()
        chip, core = f // 2, lax.rem(f, 2)
        twin = (chip * 2 + 1 - core, c)
        nears, owns, fars, outs = {}, {}, {}, {}

        def chip_at(j):
            return lax.rem(chip + j, chips)

        def start():
            for p in range(parts):
                rows = pl.ds(p * step, step)
                for j in list(range(1, chips)) + [0]:
                    at = chip_at(j) * 2
                    owns[p, j] = pltpu.make_async_copy(
                        x_ref.at[at + core, rows], own.at[j, p], s_own.at[j, p]
                    )
                    owns[p, j].start()
                    nears[p, j] = remote(
                        x_ref.at[at + 1 - core, rows],
                        near.at[j, p],
                        s_near.at[j, p],
                        r_near.at[j, p],
                        twin,
                    )
                    nears[p, j].start()

        def middle():
            for p in range(parts):
                for j in range(1, chips):
                    owns[p, j].wait()
                    nears[p, j].wait_recv()
                    mine[j, p] = (own[j, p].astype(F32) + near[j, p].astype(F32)).astype(BF16)
                    fars[p, j] = remote(
                        mine.at[j, p],
                        far.at[j, p],
                        s_far.at[j, p],
                        r_far.at[j, p],
                        (chip_at(j) * 2 + core, c),
                    )
                    fars[p, j].start()
            for p in range(parts):
                owns[p, 0].wait()
                nears[p, 0].wait_recv()
                ss[p] = own[0, p].astype(F32) + near[0, p].astype(F32)

        def end():
            for p in range(parts):
                for j in range(1, chips):
                    fars[p, j].wait_recv()
                    ss[p] += far[j, p].astype(F32)
                outs[p] = pltpu.make_async_copy(
                    ss.at[p], o_ref.at[pl.ds(p * step, step)], s_far.at[0, p]
                )
                outs[p].start()
            for p in range(parts):
                outs[p].wait()
                for j in range(chips):
                    nears[p, j].wait_send()
                for j in range(1, chips):
                    fars[p, j].wait_send()

        return start, middle, end

    block = pltpu.VMEM((chips, parts, step, d), BF16)
    scratch = [block] * 4 + [pltpu.VMEM((parts, step, d), F32)] + [dma(chips, parts)] * 5
    return (links_and_twin, x, jax.ShapeDtypeStruct((n, d), F32), ANY, ANY, scratch, body)


def plane_others():
    fn = lax.axis_size("fsdp")
    f, c = place()
    (pair,) = the_pair()
    return [(lax.rem(f + a, fn), (c, pair[1])[b]) for a in range(fn) for b in range(2) if a or b]


def plane_sides():
    return [t for i, t in enumerate(plane_others()) if i > 0]


def exchange_plane(x, peers):
    fn = lax.axis_size("fsdp")

    def body(x_ref, o_ref, s, r, own):
        f, c = place()
        lo = lax.rem(c, 2)
        (pair,) = the_pair()

        def index(a, b):
            return lax.rem(f + a + fn, fn), (lo if b == 0 else 1 - lo)

        def copy(a, b, slot):
            fa, lb = index(a, b)
            return remote(
                x_ref.at[fa, lb],
                o_ref.at[slot[0], slot[1]],
                s.at[a, b],
                r.at[a, b],
                (fa, c if b == 0 else pair[1]),
            )

        steps = [(a, b) for a in range(fn) for b in range(2) if a or b]
        mine = pltpu.make_async_copy(x_ref.at[f, lo], o_ref.at[f, lo], own)

        def start():
            for a, b in steps:
                copy(a, b, (f, lo)).start()
            mine.start()

        def end():
            mine.wait()
            for a, b in steps:
                copy(a, b, index(-a, b)).wait_recv()
            for a, b in steps:
                copy(a, b, (f, lo)).wait_send()

        return start, lambda: None, end

    shape = jax.ShapeDtypeStruct(x.shape, x.dtype)
    return (peers, x, shape, ANY, ANY, [dma(fn, 2), dma(fn, 2), dma()], body)


def exchange_columns(x, wide, peers):
    fn = lax.axis_size("fsdp")
    _, _, rows, cols = x.shape
    count = cols // wide

    def body(x_ref, o_ref, s, r, own):
        f, c = place()
        lo = lax.rem(c, 2)
        (pair,) = the_pair()

        def index(a, b):
            return lax.rem(f + a + fn, fn), (lo if b == 0 else 1 - lo)

        def target(slot, h):
            at = ((slot[0] * count + h) * 2 + slot[1]) * wide
            return o_ref.at[:, pl.ds(pl.multiple_of(at, wide), wide)]

        def copy(a, b, h, slot):
            fa, lb = index(a, b)
            return remote(
                x_ref.at[fa, lb, :, pl.ds(h * wide, wide)],
                target(slot, h),
                s.at[a, b, h],
                r.at[a, b, h],
                (fa, c if b == 0 else pair[1]),
            )

        steps = [
            (a, b, h) for a in range(fn) for b in range(2) for h in range(count) if a or b
        ]
        mine = [
            pltpu.make_async_copy(
                x_ref.at[f, lo, :, pl.ds(h * wide, wide)], target((f, lo), h), own.at[h]
            )
            for h in range(count)
        ]

        def start():
            for a, b, h in steps:
                copy(a, b, h, (f, lo)).start()
            for m in mine:
                m.start()

        def end():
            for m in mine:
                m.wait()
            for a, b, h in steps:
                copy(a, b, h, index(-a, b)).wait_recv()
            for a, b, h in steps:
                copy(a, b, h, (f, lo)).wait_send()

        return start, lambda: None, end

    shape = jax.ShapeDtypeStruct((rows, fn * 2 * cols), x.dtype)
    scratch = [dma(fn, 2, count), dma(fn, 2, count), dma(count)]
    return (peers, x, shape, ANY, ANY, scratch, body)


def links_twin_pair():
    return links_and_twin() + the_pair()


def gather_plane(x, parts=8):
    fn = lax.axis_size("fsdp")
    chips = fn // 2
    n, d = x.shape
    step = n // parts
    first, second = list(range(parts // 2)), list(range(parts // 2, parts))
    others = list(range(1, chips))

    def body(x_ref, o_ref, own_sem, sx, rx, sy, ry, st, rt):
        f, c = place()
        chip, core, lo = f // 2, lax.rem(f, 2), lax.rem(c, 2)
        twin = (chip * 2 + 1 - core, c)
        (pair,) = the_pair()

        def rows(p):
            return pl.ds(p * step, step)

        def block(j, core_id, kind, p):
            slot = lax.rem(chip + chips - j, chips) * 2 + core_id
            return o_ref.at[slot, lo if kind == 0 else 1 - lo, rows(p)]

        def source(j, kind, p):
            return x_ref.at[rows(p)] if j == 0 and kind == 0 else block(j, core, kind, p)

        def to(j):
            return (lax.rem(chip + j, chips) * 2 + core, c)

        def x_copy(j, kind, p):
            return remote(
                source(0, kind, p), block(0, core, kind, p), sx.at[j, kind, p], rx.at[j, kind, p], to(j)
            )

        def y_copy(j, p):
            return remote(source(j, 0, p), block(j, core, 0, p), sy.at[j, p], ry.at[j, p], pair)

        def t_copy(j, kind, p):
            return remote(
                source(j, kind, p), block(j, core, kind, p), st.at[j, kind, p], rt.at[j, kind, p], twin
            )

        def x_come(j, kind, p):
            here = block(j, core, kind, p)
            remote(here, here, sx.at[j, kind, p], rx.at[j, kind, p], to(j)).wait_recv()

        def y_come(j, p):
            here = block(j, core, 1, p)
            remote(here, here, sy.at[j, p], ry.at[j, p], pair).wait_recv()

        own = pltpu.make_async_copy(x_ref, o_ref.at[f, lo], own_sem)

        def start():
            for p in first:
                for j in others:
                    x_copy(j, 0, p).start()
            for p in second + first:
                y_copy(0, p).start()
            for p in second:
                for j in others:
                    x_copy(j, 0, p).start()
            for p in range(parts):
                t_copy(0, 0, p).start()
            own.start()

        def middle():
            for p, q in zip(first, second, strict=True):
                for j in others:
                    x_come(j, 0, p)
                    y_copy(j, p).start()
                    t_copy(j, 0, p).start()
                y_come(0, q)
                for j in others:
                    x_copy(j, 1, q).start()
                t_copy(0, 1, q).start()
            for p, q in zip(first, second, strict=True):
                y_come(0, p)
                t_copy(0, 1, p).start()
                for j in others:
                    x_come(j, 0, q)
                    t_copy(j, 0, q).start()

        def end():
            for p, q in zip(first, second, strict=True):
                for j in others:
                    y_come(j, p)
                    t_copy(j, 1, p).start()
                    x_come(j, 1, q)
                    t_copy(j, 1, q).start()
            own.wait()
            for p in range(parts):
                for j in range(chips):
                    for kind in range(2):
                        there = block(j, 1 - core, kind, p)
                        remote(
                            there, there, st.at[j, kind, p], rt.at[j, kind, p], twin
                        ).wait_recv()
                        t_copy(j, kind, p).wait_send()
                y_copy(0, p).wait_send()
                for j in others:
                    x_copy(j, 0, p).wait_send()
            for p, q in zip(first, second, strict=True):
                for j in others:
                    y_copy(j, p).wait_send()
                    x_copy(j, 1, q).wait_send()

        return start, middle, end

    shape = jax.ShapeDtypeStruct((fn, 2, n, d), x.dtype)
    scratch = [dma()] + [dma(chips, 2, parts)] * 2 + [dma(chips, parts)] * 2
    scratch = scratch + [dma(chips, 2, parts)] * 2
    return (links_twin_pair, x, shape, ANY, ANY, scratch, body)


def scatter_plane(x, parts=4):
    fn = lax.axis_size("fsdp")
    chips = fn // 2
    _, _, n, d = x.shape
    step = n // parts
    half = parts // 2
    others = list(range(1, chips))

    def body(
        x_ref, o_ref, own, near, send1, come_y, send_x, come_x, come_x2, send_y, come_y2, acc,
        s_own, s_near, r_near, s_1, r_y, r_x, s_2, r_x2, s_3, r_y2, s_out,
    ):
        f, c = place()
        chip, core, lo = f // 2, lax.rem(f, 2), lax.rem(c, 2)
        twin = (chip * 2 + 1 - core, c)
        (pair,) = the_pair()

        def chip_at(j):
            return lax.rem(chip + j, chips)

        def to(j):
            return (chip_at(j) * 2 + core, c)

        def part(j, core_id, kind, p):
            return x_ref.at[
                chip_at(j) * 2 + core_id, lo if kind == 0 else 1 - lo, pl.ds(p * step, step)
            ]

        def own_copy(j, k, p):
            return pltpu.make_async_copy(part(j, core, k, p), own.at[j, k, p], s_own.at[j, k, p])

        def near_copy(j, k, p):
            return remote(
                part(j, 1 - core, k, p), near.at[j, k, p], s_near.at[j, k, p], r_near.at[j, k, p], twin
            )

        def both(j, k, p):
            return own[j, k, p].astype(F32) + near[j, k, p].astype(F32)

        def ready(j, k, p):
            own_copy(j, k, p).wait()
            near_copy(j, k, p).wait_recv()

        def y_first(j, p):
            return remote(send1.at[j, 1, p], come_y.at[j, p], s_1.at[j, 1, p], r_y.at[j, p], pair)

        def x_first(j, k, p):
            q = p - half
            return remote(
                send1.at[j, k, p], come_x.at[j, k, q], s_1.at[j, k, p], r_x.at[j, k, q], to(j)
            )

        def x_then(j, p):
            return remote(send_x.at[j, p], come_x2.at[j, p], s_2.at[j, p], r_x2.at[j, p], to(j))

        def y_then(q):
            return remote(send_y.at[q], come_y2.at[q], s_3.at[q], r_y2.at[q], pair)

        def out(p):
            return pltpu.make_async_copy(acc.at[p], o_ref.at[pl.ds(p * step, step)], s_out.at[p])

        order = [(j, k, i) for i in range(half) for j in others + [0] for k in (1, 0)]

        def start():
            for j, k, i in order:
                for p in (i, i + half):
                    own_copy(j, k, p).start()
                    near_copy(j, k, p).start()

        def middle():
            for i in range(half):
                for j in range(chips):
                    ready(j, 1, i)
                    send1[j, 1, i] = both(j, 1, i).astype(BF16)
                    y_first(j, i).start()
                for j in others:
                    for k in (1, 0):
                        ready(j, k, i + half)
                        send1[j, k, i + half] = both(j, k, i + half).astype(BF16)
                        x_first(j, k, i + half).start()
            for i in range(half):
                for j in range(chips):
                    ready(j, 0, i)
                for k in range(2):
                    ready(0, k, i + half)

        def end():
            for i in range(half):
                for j in others:
                    y_first(j, i).wait_recv()
                    send_x[j, i] = (both(j, 0, i) + come_y[j, i].astype(F32)).astype(BF16)
                    x_then(j, i).start()
                total = both(0, 1, i + half)
                for j in others:
                    x_first(j, 1, i + half).wait_recv()
                    total += come_x[j, 1, i].astype(F32)
                send_y[i] = total.astype(BF16)
                y_then(i).start()
            for i in range(half):
                y_first(0, i).wait_recv()
                acc[i] = both(0, 0, i) + come_y[0, i].astype(F32)
                acc[i + half] = both(0, 0, i + half)
                for j in others:
                    x_first(j, 0, i + half).wait_recv()
                    acc[i + half] += come_x[j, 0, i].astype(F32)
            for i in range(half):
                for j in others:
                    x_then(j, i).wait_recv()
                    acc[i] += come_x2[j, i].astype(F32)
                out(i).start()
                y_then(i).wait_recv()
                acc[i + half] += come_y2[i].astype(F32)
                out(i + half).start()
            for i in range(half):
                out(i).wait()
                out(i + half).wait()
                y_then(i).wait_send()
                for j in others:
                    x_then(j, i).wait_send()
                    for k in range(2):
                        x_first(j, k, i + half).wait_send()
                for j in range(chips):
                    y_first(j, i).wait_send()
                    for k in range(2):
                        near_copy(j, k, i).wait_send()
                        near_copy(j, k, i + half).wait_send()

        return start, middle, end

    def buffer(*lead):
        return pltpu.VMEM((*lead, step, d), BF16)

    scratch = [
        buffer(chips, 2, parts),
        buffer(chips, 2, parts),
        buffer(chips, 2, parts),
        buffer(chips, half),
        buffer(chips, half),
        buffer(chips, 2, half),
        buffer(chips, half),
        buffer(half),
        buffer(half),
        pltpu.VMEM((parts, step, d), F32),
        dma(chips, 2, parts),
        dma(chips, 2, parts),
        dma(chips, 2, parts),
        dma(chips, 2, parts),
        dma(chips, half),
        dma(chips, 2, half),
        dma(chips, half),
        dma(chips, half),
        dma(half),
        dma(half),
        dma(parts),
    ]
    return (links_twin_pair, x, jax.ShapeDtypeStruct((n, d), F32), ANY, ANY, scratch, body)


def nobody():
    return []


def product_beside(x, g, groups, lines, tile=512):
    n, d = g.shape
    block = x.shape[1] // groups
    r = block // lines

    def body(x_ref, g_ref, o_ref, xs, gs, turned, ys, s_x, s_g, s_y):
        def x_copy(i):
            at = pl.ds(pl.multiple_of(i * block, block), block)
            return pltpu.make_async_copy(x_ref.at[:, at], xs.at[i], s_x.at[i])

        def y_copy(i):
            return pltpu.make_async_copy(ys.at[i], o_ref.at[:, i], s_y.at[i])

        g_copy = pltpu.make_async_copy(g_ref, gs, s_g)

        def start():
            g_copy.start()
            for i in range(groups):
                x_copy(i).start()

        def middle():
            g_copy.wait()

            def one(i, _):
                x_copy(i).wait()
                turned[...] = xs[i].T
                for j in range(0, d, tile):
                    cut = slice(j, j + tile)
                    y = nn(turned[...], gs[:, cut]).astype(BF16)
                    ys[i, :, :, cut] = y.reshape(lines, r, tile)
                y_copy(i).start()
                return 0

            lax.fori_loop(0, groups, one, 0)

        def end():
            for i in range(groups):
                y_copy(i).wait()

        return start, middle, end

    shape = jax.ShapeDtypeStruct((lines, groups, r, d), BF16)
    scratch = [
        pltpu.VMEM((groups, n, block), BF16),
        pltpu.VMEM((n, d), BF16),
        pltpu.VMEM((block, n), BF16),
        pltpu.VMEM((groups, lines, r, d), BF16),
        dma(groups),
        dma(),
        dma(groups),
    ]
    return (nobody, (x, g), shape, ANY, ANY, scratch, body)


def scatter_small(x):
    fn, cn = lax.axis_size("fsdp"), lax.axis_size("ctx")

    def body(x_ref, o_ref, got, sums, got2, s1, r1, s2, r2):
        f, c = place()

        def first(j):
            t = lax.rem(f + j, fn)
            return remote(x_ref.at[t], got.at[j], s1.at[j], r1.at[j], (t, c))

        def second(j):
            t = lax.rem(c + j, cn)
            return remote(sums.at[t], got2.at[j], s2.at[j], r2.at[j], (f, t))

        def start():
            for j in range(1, fn):
                first(j).start()
            sums[...] = x_ref[f]

        def middle():
            for j in range(1, fn):
                first(j).wait_recv()
                sums[...] += got[j]
            for j in range(1, cn):
                second(j).start()
            o_ref[...] = sums[c]

        def end():
            for j in range(1, cn):
                second(j).wait_recv()
                o_ref[...] += got2[j]
            for j in range(1, fn):
                first(j).wait_send()
            for j in range(1, cn):
                second(j).wait_send()

        return start, middle, end

    tail = x.shape[2:]
    scratch = [
        pltpu.VMEM(x.shape, x.dtype),
        pltpu.VMEM(x.shape[1:], x.dtype),
        pltpu.VMEM(x.shape[1:], x.dtype),
        dma(fn),
        dma(fn),
        dma(cn),
        dma(cn),
    ]
    return (along_both, x, jax.ShapeDtypeStruct(tail, x.dtype), VMEM, VMEM, scratch, body)


def nt(a, b):
    return lax.dot_general(a, b, (((1,), (1,)), ((), ())), preferred_element_type=F32)


def nn(a, b):
    return lax.dot_general(a, b, (((1,), (0,)), ((), ())), preferred_element_type=F32)


def attend(q, k, v, starts, block=512):
    u, t, _ = q.shape
    scale = HEAD_DIM**-0.5 * LOG2E

    def kernel(q_ref, k_ref, v_ref, s_ref, o_ref, l_ref, vt):
        i = pl.program_id(1)

        @pl.when(i == 0)
        def _():
            vt[...] = v_ref[0].T

        rows = q_ref[0]
        first = s_ref[0]
        base = lax.broadcasted_iota(jnp.int32, (block, block), 0)
        qpos = i * block + lax.broadcasted_iota(jnp.int32, (1, block), 1)

        def one(j, carry, diagonal):
            peak, total, acc = carry
            at = pl.multiple_of(j * block, block)
            s = nt(k_ref[0, pl.ds(at, block)], rows) * scale
            kpos = base + at
            keep = kpos >= first
            if diagonal:
                keep = keep & (kpos <= qpos)
            s = jnp.where(keep, s, NEG_BIG)
            new = jnp.maximum(peak, jnp.max(s, axis=0, keepdims=True))
            p = jnp.exp2(s - new)
            shrink = jnp.exp2(peak - new)
            total = total * shrink + jnp.sum(p, axis=0, keepdims=True)
            acc = acc * shrink + nn(vt[:, pl.ds(at, block)], p.astype(BF16))
            return new, total, acc

        start = (
            jnp.full((1, block), NEG_BIG, F32),
            jnp.zeros((1, block), F32),
            jnp.zeros((HEAD_DIM, block), F32),
        )
        start = one(i, start, True)
        peak, total, acc = lax.fori_loop(0, i, lambda j, c: one(j, c, False), start)
        o_ref[0] = (acc / total).T.astype(BF16)
        l_ref[0] = peak + jnp.log2(total)

    return pl.pallas_call(
        kernel,
        grid=(u, t // block),
        in_specs=[
            pl.BlockSpec((1, block, HEAD_DIM), lambda a, b: (a, b, 0)),
            pl.BlockSpec((1, t, HEAD_DIM), lambda a, b: (a, 0, 0)),
            pl.BlockSpec((1, t, HEAD_DIM), lambda a, b: (a, 0, 0)),
            pl.BlockSpec((1, 1, block), lambda a, b: (a, 0, b)),
        ],
        out_specs=[
            pl.BlockSpec((1, block, HEAD_DIM), lambda a, b: (a, b, 0)),
            pl.BlockSpec((1, 1, block), lambda a, b: (a, 0, b)),
        ],
        out_shape=[
            jax.ShapeDtypeStruct((u, t, HEAD_DIM), BF16),
            jax.ShapeDtypeStruct((u, 1, t), F32),
        ],
        scratch_shapes=[pltpu.VMEM((HEAD_DIM, t), BF16)],
        compiler_params=pltpu.CompilerParams(vmem_limit_bytes=32 * 2**20),
        cost_estimate=pl.CostEstimate(
            flops=2 * u * t * t * HEAD_DIM, bytes_accessed=8 * u * t * 256, transcendentals=u * t * t // 2
        ),
    )(q, k, v, starts)


def attend_back(q, k, v, starts, lse, o, g, tables, block=512):
    u, t, _ = q.shape
    scale = HEAD_DIM**-0.5

    def kernel(
        q_ref, k_ref, v_ref, s_ref, l_ref, o_ref, g_ref, t_ref, dq_ref, dk_ref, dv_ref, kt, dk, dv
    ):
        i = pl.program_id(1)

        @pl.when(i == 0)
        def _():
            kt[...] = k_ref[0].T
            dk[...] = jnp.zeros_like(dk)
            dv[...] = jnp.zeros_like(dv)

        rows, grows = q_ref[0], g_ref[0]
        first, logs = s_ref[0], l_ref[0]
        prod = o_ref[0].astype(F32) * grows.astype(F32)
        centre = jnp.sum(prod.T, axis=0, keepdims=True)
        base = lax.broadcasted_iota(jnp.int32, (block, block), 0)
        qpos = i * block + lax.broadcasted_iota(jnp.int32, (1, block), 1)

        def one(j, acc, diagonal):
            at = pl.multiple_of(j * block, block)
            here = pl.ds(at, block)
            p = jnp.exp2(nt(k_ref[0, here], rows) * (scale * LOG2E) - logs)
            kpos = base + at
            keep = kpos >= first
            if diagonal:
                keep = keep & (kpos <= qpos)
            p = jnp.where(keep, p, 0.0)
            gp = nt(v_ref[0, here], grows)
            ds = (p * (gp - centre)).astype(BF16)
            dv[here] += nn(p.astype(BF16), grows)
            dk[here] += nn(ds, rows)
            return acc + nn(kt[:, here], ds)

        acc = one(i, jnp.zeros((HEAD_DIM, block), F32), True)
        acc = lax.fori_loop(0, i, lambda j, a: one(j, a, False), acc)
        there = pl.ds(pl.multiple_of(i * block, block), block)
        straight, right, left = t_ref[0, there], t_ref[1, there], t_ref[2, there]
        dq_ref[0] = turn((acc * scale).T, straight, -right, -left).astype(BF16)

        @pl.when(i == t // block - 1)
        def _():
            for b in range(t // block):
                at = pl.ds(b * block, block)
                dk_ref[0, at] = turn(
                    dk[at] * scale, t_ref[0, at], -t_ref[1, at], -t_ref[2, at]
                ).astype(BF16)
                dv_ref[0, at] = dv[at].astype(BF16)

    def whole(a, b):
        return (a, 0, 0)

    def part(a, b):
        return (a, b, 0)

    def row(a, b):
        return (a, 0, b)

    spec, full, line = (1, block, HEAD_DIM), (1, t, HEAD_DIM), (1, 1, block)
    return pl.pallas_call(
        kernel,
        grid=(u, t // block),
        in_specs=[
            pl.BlockSpec(spec, part),
            pl.BlockSpec(full, whole),
            pl.BlockSpec(full, whole),
            pl.BlockSpec(line, row),
            pl.BlockSpec(line, row),
            pl.BlockSpec(spec, part),
            pl.BlockSpec(spec, part),
            pl.BlockSpec((3, t, HEAD_DIM), lambda a, b: (0, 0, 0)),
        ],
        out_specs=[
            pl.BlockSpec(spec, part),
            pl.BlockSpec(full, whole),
            pl.BlockSpec(full, whole),
        ],
        out_shape=[jax.ShapeDtypeStruct((u, t, HEAD_DIM), BF16)] * 3,
        scratch_shapes=[
            pltpu.VMEM((HEAD_DIM, t), BF16),
            pltpu.VMEM((t, HEAD_DIM), F32),
            pltpu.VMEM((t, HEAD_DIM), F32),
        ],
        compiler_params=pltpu.CompilerParams(vmem_limit_bytes=48 * 2**20),
        cost_estimate=pl.CostEstimate(
            flops=5 * u * t * t * HEAD_DIM, bytes_accessed=20 * u * t * 256, transcendentals=u * t * t // 2
        ),
    )(q, k, v, starts, lse, o, g, tables)


def project(x, w, stream, bias, tables):
    count, length, width = x.shape
    cn, fn, _, rows, cols = w.shape
    heads = cols // HEAD_DIM

    def kernel(*refs):
        x_ref, w_ref, b_ref = refs[:3]
        o_ref, held, sem = refs[-3:]

        @pl.when(pl.program_id(0) == 0)
        def _():
            copies = [
                pltpu.make_async_copy(w_ref.at[:, f, stream], held.at[f], sem.at[f])
                for f in range(fn)
            ]
            for c in copies:
                c.start()
            for c in copies:
                c.wait()

        y = nn(x_ref[0], held[...].reshape(width, cols)) + b_ref[...]
        for h in range(heads):
            part = y[:, h * HEAD_DIM : (h + 1) * HEAD_DIM]
            if tables is not None:
                t_ref = refs[3]
                part = turn(part, t_ref[0], t_ref[1], t_ref[2])
            o_ref[h] = part.astype(BF16)

    extra = [] if tables is None else [tables]
    return pl.pallas_call(
        kernel,
        grid=(count,),
        in_specs=[
            pl.BlockSpec((1, length, width), lambda i: (i, 0, 0)),
            ANY,
            pl.BlockSpec((1, cols), lambda i: (0, 0)),
        ]
        + [pl.BlockSpec((3, length, HEAD_DIM), lambda i: (0, 0, 0)) for _ in extra],
        out_specs=pl.BlockSpec((heads, length, HEAD_DIM), lambda i: (i, 0, 0)),
        out_shape=jax.ShapeDtypeStruct((count * heads, length, HEAD_DIM), BF16),
        scratch_shapes=[pltpu.VMEM((fn, cn, rows, cols), BF16), dma(fn)],
        compiler_params=pltpu.CompilerParams(vmem_limit_bytes=32 * 2**20),
        cost_estimate=pl.CostEstimate(
            flops=2 * count * length * width * cols,
            bytes_accessed=2 * (count * length * (width + cols) + width * cols),
            transcendentals=0,
        ),
    )(x, w, bias, *extra)


def widen(x, w, bias, tile=256, rows_at_once=512):
    n, d = x.shape
    cn, fn, rows, cols = w.shape
    tiles = cols // tile

    def kernel(x_ref, w_ref, b_ref, a_ref, g_ref, o_ref, held, sem):
        i = pl.program_id(0)

        def copy(j, f):
            at = pl.ds(pl.multiple_of(j * tile, tile), tile)
            return pltpu.make_async_copy(w_ref.at[:, f, :, at], held.at[j, f], sem.at[j, f])

        @pl.when(i == 0)
        def _():
            for j in range(tiles):
                for f in range(fn):
                    copy(j, f).start()

        for f in range(fn):
            copy(i, f).wait()
        w_tile = held[i].reshape(d, tile)
        o_ref[...] = w_tile
        for r in range(0, n, rows_at_once):
            part = pl.ds(r, rows_at_once)
            y = nn(x_ref[part], w_tile) + b_ref[...]
            t = y * math.sqrt(0.5)
            below = 0.5 + 0.5 * lax.erf(t)
            a_ref[part] = (y * below).astype(BF16)
            density = jnp.exp(-t * t) * (1.0 / math.sqrt(2.0 * math.pi))
            g_ref[part] = (below + y * density).astype(BF16)

    column = pl.BlockSpec((n, tile), lambda i: (0, i))
    return pl.pallas_call(
        kernel,
        grid=(tiles,),
        in_specs=[
            pl.BlockSpec((n, d), lambda i: (0, 0)),
            ANY,
            pl.BlockSpec((1, tile), lambda i: (0, i)),
        ],
        out_specs=[column, column, pl.BlockSpec((d, tile), lambda i: (0, i))],
        out_shape=[
            jax.ShapeDtypeStruct((n, cols), BF16),
            jax.ShapeDtypeStruct((n, cols), BF16),
            jax.ShapeDtypeStruct((d, cols), BF16),
        ],
        scratch_shapes=[pltpu.VMEM((tiles, fn, cn, rows, tile), BF16), dma(tiles, fn)],
        compiler_params=pltpu.CompilerParams(vmem_limit_bytes=48 * 2**20),
        cost_estimate=pl.CostEstimate(
            flops=2 * n * d * cols, bytes_accessed=60_000_000, transcendentals=0
        ),
    )(x, w, bias)


def line_product(x, g, groups, lines, tile=512, shelf=None):
    n, d = g.shape
    block = x.shape[1] // groups
    r = block // lines
    tile = min(tile, d)
    held, first, count = shelf or (None, 0, groups)

    def kernel(x_ref, g_ref, *refs):
        o_ref, turned = refs[-2:]

        @pl.when(pl.program_id(1) == 0)
        def _():
            turned[...] = x_ref[...].T

        y = nn(turned[...], g_ref[...]).astype(BF16)
        o_ref[:, 0] = y.reshape(lines, r, tile)

    extra = [] if held is None else [held]
    return pl.pallas_call(
        kernel,
        grid=(groups, d // tile),
        in_specs=[
            pl.BlockSpec((n, block), lambda i, j: (0, i)),
            pl.BlockSpec((n, tile), lambda i, j: (0, j)),
        ]
        + [ANY] * len(extra),
        out_specs=pl.BlockSpec((lines, 1, r, tile), lambda i, j: (0, first + i, 0, j)),
        out_shape=jax.ShapeDtypeStruct((lines, count, r, d), BF16),
        scratch_shapes=[pltpu.VMEM((block, n), BF16)],
        input_output_aliases={2: 0} if extra else {},
        compiler_params=pltpu.CompilerParams(vmem_limit_bytes=48 * 2**20),
        cost_estimate=pl.CostEstimate(
            flops=2 * n * d * x.shape[1],
            bytes_accessed=2 * (n * d + n * x.shape[1] + d * x.shape[1]),
            transcendentals=0,
        ),
    )(x, g, *extra)


def front(hist, mix, gain, shift, tokens=32, wide=128):
    h, n, d = hist.shape
    rest = gain.shape[0]

    def kernel(h_ref, m_ref, g_ref, b_ref, s_ref, *n_refs):
        for start in range(0, tokens, 16):
            t = slice(start, start + 16)
            m = m_ref[t]
            across = [jnp.broadcast_to(m[:, i : i + 1], (16, wide)) for i in range(4 * h)]
            for at in range(0, d, wide):
                cut = slice(at, at + wide)
                rows = [h_ref[j, t, cut].astype(F32) for j in range(h)]
                for s in range(4):
                    acc = across[s * h] * rows[0]
                    for j in range(1, h):
                        acc += across[s * h + j] * rows[j]
                    s_ref[s, t, cut] = acc
            for s in range(rest):
                x = s_ref[s, t]
                centre = x - jnp.mean(x, axis=-1, keepdims=True)
                spread = jnp.mean(centre * centre, axis=-1, keepdims=True)
                y = centre * lax.rsqrt(spread + EPS_NORM) * g_ref[s : s + 1] + b_ref[s : s + 1]
                n_refs[s][t] = y.astype(BF16)

    return pl.pallas_call(
        kernel,
        grid=(n // tokens,),
        in_specs=[
            pl.BlockSpec((h, tokens, d), lambda i: (0, i, 0)),
            pl.BlockSpec((tokens, 128), lambda i: (i, 0)),
            pl.BlockSpec((rest, d), lambda i: (0, 0)),
            pl.BlockSpec((rest, d), lambda i: (0, 0)),
        ],
        out_specs=[
            pl.BlockSpec((4, tokens, d), lambda i: (0, i, 0)),
        ]
        + [pl.BlockSpec((tokens, d), lambda i: (i, 0))] * rest,
        out_shape=[jax.ShapeDtypeStruct((4, n, d), F32)]
        + [jax.ShapeDtypeStruct((n, d), BF16)] * rest,
        compiler_params=pltpu.CompilerParams(vmem_limit_bytes=60 * 2**20),
        cost_estimate=pl.CostEstimate(
            flops=2 * 4 * h * n * d, bytes_accessed=n * d * (2 * h + 22), transcendentals=0
        ),
    )(hist, mix, gain, shift)


def last(hist, mix, streams, gain, grads, grad_hidden, tokens=32, wide=256):
    h, n, d = hist.shape
    rest = gain.shape[0]

    def kernel(h_ref, m_ref, s_ref, g_ref, d0, d1, d2, r_ref, gh_ref, gm_ref, gg_ref, gb_ref, ds):
        @pl.when(pl.program_id(0) == 0)
        def _():
            gg_ref[...] = jnp.zeros_like(gg_ref)
            gb_ref[...] = jnp.zeros_like(gb_ref)

        for start in range(0, tokens, 16):
            t = slice(start, start + 16)
            for s, d_ref in enumerate((d0, d1, d2)):
                x = s_ref[s, t]
                centre = x - jnp.mean(x, axis=-1, keepdims=True)
                inverse = lax.rsqrt(jnp.mean(centre * centre, axis=-1, keepdims=True) + EPS_NORM)
                unit = centre * inverse
                dn = d_ref[t]
                gg_ref[s : s + 1] += jnp.sum(dn * unit, axis=0, keepdims=True)
                gb_ref[s : s + 1] += jnp.sum(dn, axis=0, keepdims=True)
                du = dn * g_ref[s : s + 1]
                ds[s] = inverse * (
                    du
                    - jnp.mean(du, axis=-1, keepdims=True)
                    - unit * jnp.mean(du * unit, axis=-1, keepdims=True)
                )
            ds[rest] = r_ref[t]
            m = m_ref[t]
            across = [jnp.broadcast_to(m[:, i : i + 1], (16, 128)) for i in range(4 * h)]
            sums = [[jnp.zeros((16, 128), F32) for _ in range(h)] for _ in range(4)]
            for at in range(0, d, wide):
                cuts = [slice(b, b + 128) for b in range(at, at + wide, 128)]
                parts = [[ds[s, :, cut] for cut in cuts] for s in range(4)]
                for j in range(h):
                    for i, cut in enumerate(cuts):
                        acc = across[j] * parts[0][i]
                        for s in range(1, 4):
                            acc += across[s * h + j] * parts[s][i]
                        gh_ref[j, t, cut] = acc
                    rows = [h_ref[j, t, cut].astype(F32) for cut in cuts]
                    for s in range(4):
                        prod = rows[0] * parts[s][0]
                        for i in range(1, len(cuts)):
                            prod += rows[i] * parts[s][i]
                        sums[s][j] += prod
            lane = lax.broadcasted_iota(jnp.int32, (16, 128), 1)
            total = jnp.zeros((16, 128), F32)
            for s in range(4):
                for j in range(h):
                    value = jnp.sum(sums[s][j], axis=-1, keepdims=True)
                    total = jnp.where(lane == s * h + j, value, total)
            gm_ref[t] = total

    row = pl.BlockSpec((tokens, d), lambda i: (i, 0))
    lines = pl.BlockSpec((rest, d), lambda i: (0, 0))
    return pl.pallas_call(
        kernel,
        grid=(n // tokens,),
        in_specs=[
            pl.BlockSpec((h, tokens, d), lambda i: (0, i, 0)),
            pl.BlockSpec((tokens, 128), lambda i: (i, 0)),
            pl.BlockSpec((rest, tokens, d), lambda i: (0, i, 0)),
            lines,
            row,
            row,
            row,
            row,
        ],
        out_specs=[
            pl.BlockSpec((h, tokens, d), lambda i: (0, i, 0)),
            pl.BlockSpec((tokens, 128), lambda i: (i, 0)),
            lines,
            lines,
        ],
        out_shape=[
            jax.ShapeDtypeStruct((h, n, d), F32),
            jax.ShapeDtypeStruct((n, 128), F32),
            jax.ShapeDtypeStruct((rest, d), F32),
            jax.ShapeDtypeStruct((rest, d), F32),
        ],
        scratch_shapes=[pltpu.VMEM((4, 16, d), F32)],
        compiler_params=pltpu.CompilerParams(vmem_limit_bytes=60 * 2**20),
        cost_estimate=pl.CostEstimate(
            flops=4 * 4 * h * n * d, bytes_accessed=n * d * (6 * h + 32), transcendentals=0
        ),
    )(hist, mix, streams, gain, *grads, grad_hidden)


def body(
    history,
    dense_mix,
    doc_starts,
    norm_gain,
    norm_bias,
    qkv_weight,
    qkv_bias,
    out_weight,
    out_bias,
    up_weight,
    up_bias,
    down_weight,
    down_bias,
    root_gain,
    mix_in_weight,
    mix_out_weight,
    mix_out_bias,
    out_cotangent,
    mix_cotangent,
):
    fn, cn = lax.axis_size("fsdp"), lax.axis_size("ctx")
    dn = fn * cn
    fi, ci = lax.axis_index("fsdp"), lax.axis_index("ctx")
    hist, seqs, length, width = history.shape
    nloc = seqs * length
    ntp = fn * nloc
    rows = qkv_weight.shape[0]
    ff = up_weight.shape[1]
    wcol, pcol = width // fn, ff // (2 * fn)
    count = cn // 2
    lo = lax.rem(ci, 2)
    lines = [list(range(b, cn, 2)) for b in range(2)]
    heads = wcol // HEAD_DIM
    units = fn * seqs * heads // cn
    total = cn * length
    mixn = mix_in_weight.shape[1]

    def line_gather(w):
        return lax.all_gather(w, "ctx", axis=0, axis_index_groups=lines)

    parts = [
        norm_gain,
        norm_bias,
        qkv_bias,
        out_bias,
        up_bias,
        down_bias,
        root_gain,
        mix_in_weight,
        doc_starts.astype(F32),
    ]
    flat = jnp.concatenate([a.reshape(-1) for a in parts])
    flat = jnp.pad(flat, (0, -flat.size % 1024)).reshape(-1, 128)
    wout = lax.all_gather(out_weight, "ctx", axis=0, tiled=True)
    flats, qkv_cols = comm(
        1,
        gather_small(flat),
        exchange_fsdp(qkv_weight.reshape(rows, 3, fn, wcol).transpose(2, 1, 0, 3)),
    )
    flats = flats.reshape(dn, -1)
    pieces, at = [], 0
    for a in parts:
        pieces.append(flats[:, at : at + a.size])
        at += a.size

    def joined(piece, lead):
        return piece.reshape(dn, lead, -1).transpose(1, 0, 2).reshape(lead, -1)

    gain_all = joined(pieces[0], 4)
    shift_all = joined(pieces[1], 4)
    qkv_shift = joined(pieces[2], 3)
    out_shift = pieces[3].reshape(-1)
    up_shift = pieces[4].reshape(-1)
    down_shift = pieces[5].reshape(-1)
    root_full = pieces[6].reshape(-1)
    mix_in_full = pieces[7].reshape(width, mixn)
    starts = pieces[8].reshape(fn, cn, seqs, -1)[:, 0].astype(jnp.int32)

    hist2 = history.reshape(hist, nloc, width)
    mix2 = dense_mix.reshape(dense_mix.shape[0], hist, nloc)
    mixes = jnp.pad(mix2.reshape(-1, nloc).T, ((0, 0), (0, 128 - mix2.shape[0] * hist)))
    streams, *normed = front(hist2, mixes, gain_all[:3], shift_all[:3])

    bias_cols = lax.dynamic_slice_in_dim(qkv_shift, fi * wcol, wcol, 1)
    tables = rotary_tables(total)
    tables_l = lax.dynamic_slice_in_dim(tables, ci * length, length, 1)

    def projected(x, w, at, s):
        y = project(
            x.reshape(fn * seqs, length, width),
            w,
            at,
            bias_cols[s : s + 1],
            tables_l if s < 2 else None,
        )
        return y.reshape(cn, units, length, HEAD_DIM)

    def whole_units(x):
        return x.reshape(units, total, HEAD_DIM)

    def from_units(x):
        return exchange_ctx(x.reshape(units, cn, length, HEAD_DIM), False)

    def columns(x):
        x = x.reshape(fn * seqs, heads, length, HEAD_DIM)
        return x.transpose(0, 2, 1, 3).reshape(ntp, wcol)

    w01, g0 = comm(9, gather_ctx(qkv_cols[:, :2]), gather_fsdp(normed[0]))
    g0, cols_2, wout = lax.optimization_barrier((g0, qkv_cols[:, 2], wout))
    w2 = lax.all_gather(cols_2, "ctx", axis=0)
    p0 = projected(g0, w01, 0, 0)
    q_u, g1 = comm(4, exchange_ctx(p0, True), gather_fsdp(normed[1]))
    p1 = projected(g1, w01, 1, 1)
    p1, down_rows = lax.optimization_barrier((p1, down_weight))
    wdown = line_gather(down_rows).reshape(pcol, width)
    k_u, g2 = comm(4, exchange_ctx(p1, True), gather_fsdp(normed[2]))
    p2 = projected(g2, w2[:, :, None], 0, 2)
    v_u, up_cols = comm(
        11,
        exchange_ctx(p2, True),
        exchange_plane(
            up_weight.reshape(rows, fn, count, 2, -1).transpose(1, 3, 0, 2, 4).reshape(fn, 2, rows, pcol),
            plane_sides,
        ),
    )
    up_g = line_gather(up_cols).reshape(count, fn, 2 * rows, pcol)
    wqkv = [w.transpose(1, 0, 2, 3).reshape(width, wcol) for w in (w01[:, :, 0], w01[:, :, 1], w2)]
    q_u, k_u, v_u = whole_units(q_u), whole_units(k_u), whole_units(v_u)
    normed_g = [g.reshape(ntp, width) for g in (g0, g1, g2)]

    pos_all = jnp.arange(total, dtype=jnp.int32)
    unit_ids = ci * units + jnp.arange(units, dtype=jnp.int32)
    seq_ids = unit_ids // heads
    unit_starts = starts.reshape(fn * seqs, -1)[seq_ids]
    first_key = jnp.max(
        jnp.where(unit_starts[:, None, :] <= pos_all[None, :, None], unit_starts[:, None, :], 0),
        axis=-1,
    )[:, None, :]
    att_u, lse_u = attend(q_u, k_u, v_u, first_key)
    attended = columns(comm(6, from_units(att_u))[0])
    attended, wdown = lax.optimization_barrier((attended, wdown))

    def scatter_tokens(x):
        return comm(10, scatter_fsdp(x.astype(BF16).reshape(fn, nloc, width)))[0]

    def gather_tokens(x):
        return comm(3, gather_fsdp(x))[0].reshape(ntp, width)

    def scatter_plane_tokens(x):
        return comm(13, scatter_plane(x.astype(BF16).reshape(fn, 2, nloc, width)))[0]

    def gather_plane_tokens(x):
        return comm(14, gather_plane(x))[0].reshape(2 * ntp, width)

    hidden_res = streams[3] + scatter_tokens(dot("nd,de->ne", attended, wout)) + out_shift
    normed_mlp, mid_pull = jax.vjp(layer_norm, hidden_res, gain_all[3], shift_all[3])
    mlp_g = gather_plane_tokens(normed_mlp.astype(BF16))
    up_bias_cols = lax.dynamic_slice(
        up_shift.reshape(fn, count, 2, -1), (fi, 0, lo, 0), (1, count, 1, ff // dn)
    ).reshape(pcol)
    act_low, slope, wup = widen(mlp_g, up_g, up_bias_cols[None])
    result = hidden_res + scatter_plane_tokens(dot("nf,fd->nd", act_low, wdown)) + down_shift
    block_out = result.astype(BF16).reshape(seqs, length, width)

    next_rows, mixer_pull = jax.vjp(
        mixer, result, root_full, mix_in_full, mix_out_weight, mix_out_bias
    )
    next_mix = next_rows.T.reshape(-1, seqs, length)
    grad_result, grad_root, grad_mix_in, grad_mix_out, grad_mix_bias = mixer_pull(
        mix_cotangent.reshape(-1, nloc).T
    )
    grad_result = grad_result + out_cotangent.reshape(nloc, width).astype(F32)

    grad_branch = grad_result.astype(BF16)
    branch_g = gather_plane_tokens(grad_branch)
    grad_down_shift = jnp.sum(grad_branch.astype(F32), axis=0)

    def line_scatter(x):
        y = lax.psum_scatter(
            x.reshape(-1, x.shape[-1]),
            "ctx",
            scatter_dimension=0,
            axis_index_groups=lines,
            tiled=True,
        )
        return y.reshape(x.shape[1:])

    down_part = dot("nf,nd->fd", act_low, branch_g).astype(BF16)
    down_part, wdown = lax.optimization_barrier((down_part, wdown))
    grad_down = line_scatter(down_part.reshape(count, -1, width))
    grad_active = dot("nd,fd->nf", branch_g, wdown)
    grad_upward = (grad_active * slope.astype(F32)).astype(BF16)
    grad_up_shift = jnp.sum(grad_upward.astype(F32), axis=0)
    mlp_part = dot("nf,df->nd", grad_upward, wup).astype(BF16)
    grad_mlp, up_part = comm(
        17,
        scatter_plane(mlp_part.reshape(fn, 2, nloc, width)),
        product_beside(mlp_g, grad_upward, fn, count),
    )
    up_part, grad_mlp = lax.optimization_barrier((up_part, grad_mlp))
    grad_up = line_scatter(up_part.reshape(count, -1, pcol))
    grad_hidden, grad_gain_mid, grad_shift_mid = mid_pull(grad_mlp)
    grad_hidden = grad_hidden + grad_result
    grad_attn = grad_hidden.astype(BF16)
    grad_out_shift = jnp.sum(grad_attn.astype(F32), axis=0)
    attn_g = gather_tokens(grad_attn)
    out_part = dot("nd,ne->de", attended, attn_g).astype(BF16)
    grad_att = dot("ne,de->nd", attn_g, wout).astype(BF16)
    grad_att = grad_att.reshape(fn * seqs, length, heads, HEAD_DIM).transpose(0, 2, 1, 3)
    out_part = out_part.reshape(count, 2, rows, width)
    out_away = lax.dynamic_index_in_dim(out_part, 1 - lo, 1, keepdims=False)
    out_away, grad_att = lax.optimization_barrier((out_away, grad_att))
    g_u, out_come = comm(
        16,
        exchange_ctx(grad_att.reshape(cn, units, length, HEAD_DIM), True),
        exchange_pair(out_away),
    )
    out_half = lax.dynamic_index_in_dim(out_part, lo, 1, keepdims=False).astype(F32)
    out_half = (out_half + out_come.astype(F32)).astype(BF16)
    g_u, grad_down, out_half = lax.optimization_barrier((g_u, grad_down, out_half))

    def ctx_scatter(x):
        return lax.psum_scatter(x, "ctx", scatter_dimension=0, tiled=True)

    grad_out = line_scatter(out_half)

    gq, gk, gv = attend_back(q_u, k_u, v_u, first_key, lse_u, att_u, whole_units(g_u), tables)

    def back_part(p, s):
        return dot("nc,dc->nd", p, wqkv[s]).astype(BF16).reshape(fn, nloc, width)

    grad_up = grad_up.reshape(fn, 2, rows, pcol)
    if ff // dn % 128 == 0:
        gp0, grad_up = comm(12, from_units(gq), exchange_columns(grad_up, ff // dn, plane_sides))
    else:
        gp0, grad_up = comm(12, from_units(gq), exchange_plane(grad_up, plane_sides))
        grad_up = grad_up.reshape(fn, 2, rows, count, -1).transpose(2, 0, 3, 1, 4)
        grad_up = grad_up.reshape(rows, ff)
    gp0 = columns(gp0)
    q_part = line_product(normed_g[0], gp0, fn, cn)
    q_part, gk = lax.optimization_barrier((q_part, gk))
    grad_q = ctx_scatter(q_part.reshape(-1, wcol)).reshape(fn, rows, wcol)
    gp1, gn0 = comm(8, from_units(gk), scatter_fsdp(back_part(gp0, 0)))
    gp1, grad_out = lax.optimization_barrier((gp1, grad_out))
    gp1 = columns(gp1)
    gp2, gn1 = comm(8, from_units(gv), scatter_fsdp(back_part(gp1, 1)))
    gp2 = columns(gp2)
    kv_part = line_product(normed_g[1], gp1, fn, cn, shelf=(None, 0, 2 * fn))
    kv_part = line_product(normed_g[2], gp2, fn, cn, shelf=(kv_part, fn, 2 * fn))
    kv_part, gp2 = lax.optimization_barrier((kv_part, gp2))
    grad_kv = ctx_scatter(kv_part.reshape(-1, wcol)).reshape(2, fn, rows, wcol)
    grad_q, gn2 = comm(
        7,
        exchange_fsdp(grad_q),
        scatter_fsdp(back_part(gp2, 2)),
    )
    grad_proj = (gp0, gp1, gp2)
    grad_qkv_shift = jnp.stack([jnp.sum(g.astype(F32), axis=0) for g in grad_proj])

    grad_history, grad_mix, grad_gain_front, grad_shift_front = last(
        hist2, mixes, streams, gain_all[:3], (gn0, gn1, gn2), grad_hidden
    )
    grad_history = grad_history.reshape(history.shape)
    grad_mix = grad_mix[:, : mix2.shape[0] * hist].T.reshape(dense_mix.shape)

    def own_columns(x, full):
        zero = jnp.zeros((x.shape[0], full), F32)
        return lax.dynamic_update_slice_in_dim(zero, x, fi * x.shape[1], 1)

    lines_14 = [
        grad_gain_front,
        grad_gain_mid[None],
        grad_shift_front,
        grad_shift_mid[None],
        own_columns(grad_qkv_shift, width),
        grad_out_shift[None],
        grad_down_shift[None],
        grad_root[None],
    ]
    lines_14 = jnp.concatenate(lines_14, axis=0)
    up_lines = lax.dynamic_update_slice(
        jnp.zeros((fn, count, 2, ff // dn), F32),
        grad_up_shift.reshape(1, count, 1, -1),
        (fi, 0, lo, 0),
    ).reshape(dn, -1)
    same = jnp.concatenate([grad_mix_out.reshape(-1), grad_mix_bias])
    flat = jnp.concatenate(
        [
            lines_14.reshape(-1, dn, width // dn).transpose(1, 0, 2).reshape(dn, -1),
            up_lines,
            grad_mix_in.reshape(dn, -1),
            jnp.broadcast_to(same[None], (dn, same.size)),
        ],
        axis=1,
    )
    flat = jnp.pad(flat, ((0, 0), (0, -flat.shape[1] % 1024)))
    (small,) = comm(2, scatter_small(flat.reshape(fn, cn, -1, 128)))
    small = small.reshape(-1)
    out_small, at = [], 0
    order = [norm_gain, norm_bias, qkv_bias, out_bias, down_bias, root_gain, up_bias, mix_in_weight]
    for a in order:
        out_small.append(small[at : at + a.size].reshape(a.shape))
        at += a.size
    mix_sums = small[at : at + same.size]
    cut = grad_mix_out.size
    out_small += [mix_sums[:cut].reshape(grad_mix_out.shape), mix_sums[cut:]]
    out_small, grad_kv = lax.optimization_barrier((out_small, grad_kv))
    (g_gain, g_shift, g_qkv_b, g_out_b, g_down_b, g_root, g_up_b, g_mix_in) = out_small[:-2]
    grad_k, grad_v = comm(15, exchange_fsdp(grad_kv[0]), exchange_fsdp(grad_kv[1]))
    grad_qkv = jnp.stack([grad_q, grad_k, grad_v])
    grad_qkv = grad_qkv.transpose(2, 0, 1, 3).reshape(rows, 3, width).astype(F32)
    return (
        block_out,
        next_mix,
        grad_history,
        grad_mix,
        g_gain,
        g_shift,
        grad_qkv,
        g_qkv_b,
        grad_out.astype(F32),
        g_out_b,
        grad_up.astype(F32),
        g_up_b,
        grad_down.astype(F32),
        g_down_b,
        g_root,
        g_mix_in,
        out_small[-2],
        out_small[-1],
    )


def solution(mesh):
    token = P(None, "fsdp", "ctx")
    both = P(BOTH)
    cols = P(None, BOTH)
    placed = (
        token,
        P(None, None, "fsdp", "ctx"),
        P("fsdp"),
        cols,
        cols,
        both,
        cols,
        both,
        both,
        both,
        both,
        both,
        both,
        both,
        both,
        P(),
        P(),
        P("fsdp", "ctx"),
        token,
    )
    outs = (
        P("fsdp", "ctx"),
        token,
        token,
        P(None, None, "fsdp", "ctx"),
        cols,
        cols,
        both,
        cols,
        both,
        both,
        both,
        both,
        both,
        both,
        both,
        both,
        P(),
        P(),
    )
    return jax.shard_map(body, mesh=mesh, in_specs=placed, out_specs=outs, check_vma=False)
```

```python
import math

import jax
import jax.numpy as jnp
import numpy as np
from jax import lax
from jax.experimental import pallas as pl
from jax.experimental.pallas import tpu as pltpu
from jax.sharding import PartitionSpec as P

HEAD_DIM = 128
ROT = 32
TOP_PRECISION = lax.Precision.HIGHEST
EPS_NORM = 1e-05
EPS_ROOT = 1e-06
NEG_BIG = -1e30
BOTH = ("fsdp", "ctx")
BF16 = jnp.bfloat16
F32 = jnp.float32
MESH = pl.DeviceIdType.MESH
ANY = pl.BlockSpec(memory_space=pl.ANY)
VMEM = pl.BlockSpec(memory_space=pltpu.VMEM)
LOG2E = 1.4426950408889634


def layer_norm(values, gain_row, shift_row):
    centre = values - jnp.mean(values, axis=-1, keepdims=True)
    spread = jnp.mean(centre * centre, axis=-1, keepdims=True)
    return centre * lax.rsqrt(spread + EPS_NORM) * gain_row + shift_row


def gelu(values):
    return jax.nn.gelu(values, approximate=False)


def rotary_tables(count):
    half = ROT // 2
    frequency = np.exp(np.arange(half, dtype=np.float32) * np.float32(-2.0 * math.log(10000.0) / ROT))
    angles = np.arange(count, dtype=np.float32)[:, None] * frequency.astype(np.float32)[None, :]
    cosine = jnp.asarray(np.cos(angles.astype(np.float64)), F32)
    sine = jnp.asarray(np.sin(angles.astype(np.float64)), F32)
    zero, rest = jnp.zeros_like(sine), HEAD_DIM - ROT
    return jnp.stack(
        [
            jnp.pad(jnp.concatenate([cosine, cosine], 1), ((0, 0), (0, rest)), constant_values=1.0),
            jnp.pad(jnp.concatenate([zero, sine], 1), ((0, 0), (0, rest))),
            jnp.pad(jnp.concatenate([-sine, zero], 1), ((0, 0), (0, rest))),
        ]
    )


def turn(x, straight, right, left):
    half = ROT // 2
    return (
        x * straight
        + pltpu.roll(x, half, axis=1) * right
        + pltpu.roll(x, HEAD_DIM - half, axis=1) * left
    )


def mixer(rows, gain_row, opening, closing, closing_bias):
    inverse_rms = lax.rsqrt(jnp.mean(rows * rows, axis=-1, keepdims=True) + EPS_ROOT)
    rooted = rows * inverse_rms * gain_row
    hidden = jnp.dot(rooted, opening, precision=TOP_PRECISION)
    return jnp.dot(gelu(hidden), closing, precision=TOP_PRECISION) + closing_bias


def dot(pattern, left, right):
    return jnp.einsum(pattern, left, right, preferred_element_type=F32)


def remote(src, dst, send_sem, recv_sem, target):
    return pltpu.make_async_remote_copy(
        src_ref=src,
        dst_ref=dst,
        send_sem=send_sem,
        recv_sem=recv_sem,
        device_id=target,
        device_id_type=MESH,
    )


def place():
    return lax.axis_index("fsdp"), lax.axis_index("ctx")


def links_and_twin():
    chips = lax.axis_size("fsdp") // 2
    f, c = place()
    chip, core = f // 2, lax.rem(f, 2)
    return [(lax.rem(chip + j, chips) * 2 + core, c) for j in range(1, chips)] + [
        (chip * 2 + 1 - core, c)
    ]


def along_ctx():
    cn = lax.axis_size("ctx")
    f, c = place()
    return [(f, lax.rem(c + j, cn)) for j in range(1, cn)]


def along_fsdp():
    fn = lax.axis_size("fsdp")
    f, c = place()
    return [(lax.rem(f + j, fn), c) for j in range(1, fn)]


def along_both():
    return along_ctx() + along_fsdp()


def comm(cid, *tasks):
    n = len(tasks)
    counts = [len(t[5]) for t in tasks]
    given = [t[1] if isinstance(t[1], tuple) else (t[1],) for t in tasks]
    many = sum(len(g) for g in given)
    limit = 6 * 2**20
    for t in tasks:
        for x in t[5]:
            if x.dtype in (BF16, F32):
                limit += math.prod(x.shape) * jnp.dtype(x.dtype).itemsize

    def kernel(*refs):
        targets, seen = [], []
        covered = [
            (along_fsdp, [along_both]),
            (the_pair, [along_ctx]),
            (the_pair, [plane_others]),
            (links_and_twin, [plane_others]),
            (links_and_twin, [along_fsdp]),
        ]
        for t in tasks:
            if t[0] not in seen and (t[0], seen[:1]) not in covered:
                seen.append(t[0])
                targets += t[0]()
        barrier = pltpu.get_barrier_semaphore()
        for t in targets:
            pl.semaphore_signal(barrier, inc=1, device_id=t, device_id_type=MESH)
        pl.semaphore_wait(barrier, len(targets))
        inputs, scratch = list(refs[:many]), list(refs[many + n :])
        phases = []
        for i, t in enumerate(tasks):
            mine, scratch = scratch[: counts[i]], scratch[counts[i] :]
            own, inputs = inputs[: len(given[i])], inputs[len(given[i]) :]
            phases.append(t[6](*own, refs[many + i], *mine))
        for p in range(3):
            for ph in phases:
                ph[p]()

    out = pl.pallas_call(
        kernel,
        out_shape=[t[2] for t in tasks],
        in_specs=[t[3] for t, g in zip(tasks, given, strict=True) for _ in g],
        out_specs=[t[4] for t in tasks],
        scratch_shapes=[x for t in tasks for x in t[5]],
        compiler_params=pltpu.CompilerParams(
            collective_id=cid, has_side_effects=True, vmem_limit_bytes=limit
        ),
        cost_estimate=pl.CostEstimate(flops=0, bytes_accessed=15_000_000, transcendentals=0),
    )(*[x for g in given for x in g])
    return out


def dma(*shape):
    return pltpu.SemaphoreType.DMA(shape)


def gather_small(x):
    fn, cn = lax.axis_size("fsdp"), lax.axis_size("ctx")

    def body(x_ref, o_ref, s1, r1, s2, r2):
        f, c = place()

        def first(j):
            return remote(
                x_ref, o_ref.at[f, c], s1.at[j], r1.at[j], (f, lax.rem(c + j, cn))
            )

        def second(j):
            return remote(
                o_ref.at[f], o_ref.at[f], s2.at[j], r2.at[j], (lax.rem(f + j, fn), c)
            )

        def start():
            for j in range(1, cn):
                first(j).start()
            o_ref[f, c] = x_ref[...]

        def middle():
            for j in range(1, cn):
                there = o_ref.at[f, lax.rem(c + cn - j, cn)]
                remote(there, there, s1.at[j], r1.at[j], (f, lax.rem(c + j, cn))).wait_recv()
            for j in range(1, fn):
                second(j).start()

        def end():
            for j in range(1, fn):
                there = o_ref.at[lax.rem(f + fn - j, fn)]
                remote(there, there, s2.at[j], r2.at[j], (lax.rem(f + j, fn), c)).wait_recv()
            for j in range(1, cn):
                first(j).wait_send()
            for j in range(1, fn):
                second(j).wait_send()

        return start, middle, end

    shape = jax.ShapeDtypeStruct((fn, cn, *x.shape), x.dtype)
    return (along_both, x, shape, VMEM, VMEM, [dma(cn), dma(cn), dma(fn), dma(fn)], body)


def exchange_fsdp(x):
    fn = lax.axis_size("fsdp")

    def body(x_ref, o_ref, s, r, own):
        f, c = place()

        def copy(j, slot):
            t = lax.rem(f + j, fn)
            return remote(x_ref.at[t], o_ref.at[slot], s.at[j], r.at[j], (t, c))

        mine = pltpu.make_async_copy(x_ref.at[f], o_ref.at[f], own)

        def start():
            for j in range(1, fn):
                copy(j, f).start()
            mine.start()

        def end():
            mine.wait()
            for j in range(1, fn):
                copy(j, lax.rem(f + fn - j, fn)).wait_recv()
            for j in range(1, fn):
                copy(j, f).wait_send()

        return start, lambda: None, end

    shape = jax.ShapeDtypeStruct(x.shape, x.dtype)
    return (along_fsdp, x, shape, ANY, ANY, [dma(fn), dma(fn), dma()], body)


def exchange_ctx(x, to_units):
    cn = lax.axis_size("ctx")
    lead = x.shape[1] if to_units else x.shape[0]

    def body(x_ref, o_ref, s, r, own):
        f, c = place()

        def source(t):
            return x_ref.at[t] if to_units else x_ref.at[:, t]

        def target(slot):
            return o_ref.at[:, slot] if to_units else o_ref.at[slot]

        def copy(j, slot):
            t = lax.rem(c + j, cn)
            return remote(source(t), target(slot), s.at[j], r.at[j], (f, t))

        mine = pltpu.make_async_copy(source(c), target(c), own)

        def start():
            for j in range(1, cn):
                copy(j, c).start()
            mine.start()

        def end():
            mine.wait()
            for j in range(1, cn):
                copy(j, lax.rem(c + cn - j, cn)).wait_recv()
            for j in range(1, cn):
                copy(j, c).wait_send()

        return start, lambda: None, end

    dims = (lead, cn) if to_units else (cn, lead)
    shape = jax.ShapeDtypeStruct((*dims, *x.shape[2:]), x.dtype)
    return (along_ctx, x, shape, ANY, ANY, [dma(cn), dma(cn), dma()], body)


def the_pair():
    f, c = place()
    return [(f, c // 2 * 2 + 1 - lax.rem(c, 2))]


def exchange_pair(x):
    def body(x_ref, o_ref, s, r):
        (pair,) = the_pair()
        copy = remote(x_ref, o_ref, s, r, pair)
        return copy.start, lambda: None, copy.wait

    shape = jax.ShapeDtypeStruct(x.shape, x.dtype)
    return (the_pair, x, shape, ANY, ANY, [dma(), dma()], body)


def gather_fsdp(x, parts=4):
    fn = lax.axis_size("fsdp")
    chips = fn // 2
    n, d = x.shape
    step = n // parts
    pieces = [pl.ds(p * step, step) for p in range(parts)]

    def body(x_ref, o_ref, own_sem, s_link, r_link, s_core, r_core):
        f, c = place()
        chip, core = f // 2, lax.rem(f, 2)
        twin = (chip * 2 + 1 - core, c)
        links, cores = {}, {}

        def to(j):
            return (lax.rem(chip + j, chips) * 2 + core, c)

        def slot(j, core_id):
            return lax.rem(chip + chips - j, chips) * 2 + core_id

        own = pltpu.make_async_copy(x_ref, o_ref.at[f], own_sem)

        def start():
            for i, rows in enumerate(pieces):
                here, there = x_ref.at[rows], o_ref.at[f, rows]
                for j in range(1, chips):
                    links[i, j] = remote(here, there, s_link.at[j, i], r_link.at[j, i], to(j))
                    links[i, j].start()
            for i, rows in enumerate(pieces):
                here, there = x_ref.at[rows], o_ref.at[f, rows]
                cores[i, 0] = remote(here, there, s_core.at[0, i], r_core.at[0, i], twin)
                cores[i, 0].start()
            own.start()

        def middle():
            for i, rows in enumerate(pieces):
                for j in range(1, chips):
                    here = o_ref.at[slot(j, core), rows]
                    remote(here, here, s_link.at[j, i], r_link.at[j, i], to(j)).wait_recv()
                    cores[i, j] = remote(here, here, s_core.at[j, i], r_core.at[j, i], twin)
                    cores[i, j].start()

        def end():
            own.wait()
            for i, rows in enumerate(pieces):
                for j in range(chips):
                    there = o_ref.at[slot(j, 1 - core), rows]
                    cores[i, j].wait_send()
                    remote(there, there, s_core.at[j, i], r_core.at[j, i], twin).wait_recv()
                for j in range(1, chips):
                    links[i, j].wait_send()

        return start, middle, end

    shape = jax.ShapeDtypeStruct((fn, n, d), x.dtype)
    return (links_and_twin, x, shape, ANY, ANY, [dma()] + [dma(chips, parts)] * 4, body)


def gather_ctx(x):
    cn = lax.axis_size("ctx")
    count = cn // 2

    def body(x_ref, o_ref, own_sem, s_up, r_up, s_down, r_down, s_pair, r_pair):
        f, c = place()
        hi, lo = c // 2, lax.rem(c, 2)
        pair = (f, hi * 2 + 1 - lo)
        above = (f, lax.rem(hi + 1, count) * 2 + lo)
        below = (f, lax.rem(hi + count - 1, count) * 2 + lo)
        own = pltpu.make_async_copy(x_ref, o_ref.at[c], own_sem)

        def low(d):
            return lax.rem(hi + count - d, count)

        def high(d):
            return lax.rem(hi + d, count)

        def up(d):
            source = x_ref if d == 0 else o_ref.at[low(d) * 2 + lo]
            return remote(source, o_ref.at[low(d) * 2 + lo], s_up.at[d], r_up.at[d + 1], above)

        def down(d):
            source = x_ref if d == 0 else o_ref.at[high(d) * 2 + lo]
            return remote(
                source, o_ref.at[high(d) * 2 + lo], s_down.at[d], r_down.at[d + 1], below
            )

        def across(k, slot):
            source = x_ref if k == 0 else o_ref.at[slot * 2 + lo]
            return remote(source, o_ref.at[slot * 2 + lo], s_pair.at[k], r_pair.at[k], pair)

        def start():
            pl.when(hi < count - 1)(lambda: up(0).start())
            pl.when(hi > 0)(lambda: down(0).start())
            across(0, hi).start()
            own.start()

        def middle():
            for d in range(1, count):

                @pl.when(hi >= d)
                def _():
                    here = o_ref.at[low(d) * 2 + lo]
                    remote(here, here, s_up.at[d], r_up.at[d], above).wait_recv()
                    across(d, low(d)).start()
                    if d < count - 1:
                        pl.when(hi < count - 1)(lambda: up(d).start())

                @pl.when(hi + d < count)
                def _():
                    here = o_ref.at[high(d) * 2 + lo]
                    remote(here, here, s_down.at[d], r_down.at[d], below).wait_recv()
                    across(count - d, high(d)).start()
                    if d < count - 1:
                        pl.when(hi > 0)(lambda: down(d).start())

        def end():
            own.wait()
            across(0, hi).wait_send()
            for k in range(count):
                there = o_ref.at[low(k) * 2 + 1 - lo]
                remote(there, there, s_pair.at[k], r_pair.at[k], pair).wait_recv()
                if k > 0:
                    across(k, low(k)).wait_send()
            for d in range(count - 1):
                pl.when((hi >= d) & (hi < count - 1))(lambda d=d: up(d).wait_send())
                pl.when((hi + d < count) & (hi > 0))(lambda d=d: down(d).wait_send())

        return start, middle, end

    shape = jax.ShapeDtypeStruct((cn, *x.shape), x.dtype)
    scratch = [dma()] + [dma(count + 1)] * 4 + [dma(count)] * 2
    return (along_ctx, x, shape, ANY, ANY, scratch, body)


def scatter_fsdp(x, parts=4):
    fn = lax.axis_size("fsdp")
    chips = fn // 2
    _, n, d = x.shape
    step = n // parts

    def body(x_ref, o_ref, own, near, mine, far, ss, s_own, s_near, r_near, s_far, r_far):
        f, c = place()
        chip, core = f // 2, lax.rem(f, 2)
        twin = (chip * 2 + 1 - core, c)
        nears, owns, fars, outs = {}, {}, {}, {}

        def chip_at(j):
            return lax.rem(chip + j, chips)

        def start():
            for p in range(parts):
                rows = pl.ds(p * step, step)
                for j in list(range(1, chips)) + [0]:
                    at = chip_at(j) * 2
                    owns[p, j] = pltpu.make_async_copy(
                        x_ref.at[at + core, rows], own.at[j, p], s_own.at[j, p]
                    )
                    owns[p, j].start()
                    nears[p, j] = remote(
                        x_ref.at[at + 1 - core, rows],
                        near.at[j, p],
                        s_near.at[j, p],
                        r_near.at[j, p],
                        twin,
                    )
                    nears[p, j].start()

        def middle():
            for p in range(parts):
                for j in range(1, chips):
                    owns[p, j].wait()
                    nears[p, j].wait_recv()
                    mine[j, p] = (own[j, p].astype(F32) + near[j, p].astype(F32)).astype(BF16)
                    fars[p, j] = remote(
                        mine.at[j, p],
                        far.at[j, p],
                        s_far.at[j, p],
                        r_far.at[j, p],
                        (chip_at(j) * 2 + core, c),
                    )
                    fars[p, j].start()
            for p in range(parts):
                owns[p, 0].wait()
                nears[p, 0].wait_recv()
                ss[p] = own[0, p].astype(F32) + near[0, p].astype(F32)

        def end():
            for p in range(parts):
                for j in range(1, chips):
                    fars[p, j].wait_recv()
                    ss[p] += far[j, p].astype(F32)
                outs[p] = pltpu.make_async_copy(
                    ss.at[p], o_ref.at[pl.ds(p * step, step)], s_far.at[0, p]
                )
                outs[p].start()
            for p in range(parts):
                outs[p].wait()
                for j in range(chips):
                    nears[p, j].wait_send()
                for j in range(1, chips):
                    fars[p, j].wait_send()

        return start, middle, end

    block = pltpu.VMEM((chips, parts, step, d), BF16)
    scratch = [block] * 4 + [pltpu.VMEM((parts, step, d), F32)] + [dma(chips, parts)] * 5
    return (links_and_twin, x, jax.ShapeDtypeStruct((n, d), F32), ANY, ANY, scratch, body)


def plane_others():
    fn = lax.axis_size("fsdp")
    f, c = place()
    (pair,) = the_pair()
    return [(lax.rem(f + a, fn), (c, pair[1])[b]) for a in range(fn) for b in range(2) if a or b]


def plane_sides():
    return [t for i, t in enumerate(plane_others()) if i > 0]


def exchange_plane(x, peers):
    fn = lax.axis_size("fsdp")

    def body(x_ref, o_ref, s, r, own):
        f, c = place()
        lo = lax.rem(c, 2)
        (pair,) = the_pair()

        def index(a, b):
            return lax.rem(f + a + fn, fn), (lo if b == 0 else 1 - lo)

        def copy(a, b, slot):
            fa, lb = index(a, b)
            return remote(
                x_ref.at[fa, lb],
                o_ref.at[slot[0], slot[1]],
                s.at[a, b],
                r.at[a, b],
                (fa, c if b == 0 else pair[1]),
            )

        steps = [(a, b) for a in range(fn) for b in range(2) if a or b]
        mine = pltpu.make_async_copy(x_ref.at[f, lo], o_ref.at[f, lo], own)

        def start():
            for a, b in steps:
                copy(a, b, (f, lo)).start()
            mine.start()

        def end():
            mine.wait()
            for a, b in steps:
                copy(a, b, index(-a, b)).wait_recv()
            for a, b in steps:
                copy(a, b, (f, lo)).wait_send()

        return start, lambda: None, end

    shape = jax.ShapeDtypeStruct(x.shape, x.dtype)
    return (peers, x, shape, ANY, ANY, [dma(fn, 2), dma(fn, 2), dma()], body)


def exchange_columns(x, wide, peers):
    fn = lax.axis_size("fsdp")
    _, _, rows, cols = x.shape
    count = cols // wide

    def body(x_ref, o_ref, s, r, own):
        f, c = place()
        lo = lax.rem(c, 2)
        (pair,) = the_pair()

        def index(a, b):
            return lax.rem(f + a + fn, fn), (lo if b == 0 else 1 - lo)

        def target(slot, h):
            at = ((slot[0] * count + h) * 2 + slot[1]) * wide
            return o_ref.at[:, pl.ds(pl.multiple_of(at, wide), wide)]

        def copy(a, b, h, slot):
            fa, lb = index(a, b)
            return remote(
                x_ref.at[fa, lb, :, pl.ds(h * wide, wide)],
                target(slot, h),
                s.at[a, b, h],
                r.at[a, b, h],
                (fa, c if b == 0 else pair[1]),
            )

        steps = [
            (a, b, h) for a in range(fn) for b in range(2) for h in range(count) if a or b
        ]
        mine = [
            pltpu.make_async_copy(
                x_ref.at[f, lo, :, pl.ds(h * wide, wide)], target((f, lo), h), own.at[h]
            )
            for h in range(count)
        ]

        def start():
            for a, b, h in steps:
                copy(a, b, h, (f, lo)).start()
            for m in mine:
                m.start()

        def end():
            for m in mine:
                m.wait()
            for a, b, h in steps:
                copy(a, b, h, index(-a, b)).wait_recv()
            for a, b, h in steps:
                copy(a, b, h, (f, lo)).wait_send()

        return start, lambda: None, end

    shape = jax.ShapeDtypeStruct((rows, fn * 2 * cols), x.dtype)
    scratch = [dma(fn, 2, count), dma(fn, 2, count), dma(count)]
    return (peers, x, shape, ANY, ANY, scratch, body)


def links_twin_pair():
    return links_and_twin() + the_pair()


def gather_plane(x, parts=8):
    fn = lax.axis_size("fsdp")
    chips = fn // 2
    n, d = x.shape
    step = n // parts
    first, second = list(range(parts // 2)), list(range(parts // 2, parts))
    others = list(range(1, chips))

    def body(x_ref, o_ref, own_sem, sx, rx, sy, ry, st, rt):
        f, c = place()
        chip, core, lo = f // 2, lax.rem(f, 2), lax.rem(c, 2)
        twin = (chip * 2 + 1 - core, c)
        (pair,) = the_pair()

        def rows(p):
            return pl.ds(p * step, step)

        def block(j, core_id, kind, p):
            slot = lax.rem(chip + chips - j, chips) * 2 + core_id
            return o_ref.at[slot, lo if kind == 0 else 1 - lo, rows(p)]

        def source(j, kind, p):
            return x_ref.at[rows(p)] if j == 0 and kind == 0 else block(j, core, kind, p)

        def to(j):
            return (lax.rem(chip + j, chips) * 2 + core, c)

        def x_copy(j, kind, p):
            return remote(
                source(0, kind, p), block(0, core, kind, p), sx.at[j, kind, p], rx.at[j, kind, p], to(j)
            )

        def y_copy(j, p):
            return remote(source(j, 0, p), block(j, core, 0, p), sy.at[j, p], ry.at[j, p], pair)

        def t_copy(j, kind, p):
            return remote(
                source(j, kind, p), block(j, core, kind, p), st.at[j, kind, p], rt.at[j, kind, p], twin
            )

        def x_come(j, kind, p):
            here = block(j, core, kind, p)
            remote(here, here, sx.at[j, kind, p], rx.at[j, kind, p], to(j)).wait_recv()

        def y_come(j, p):
            here = block(j, core, 1, p)
            remote(here, here, sy.at[j, p], ry.at[j, p], pair).wait_recv()

        own = pltpu.make_async_copy(x_ref, o_ref.at[f, lo], own_sem)

        def start():
            for p in first:
                for j in others:
                    x_copy(j, 0, p).start()
            for p in second + first:
                y_copy(0, p).start()
            for p in second:
                for j in others:
                    x_copy(j, 0, p).start()
            for p in range(parts):
                t_copy(0, 0, p).start()
            own.start()

        def middle():
            for p, q in zip(first, second, strict=True):
                for j in others:
                    x_come(j, 0, p)
                    y_copy(j, p).start()
                    t_copy(j, 0, p).start()
                y_come(0, q)
                for j in others:
                    x_copy(j, 1, q).start()
                t_copy(0, 1, q).start()
            for p, q in zip(first, second, strict=True):
                y_come(0, p)
                t_copy(0, 1, p).start()
                for j in others:
                    x_come(j, 0, q)
                    t_copy(j, 0, q).start()

        def end():
            for p, q in zip(first, second, strict=True):
                for j in others:
                    y_come(j, p)
                    t_copy(j, 1, p).start()
                    x_come(j, 1, q)
                    t_copy(j, 1, q).start()
            own.wait()
            for p in range(parts):
                for j in range(chips):
                    for kind in range(2):
                        there = block(j, 1 - core, kind, p)
                        remote(
                            there, there, st.at[j, kind, p], rt.at[j, kind, p], twin
                        ).wait_recv()
                        t_copy(j, kind, p).wait_send()
                y_copy(0, p).wait_send()
                for j in others:
                    x_copy(j, 0, p).wait_send()
            for p, q in zip(first, second, strict=True):
                for j in others:
                    y_copy(j, p).wait_send()
                    x_copy(j, 1, q).wait_send()

        return start, middle, end

    shape = jax.ShapeDtypeStruct((fn, 2, n, d), x.dtype)
    scratch = [dma()] + [dma(chips, 2, parts)] * 2 + [dma(chips, parts)] * 2
    scratch = scratch + [dma(chips, 2, parts)] * 2
    return (links_twin_pair, x, shape, ANY, ANY, scratch, body)


def scatter_plane(x, parts=4):
    fn = lax.axis_size("fsdp")
    chips = fn // 2
    _, _, n, d = x.shape
    step = n // parts
    half = parts // 2
    others = list(range(1, chips))

    def body(
        x_ref, o_ref, own, near, send1, come_y, send_x, come_x, come_x2, send_y, come_y2, acc,
        s_own, s_near, r_near, s_1, r_y, r_x, s_2, r_x2, s_3, r_y2, s_out,
    ):
        f, c = place()
        chip, core, lo = f // 2, lax.rem(f, 2), lax.rem(c, 2)
        twin = (chip * 2 + 1 - core, c)
        (pair,) = the_pair()

        def chip_at(j):
            return lax.rem(chip + j, chips)

        def to(j):
            return (chip_at(j) * 2 + core, c)

        def part(j, core_id, kind, p):
            return x_ref.at[
                chip_at(j) * 2 + core_id, lo if kind == 0 else 1 - lo, pl.ds(p * step, step)
            ]

        def own_copy(j, k, p):
            return pltpu.make_async_copy(part(j, core, k, p), own.at[j, k, p], s_own.at[j, k, p])

        def near_copy(j, k, p):
            return remote(
                part(j, 1 - core, k, p), near.at[j, k, p], s_near.at[j, k, p], r_near.at[j, k, p], twin
            )

        def both(j, k, p):
            return own[j, k, p].astype(F32) + near[j, k, p].astype(F32)

        def ready(j, k, p):
            own_copy(j, k, p).wait()
            near_copy(j, k, p).wait_recv()

        def y_first(j, p):
            return remote(send1.at[j, 1, p], come_y.at[j, p], s_1.at[j, 1, p], r_y.at[j, p], pair)

        def x_first(j, k, p):
            q = p - half
            return remote(
                send1.at[j, k, p], come_x.at[j, k, q], s_1.at[j, k, p], r_x.at[j, k, q], to(j)
            )

        def x_then(j, p):
            return remote(send_x.at[j, p], come_x2.at[j, p], s_2.at[j, p], r_x2.at[j, p], to(j))

        def y_then(q):
            return remote(send_y.at[q], come_y2.at[q], s_3.at[q], r_y2.at[q], pair)

        def out(p):
            return pltpu.make_async_copy(acc.at[p], o_ref.at[pl.ds(p * step, step)], s_out.at[p])

        order = [(j, k, i) for i in range(half) for j in others + [0] for k in (1, 0)]

        def start():
            for j, k, i in order:
                for p in (i, i + half):
                    own_copy(j, k, p).start()
                    near_copy(j, k, p).start()

        def middle():
            for i in range(half):
                for j in range(chips):
                    ready(j, 1, i)
                    send1[j, 1, i] = both(j, 1, i).astype(BF16)
                    y_first(j, i).start()
                for j in others:
                    for k in (1, 0):
                        ready(j, k, i + half)
                        send1[j, k, i + half] = both(j, k, i + half).astype(BF16)
                        x_first(j, k, i + half).start()
            for i in range(half):
                for j in range(chips):
                    ready(j, 0, i)
                for k in range(2):
                    ready(0, k, i + half)

        def end():
            for i in range(half):
                for j in others:
                    y_first(j, i).wait_recv()
                    send_x[j, i] = (both(j, 0, i) + come_y[j, i].astype(F32)).astype(BF16)
                    x_then(j, i).start()
                total = both(0, 1, i + half)
                for j in others:
                    x_first(j, 1, i + half).wait_recv()
                    total += come_x[j, 1, i].astype(F32)
                send_y[i] = total.astype(BF16)
                y_then(i).start()
            for i in range(half):
                y_first(0, i).wait_recv()
                acc[i] = both(0, 0, i) + come_y[0, i].astype(F32)
                acc[i + half] = both(0, 0, i + half)
                for j in others:
                    x_first(j, 0, i + half).wait_recv()
                    acc[i + half] += come_x[j, 0, i].astype(F32)
            for i in range(half):
                for j in others:
                    x_then(j, i).wait_recv()
                    acc[i] += come_x2[j, i].astype(F32)
                out(i).start()
                y_then(i).wait_recv()
                acc[i + half] += come_y2[i].astype(F32)
                out(i + half).start()
            for i in range(half):
                out(i).wait()
                out(i + half).wait()
                y_then(i).wait_send()
                for j in others:
                    x_then(j, i).wait_send()
                    for k in range(2):
                        x_first(j, k, i + half).wait_send()
                for j in range(chips):
                    y_first(j, i).wait_send()
                    for k in range(2):
                        near_copy(j, k, i).wait_send()
                        near_copy(j, k, i + half).wait_send()

        return start, middle, end

    def buffer(*lead):
        return pltpu.VMEM((*lead, step, d), BF16)

    scratch = [
        buffer(chips, 2, parts),
        buffer(chips, 2, parts),
        buffer(chips, 2, parts),
        buffer(chips, half),
        buffer(chips, half),
        buffer(chips, 2, half),
        buffer(chips, half),
        buffer(half),
        buffer(half),
        pltpu.VMEM((parts, step, d), F32),
        dma(chips, 2, parts),
        dma(chips, 2, parts),
        dma(chips, 2, parts),
        dma(chips, 2, parts),
        dma(chips, half),
        dma(chips, 2, half),
        dma(chips, half),
        dma(chips, half),
        dma(half),
        dma(half),
        dma(parts),
    ]
    return (links_twin_pair, x, jax.ShapeDtypeStruct((n, d), F32), ANY, ANY, scratch, body)


def nobody():
    return []


def product_beside(x, g, groups, lines, tile=512):
    n, d = g.shape
    block = x.shape[1] // groups
    r = block // lines

    def body(x_ref, g_ref, o_ref, xs, gs, turned, ys, s_x, s_g, s_y):
        def x_copy(i):
            at = pl.ds(pl.multiple_of(i * block, block), block)
            return pltpu.make_async_copy(x_ref.at[:, at], xs.at[i], s_x.at[i])

        def y_copy(i):
            return pltpu.make_async_copy(ys.at[i], o_ref.at[:, i], s_y.at[i])

        g_copy = pltpu.make_async_copy(g_ref, gs, s_g)

        def start():
            g_copy.start()
            for i in range(groups):
                x_copy(i).start()

        def middle():
            g_copy.wait()

            def one(i, _):
                x_copy(i).wait()
                turned[...] = xs[i].T
                for j in range(0, d, tile):
                    cut = slice(j, j + tile)
                    y = nn(turned[...], gs[:, cut]).astype(BF16)
                    ys[i, :, :, cut] = y.reshape(lines, r, tile)
                y_copy(i).start()
                return 0

            lax.fori_loop(0, groups, one, 0)

        def end():
            for i in range(groups):
                y_copy(i).wait()

        return start, middle, end

    shape = jax.ShapeDtypeStruct((lines, groups, r, d), BF16)
    scratch = [
        pltpu.VMEM((groups, n, block), BF16),
        pltpu.VMEM((n, d), BF16),
        pltpu.VMEM((block, n), BF16),
        pltpu.VMEM((groups, lines, r, d), BF16),
        dma(groups),
        dma(),
        dma(groups),
    ]
    return (nobody, (x, g), shape, ANY, ANY, scratch, body)


def scatter_small(x):
    fn, cn = lax.axis_size("fsdp"), lax.axis_size("ctx")

    def body(x_ref, o_ref, got, sums, got2, s1, r1, s2, r2):
        f, c = place()

        def first(j):
            t = lax.rem(f + j, fn)
            return remote(x_ref.at[t], got.at[j], s1.at[j], r1.at[j], (t, c))

        def second(j):
            t = lax.rem(c + j, cn)
            return remote(sums.at[t], got2.at[j], s2.at[j], r2.at[j], (f, t))

        def start():
            for j in range(1, fn):
                first(j).start()
            sums[...] = x_ref[f]

        def middle():
            for j in range(1, fn):
                first(j).wait_recv()
                sums[...] += got[j]
            for j in range(1, cn):
                second(j).start()
            o_ref[...] = sums[c]

        def end():
            for j in range(1, cn):
                second(j).wait_recv()
                o_ref[...] += got2[j]
            for j in range(1, fn):
                first(j).wait_send()
            for j in range(1, cn):
                second(j).wait_send()

        return start, middle, end

    tail = x.shape[2:]
    scratch = [
        pltpu.VMEM(x.shape, x.dtype),
        pltpu.VMEM(x.shape[1:], x.dtype),
        pltpu.VMEM(x.shape[1:], x.dtype),
        dma(fn),
        dma(fn),
        dma(cn),
        dma(cn),
    ]
    return (along_both, x, jax.ShapeDtypeStruct(tail, x.dtype), VMEM, VMEM, scratch, body)


def nt(a, b):
    return lax.dot_general(a, b, (((1,), (1,)), ((), ())), preferred_element_type=F32)


def nn(a, b):
    return lax.dot_general(a, b, (((1,), (0,)), ((), ())), preferred_element_type=F32)


def attend(q, k, v, starts, block=512):
    u, t, _ = q.shape
    scale = HEAD_DIM**-0.5 * LOG2E

    def kernel(q_ref, k_ref, v_ref, s_ref, o_ref, l_ref, vt):
        i = pl.program_id(1)

        @pl.when(i == 0)
        def _():
            vt[...] = v_ref[0].T

        rows = q_ref[0]
        first = s_ref[0]
        base = lax.broadcasted_iota(jnp.int32, (block, block), 0)
        qpos = i * block + lax.broadcasted_iota(jnp.int32, (1, block), 1)

        def one(j, carry, diagonal):
            peak, total, acc = carry
            at = pl.multiple_of(j * block, block)
            s = nt(k_ref[0, pl.ds(at, block)], rows) * scale
            kpos = base + at
            keep = kpos >= first
            if diagonal:
                keep = keep & (kpos <= qpos)
            s = jnp.where(keep, s, NEG_BIG)
            new = jnp.maximum(peak, jnp.max(s, axis=0, keepdims=True))
            p = jnp.exp2(s - new)
            shrink = jnp.exp2(peak - new)
            total = total * shrink + jnp.sum(p, axis=0, keepdims=True)
            acc = acc * shrink + nn(vt[:, pl.ds(at, block)], p.astype(BF16))
            return new, total, acc

        start = (
            jnp.full((1, block), NEG_BIG, F32),
            jnp.zeros((1, block), F32),
            jnp.zeros((HEAD_DIM, block), F32),
        )
        start = one(i, start, True)
        peak, total, acc = lax.fori_loop(0, i, lambda j, c: one(j, c, False), start)
        o_ref[0] = (acc / total).T.astype(BF16)
        l_ref[0] = peak + jnp.log2(total)

    return pl.pallas_call(
        kernel,
        grid=(u, t // block),
        in_specs=[
            pl.BlockSpec((1, block, HEAD_DIM), lambda a, b: (a, b, 0)),
            pl.BlockSpec((1, t, HEAD_DIM), lambda a, b: (a, 0, 0)),
            pl.BlockSpec((1, t, HEAD_DIM), lambda a, b: (a, 0, 0)),
            pl.BlockSpec((1, 1, block), lambda a, b: (a, 0, b)),
        ],
        out_specs=[
            pl.BlockSpec((1, block, HEAD_DIM), lambda a, b: (a, b, 0)),
            pl.BlockSpec((1, 1, block), lambda a, b: (a, 0, b)),
        ],
        out_shape=[
            jax.ShapeDtypeStruct((u, t, HEAD_DIM), BF16),
            jax.ShapeDtypeStruct((u, 1, t), F32),
        ],
        scratch_shapes=[pltpu.VMEM((HEAD_DIM, t), BF16)],
        compiler_params=pltpu.CompilerParams(vmem_limit_bytes=32 * 2**20),
        cost_estimate=pl.CostEstimate(
            flops=2 * u * t * t * HEAD_DIM, bytes_accessed=8 * u * t * 256, transcendentals=u * t * t // 2
        ),
    )(q, k, v, starts)


def attend_back(q, k, v, starts, lse, o, g, tables, block=512):
    u, t, _ = q.shape
    scale = HEAD_DIM**-0.5

    def kernel(
        q_ref, k_ref, v_ref, s_ref, l_ref, o_ref, g_ref, t_ref, dq_ref, dk_ref, dv_ref, kt, dk, dv
    ):
        i = pl.program_id(1)

        @pl.when(i == 0)
        def _():
            kt[...] = k_ref[0].T
            dk[...] = jnp.zeros_like(dk)
            dv[...] = jnp.zeros_like(dv)

        rows, grows = q_ref[0], g_ref[0]
        first, logs = s_ref[0], l_ref[0]
        prod = o_ref[0].astype(F32) * grows.astype(F32)
        centre = jnp.sum(prod.T, axis=0, keepdims=True)
        base = lax.broadcasted_iota(jnp.int32, (block, block), 0)
        qpos = i * block + lax.broadcasted_iota(jnp.int32, (1, block), 1)

        def one(j, acc, diagonal):
            at = pl.multiple_of(j * block, block)
            here = pl.ds(at, block)
            p = jnp.exp2(nt(k_ref[0, here], rows) * (scale * LOG2E) - logs)
            kpos = base + at
            keep = kpos >= first
            if diagonal:
                keep = keep & (kpos <= qpos)
            p = jnp.where(keep, p, 0.0)
            gp = nt(v_ref[0, here], grows)
            ds = (p * (gp - centre)).astype(BF16)
            dv[here] += nn(p.astype(BF16), grows)
            dk[here] += nn(ds, rows)
            return acc + nn(kt[:, here], ds)

        acc = one(i, jnp.zeros((HEAD_DIM, block), F32), True)
        acc = lax.fori_loop(0, i, lambda j, a: one(j, a, False), acc)
        there = pl.ds(pl.multiple_of(i * block, block), block)
        straight, right, left = t_ref[0, there], t_ref[1, there], t_ref[2, there]
        dq_ref[0] = turn((acc * scale).T, straight, -right, -left).astype(BF16)

        @pl.when(i == t // block - 1)
        def _():
            for b in range(t // block):
                at = pl.ds(b * block, block)
                dk_ref[0, at] = turn(
                    dk[at] * scale, t_ref[0, at], -t_ref[1, at], -t_ref[2, at]
                ).astype(BF16)
                dv_ref[0, at] = dv[at].astype(BF16)

    def whole(a, b):
        return (a, 0, 0)

    def part(a, b):
        return (a, b, 0)

    def row(a, b):
        return (a, 0, b)

    spec, full, line = (1, block, HEAD_DIM), (1, t, HEAD_DIM), (1, 1, block)
    return pl.pallas_call(
        kernel,
        grid=(u, t // block),
        in_specs=[
            pl.BlockSpec(spec, part),
            pl.BlockSpec(full, whole),
            pl.BlockSpec(full, whole),
            pl.BlockSpec(line, row),
            pl.BlockSpec(line, row),
            pl.BlockSpec(spec, part),
            pl.BlockSpec(spec, part),
            pl.BlockSpec((3, t, HEAD_DIM), lambda a, b: (0, 0, 0)),
        ],
        out_specs=[
            pl.BlockSpec(spec, part),
            pl.BlockSpec(full, whole),
            pl.BlockSpec(full, whole),
        ],
        out_shape=[jax.ShapeDtypeStruct((u, t, HEAD_DIM), BF16)] * 3,
        scratch_shapes=[
            pltpu.VMEM((HEAD_DIM, t), BF16),
            pltpu.VMEM((t, HEAD_DIM), F32),
            pltpu.VMEM((t, HEAD_DIM), F32),
        ],
        compiler_params=pltpu.CompilerParams(vmem_limit_bytes=48 * 2**20),
        cost_estimate=pl.CostEstimate(
            flops=5 * u * t * t * HEAD_DIM, bytes_accessed=20 * u * t * 256, transcendentals=u * t * t // 2
        ),
    )(q, k, v, starts, lse, o, g, tables)


def project(x, w, stream, bias, tables):
    count, length, width = x.shape
    cn, fn, _, rows, cols = w.shape
    heads = cols // HEAD_DIM

    def kernel(*refs):
        x_ref, w_ref, b_ref = refs[:3]
        o_ref, held, sem = refs[-3:]

        @pl.when(pl.program_id(0) == 0)
        def _():
            copies = [
                pltpu.make_async_copy(w_ref.at[:, f, stream], held.at[f], sem.at[f])
                for f in range(fn)
            ]
            for c in copies:
                c.start()
            for c in copies:
                c.wait()

        y = nn(x_ref[0], held[...].reshape(width, cols)) + b_ref[...]
        for h in range(heads):
            part = y[:, h * HEAD_DIM : (h + 1) * HEAD_DIM]
            if tables is not None:
                t_ref = refs[3]
                part = turn(part, t_ref[0], t_ref[1], t_ref[2])
            o_ref[h] = part.astype(BF16)

    extra = [] if tables is None else [tables]
    return pl.pallas_call(
        kernel,
        grid=(count,),
        in_specs=[
            pl.BlockSpec((1, length, width), lambda i: (i, 0, 0)),
            ANY,
            pl.BlockSpec((1, cols), lambda i: (0, 0)),
        ]
        + [pl.BlockSpec((3, length, HEAD_DIM), lambda i: (0, 0, 0)) for _ in extra],
        out_specs=pl.BlockSpec((heads, length, HEAD_DIM), lambda i: (i, 0, 0)),
        out_shape=jax.ShapeDtypeStruct((count * heads, length, HEAD_DIM), BF16),
        scratch_shapes=[pltpu.VMEM((fn, cn, rows, cols), BF16), dma(fn)],
        compiler_params=pltpu.CompilerParams(vmem_limit_bytes=32 * 2**20),
        cost_estimate=pl.CostEstimate(
            flops=2 * count * length * width * cols,
            bytes_accessed=2 * (count * length * (width + cols) + width * cols),
            transcendentals=0,
        ),
    )(x, w, bias, *extra)


def widen(x, w, bias, tile=256, rows_at_once=512):
    n, d = x.shape
    cn, fn, rows, cols = w.shape
    tiles = cols // tile

    def kernel(x_ref, w_ref, b_ref, a_ref, g_ref, o_ref, held, sem):
        i = pl.program_id(0)

        def copy(j, f):
            at = pl.ds(pl.multiple_of(j * tile, tile), tile)
            return pltpu.make_async_copy(w_ref.at[:, f, :, at], held.at[j, f], sem.at[j, f])

        @pl.when(i == 0)
        def _():
            for j in range(tiles):
                for f in range(fn):
                    copy(j, f).start()

        for f in range(fn):
            copy(i, f).wait()
        w_tile = held[i].reshape(d, tile)
        o_ref[...] = w_tile
        for r in range(0, n, rows_at_once):
            part = pl.ds(r, rows_at_once)
            y = nn(x_ref[part], w_tile) + b_ref[...]
            t = y * math.sqrt(0.5)
            below = 0.5 + 0.5 * lax.erf(t)
            a_ref[part] = (y * below).astype(BF16)
            density = jnp.exp(-t * t) * (1.0 / math.sqrt(2.0 * math.pi))
            g_ref[part] = (below + y * density).astype(BF16)

    column = pl.BlockSpec((n, tile), lambda i: (0, i))
    return pl.pallas_call(
        kernel,
        grid=(tiles,),
        in_specs=[
            pl.BlockSpec((n, d), lambda i: (0, 0)),
            ANY,
            pl.BlockSpec((1, tile), lambda i: (0, i)),
        ],
        out_specs=[column, column, pl.BlockSpec((d, tile), lambda i: (0, i))],
        out_shape=[
            jax.ShapeDtypeStruct((n, cols), BF16),
            jax.ShapeDtypeStruct((n, cols), BF16),
            jax.ShapeDtypeStruct((d, cols), BF16),
        ],
        scratch_shapes=[pltpu.VMEM((tiles, fn, cn, rows, tile), BF16), dma(tiles, fn)],
        compiler_params=pltpu.CompilerParams(vmem_limit_bytes=48 * 2**20),
        cost_estimate=pl.CostEstimate(
            flops=2 * n * d * cols, bytes_accessed=60_000_000, transcendentals=0
        ),
    )(x, w, bias)


def line_product(x, g, groups, lines, tile=512, shelf=None):
    n, d = g.shape
    block = x.shape[1] // groups
    r = block // lines
    tile = min(tile, d)
    held, first, count = shelf or (None, 0, groups)

    def kernel(x_ref, g_ref, *refs):
        o_ref, turned = refs[-2:]

        @pl.when(pl.program_id(1) == 0)
        def _():
            turned[...] = x_ref[...].T

        y = nn(turned[...], g_ref[...]).astype(BF16)
        o_ref[:, 0] = y.reshape(lines, r, tile)

    extra = [] if held is None else [held]
    return pl.pallas_call(
        kernel,
        grid=(groups, d // tile),
        in_specs=[
            pl.BlockSpec((n, block), lambda i, j: (0, i)),
            pl.BlockSpec((n, tile), lambda i, j: (0, j)),
        ]
        + [ANY] * len(extra),
        out_specs=pl.BlockSpec((lines, 1, r, tile), lambda i, j: (0, first + i, 0, j)),
        out_shape=jax.ShapeDtypeStruct((lines, count, r, d), BF16),
        scratch_shapes=[pltpu.VMEM((block, n), BF16)],
        input_output_aliases={2: 0} if extra else {},
        compiler_params=pltpu.CompilerParams(vmem_limit_bytes=48 * 2**20),
        cost_estimate=pl.CostEstimate(
            flops=2 * n * d * x.shape[1],
            bytes_accessed=2 * (n * d + n * x.shape[1] + d * x.shape[1]),
            transcendentals=0,
        ),
    )(x, g, *extra)


def front(hist, mix, gain, shift, tokens=64, wide=128):
    h, n, d = hist.shape
    rest = gain.shape[0]

    def kernel(h_ref, m_ref, g_ref, b_ref, s_ref, *n_refs):
        for start in range(0, tokens, 16):
            t = slice(start, start + 16)
            m = m_ref[t]
            across = [jnp.broadcast_to(m[:, i : i + 1], (16, wide)) for i in range(4 * h)]
            for at in range(0, d, wide):
                cut = slice(at, at + wide)
                rows = [h_ref[j, t, cut].astype(F32) for j in range(h)]
                for s in range(4):
                    acc = across[s * h] * rows[0]
                    for j in range(1, h):
                        acc += across[s * h + j] * rows[j]
                    s_ref[s, t, cut] = acc
            for s in range(rest):
                x = s_ref[s, t]
                centre = x - jnp.mean(x, axis=-1, keepdims=True)
                spread = jnp.mean(centre * centre, axis=-1, keepdims=True)
                y = centre * lax.rsqrt(spread + EPS_NORM) * g_ref[s : s + 1] + b_ref[s : s + 1]
                n_refs[s][t] = y.astype(BF16)

    return pl.pallas_call(
        kernel,
        grid=(n // tokens,),
        in_specs=[
            pl.BlockSpec((h, tokens, d), lambda i: (0, i, 0)),
            pl.BlockSpec((tokens, 128), lambda i: (i, 0)),
            pl.BlockSpec((rest, d), lambda i: (0, 0)),
            pl.BlockSpec((rest, d), lambda i: (0, 0)),
        ],
        out_specs=[
            pl.BlockSpec((4, tokens, d), lambda i: (0, i, 0)),
        ]
        + [pl.BlockSpec((tokens, d), lambda i: (i, 0))] * rest,
        out_shape=[jax.ShapeDtypeStruct((4, n, d), F32)]
        + [jax.ShapeDtypeStruct((n, d), BF16)] * rest,
        compiler_params=pltpu.CompilerParams(vmem_limit_bytes=60 * 2**20),
        cost_estimate=pl.CostEstimate(
            flops=2 * 4 * h * n * d, bytes_accessed=n * d * (2 * h + 22), transcendentals=0
        ),
    )(hist, mix, gain, shift)


def last(hist, mix, streams, gain, grads, grad_hidden, tokens=64, wide=256):
    h, n, d = hist.shape
    rest = gain.shape[0]

    def kernel(h_ref, m_ref, s_ref, g_ref, d0, d1, d2, r_ref, gh_ref, gm_ref, gg_ref, gb_ref, ds):
        @pl.when(pl.program_id(0) == 0)
        def _():
            gg_ref[...] = jnp.zeros_like(gg_ref)
            gb_ref[...] = jnp.zeros_like(gb_ref)

        for start in range(0, tokens, 16):
            t = slice(start, start + 16)
            for s, d_ref in enumerate((d0, d1, d2)):
                x = s_ref[s, t]
                centre = x - jnp.mean(x, axis=-1, keepdims=True)
                inverse = lax.rsqrt(jnp.mean(centre * centre, axis=-1, keepdims=True) + EPS_NORM)
                unit = centre * inverse
                dn = d_ref[t]
                gg_ref[s : s + 1] += jnp.sum(dn * unit, axis=0, keepdims=True)
                gb_ref[s : s + 1] += jnp.sum(dn, axis=0, keepdims=True)
                du = dn * g_ref[s : s + 1]
                ds[s] = inverse * (
                    du
                    - jnp.mean(du, axis=-1, keepdims=True)
                    - unit * jnp.mean(du * unit, axis=-1, keepdims=True)
                )
            ds[rest] = r_ref[t]
            m = m_ref[t]
            across = [jnp.broadcast_to(m[:, i : i + 1], (16, 128)) for i in range(4 * h)]
            sums = [[jnp.zeros((16, 128), F32) for _ in range(h)] for _ in range(4)]
            for at in range(0, d, wide):
                cuts = [slice(b, b + 128) for b in range(at, at + wide, 128)]
                parts = [[ds[s, :, cut] for cut in cuts] for s in range(4)]
                for j in range(h):
                    for i, cut in enumerate(cuts):
                        acc = across[j] * parts[0][i]
                        for s in range(1, 4):
                            acc += across[s * h + j] * parts[s][i]
                        gh_ref[j, t, cut] = acc
                    rows = [h_ref[j, t, cut].astype(F32) for cut in cuts]
                    for s in range(4):
                        prod = rows[0] * parts[s][0]
                        for i in range(1, len(cuts)):
                            prod += rows[i] * parts[s][i]
                        sums[s][j] += prod
            lane = lax.broadcasted_iota(jnp.int32, (16, 128), 1)
            total = jnp.zeros((16, 128), F32)
            for s in range(4):
                for j in range(h):
                    value = jnp.sum(sums[s][j], axis=-1, keepdims=True)
                    total = jnp.where(lane == s * h + j, value, total)
            gm_ref[t] = total

    row = pl.BlockSpec((tokens, d), lambda i: (i, 0))
    lines = pl.BlockSpec((rest, d), lambda i: (0, 0))
    return pl.pallas_call(
        kernel,
        grid=(n // tokens,),
        in_specs=[
            pl.BlockSpec((h, tokens, d), lambda i: (0, i, 0)),
            pl.BlockSpec((tokens, 128), lambda i: (i, 0)),
            pl.BlockSpec((rest, tokens, d), lambda i: (0, i, 0)),
            lines,
            row,
            row,
            row,
            row,
        ],
        out_specs=[
            pl.BlockSpec((h, tokens, d), lambda i: (0, i, 0)),
            pl.BlockSpec((tokens, 128), lambda i: (i, 0)),
            lines,
            lines,
        ],
        out_shape=[
            jax.ShapeDtypeStruct((h, n, d), F32),
            jax.ShapeDtypeStruct((n, 128), F32),
            jax.ShapeDtypeStruct((rest, d), F32),
            jax.ShapeDtypeStruct((rest, d), F32),
        ],
        scratch_shapes=[pltpu.VMEM((4, 16, d), F32)],
        compiler_params=pltpu.CompilerParams(vmem_limit_bytes=60 * 2**20),
        cost_estimate=pl.CostEstimate(
            flops=4 * 4 * h * n * d, bytes_accessed=n * d * (6 * h + 32), transcendentals=0
        ),
    )(hist, mix, streams, gain, *grads, grad_hidden)


def body(
    history,
    dense_mix,
    doc_starts,
    norm_gain,
    norm_bias,
    qkv_weight,
    qkv_bias,
    out_weight,
    out_bias,
    up_weight,
    up_bias,
    down_weight,
    down_bias,
    root_gain,
    mix_in_weight,
    mix_out_weight,
    mix_out_bias,
    out_cotangent,
    mix_cotangent,
):
    fn, cn = lax.axis_size("fsdp"), lax.axis_size("ctx")
    dn = fn * cn
    fi, ci = lax.axis_index("fsdp"), lax.axis_index("ctx")
    hist, seqs, length, width = history.shape
    nloc = seqs * length
    ntp = fn * nloc
    rows = qkv_weight.shape[0]
    ff = up_weight.shape[1]
    wcol, pcol = width // fn, ff // (2 * fn)
    count = cn // 2
    lo = lax.rem(ci, 2)
    lines = [list(range(b, cn, 2)) for b in range(2)]
    heads = wcol // HEAD_DIM
    units = fn * seqs * heads // cn
    total = cn * length
    mixn = mix_in_weight.shape[1]

    def line_gather(w):
        return lax.all_gather(w, "ctx", axis=0, axis_index_groups=lines)

    parts = [
        norm_gain,
        norm_bias,
        qkv_bias,
        out_bias,
        up_bias,
        down_bias,
        root_gain,
        mix_in_weight,
        doc_starts.astype(F32),
    ]
    flat = jnp.concatenate([a.reshape(-1) for a in parts])
    flat = jnp.pad(flat, (0, -flat.size % 1024)).reshape(-1, 128)
    wout = lax.all_gather(out_weight, "ctx", axis=0, tiled=True)
    flats, qkv_cols = comm(
        1,
        gather_small(flat),
        exchange_fsdp(qkv_weight.reshape(rows, 3, fn, wcol).transpose(2, 1, 0, 3)),
    )
    flats = flats.reshape(dn, -1)
    pieces, at = [], 0
    for a in parts:
        pieces.append(flats[:, at : at + a.size])
        at += a.size

    def joined(piece, lead):
        return piece.reshape(dn, lead, -1).transpose(1, 0, 2).reshape(lead, -1)

    gain_all = joined(pieces[0], 4)
    shift_all = joined(pieces[1], 4)
    qkv_shift = joined(pieces[2], 3)
    out_shift = pieces[3].reshape(-1)
    up_shift = pieces[4].reshape(-1)
    down_shift = pieces[5].reshape(-1)
    root_full = pieces[6].reshape(-1)
    mix_in_full = pieces[7].reshape(width, mixn)
    starts = pieces[8].reshape(fn, cn, seqs, -1)[:, 0].astype(jnp.int32)

    hist2 = history.reshape(hist, nloc, width)
    mix2 = dense_mix.reshape(dense_mix.shape[0], hist, nloc)
    mixes = jnp.pad(mix2.reshape(-1, nloc).T, ((0, 0), (0, 128 - mix2.shape[0] * hist)))
    streams, *normed = front(hist2, mixes, gain_all[:3], shift_all[:3])

    bias_cols = lax.dynamic_slice_in_dim(qkv_shift, fi * wcol, wcol, 1)
    tables = rotary_tables(total)
    tables_l = lax.dynamic_slice_in_dim(tables, ci * length, length, 1)

    def projected(x, w, at, s):
        y = project(
            x.reshape(fn * seqs, length, width),
            w,
            at,
            bias_cols[s : s + 1],
            tables_l if s < 2 else None,
        )
        return y.reshape(cn, units, length, HEAD_DIM)

    def whole_units(x):
        return x.reshape(units, total, HEAD_DIM)

    def from_units(x):
        return exchange_ctx(x.reshape(units, cn, length, HEAD_DIM), False)

    def columns(x):
        x = x.reshape(fn * seqs, heads, length, HEAD_DIM)
        return x.transpose(0, 2, 1, 3).reshape(ntp, wcol)

    w01, g0 = comm(9, gather_ctx(qkv_cols[:, :2]), gather_fsdp(normed[0]))
    g0, cols_2, wout = lax.optimization_barrier((g0, qkv_cols[:, 2], wout))
    w2 = lax.all_gather(cols_2, "ctx", axis=0)
    p0 = projected(g0, w01, 0, 0)
    q_u, g1 = comm(4, exchange_ctx(p0, True), gather_fsdp(normed[1]))
    p1 = projected(g1, w01, 1, 1)
    p1, down_rows = lax.optimization_barrier((p1, down_weight))
    wdown = line_gather(down_rows).reshape(pcol, width)
    k_u, g2 = comm(4, exchange_ctx(p1, True), gather_fsdp(normed[2]))
    p2 = projected(g2, w2[:, :, None], 0, 2)
    v_u, up_cols = comm(
        11,
        exchange_ctx(p2, True),
        exchange_plane(
            up_weight.reshape(rows, fn, count, 2, -1).transpose(1, 3, 0, 2, 4).reshape(fn, 2, rows, pcol),
            plane_sides,
        ),
    )
    up_g = line_gather(up_cols).reshape(count, fn, 2 * rows, pcol)
    wqkv = [w.transpose(1, 0, 2, 3).reshape(width, wcol) for w in (w01[:, :, 0], w01[:, :, 1], w2)]
    q_u, k_u, v_u = whole_units(q_u), whole_units(k_u), whole_units(v_u)
    normed_g = [g.reshape(ntp, width) for g in (g0, g1, g2)]

    pos_all = jnp.arange(total, dtype=jnp.int32)
    unit_ids = ci * units + jnp.arange(units, dtype=jnp.int32)
    seq_ids = unit_ids // heads
    unit_starts = starts.reshape(fn * seqs, -1)[seq_ids]
    first_key = jnp.max(
        jnp.where(unit_starts[:, None, :] <= pos_all[None, :, None], unit_starts[:, None, :], 0),
        axis=-1,
    )[:, None, :]
    att_u, lse_u = attend(q_u, k_u, v_u, first_key)
    attended = columns(comm(6, from_units(att_u))[0])
    attended, wdown = lax.optimization_barrier((attended, wdown))

    def scatter_tokens(x):
        return comm(10, scatter_fsdp(x.astype(BF16).reshape(fn, nloc, width)))[0]

    def gather_tokens(x):
        return comm(3, gather_fsdp(x))[0].reshape(ntp, width)

    def scatter_plane_tokens(x):
        return comm(13, scatter_plane(x.astype(BF16).reshape(fn, 2, nloc, width)))[0]

    def gather_plane_tokens(x):
        return comm(14, gather_plane(x))[0].reshape(2 * ntp, width)

    hidden_res = streams[3] + scatter_tokens(dot("nd,de->ne", attended, wout)) + out_shift
    normed_mlp, mid_pull = jax.vjp(layer_norm, hidden_res, gain_all[3], shift_all[3])
    mlp_g = gather_plane_tokens(normed_mlp.astype(BF16))
    up_bias_cols = lax.dynamic_slice(
        up_shift.reshape(fn, count, 2, -1), (fi, 0, lo, 0), (1, count, 1, ff // dn)
    ).reshape(pcol)
    act_low, slope, wup = widen(mlp_g, up_g, up_bias_cols[None])
    result = hidden_res + scatter_plane_tokens(dot("nf,fd->nd", act_low, wdown)) + down_shift
    block_out = result.astype(BF16).reshape(seqs, length, width)

    next_rows, mixer_pull = jax.vjp(
        mixer, result, root_full, mix_in_full, mix_out_weight, mix_out_bias
    )
    next_mix = next_rows.T.reshape(-1, seqs, length)
    grad_result, grad_root, grad_mix_in, grad_mix_out, grad_mix_bias = mixer_pull(
        mix_cotangent.reshape(-1, nloc).T
    )
    grad_result = grad_result + out_cotangent.reshape(nloc, width).astype(F32)

    grad_branch = grad_result.astype(BF16)
    branch_g = gather_plane_tokens(grad_branch)
    grad_down_shift = jnp.sum(grad_branch.astype(F32), axis=0)

    def line_scatter(x):
        y = lax.psum_scatter(
            x.reshape(-1, x.shape[-1]),
            "ctx",
            scatter_dimension=0,
            axis_index_groups=lines,
            tiled=True,
        )
        return y.reshape(x.shape[1:])

    down_part = dot("nf,nd->fd", act_low, branch_g).astype(BF16)
    down_part, wdown = lax.optimization_barrier((down_part, wdown))
    grad_down = line_scatter(down_part.reshape(count, -1, width))
    grad_active = dot("nd,fd->nf", branch_g, wdown)
    grad_upward = (grad_active * slope.astype(F32)).astype(BF16)
    grad_up_shift = jnp.sum(grad_upward.astype(F32), axis=0)
    mlp_part = dot("nf,df->nd", grad_upward, wup).astype(BF16)
    grad_mlp, up_part = comm(
        17,
        scatter_plane(mlp_part.reshape(fn, 2, nloc, width)),
        product_beside(mlp_g, grad_upward, fn, count),
    )
    up_part, grad_mlp = lax.optimization_barrier((up_part, grad_mlp))
    grad_up = line_scatter(up_part.reshape(count, -1, pcol))
    grad_hidden, grad_gain_mid, grad_shift_mid = mid_pull(grad_mlp)
    grad_hidden = grad_hidden + grad_result
    grad_attn = grad_hidden.astype(BF16)
    grad_out_shift = jnp.sum(grad_attn.astype(F32), axis=0)
    attn_g = gather_tokens(grad_attn)
    out_part = dot("nd,ne->de", attended, attn_g).astype(BF16)
    grad_att = dot("ne,de->nd", attn_g, wout).astype(BF16)
    grad_att = grad_att.reshape(fn * seqs, length, heads, HEAD_DIM).transpose(0, 2, 1, 3)
    out_part = out_part.reshape(count, 2, rows, width)
    out_away = lax.dynamic_index_in_dim(out_part, 1 - lo, 1, keepdims=False)
    out_away, grad_att = lax.optimization_barrier((out_away, grad_att))
    g_u, out_come = comm(
        16,
        exchange_ctx(grad_att.reshape(cn, units, length, HEAD_DIM), True),
        exchange_pair(out_away),
    )
    out_half = lax.dynamic_index_in_dim(out_part, lo, 1, keepdims=False).astype(F32)
    out_half = (out_half + out_come.astype(F32)).astype(BF16)
    g_u, grad_down, out_half = lax.optimization_barrier((g_u, grad_down, out_half))

    def ctx_scatter(x):
        return lax.psum_scatter(x, "ctx", scatter_dimension=0, tiled=True)

    grad_out = line_scatter(out_half)

    gq, gk, gv = attend_back(q_u, k_u, v_u, first_key, lse_u, att_u, whole_units(g_u), tables)

    def back_part(p, s):
        return dot("nc,dc->nd", p, wqkv[s]).astype(BF16).reshape(fn, nloc, width)

    grad_up = grad_up.reshape(fn, 2, rows, pcol)
    if ff // dn % 128 == 0:
        gp0, grad_up = comm(12, from_units(gq), exchange_columns(grad_up, ff // dn, plane_sides))
    else:
        gp0, grad_up = comm(12, from_units(gq), exchange_plane(grad_up, plane_sides))
        grad_up = grad_up.reshape(fn, 2, rows, count, -1).transpose(2, 0, 3, 1, 4)
        grad_up = grad_up.reshape(rows, ff)
    gp0 = columns(gp0)
    q_part = line_product(normed_g[0], gp0, fn, cn)
    q_part, gk = lax.optimization_barrier((q_part, gk))
    grad_q = ctx_scatter(q_part.reshape(-1, wcol)).reshape(fn, rows, wcol)
    gp1, gn0 = comm(8, from_units(gk), scatter_fsdp(back_part(gp0, 0)))
    gp1, grad_out = lax.optimization_barrier((gp1, grad_out))
    gp1 = columns(gp1)
    gp2, gn1 = comm(8, from_units(gv), scatter_fsdp(back_part(gp1, 1)))
    gp2 = columns(gp2)
    kv_part = line_product(normed_g[1], gp1, fn, cn, shelf=(None, 0, 2 * fn))
    kv_part = line_product(normed_g[2], gp2, fn, cn, shelf=(kv_part, fn, 2 * fn))
    kv_part, gp2 = lax.optimization_barrier((kv_part, gp2))
    grad_kv = ctx_scatter(kv_part.reshape(-1, wcol)).reshape(2, fn, rows, wcol)
    grad_q, gn2 = comm(
        7,
        exchange_fsdp(grad_q),
        scatter_fsdp(back_part(gp2, 2)),
    )
    grad_proj = (gp0, gp1, gp2)
    grad_qkv_shift = jnp.stack([jnp.sum(g.astype(F32), axis=0) for g in grad_proj])

    grad_history, grad_mix, grad_gain_front, grad_shift_front = last(
        hist2, mixes, streams, gain_all[:3], (gn0, gn1, gn2), grad_hidden
    )
    grad_history = grad_history.reshape(history.shape)
    grad_mix = grad_mix[:, : mix2.shape[0] * hist].T.reshape(dense_mix.shape)

    def own_columns(x, full):
        zero = jnp.zeros((x.shape[0], full), F32)
        return lax.dynamic_update_slice_in_dim(zero, x, fi * x.shape[1], 1)

    lines_14 = [
        grad_gain_front,
        grad_gain_mid[None],
        grad_shift_front,
        grad_shift_mid[None],
        own_columns(grad_qkv_shift, width),
        grad_out_shift[None],
        grad_down_shift[None],
        grad_root[None],
    ]
    lines_14 = jnp.concatenate(lines_14, axis=0)
    up_lines = lax.dynamic_update_slice(
        jnp.zeros((fn, count, 2, ff // dn), F32),
        grad_up_shift.reshape(1, count, 1, -1),
        (fi, 0, lo, 0),
    ).reshape(dn, -1)
    same = jnp.concatenate([grad_mix_out.reshape(-1), grad_mix_bias])
    flat = jnp.concatenate(
        [
            lines_14.reshape(-1, dn, width // dn).transpose(1, 0, 2).reshape(dn, -1),
            up_lines,
            grad_mix_in.reshape(dn, -1),
            jnp.broadcast_to(same[None], (dn, same.size)),
        ],
        axis=1,
    )
    flat = jnp.pad(flat, ((0, 0), (0, -flat.shape[1] % 1024)))
    (small,) = comm(2, scatter_small(flat.reshape(fn, cn, -1, 128)))
    small = small.reshape(-1)
    out_small, at = [], 0
    order = [norm_gain, norm_bias, qkv_bias, out_bias, down_bias, root_gain, up_bias, mix_in_weight]
    for a in order:
        out_small.append(small[at : at + a.size].reshape(a.shape))
        at += a.size
    mix_sums = small[at : at + same.size]
    cut = grad_mix_out.size
    out_small += [mix_sums[:cut].reshape(grad_mix_out.shape), mix_sums[cut:]]
    out_small, grad_kv = lax.optimization_barrier((out_small, grad_kv))
    (g_gain, g_shift, g_qkv_b, g_out_b, g_down_b, g_root, g_up_b, g_mix_in) = out_small[:-2]
    grad_k, grad_v = comm(15, exchange_fsdp(grad_kv[0]), exchange_fsdp(grad_kv[1]))
    grad_qkv = jnp.stack([grad_q, grad_k, grad_v])
    grad_qkv = grad_qkv.transpose(2, 0, 1, 3).reshape(rows, 3, width).astype(F32)
    return (
        block_out,
        next_mix,
        grad_history,
        grad_mix,
        g_gain,
        g_shift,
        grad_qkv,
        g_qkv_b,
        grad_out.astype(F32),
        g_out_b,
        grad_up.astype(F32),
        g_up_b,
        grad_down.astype(F32),
        g_down_b,
        g_root,
        g_mix_in,
        out_small[-2],
        out_small[-1],
    )


def solution(mesh):
    token = P(None, "fsdp", "ctx")
    both = P(BOTH)
    cols = P(None, BOTH)
    placed = (
        token,
        P(None, None, "fsdp", "ctx"),
        P("fsdp"),
        cols,
        cols,
        both,
        cols,
        both,
        both,
        both,
        both,
        both,
        both,
        both,
        both,
        P(),
        P(),
        P("fsdp", "ctx"),
        token,
    )
    outs = (
        P("fsdp", "ctx"),
        token,
        token,
        P(None, None, "fsdp", "ctx"),
        cols,
        cols,
        both,
        cols,
        both,
        both,
        both,
        both,
        both,
        both,
        both,
        both,
        P(),
        P(),
    )
    return jax.shard_map(body, mesh=mesh, in_specs=placed, out_specs=outs, check_vma=False)
```
